128 devices in a mesh: ctx: 32 (over y, z, core), tp: 4 (over x).
Axes of the slice: x: 4, y: 4, z: 4, core: 2. Of those that a mesh axis runs over, the one named last changes fastest.
Arguments:
- tokens: bfloat16 [8192, 5120], P('ctx', 'tp'), may hold values from -6 to 6
- span_order: int32 [64], replicated, may hold values from 0 to 63, as said below
- w_query: bfloat16 [5120, 2560], P(None, 'tp'), may hold values from -0.2795085 to 0.2795085
- w_key: bfloat16 [5120, 512], P(None, 'tp'), may hold values from -0.2795085 to 0.2795085
- value_weight: bfloat16 [5120, 512], P(None, 'tp'), may hold values from -0.078125 to 0.078125
- w_out: bfloat16 [2560, 5120], P('tp'), may hold values from -0.125 to 0.125
- gain_query: float32 [2560], P('tp'), may hold values from 0.5 to 6
- gain_key: float32 [512], P('tp'), may hold values from 0.5 to 6
- out_grad: bfloat16 [8192, 5120], P('ctx', 'tp'), may hold values from -6 to 6
Outputs:
- attn_out: bfloat16 [8192, 5120], P('ctx', 'tp')
- input_grad: bfloat16 [8192, 5120], P('ctx', 'tp')
- gain_query_grad: float32 [2560], P('tp')
- gain_key_grad: float32 [512], P('tp')
The draws below stay inside these ranges and needn't reach their ends.
Inputs may be any that keep to these rules, and one draw needn't show every extreme that they name: `span_order`: entries 2 i and 2 i + 1 are c and 63 - c for some c, in either order; every span number appears once.
All inputs are finite; a program needn't handle non-finite values.
Results may differ from the reference program's by a relative error of at most 0.034.
The reference program's roundings to bfloat16 on the way count: a program that leaves them out, or rounds other values in their place, can miss the bound.
Values may be sent and summed in bfloat16 or wider, within the bound.
No kernel may reach another device: no remote copies, remote signals or barrier semaphores. Data moves between devices by JAX's collectives and lax.ppermute only.
A program may use at most 128 MiB of HBM per device.

```python
import math
import jax
import jax.numpy as jnp
from jax import lax

MODEL_WIDTH = 5120
QUERY_HEADS = 20
KEY_VALUE_HEADS = 4
HEAD_SIZE = 128
TOKENS = 8192
N_CTX = 32


def scaled_head(key, row_count, head_count, spread):
    entry_key, scale_key = jax.random.split(key)
    entries = jax.random.truncated_normal(entry_key, -4.0, 4.0, (row_count, head_count, HEAD_SIZE), jnp.float32) * row_count ** (-0.5)
    scales = jnp.exp(jax.random.uniform(scale_key, (head_count,), jnp.float32, -spread, spread))
    return (entries * scales[None, :, None]).reshape(row_count, head_count * HEAD_SIZE)


def draw_span_order(key, part):
    key = jax.random.fold_in(key, 11)
    pick_key, flip_key = jax.random.split(key)
    lower = jax.random.permutation(pick_key, N_CTX).astype(jnp.int32)
    flips = jax.random.randint(flip_key, (N_CTX,), 0, 2).astype(jnp.int32)
    upper = 2 * N_CTX - 1 - lower
    leading = jnp.where(flips == 1, upper, lower)
    trailing = jnp.where(flips == 1, lower, upper)
    return jnp.stack([leading, trailing], axis=1).reshape(-1).astype(jnp.int32)


def draw_w_query(key, part):
    key = jax.random.fold_in(key, 21)
    return scaled_head(key, MODEL_WIDTH, QUERY_HEADS, 1.15).astype(jnp.bfloat16)


def draw_w_key(key, part):
    key = jax.random.fold_in(key, 22)
    return scaled_head(key, MODEL_WIDTH, KEY_VALUE_HEADS, 1.15).astype(jnp.bfloat16)


def draw_gain_query(key, part):
    key = jax.random.fold_in(key, 31)
    return jnp.exp(jax.random.uniform(key, (QUERY_HEADS * HEAD_SIZE,), jnp.float32, math.log(0.5), math.log(2.0)))


def draw_gain_key(key, part):
    key = jax.random.fold_in(key, 32)
    return jnp.exp(jax.random.uniform(key, (KEY_VALUE_HEADS * HEAD_SIZE,), jnp.float32, math.log(0.5), math.log(2.0)))


def shard_levels(key, dims, pieces, smallest, largest):
    loudness = 1.0
    for dim, shards_of in pieces:
        heights = jax.random.uniform(jax.random.fold_in(jax.random.fold_in(key, 6), dim), (shards_of,), jnp.float32, smallest / len(pieces), largest / len(pieces))
        loudness = loudness * jnp.repeat(jnp.exp(heights), dims[dim] // shards_of).reshape((-1,) + (1,) * (len(dims) - 1 - dim))
    return loudness


def noise(own_key, dims, scale, limit, shards=(), kind=jnp.bfloat16):
    array = jax.random.normal(own_key, dims, jnp.float32) * scale
    if len(shards) > 0:
        array = shard_levels(own_key, dims, shards, -0.22, 0.18) * array
    return jnp.clip(array, min=-limit, max=limit).astype(kind)


def setup_inputs(seed: int = 0) -> dict:
    keys = jax.random.split(jax.random.key(seed), 10)
    return {
        "tokens": noise(keys[0], (TOKENS, MODEL_WIDTH), 1.0, 6.0, ((0, 32), (1, 4))),
        "span_order": draw_span_order(jax.random.fold_in(keys[9], 71), 0),
        "w_query": draw_w_query(jax.random.fold_in(keys[9], 71), 0),
        "w_key": draw_w_key(jax.random.fold_in(keys[9], 71), 0),
        "value_weight": noise(keys[4], (MODEL_WIDTH, KEY_VALUE_HEADS * HEAD_SIZE), MODEL_WIDTH ** -0.5, 0.078125, ((1, 4),)),
        "w_out": noise(keys[5], (QUERY_HEADS * HEAD_SIZE, MODEL_WIDTH), (QUERY_HEADS * HEAD_SIZE) ** -0.5, 0.125, ((0, 4),)),
        "gain_query": draw_gain_query(jax.random.fold_in(keys[9], 71), 0),
        "gain_key": draw_gain_key(jax.random.fold_in(keys[9], 71), 0),
        "out_grad": noise(keys[8], (TOKENS, MODEL_WIDTH), 1.0, 6.0, ((0, 32), (1, 4))),
    }


def apply_rotary(vectors, token_position, turn_sign):
    half_dim = vectors.shape[-1] // 2
    freq_index = jnp.arange(half_dim).astype(jnp.float32)
    frequency = jnp.exp(freq_index * (-2.0 * math.log(500000.0) / vectors.shape[-1]))
    angles = token_position.astype(jnp.float32)[:, None] * frequency[None, :]
    cosine = jnp.cos(angles)[:, None, :]
    sine_part = turn_sign * jnp.sin(angles)[:, None, :]
    first_half = vectors[..., :half_dim]
    second_half = vectors[..., half_dim:]
    return jnp.concatenate([first_half * cosine - second_half * sine_part, second_half * cosine + first_half * sine_part], axis=-1)

def normalize(raw_proj, gain_vec):
    inv_norm = lax.rsqrt(lax.optimization_barrier(jnp.mean(raw_proj * raw_proj, axis=-1, keepdims=True)) + 1e-06)
    unit_rows = raw_proj * inv_norm
    return (unit_rows, inv_norm, unit_rows * gain_vec)

def norm_back(grad_in, unit_rows, inv_norm, gain_vec):
    upstream = grad_in * gain_vec
    mixing = lax.optimization_barrier(jnp.mean(upstream * unit_rows, axis=-1, keepdims=True))
    return (inv_norm * (upstream - unit_rows * mixing)).astype(jnp.bfloat16)

def reference(tokens, span_order, w_query, w_key, value_weight, w_out, gain_query, gain_key, out_grad):
    token_count = tokens.shape[0]
    span_len = token_count // span_order.shape[0]
    heads_per_group = QUERY_HEADS // KEY_VALUE_HEADS
    score_scale = HEAD_SIZE ** (-0.5)
    offsets = jnp.arange(span_len).astype(jnp.int32)
    token_position = (span_order.astype(jnp.int32)[:, None] * span_len + offsets[None, :]).reshape(-1)
    query_raw = jnp.dot(tokens, w_query, preferred_element_type=jnp.float32)
    key_raw = jnp.dot(tokens, w_key, preferred_element_type=jnp.float32)
    value_row_block = jnp.dot(tokens, value_weight, preferred_element_type=jnp.float32).astype(jnp.bfloat16)
    head_grad = jnp.dot(out_grad, w_out.T, preferred_element_type=jnp.float32).astype(jnp.bfloat16)
    query_unit, query_inv, query_normed = normalize(query_raw, gain_query)
    key_unit_rows, key_inverse_norm, key_after_norm = normalize(key_raw, gain_key)
    query_rotated = apply_rotary(query_normed.reshape(token_count, QUERY_HEADS, HEAD_SIZE), token_position, 1.0).astype(jnp.bfloat16)
    key_rotated = apply_rotary(key_after_norm.reshape(token_count, KEY_VALUE_HEADS, HEAD_SIZE), token_position, 1.0).astype(jnp.bfloat16)
    causal = token_position[None, :] <= token_position[:, None]

    def per_head(head_items):
        head_query, head_key, head_value, head_dout = head_items
        scores = jnp.dot(head_query, head_key.T, preferred_element_type=jnp.float32) * score_scale
        scores = jnp.where(causal, scores, -1e+30)
        row_max = lax.optimization_barrier(jnp.max(scores, axis=-1, keepdims=True))
        unnorm = jnp.exp(scores - row_max)
        row_total = lax.optimization_barrier(jnp.sum(unnorm, axis=-1, keepdims=True))
        head_out = (jnp.dot(unnorm.astype(jnp.bfloat16), head_value, preferred_element_type=jnp.float32) / row_total).astype(jnp.bfloat16)
        probability = unnorm / row_total
        row_delta = lax.optimization_barrier(jnp.sum(head_dout.astype(jnp.float32) * head_out.astype(jnp.float32), axis=-1, keepdims=True))
        prob_grad = jnp.dot(head_dout, head_value.T, preferred_element_type=jnp.float32)
        score_gradient = (probability * (prob_grad - row_delta)).astype(jnp.bfloat16)
        query_part = jnp.dot(score_gradient, head_key, preferred_element_type=jnp.float32) * score_scale
        key_part = jnp.dot(score_gradient.T, head_query, preferred_element_type=jnp.float32) * score_scale
        value_part = jnp.dot(probability.astype(jnp.bfloat16).T, head_dout, preferred_element_type=jnp.float32)
        return (head_out, query_part, key_part, value_part)
    query_heads = query_rotated.transpose(1, 0, 2)
    key_heads = jnp.repeat(key_rotated, heads_per_group, axis=1).transpose(1, 0, 2)
    value_head_rows = jnp.repeat(value_row_block.reshape(token_count, KEY_VALUE_HEADS, HEAD_SIZE), heads_per_group, axis=1).transpose(1, 0, 2)
    dout_heads = head_grad.reshape(token_count, QUERY_HEADS, HEAD_SIZE).transpose(1, 0, 2)
    head_outs, query_parts, key_slices, value_slices = lax.map(per_head, (query_heads, key_heads, value_head_rows, dout_heads))
    attended = head_outs.transpose(1, 0, 2).reshape(token_count, QUERY_HEADS * HEAD_SIZE)
    attn_out = jnp.dot(attended, w_out, preferred_element_type=jnp.float32).astype(jnp.bfloat16)
    key_running_sum = lax.optimization_barrier(jnp.sum(key_slices.reshape(KEY_VALUE_HEADS, heads_per_group, token_count, HEAD_SIZE), axis=1)).transpose(1, 0, 2)
    value_running_sum = lax.optimization_barrier(jnp.sum(value_slices.reshape(KEY_VALUE_HEADS, heads_per_group, token_count, HEAD_SIZE), axis=1)).transpose(1, 0, 2)
    value_gradient = value_running_sum.reshape(token_count, KEY_VALUE_HEADS * HEAD_SIZE).astype(jnp.bfloat16)
    query_grad = apply_rotary(query_parts.transpose(1, 0, 2), token_position, -1.0).reshape(token_count, QUERY_HEADS * HEAD_SIZE)
    key_gradient = apply_rotary(key_running_sum, token_position, -1.0).reshape(token_count, KEY_VALUE_HEADS * HEAD_SIZE)
    gain_query_grad = lax.optimization_barrier(jnp.sum(query_grad * query_unit, axis=0))
    gain_key_grad = lax.optimization_barrier(jnp.sum(key_gradient * key_unit_rows, axis=0))
    raw_query_grad = norm_back(query_grad, query_unit, query_inv, gain_query)
    unrotated_key_gradient = norm_back(key_gradient, key_unit_rows, key_inverse_norm, gain_key)
    total_grad = jnp.dot(raw_query_grad, w_query.T, preferred_element_type=jnp.float32)
    total_grad = total_grad + jnp.dot(unrotated_key_gradient, w_key.T, preferred_element_type=jnp.float32)
    total_grad = total_grad + jnp.dot(value_gradient, value_weight.T, preferred_element_type=jnp.float32)
    input_grad = total_grad.astype(jnp.bfloat16)
    return (attn_out, input_grad, gain_query_grad, gain_key_grad)
```

```python
import math

import jax
import jax.numpy as jnp
from jax import lax
from jax.experimental import pallas as pl
from jax.experimental.pallas import tpu as pltpu
from jax.sharding import PartitionSpec as P

D=128; SPAN=128; G=5; R=G*SPAN; CH=4; KC=CH*SPAN
SCALE=D**-0.5; LOG2E=math.log2(math.e)
NEG=-1e30
GROUPS=((0,256),(256,512),(512,640))

def nt(a,b): return lax.dot_general(a,b,(((1,),(1,)),((),())),preferred_element_type=jnp.float32)
def tn(a,b): return lax.dot_general(a,b,(((0,),(0,)),((),())),preferred_element_type=jnp.float32)
def nn(a,b): return lax.dot_general(a,b,(((1,),(0,)),((),())),preferred_element_type=jnp.float32)

def rows_at(ref, loc, w, j):
    return jnp.concatenate([ref[pl.ds(pl.multiple_of(loc[w,CH*j+t]*SPAN,SPAN),SPAN),:] for t in range(CH)],axis=0)

def visible(j, c, width):
    key=j*KC+lax.broadcasted_iota(jnp.int32,(KC,width),0)
    row=c*SPAN+lax.rem(lax.broadcasted_iota(jnp.int32,(KC,width),1),SPAN)
    return key<=row

def fwd_kernel(loc, own, q_ref, k_ref, v_ref, o_ref, lse_ref):
    for i in range(2):
        c=own[i]
        qs=[q_ref[i,a:b,:] for a,b in GROUPS]
        def step(j, carry, masked):
            kk=rows_at(k_ref,loc,0,j); vv=rows_at(v_ref,loc,1,j)
            out=[]
            for (a,b),q,(m,l,acc) in zip(GROUPS,qs,carry):
                s=nt(kk,q)
                if masked: s=jnp.where(visible(j,c,b-a),s,NEG)
                mn=jnp.maximum(m,jnp.max(s,axis=0,keepdims=True))
                al=jnp.exp2((m-mn)*(SCALE*LOG2E))
                p=jnp.exp2((s-mn)*(SCALE*LOG2E))
                l=l*al+jnp.sum(p,axis=0,keepdims=True)
                acc=acc*al+tn(vv,p.astype(jnp.bfloat16))
                out.append((mn,l,acc))
            return tuple(out)
        init=tuple((jnp.full((1,b-a),NEG,jnp.float32),jnp.zeros((1,b-a),jnp.float32),jnp.zeros((D,b-a),jnp.float32)) for a,b in GROUPS)
        last=c//CH
        carry=lax.fori_loop(0,last,lambda j,x: step(j,x,False),init)
        carry=step(last,carry,True)
        for (a,b),(m,l,acc) in zip(GROUPS,carry):
            o_ref[i,a:b,:]=(acc/l).T.astype(jnp.bfloat16)
            lse_ref[i,:,a:b]=m*(SCALE*LOG2E)+jnp.log2(l)

def bwd_kernel(loc, own, q_ref, k_ref, v_ref, do_ref, o_ref, lse_ref, dq_ref, dk_ref, dv_ref, dka, dva):
    dka[...]=jnp.zeros_like(dka); dva[...]=jnp.zeros_like(dva)
    for i in range(2):
        c=own[i]
        qs=[q_ref[i,a:b,:] for a,b in GROUPS]
        dos=[do_ref[i,a:b,:] for a,b in GROUPS]
        lses=[lse_ref[i,:,a:b] for a,b in GROUPS]
        deltas=[jnp.sum((do_ref[i,a:b,:].astype(jnp.float32)*o_ref[i,a:b,:].astype(jnp.float32)).T,axis=0,keepdims=True) for a,b in GROUPS]
        def step(j, carry, masked):
            kk=rows_at(k_ref,loc,0,j); vv=rows_at(v_ref,loc,1,j)
            out=[]; ps=[]; dss=[]
            for (a,b),q,do,ls,dl,dq in zip(GROUPS,qs,dos,lses,deltas,carry):
                s=nt(kk,q)
                p=jnp.exp2(s*(SCALE*LOG2E)-ls)
                if masked: p=jnp.where(visible(j,c,b-a),p,0.0)
                dp=nt(vv,do)
                ds=(p*(dp-dl)).astype(jnp.bfloat16)
                ps.append(p.astype(jnp.bfloat16)); dss.append(ds)
                out.append(dq+tn(kk,ds))
            pb=jnp.concatenate(ps,axis=1); dsb=jnp.concatenate(dss,axis=1)
            dv=nn(pb,do_ref[i]); dk=nn(dsb,q_ref[i])
            for t in range(CH):
                at=pl.ds(pl.multiple_of(loc[3,CH*j+t]*SPAN,SPAN),SPAN)
                dva[at,:]+=dv[t*SPAN:(t+1)*SPAN]
                at=pl.ds(pl.multiple_of(loc[2,CH*j+t]*SPAN,SPAN),SPAN)
                dka[at,:]+=dk[t*SPAN:(t+1)*SPAN]
            return tuple(out)
        init=tuple(jnp.zeros((D,b-a),jnp.float32) for a,b in GROUPS)
        last=c//CH
        carry=lax.fori_loop(0,last,lambda j,x: step(j,x,False),init)
        carry=step(last,carry,True)
        for (a,b),dq in zip(GROUPS,carry):
            dq_ref[i,a:b,:]=(dq*SCALE).T
    dk_ref[...]=(dka[...]*SCALE).astype(dk_ref.dtype)
    dv_ref[...]=dva[...].astype(dv_ref.dtype)

VM=pl.BlockSpec(memory_space=pltpu.VMEM)
def cparams(): return pltpu.CompilerParams(vmem_limit_bytes=56*2**20)
def attn_fwd(loc,own,q,k,v):
    return pl.pallas_call(fwd_kernel,out_shape=(jax.ShapeDtypeStruct((2,R,D),jnp.bfloat16),jax.ShapeDtypeStruct((2,1,R),jnp.float32)),
      grid_spec=pltpu.PrefetchScalarGridSpec(num_scalar_prefetch=2,grid=(),in_specs=[VM]*3,out_specs=(VM,VM)),
      compiler_params=cparams(),cost_estimate=pl.CostEstimate(flops=int(2.8e9),bytes_accessed=6*2**20,transcendentals=6*10**6))(loc,own,q,k,v)
def attn_bwd(loc,own,q,k,v,do,o,lse):
    n=k.shape[0]
    return pl.pallas_call(bwd_kernel,out_shape=(jax.ShapeDtypeStruct((2,R,D),jnp.float32),jax.ShapeDtypeStruct((n,D),jnp.bfloat16),jax.ShapeDtypeStruct((n,D),jnp.bfloat16)),
      grid_spec=pltpu.PrefetchScalarGridSpec(num_scalar_prefetch=2,grid=(),in_specs=[VM]*6,out_specs=(VM,VM,VM),
        scratch_shapes=[pltpu.VMEM((n,D),jnp.float32),pltpu.VMEM((n,D),jnp.float32)]),
      compiler_params=cparams(),cost_estimate=pl.CostEstimate(flops=int(7e9),bytes_accessed=10*2**20,transcendentals=6*10**6))(loc,own,q,k,v,do,o,lse)

QUERY_HEADS = 20
KEY_VALUE_HEADS = 4
Q_CHANNELS = QUERY_HEADS * D
K_CHANNELS = KEY_VALUE_HEADS * D
N_Y, N_Z, N_CORE, N_TP = 4, 4, 2, 4
BF = jnp.bfloat16
F32 = jnp.float32


def ctx_index(y, z, c):
    return (y * N_Z + z) * N_CORE + c


def ctx_pairs(move):
    return [
        (ctx_index(y, z, c), ctx_index(*move(y, z, c)))
        for y in range(N_Y)
        for z in range(N_Z)
        for c in range(N_CORE)
    ]


def shift_y(x, d):
    return lax.ppermute(x, "ctx", ctx_pairs(lambda y, z, c: ((y + d) % N_Y, z, c)))


def shift_z(x, d):
    return lax.ppermute(x, "ctx", ctx_pairs(lambda y, z, c: (y, (z + d) % N_Z, c)))


def swap_core(x):
    return lax.ppermute(x, "ctx", ctx_pairs(lambda y, z, c: (y, z, 1 - c)))


def shift_tp(x, d):
    return lax.ppermute(x, "tp", [(i, (i + d) % N_TP) for i in range(N_TP)])


def sum_tp(x):
    x = x + lax.ppermute(x, "tp", [(i, i ^ 1) for i in range(N_TP)])
    return x + lax.ppermute(x, "tp", [(i, 3 - i) for i in range(N_TP)])


def sum_ctx(x):
    x = x + swap_core(x)
    x = x + lax.ppermute(x, "ctx", ctx_pairs(lambda y, z, c: (y, z ^ 1, c)))
    x = x + lax.ppermute(x, "ctx", ctx_pairs(lambda y, z, c: (y, 3 - z, c)))
    x = x + lax.ppermute(x, "ctx", ctx_pairs(lambda y, z, c: (y ^ 1, z, c)))
    return x + lax.ppermute(x, "ctx", ctx_pairs(lambda y, z, c: (3 - y, z, c)))


def after(x, *others):
    return lax.optimization_barrier((x,) + others)[0]


def rotate(x, cosine, sine):
    first, second = x[..., : D // 2], x[..., D // 2 :]
    return jnp.concatenate(
        [first * cosine - second * sine, second * cosine + first * sine], axis=-1
    )


def gather_ctx(shift_a, shift_b, x):
    part = jnp.concatenate([x] + [shift_a(x, d) for d in (1, 3, 2)], axis=0)
    return jnp.concatenate([part] + [shift_b(part, d) for d in (1, 3, 2)], axis=0)


def scatter_sum(shift_a, shift_b, x):
    for shift in (shift_a, shift_b):
        rows = x.shape[0] // 4
        sent = x.astype(BF)
        total = x[:rows]
        for d in (1, 3, 2):
            total = total + shift(sent[d * rows : (d + 1) * rows], d).astype(F32)
        x = total
    return x


def local(tokens, span_order, w_query, w_key, value_weight, w_out, gain_query, gain_key, out_grad):
    rows = tokens.shape[0]
    feats = tokens.shape[1]
    width = w_query.shape[1]
    me = lax.axis_index("ctx")
    tp = lax.axis_index("tp")
    my_y, my_z, my_c = me // 8, (me // 2) % 4, me % 2

    place = jnp.arange(64, dtype=jnp.int32)
    stored = jnp.sum(jnp.where(span_order[None, :] == place[:, None], place[None, :], 0), axis=1)
    src, half = stored // 2, stored % 2
    src_y, src_z, src_c = src // 8, (src // 2) % 4, src % 2
    other = (src_c != my_c).astype(jnp.int32)
    back_y, back_z = (my_y - src_y) % 4, (my_z - src_z) % 4
    slot_y = jnp.where(back_y == 2, 3, jnp.where(back_y == 3, 2, back_y))
    slot_z = jnp.where(back_z == 2, 3, jnp.where(back_z == 3, 2, back_z))
    to_y, to_z = (src_y - my_y) % 4, (src_z - my_z) % 4
    loc_v = ((other * 4 + slot_y) * 4 + slot_z) * 2 + half
    loc_k = ((other * 4 + slot_z) * 4 + slot_y) * 2 + half
    out_v = ((other * 4 + to_z) * 4 + to_y) * 2 + half
    out_k = ((other * 4 + to_y) * 4 + to_z) * 2 + half
    table = jnp.stack([loc_k, loc_v, out_k, out_v]).astype(jnp.int32)
    own = lax.dynamic_slice_in_dim(span_order, 2 * me, 2)

    offsets = jnp.arange(SPAN)
    query_pos = (own[:, None] * SPAN + offsets[None, :]).reshape(-1)
    frequency = jnp.exp(jnp.arange(D // 2).astype(F32) * (-2.0 * math.log(500000.0) / D))
    angles = query_pos.astype(F32)[:, None] * frequency[None, :]
    cosine, sine = jnp.cos(angles)[:, None, :], jnp.sin(angles)[:, None, :]

    mid = rows // 2
    with jax.named_scope("gather_tokens"):
        left = shift_tp(tokens, 1)
        right = shift_tp(tokens, 3)
        far = jnp.concatenate([shift_tp(left[:mid], 1), shift_tp(right[mid:], 3)], axis=0)
        pieces = [tokens, left, right, far]

    with jax.named_scope("weight_rows"):
        w_kv = jnp.concatenate([w_key, value_weight], axis=1)
        share = feats // 32
        cut = [
            lax.dynamic_slice_in_dim(w_kv, feats * ((tp + d) % 4) + share * me, share, 0)
            for d in range(4)
        ]
        cut = jnp.stack([cut[0]] + [shift_tp(cut[d], d) for d in (1, 3, 2)])
        w_rows = lax.all_gather(cut, "ctx", axis=0, tiled=False)

    def weight_piece(w, d):
        return lax.dynamic_slice_in_dim(w, feats * ((tp - d) % 4), feats, 0)

    dist = (0, 1, 3, 2)

    def project(xs, w):
        total = None
        for x, d in zip(xs, dist):
            part = jnp.dot(x, weight_piece(w, d), preferred_element_type=F32)
            total = part if total is None else total + part
        return total

    with jax.named_scope("project"):
        kv_raw = project(pieces, w_kv)
        query_raw = project(pieces, w_query)
    key_raw, value = kv_raw[:, :D], kv_raw[:, D:].astype(BF)
    squares = sum_tp(
        jnp.stack([jnp.sum(query_raw * query_raw, axis=1), jnp.sum(key_raw * key_raw, axis=1)])
    )
    query_inv = lax.rsqrt(squares[0] / Q_CHANNELS + 1e-06)[:, None]
    key_inv = lax.rsqrt(squares[1] / K_CHANNELS + 1e-06)[:, None]
    query_unit = query_raw * query_inv
    key_unit = key_raw * key_inv
    key = rotate((key_unit * gain_key)[:, None, :], cosine, sine).astype(BF)[:, 0, :]

    with jax.named_scope("gather_keys_values"):
        values = gather_ctx(shift_z, shift_y, value)
        keys = gather_ctx(shift_y, shift_z, key)
        values = jnp.concatenate([values, swap_core(values)], axis=0)
        keys = jnp.concatenate([keys, swap_core(keys)], axis=0)

    def to_kernel(x):
        return x.reshape(2, SPAN, G, D).transpose(0, 2, 1, 3).reshape(2, R, D)

    def from_kernel(x):
        return x.reshape(2, G, SPAN, D).transpose(0, 2, 1, 3).reshape(rows, width)

    query = to_kernel(
        rotate((query_unit * gain_query).reshape(rows, G, D), cosine, sine).astype(BF).reshape(rows, width)
    )

    with jax.named_scope("gather_out_grad"):
        grad_in = after(out_grad, far)
        grad_part = lax.all_gather(grad_in, "tp", axis=1, tiled=True)
        head_grad = jnp.einsum("tc,qc->tq", grad_part, w_out, preferred_element_type=F32).astype(BF)
        head_grad = to_kernel(head_grad)

    heads, log_total = attn_fwd(table, own, query, keys, values)
    attended = from_kernel(heads)
    out_partial = jnp.dot(attended, w_out, preferred_element_type=F32).astype(BF)
    attn_out = lax.psum_scatter(out_partial, "tp", scatter_dimension=1, tiled=True)

    grad_query, key_grads, value_grads = attn_bwd(
        table, own, query, keys, values, head_grad, heads, log_total
    )

    with jax.named_scope("sum_key_value_grads"):
        half_rows = key_grads.shape[0] // 2
        value_part = value_grads[:half_rows].astype(F32) + swap_core(value_grads[half_rows:]).astype(F32)
        key_part = key_grads[:half_rows].astype(F32) + swap_core(key_grads[half_rows:]).astype(F32)
        value_grad = scatter_sum(shift_z, shift_y, value_part).astype(BF)
        key_grad_rot = scatter_sum(shift_y, shift_z, key_part)

    query_grad = rotate(
        from_kernel(grad_query).reshape(rows, G, D), cosine, -sine
    ).reshape(rows, width)
    up_query = query_grad * gain_query
    mix_query = sum_tp(jnp.sum(up_query * query_unit, axis=1)[None])[0] / Q_CHANNELS
    raw_query_grad = (query_inv * (up_query - query_unit * mix_query[:, None])).astype(BF)
    query_partial = jnp.einsum(
        "tq,cq->tc", raw_query_grad, w_query, preferred_element_type=F32
    ).astype(BF)
    query_side = lax.psum_scatter(query_partial, "tp", scatter_dimension=1, tiled=True)
    gain_query_grad = sum_ctx(jnp.sum(query_grad * query_unit, axis=0)[None])[0]

    key_grad = rotate(key_grad_rot[:, None, :], cosine, -sine)[:, 0, :]
    up_key = key_grad * gain_key
    mix_key = sum_tp(jnp.sum(up_key * key_unit, axis=1)[None])[0] / K_CHANNELS
    raw_key_grad = (key_inv * (up_key - key_unit * mix_key[:, None])).astype(BF)
    gain_key_grad = sum_ctx(jnp.sum(key_grad * key_unit, axis=0)[None])[0]
    with jax.named_scope("gather_key_value_grads"):
        mine = jnp.concatenate([raw_key_grad, value_grad], axis=1)
        grads = jnp.concatenate([mine] + [shift_tp(mine, d) for d in (1, 3, 2)], axis=1)
    by_rows = w_rows.transpose(0, 2, 1, 3).reshape(feats, -1)
    key_value_side = jnp.einsum("tq,cq->tc", grads, by_rows, preferred_element_type=F32)
    input_grad = (query_side.astype(F32) + key_value_side).astype(BF)
    return (attn_out, input_grad, gain_query_grad, gain_key_grad)


def solution(mesh):
    return jax.shard_map(
        local,
        mesh=mesh,
        in_specs=(
            P("ctx", "tp"),
            P(),
            P(None, "tp"),
            P(None, "tp"),
            P(None, "tp"),
            P("tp", None),
            P("tp"),
            P("tp"),
            P("ctx", "tp"),
        ),
        out_specs=(P("ctx", "tp"), P("ctx", "tp"), P("tp"), P("tp")),
        check_vma=False,
    )
```

```python
import math

import jax
import jax.numpy as jnp
from jax import lax
from jax.experimental import pallas as pl
from jax.experimental.pallas import tpu as pltpu
from jax.sharding import PartitionSpec as P

D = 128
SPAN = 128
G = 5
R = G * SPAN
CH = 8
KC = CH * SPAN
SCALE = D**-0.5
LOG2E = math.log2(math.e)
NEG = -1e30
BF = jnp.bfloat16
F32 = jnp.float32
DIST = (0, 1, 3, 2)


def nt(a, b):
    return lax.dot_general(a, b, (((1,), (1,)), ((), ())), preferred_element_type=F32)


def tn(a, b):
    return lax.dot_general(a, b, (((0,), (0,)), ((), ())), preferred_element_type=F32)


def nn(a, b):
    return lax.dot_general(a, b, (((1,), (0,)), ((), ())), preferred_element_type=F32)


VM = pl.BlockSpec(memory_space=pltpu.VMEM)
HB = pl.BlockSpec(memory_space=pl.ANY)


def params():
    return pltpu.CompilerParams(vmem_limit_bytes=56 * 2**20)


def cost(flops, mib, exps=0):
    return pl.CostEstimate(
        flops=int(flops), bytes_accessed=int(mib * 2**20), transcendentals=int(exps)
    )


def turn(x, cosine, sine):
    return x * cosine + pltpu.roll(x, D // 2, 1) * sine


def lane_sums(x):
    return jnp.sum(x.T, axis=0, keepdims=True)


def project_kernel(
    off, x0, x1, x2, xa, xb, wq, wk, wv, cosine, sine, gain_q, gain_k,
    q_rot, q_raw, k_rot, k_raw, v_out, squares, acc,
):
    g = pl.program_id(0)

    def add(x, rows, first):
        for w, at in ((wq, slice(0, R)), (wk, slice(R, R + D)), (wv, slice(R + D, R + 2 * D))):
            part = nn(x, w[...])
            if first:
                acc[rows, at] = part
            else:
                acc[rows, at] += part

    @pl.when(g == 0)
    def _():
        add(x0[...], slice(0, 256), True)

    @pl.when(g == 1)
    def _():
        add(x1[...], slice(0, 256), False)

    @pl.when(g == 2)
    def _():
        add(x2[...], slice(0, 256), False)

    @pl.when(g == 3)
    def _():
        add(jnp.concatenate([xa[...], xb[...]], axis=0), slice(0, 256), False)
        cs, sn = cosine[...], sine[...]
        k = acc[:, R : R + D]
        k_raw[...] = k
        k_rot[...] = turn(k * gain_k[...], cs, sn)
        v_out[...] = acc[:, R + D :].astype(BF)
        squares[1:2, :] = lane_sums(k * k)
        total = None
        for h in range(G):
            q = acc[:, h * D : (h + 1) * D]
            total = q * q if total is None else total + q * q
            rotated = turn(q * gain_q[:, h * D : (h + 1) * D], cs, sn)
            for i in range(2):
                q_rot[i, h * SPAN : (h + 1) * SPAN, :] = rotated[i * SPAN : (i + 1) * SPAN]
        q_raw[...] = acc[:, :R]
        squares[0:1, :] = lane_sums(total)


def project(off, pieces, w_query, w_key, value_weight, cosine, sine, gain_q, gain_k):
    feats = pieces[0].shape[1]
    rows = 2 * SPAN

    def full(x):
        return pl.BlockSpec(x.shape, lambda g, off: (0,) * len(x.shape))

    def wspec(w):
        return pl.BlockSpec((feats, w.shape[1]), lambda g, off: (off[g], 0))

    outs = (
        jax.ShapeDtypeStruct((2, R, D), F32),
        jax.ShapeDtypeStruct((rows, R), F32),
        jax.ShapeDtypeStruct((rows, D), F32),
        jax.ShapeDtypeStruct((rows, D), F32),
        jax.ShapeDtypeStruct((rows, D), BF),
        jax.ShapeDtypeStruct((2, rows), F32),
    )
    rest = (cosine, sine, gain_q, gain_k)
    return pl.pallas_call(
        project_kernel,
        out_shape=outs,
        grid_spec=pltpu.PrefetchScalarGridSpec(
            num_scalar_prefetch=1,
            grid=(4,),
            in_specs=[full(x) for x in pieces]
            + [wspec(w) for w in (w_query, w_key, value_weight)]
            + [full(x) for x in rest],
            out_specs=tuple(full(o) for o in outs),
            scratch_shapes=[pltpu.VMEM((rows, R + 2 * D), F32)],
        ),
        compiler_params=params(),
        cost_estimate=cost(2.4e9, 14),
    )(off, *pieces, w_query, w_key, value_weight, *rest)


def join_kernel(*refs):
    half = (len(refs) - 2) // 2
    for g in range(2):
        at = 0
        for ref in refs[g * half : (g + 1) * half]:
            n = ref.shape[0]
            refs[2 * half + g][at : at + n, :] = ref[...]
            at += n


def join(a, b):
    outs = tuple(
        jax.ShapeDtypeStruct((sum(x.shape[0] for x in xs), xs[0].shape[1]), xs[0].dtype)
        for xs in (a, b)
    )
    return pl.pallas_call(
        join_kernel,
        out_shape=outs,
        in_specs=[VM] * (len(a) + len(b)),
        out_specs=(VM, VM),
        compiler_params=params(),
        cost_estimate=cost(0, 4),
    )(*a, *b)


def spans_at(ref, loc, which, j):
    return jnp.concatenate(
        [
            ref[pl.ds(pl.multiple_of(loc[which, CH * j + t] * SPAN, SPAN), SPAN), :]
            for t in range(CH)
        ],
        axis=0,
    )


def load_halves(pairs, sems):
    copies = []
    for n, (own_half, other_half, whole) in enumerate(pairs):
        rows = own_half.shape[0]
        for m, src in enumerate((own_half, other_half)):
            copy = pltpu.make_async_copy(
                src, whole.at[pl.ds(m * rows, rows), :], sems.at[2 * n + m]
            )
            copy.start()
            copies.append(copy)
    for copy in copies:
        copy.wait()


def fwd_kernel(
    loc, own, q_ref, k_own, k_other, v_own, v_other, o_ref, lse_ref, k_ref, v_ref, m_s, acc_s, sems
):
    load_halves(((k_own, k_other, k_ref), (v_own, v_other, v_ref)), sems)
    ones = (lax.broadcasted_iota(jnp.int32, (KC, D), 1) == 0).astype(BF)
    for i in range(2):
        c = own[i]
        m_s[...] = jnp.full_like(m_s, NEG)
        acc_s[...] = jnp.zeros_like(acc_s)

        def step(j, masked):
            kk = spans_at(k_ref, loc, 0, j)
            vv = jnp.concatenate([spans_at(v_ref, loc, 1, j), ones], axis=1)
            for h in range(G):
                at = slice(h * SPAN, (h + 1) * SPAN)
                s = nt(q_ref[i, at, :], kk)
                if masked:
                    key = j * KC + lax.broadcasted_iota(jnp.int32, (SPAN, KC), 1)
                    row = c * SPAN + lax.broadcasted_iota(jnp.int32, (SPAN, KC), 0)
                    s = jnp.where(key <= row, s, NEG)
                m = m_s[at, :]
                new = jnp.maximum(m, jnp.max(s, axis=1, keepdims=True))
                shrink = jnp.exp2((m - new) * (SCALE * LOG2E))
                p = jnp.exp2((s - new[:, :1]) * (SCALE * LOG2E))
                m_s[at, :] = new
                acc_s[at, :] = acc_s[at, :] * shrink[:, :1] + nn(p.astype(BF), vv)

        last = c // CH

        def body(j, _):
            step(j, False)
            return 0

        lax.fori_loop(0, last, body, 0)
        step(last, True)
        total = acc_s[:, D : D + 1]
        o_ref[i] = (acc_s[:, :D] / total).astype(BF)
        lse = m_s[...] * (SCALE * LOG2E) + jnp.log2(jnp.broadcast_to(total, (R, D)))
        lse_ref[i] = lse.T[0:1, :]


def attn_fwd(table, own, q, k_own, k_other, v_own, v_other):
    n = 2 * k_own.shape[0]
    return pl.pallas_call(
        fwd_kernel,
        out_shape=(jax.ShapeDtypeStruct((2, R, D), BF), jax.ShapeDtypeStruct((2, 1, R), F32)),
        grid_spec=pltpu.PrefetchScalarGridSpec(
            num_scalar_prefetch=2,
            grid=(),
            in_specs=[VM] + [HB] * 4,
            out_specs=(VM, VM),
            scratch_shapes=[
                pltpu.VMEM((n, D), BF),
                pltpu.VMEM((n, D), BF),
                pltpu.VMEM((R, D), F32),
                pltpu.VMEM((R, 2 * D), F32),
                pltpu.SemaphoreType.DMA((4,)),
            ],
        ),
        compiler_params=params(),
        cost_estimate=cost(1.6e10, 6, 6e6),
    )(table, own, q, k_own, k_other, v_own, v_other)


def bwd_kernel(
    loc, own, q_ref, k_own, k_other, v_own, v_other, do_ref, o_ref, lse_ref, cosine, sine,
    gain_q, unit_ref, up_ref, mix_ref, gain_ref, dk_ref, dv_ref, k_ref, v_ref, dka, dva, dqa, sems,
):
    load_halves(((k_own, k_other, k_ref), (v_own, v_other, v_ref)), sems)
    dka[...] = jnp.zeros_like(dka)
    dva[...] = jnp.zeros_like(dva)
    dqa[...] = jnp.zeros_like(dqa)
    for i in range(2):
        c = own[i]
        q, do, lse = q_ref[i], do_ref[i], lse_ref[i]
        delta = lane_sums(do.astype(F32) * o_ref[i].astype(F32))

        def step(j, masked):
            kk = spans_at(k_ref, loc, 0, j)
            vv = spans_at(v_ref, loc, 1, j)
            p = jnp.exp2(nt(kk, q) * (SCALE * LOG2E) - lse)
            if masked:
                key = j * KC + lax.broadcasted_iota(jnp.int32, (KC, R), 0)
                row = c * SPAN + lax.rem(lax.broadcasted_iota(jnp.int32, (KC, R), 1), SPAN)
                p = jnp.where(key <= row, p, 0.0)
            ds = (p * (nt(vv, do) - delta)).astype(BF)
            dqa[i] += tn(kk, ds)
            dv = nn(p.astype(BF), do)
            dk = nn(ds, q)
            for t in range(CH):
                part = slice(t * SPAN, (t + 1) * SPAN)
                at = pl.ds(pl.multiple_of(loc[3, CH * j + t] * SPAN, SPAN), SPAN)
                dva[at, :] += dv[part]
                at = pl.ds(pl.multiple_of(loc[2, CH * j + t] * SPAN, SPAN), SPAN)
                dka[at, :] += dk[part]

        last = c // CH

        def body(j, _):
            step(j, False)
            return 0

        lax.fori_loop(0, last, body, 0)
        step(last, True)
    dk_ref[...] = (dka[...] * SCALE).astype(BF)
    dv_ref[...] = dva[...].astype(BF)
    for i in range(2):
        rows = slice(i * SPAN, (i + 1) * SPAN)
        cs, sn = cosine[rows, :], -sine[rows, :]
        mix = None
        for h in range(G):
            cols = slice(h * D, (h + 1) * D)
            grad = turn((dqa[i, :, cols] * SCALE).T, cs, sn)
            unit = unit_ref[rows, cols]
            up = grad * gain_q[:, cols]
            up_ref[rows, cols] = up
            mix = up * unit if mix is None else mix + up * unit
            gain = jnp.sum(grad * unit, axis=0, keepdims=True)
            if i == 0:
                gain_ref[:, cols] = gain
            else:
                gain_ref[:, cols] += gain
        mix_ref[:, rows] = lane_sums(mix)


def attn_bwd(table, own, q, k_own, k_other, v_own, v_other, do, o, lse, cosine, sine, gain_q, unit):
    n = 2 * k_own.shape[0]
    rows = 2 * SPAN
    return pl.pallas_call(
        bwd_kernel,
        out_shape=(
            jax.ShapeDtypeStruct((rows, R), F32),
            jax.ShapeDtypeStruct((1, rows), F32),
            jax.ShapeDtypeStruct((1, R), F32),
            jax.ShapeDtypeStruct((n, D), BF),
            jax.ShapeDtypeStruct((n, D), BF),
        ),
        grid_spec=pltpu.PrefetchScalarGridSpec(
            num_scalar_prefetch=2,
            grid=(),
            in_specs=[VM] + [HB] * 4 + [VM] * 7,
            out_specs=(VM,) * 5,
            scratch_shapes=[
                pltpu.VMEM((n, D), BF),
                pltpu.VMEM((n, D), BF),
                pltpu.VMEM((n, D), F32),
                pltpu.VMEM((n, D), F32),
                pltpu.VMEM((2, D, R), F32),
                pltpu.SemaphoreType.DMA((4,)),
            ],
        ),
        compiler_params=params(),
        cost_estimate=cost(2.2e10, 12, 6e6),
    )(table, own, q, k_own, k_other, v_own, v_other, do, o, lse, cosine, sine, gain_q, unit)


def head_grad_kernel(x, w, out, acc):
    g = pl.program_id(0)
    part = nt(x[...], w[...])

    @pl.when(g == 0)
    def _():
        acc[...] = part

    @pl.when(g > 0)
    def _():
        acc[...] += part

    @pl.when(g == pl.num_programs(0) - 1)
    def _():
        for i in range(2):
            for h in range(G):
                out[i, h * SPAN : (h + 1) * SPAN, :] = acc[
                    i * SPAN : (i + 1) * SPAN, h * D : (h + 1) * D
                ].astype(BF)


def head_grad_of(x, w_out):
    rows, feats = x.shape
    block = feats // 4
    return pl.pallas_call(
        head_grad_kernel,
        out_shape=jax.ShapeDtypeStruct((2, R, D), BF),
        grid=(4,),
        in_specs=[
            pl.BlockSpec((rows, block), lambda g: (0, g)),
            pl.BlockSpec((R, block), lambda g: (0, g)),
        ],
        out_specs=pl.BlockSpec((2, R, D), lambda g: (0, 0, 0)),
        scratch_shapes=[pltpu.VMEM((rows, R), F32)],
        compiler_params=params(),
        cost_estimate=cost(1.7e9, 9),
    )(x, w_out)


def out_kernel(heads, w, out):
    x = jnp.concatenate(
        [
            jnp.concatenate(
                [heads[i, h * SPAN : (h + 1) * SPAN, :] for h in range(G)], axis=1
            )
            for i in range(2)
        ],
        axis=0,
    )
    out[0] = nn(x, w[...]).astype(BF)


def out_partial_of(heads, w_out):
    feats = w_out.shape[1]
    block = feats // 4
    rows = 2 * SPAN
    return pl.pallas_call(
        out_kernel,
        out_shape=jax.ShapeDtypeStruct((4, rows, block), BF),
        grid=(4,),
        in_specs=[
            pl.BlockSpec((2, R, D), lambda g: (0, 0, 0)),
            pl.BlockSpec((R, block), lambda g: (0, g)),
        ],
        out_specs=pl.BlockSpec((1, rows, block), lambda g: (g, 0, 0)),
        compiler_params=params(),
        cost_estimate=cost(1.7e9, 9),
    )(heads, w_out)


def query_kernel(x, w, out):
    out[0] = nt(x[...], w[...]).astype(BF)


def query_partial_of(x, w_query):
    rows = x.shape[0]
    feats = w_query.shape[0]
    block = feats // 4
    return pl.pallas_call(
        query_kernel,
        out_shape=jax.ShapeDtypeStruct((4, rows, block), BF),
        grid=(4,),
        in_specs=[
            pl.BlockSpec((rows, R), lambda g: (0, 0)),
            pl.BlockSpec((block, R), lambda g: (g, 0)),
        ],
        out_specs=pl.BlockSpec((1, rows, block), lambda g: (g, 0, 0)),
        compiler_params=params(),
        cost_estimate=cost(1.7e9, 9),
    )(x, w_query)


def last_kernel(g0, g1, g2, g3, u0, u1, u2, u3, inv, w, query_side, out):
    gs, us = (g0, g1, g2, g3), (u0, u1, u2, u3)
    mix = None
    for g, u in zip(gs, us):
        part = g[:, :D].astype(F32) * u[...].astype(F32)
        mix = part if mix is None else mix + part
    mix = jnp.sum(mix, axis=1, keepdims=True) * (1.0 / K_CHANNELS)
    total = query_side[...].astype(F32)
    for n, (g, u) in enumerate(zip(gs, us)):
        raw = (inv[...] * (g[:, :D].astype(F32) - u[...].astype(F32) * mix)).astype(BF)
        total = total + nt(jnp.concatenate([raw, g[:, D:]], axis=1), w[n])
    out[...] = total.astype(BF)


def last_of(grads, units, inv, w, query_side):
    return pl.pallas_call(
        last_kernel,
        out_shape=jax.ShapeDtypeStruct(query_side.shape, BF),
        in_specs=[VM] * 11,
        out_specs=VM,
        compiler_params=params(),
        cost_estimate=cost(7e8, 5),
    )(*grads, *units, inv, w, query_side)

QUERY_HEADS = 20
KEY_VALUE_HEADS = 4
Q_CHANNELS = QUERY_HEADS * D
K_CHANNELS = KEY_VALUE_HEADS * D
N_Y, N_Z, N_CORE, N_TP = 4, 4, 2, 4


def ctx_index(y, z, c):
    return (y * N_Z + z) * N_CORE + c


def ctx_pairs(move):
    return [
        (ctx_index(y, z, c), ctx_index(*move(y, z, c)))
        for y in range(N_Y)
        for z in range(N_Z)
        for c in range(N_CORE)
    ]


def shift_y(x, d):
    return lax.ppermute(x, "ctx", ctx_pairs(lambda y, z, c: ((y + d) % N_Y, z, c)))


def shift_z(x, d):
    return lax.ppermute(x, "ctx", ctx_pairs(lambda y, z, c: (y, (z + d) % N_Z, c)))


def swap_core(x):
    return lax.ppermute(x, "ctx", ctx_pairs(lambda y, z, c: (y, z, 1 - c)))


def shift_tp(x, d):
    return lax.ppermute(x, "tp", [(i, (i + d) % N_TP) for i in range(N_TP)])


def shifts(shift, x):
    return [x] + [shift(x, d) for d in DIST[1:]]


def sum_tp(x):
    x = x + lax.ppermute(x, "tp", [(i, i ^ 1) for i in range(N_TP)])
    return x + lax.ppermute(x, "tp", [(i, 3 - i) for i in range(N_TP)])


def sum_ctx(x):
    x = x + swap_core(x)
    x = x + lax.ppermute(x, "ctx", ctx_pairs(lambda y, z, c: (y, z ^ 1, c)))
    x = x + lax.ppermute(x, "ctx", ctx_pairs(lambda y, z, c: (y, 3 - z, c)))
    x = x + lax.ppermute(x, "ctx", ctx_pairs(lambda y, z, c: (y ^ 1, z, c)))
    return x + lax.ppermute(x, "ctx", ctx_pairs(lambda y, z, c: (3 - y, z, c)))


def after(x, *others):
    return lax.optimization_barrier((x,) + others)[0]


def scatter_step(shift, x):
    rows = x.shape[0] // 4
    sent = x.astype(BF)
    total = x[:rows]
    for d in DIST[1:]:
        total = total + shift(sent[d * rows : (d + 1) * rows], d).astype(F32)
    return total


def local(tokens, span_order, w_query, w_key, value_weight, w_out, gain_query, gain_key, out_grad):
    rows, feats = tokens.shape
    me = lax.axis_index("ctx")
    tp = lax.axis_index("tp")
    my_y, my_z, my_c = me // 8, (me // 2) % 4, me % 2

    mid = rows // 2
    with jax.named_scope("gather_tokens"):
        left = shift_tp(tokens, 1)
        right = shift_tp(tokens, 3)
        far_a = shift_tp(left[:mid], 1)
        far_b = shift_tp(right[mid:], 3)
        pieces = (tokens, left, right, far_a, far_b)

    place = jnp.arange(64, dtype=jnp.int32)
    stored = jnp.sum(jnp.where(span_order[None, :] == place[:, None], place[None, :], 0), axis=1)
    src, half = stored // 2, stored % 2
    src_y, src_z, src_c = src // 8, (src // 2) % 4, src % 2
    other = (src_c != my_c).astype(jnp.int32)
    to_y, to_z = (src_y - my_y) % 4, (src_z - my_z) % 4
    back_y, back_z = (4 - to_y) % 4, (4 - to_z) % 4
    slot_y = jnp.where(back_y >= 2, 5 - back_y, back_y)
    slot_z = jnp.where(back_z >= 2, 5 - back_z, back_z)
    table = jnp.stack(
        [
            ((other * 4 + slot_z) * 4 + slot_y) * 2 + half,
            ((other * 4 + slot_y) * 4 + slot_z) * 2 + half,
            ((other * 4 + to_y) * 4 + to_z) * 2 + half,
            ((other * 4 + to_z) * 4 + to_y) * 2 + half,
        ]
    ).astype(jnp.int32)
    own = lax.dynamic_slice_in_dim(span_order, 2 * me, 2)

    query_pos = (own[:, None] * SPAN + jnp.arange(SPAN)[None, :]).reshape(-1)
    frequency = jnp.exp(jnp.arange(D // 2).astype(F32) * (-2.0 * math.log(500000.0) / D))
    angles = query_pos.astype(F32)[:, None] * frequency[None, :]
    cosine, sine = jnp.cos(angles), jnp.sin(angles)
    cosine = jnp.concatenate([cosine, cosine], axis=1)
    sine = jnp.concatenate([-sine, sine], axis=1)

    offs = jnp.stack([(tp - d) % 4 for d in DIST]).astype(jnp.int32)
    gain_q, gain_k = gain_query[None, :], gain_key[None, :]
    q_rot, q_raw, k_rot, k_raw, value, squares = project(
        offs, pieces, w_query, w_key, value_weight, cosine, sine, gain_q, gain_k
    )
    with jax.named_scope("norm_sums"):
        squares = sum_tp(squares)
    query_inv = lax.rsqrt(squares[0] / Q_CHANNELS + 1e-06)[:, None]
    key_inv = lax.rsqrt(squares[1] / K_CHANNELS + 1e-06)[:, None]
    key = (k_rot * key_inv).astype(BF)

    with jax.named_scope("gather_keys_values"):
        values, keys = join(shifts(shift_z, value), shifts(shift_y, key))
        values, keys = join(shifts(shift_y, values), shifts(shift_z, keys))
        kv = (keys, swap_core(keys), values, swap_core(values))

    query_unit = q_raw * query_inv
    key_unit = k_raw * key_inv
    query = (
        (q_rot.reshape(2, G, SPAN, D) * query_inv.reshape(2, 1, SPAN, 1)).astype(BF).reshape(2, R, D)
    )
    with jax.named_scope("gather_key_units"):
        key_units = shifts(shift_tp, key_unit.astype(BF))

    with jax.named_scope("gather_out_grad"):
        grad_part = lax.all_gather(after(out_grad, far_a, far_b), "tp", axis=1, tiled=True)
        head_grad = head_grad_of(grad_part, w_out)

    with jax.named_scope("weight_rows"):
        share = feats // 32
        cut = []
        for d in DIST:
            start = feats * ((tp + d) % 4) + share * me
            piece = jnp.concatenate(
                [lax.dynamic_slice_in_dim(w, start, share, 0) for w in (w_key, value_weight)],
                axis=1,
            )
            cut.append(shift_tp(piece, d) if d else piece)
        cut = after(jnp.stack(cut), grad_part)
        w_rows = lax.all_gather(cut, "ctx", axis=0, tiled=False)
        w_rows = w_rows.transpose(1, 0, 2, 3).reshape(4, feats, 2 * D)

    heads, log_total = attn_fwd(table, own, query, *kv)
    out_partial = out_partial_of(heads, w_out)
    attn_out = lax.psum_scatter(out_partial, "tp", scatter_dimension=0, tiled=False)

    up_query, mix_query, gain_part, key_grads, value_grads = attn_bwd(
        table, own, after(query, out_partial), *kv, head_grad, heads, log_total,
        cosine, sine, gain_q, query_unit,
    )

    with jax.named_scope("sum_key_value_grads"):
        half_rows = key_grads.shape[0] // 2
        value_part = value_grads[:half_rows].astype(F32) + swap_core(value_grads[half_rows:]).astype(F32)
        key_part = key_grads[:half_rows].astype(F32) + swap_core(key_grads[half_rows:]).astype(F32)
        value_part = scatter_step(shift_z, value_part)
        key_part = scatter_step(shift_y, key_part)
        value_grad = scatter_step(shift_y, value_part).astype(BF)
        key_grad_rot = scatter_step(shift_z, key_part)

    with jax.named_scope("query_side"):
        mix_query = sum_tp(mix_query)[0] / Q_CHANNELS
        raw_query_grad = (query_inv * (up_query - query_unit * mix_query[:, None])).astype(BF)
        query_partial = query_partial_of(raw_query_grad, w_query)
        query_side = lax.psum_scatter(query_partial, "tp", scatter_dimension=0, tiled=False)
        gain_query_grad = sum_ctx(gain_part)[0]

    with jax.named_scope("key_value_side"):
        first, second = key_grad_rot[:, : D // 2], key_grad_rot[:, D // 2 :]
        cs, sn = cosine[:, : D // 2], sine[:, D // 2 :]
        key_grad = jnp.concatenate([first * cs + second * sn, second * cs - first * sn], axis=1)
        mine = jnp.concatenate([(key_grad * gain_k).astype(BF), value_grad], axis=1)
        grads = shifts(shift_tp, mine)
        gain_key_grad = sum_ctx(jnp.sum(key_grad * key_unit, axis=0)[None])[0]
        input_grad = last_of(grads, key_units, key_inv, w_rows, query_side)
    return (attn_out, input_grad, gain_query_grad, gain_key_grad)


def solution(mesh):
    return jax.shard_map(
        local,
        mesh=mesh,
        in_specs=(
            P("ctx", "tp"),
            P(),
            P(None, "tp"),
            P(None, "tp"),
            P(None, "tp"),
            P("tp", None),
            P("tp"),
            P("tp"),
            P("ctx", "tp"),
        ),
        out_specs=(P("ctx", "tp"), P("ctx", "tp"), P("tp"), P("tp")),
        check_vma=False,
    )
```

```python
import math

import jax
import jax.numpy as jnp
from jax import lax
from jax.experimental import pallas as pl
from jax.experimental.pallas import tpu as pltpu
from jax.sharding import PartitionSpec as P

D = 128
SPAN = 128
G = 5
R = G * SPAN
CH = 8
KC = CH * SPAN
SCALE = D**-0.5
LOG2E = math.log2(math.e)
NEG = -1e30
BF = jnp.bfloat16
F32 = jnp.float32
DIST = (0, 1, 3, 2)
PIECES = 8


def nt(a, b):
    return lax.dot_general(a, b, (((1,), (1,)), ((), ())), preferred_element_type=F32)


def tn(a, b):
    return lax.dot_general(a, b, (((0,), (0,)), ((), ())), preferred_element_type=F32)


def nn(a, b):
    return lax.dot_general(a, b, (((1,), (0,)), ((), ())), preferred_element_type=F32)


VM = pl.BlockSpec(memory_space=pltpu.VMEM)
HB = pl.BlockSpec(memory_space=pl.ANY)


def params(mib):
    return pltpu.CompilerParams(vmem_limit_bytes=mib * 2**20)


def cost(flops, mib, exps=0):
    return pl.CostEstimate(
        flops=int(flops), bytes_accessed=int(mib * 2**20), transcendentals=int(exps)
    )


def turn(x, cosine, sine):
    return x * cosine + pltpu.roll(x, D // 2, 1) * sine


def lane_sums(x):
    return jnp.sum(x.T, axis=0, keepdims=True)


def project_kernel(
    off, x0, x1, x2, xa, xb, wq, wk, wv, cosine, sine, gain_q, gain_k,
    q_rot, q_raw, k_rot, k_raw, v_out, squares, acc,
):
    g = pl.program_id(0)

    def add(x, rows, first):
        for w, at in ((wq, slice(0, R)), (wk, slice(R, R + D)), (wv, slice(R + D, R + 2 * D))):
            part = nn(x, w[...])
            if first:
                acc[rows, at] = part
            else:
                acc[rows, at] += part

    @pl.when(g == 0)
    def _():
        add(x0[...], slice(0, 256), True)

    @pl.when(g == 1)
    def _():
        add(x1[...], slice(0, 256), False)

    @pl.when(g == 2)
    def _():
        add(x2[...], slice(0, 256), False)

    @pl.when(g == 3)
    def _():
        add(jnp.concatenate([xa[...], xb[...]], axis=0), slice(0, 256), False)
        cs, sn = cosine[...], sine[...]
        k = acc[:, R : R + D]
        k_raw[...] = k
        k_rot[...] = turn(k * gain_k[...], cs, sn)
        v_out[...] = acc[:, R + D :].astype(BF)
        squares[1:2, :] = lane_sums(k * k)
        total = None
        for h in range(G):
            q = acc[:, h * D : (h + 1) * D]
            total = q * q if total is None else total + q * q
            rotated = turn(q * gain_q[:, h * D : (h + 1) * D], cs, sn)
            for i in range(2):
                q_rot[i, h * SPAN : (h + 1) * SPAN, :] = rotated[i * SPAN : (i + 1) * SPAN]
        q_raw[...] = acc[:, :R]
        squares[0:1, :] = lane_sums(total)


def project(off, pieces, w_query, w_key, value_weight, cosine, sine, gain_q, gain_k):
    feats = pieces[0].shape[1]
    rows = 2 * SPAN

    def full(x):
        return pl.BlockSpec(x.shape, lambda g, off: (0,) * len(x.shape))

    def wspec(w):
        return pl.BlockSpec((feats, w.shape[1]), lambda g, off: (off[g], 0))

    outs = (
        jax.ShapeDtypeStruct((2, R, D), F32),
        jax.ShapeDtypeStruct((rows, R), F32),
        jax.ShapeDtypeStruct((rows, D), F32),
        jax.ShapeDtypeStruct((rows, D), F32),
        jax.ShapeDtypeStruct((rows, D), BF),
        jax.ShapeDtypeStruct((2, rows), F32),
    )
    rest = (cosine, sine, gain_q, gain_k)
    return pl.pallas_call(
        project_kernel,
        out_shape=outs,
        grid_spec=pltpu.PrefetchScalarGridSpec(
            num_scalar_prefetch=1,
            grid=(4,),
            in_specs=[full(x) for x in pieces]
            + [wspec(w) for w in (w_query, w_key, value_weight)]
            + [full(x) for x in rest],
            out_specs=tuple(full(o) for o in outs),
            scratch_shapes=[pltpu.VMEM((rows, R + 2 * D), F32)],
        ),
        compiler_params=params(20),
        cost_estimate=cost(2.4e9, 14),
    )(off, *pieces, w_query, w_key, value_weight, *rest)


def join_kernel(*refs):
    at = 0
    for ref in refs[:-1]:
        n = ref.shape[0]
        refs[-1][at : at + n, :] = ref[...]
        at += n


def join(*xs):
    rows = sum(x.shape[0] for x in xs)
    return pl.pallas_call(
        join_kernel,
        out_shape=jax.ShapeDtypeStruct((rows,) + xs[0].shape[1:], xs[0].dtype),
        in_specs=[VM] * len(xs),
        out_specs=VM,
        compiler_params=params(8),
        cost_estimate=cost(0, 1),
    )(*xs)


def spans_at(ref, loc, which, j):
    return jnp.concatenate(
        [
            ref[pl.ds(pl.multiple_of(loc[which, CH * j + t] * SPAN, SPAN), SPAN), :]
            for t in range(CH)
        ],
        axis=0,
    )


def load_pieces(refs, whole, core, sems):
    count = len(refs) // 2
    copies = []
    for n, src in enumerate(refs):
        rows = src.shape[0]
        to = core if n < count else 1 - core
        copy = pltpu.make_async_copy(
            src, whole.at[to, pl.ds((n % count) * rows, rows), :], sems.at[n]
        )
        copy.start()
        copies.append(copy)
    for copy in copies:
        copy.wait()


def fwd_kernel(loc, own, q_ref, *refs):
    kv_refs, (o_ref, lse_ref, kv, m_s, acc_s, sems) = refs[:PIECES], refs[PIECES:]
    load_pieces(kv_refs, kv, own[2], sems)
    k_ref, v_ref = kv.at[0], kv.at[1]
    ones = (lax.broadcasted_iota(jnp.int32, (KC, D), 1) == 0).astype(BF)
    for i in range(2):
        c = own[i]
        m_s[...] = jnp.full_like(m_s, NEG)
        acc_s[...] = jnp.zeros_like(acc_s)

        def step(j, masked):
            kk = spans_at(k_ref, loc, 0, j)
            vv = jnp.concatenate([spans_at(v_ref, loc, 1, j), ones], axis=1)
            for h in range(G):
                at = slice(h * SPAN, (h + 1) * SPAN)
                s = nt(q_ref[i, at, :], kk)
                if masked:
                    key = j * KC + lax.broadcasted_iota(jnp.int32, (SPAN, KC), 1)
                    row = c * SPAN + lax.broadcasted_iota(jnp.int32, (SPAN, KC), 0)
                    s = jnp.where(key <= row, s, NEG)
                m = m_s[at, :]
                new = jnp.maximum(m, jnp.max(s, axis=1, keepdims=True))
                shrink = jnp.exp2((m - new) * (SCALE * LOG2E))
                p = jnp.exp2((s - new[:, :1]) * (SCALE * LOG2E))
                m_s[at, :] = new
                acc_s[at, :] = acc_s[at, :] * shrink[:, :1] + nn(p.astype(BF), vv)

        last = c // CH

        def body(j, _):
            step(j, False)
            return 0

        lax.fori_loop(0, last, body, 0)
        step(last, True)
        total = acc_s[:, D : D + 1]
        o_ref[i] = (acc_s[:, :D] / total).astype(BF)
        lse = m_s[...] * (SCALE * LOG2E) + jnp.log2(jnp.broadcast_to(total, (R, D)))
        lse_ref[i] = lse.T[0:1, :]


def attn_fwd(table, own, q, kv):
    n = sum(x.shape[0] for x in kv) // 2
    return pl.pallas_call(
        fwd_kernel,
        out_shape=(jax.ShapeDtypeStruct((2, R, D), BF), jax.ShapeDtypeStruct((2, 1, R), F32)),
        grid_spec=pltpu.PrefetchScalarGridSpec(
            num_scalar_prefetch=2,
            grid=(),
            in_specs=[VM] + [HB] * PIECES,
            out_specs=(VM, VM),
            scratch_shapes=[
                pltpu.VMEM((2, n, D), BF),
                pltpu.VMEM((R, D), F32),
                pltpu.VMEM((R, 2 * D), F32),
                pltpu.SemaphoreType.DMA((PIECES,)),
            ],
        ),
        compiler_params=params(24),
        cost_estimate=cost(1.6e10, 6, 6e6),
    )(table, own, q, *kv)


def bwd_kernel(loc, own, q_ref, *refs):
    kv_refs = refs[:PIECES]
    (do_ref, o_ref, lse_ref, cosine, sine, gain_q, unit_ref) = refs[PIECES : PIECES + 7]
    (up_ref, mix_ref, gain_ref, mine_ref, theirs_ref, kv, dkv, dqa, sems) = refs[PIECES + 7 :]
    core = own[2]
    load_pieces(kv_refs, kv, core, sems)
    k_ref, v_ref = kv.at[0], kv.at[1]
    dkv[...] = jnp.zeros_like(dkv)
    dqa[...] = jnp.zeros_like(dqa)
    for i in range(2):
        c = own[i]
        q, do, lse = q_ref[i], do_ref[i], lse_ref[i]
        delta = lane_sums(do.astype(F32) * o_ref[i].astype(F32))

        def step(j, masked):
            kk = spans_at(k_ref, loc, 0, j)
            vv = spans_at(v_ref, loc, 1, j)
            p = jnp.exp2(nt(kk, q) * (SCALE * LOG2E) - lse)
            if masked:
                key = j * KC + lax.broadcasted_iota(jnp.int32, (KC, R), 0)
                row = c * SPAN + lax.rem(lax.broadcasted_iota(jnp.int32, (KC, R), 1), SPAN)
                p = jnp.where(key <= row, p, 0.0)
            ds = (p * (nt(vv, do) - delta)).astype(BF)
            dqa[i] += tn(kk, ds)
            dv = nn(p.astype(BF), do)
            dk = nn(ds, q) * SCALE
            for t in range(CH):
                part = slice(t * SPAN, (t + 1) * SPAN)
                at = pl.ds(pl.multiple_of(loc[2, CH * j + t] * SPAN, SPAN), SPAN)
                dkv[0, at, :] += dk[part]
                at = pl.ds(pl.multiple_of(loc[3, CH * j + t] * SPAN, SPAN), SPAN)
                dkv[1, at, :] += dv[part]

        last = c // CH

        def body(j, _):
            step(j, False)
            return 0

        lax.fori_loop(0, last, body, 0)
        step(last, True)
    mine_ref[...] = dkv[core].astype(BF)
    theirs_ref[...] = dkv[1 - core].astype(BF)
    for i in range(2):
        rows = slice(i * SPAN, (i + 1) * SPAN)
        cs, sn = cosine[rows, :], -sine[rows, :]
        mix = None
        for h in range(G):
            cols = slice(h * D, (h + 1) * D)
            grad = turn((dqa[i, :, cols] * SCALE).T, cs, sn)
            unit = unit_ref[rows, cols]
            up = grad * gain_q[:, cols]
            up_ref[rows, cols] = up
            mix = up * unit if mix is None else mix + up * unit
            gain = jnp.sum(grad * unit, axis=0, keepdims=True)
            if i == 0:
                gain_ref[:, cols] = gain
            else:
                gain_ref[:, cols] += gain
        mix_ref[:, rows] = lane_sums(mix)


def attn_bwd(table, own, q, kv, do, o, lse, cosine, sine, gain_q, unit):
    n = sum(x.shape[0] for x in kv) // 2
    rows = 2 * SPAN
    return pl.pallas_call(
        bwd_kernel,
        out_shape=(
            jax.ShapeDtypeStruct((rows, R), F32),
            jax.ShapeDtypeStruct((1, rows), F32),
            jax.ShapeDtypeStruct((1, R), F32),
            jax.ShapeDtypeStruct((n, D), BF),
            jax.ShapeDtypeStruct((n, D), BF),
        ),
        grid_spec=pltpu.PrefetchScalarGridSpec(
            num_scalar_prefetch=2,
            grid=(),
            in_specs=[VM] + [HB] * PIECES + [VM] * 7,
            out_specs=(VM,) * 5,
            scratch_shapes=[
                pltpu.VMEM((2, n, D), BF),
                pltpu.VMEM((2, n, D), F32),
                pltpu.VMEM((2, D, R), F32),
                pltpu.SemaphoreType.DMA((PIECES,)),
            ],
        ),
        compiler_params=params(48),
        cost_estimate=cost(2.2e10, 12, 6e6),
    )(table, own, q, *kv, do, o, lse, cosine, sine, gain_q, unit)


def head_grad_kernel(x, w, out, acc):
    g = pl.program_id(0)
    part = nt(x[...], w[...])

    @pl.when(g == 0)
    def _():
        acc[...] = part

    @pl.when(g > 0)
    def _():
        acc[...] += part

    @pl.when(g == pl.num_programs(0) - 1)
    def _():
        for i in range(2):
            for h in range(G):
                out[i, h * SPAN : (h + 1) * SPAN, :] = acc[
                    i * SPAN : (i + 1) * SPAN, h * D : (h + 1) * D
                ].astype(BF)


def head_grad_of(x, w_out):
    rows, feats = x.shape
    block = feats // 4
    return pl.pallas_call(
        head_grad_kernel,
        out_shape=jax.ShapeDtypeStruct((2, R, D), BF),
        grid=(4,),
        in_specs=[
            pl.BlockSpec((rows, block), lambda g: (0, g)),
            pl.BlockSpec((R, block), lambda g: (0, g)),
        ],
        out_specs=pl.BlockSpec((2, R, D), lambda g: (0, 0, 0)),
        scratch_shapes=[pltpu.VMEM((rows, R), F32)],
        compiler_params=params(14),
        cost_estimate=cost(1.7e9, 9),
    )(x, w_out)


def out_kernel(heads, w, out):
    x = jnp.concatenate(
        [
            jnp.concatenate(
                [heads[i, h * SPAN : (h + 1) * SPAN, :] for h in range(G)], axis=1
            )
            for i in range(2)
        ],
        axis=0,
    )
    out[0] = nn(x, w[...]).astype(BF)


def out_partial_of(heads, w_out):
    feats = w_out.shape[1]
    block = feats // 4
    rows = 2 * SPAN
    return pl.pallas_call(
        out_kernel,
        out_shape=jax.ShapeDtypeStruct((4, rows, block), BF),
        grid=(4,),
        in_specs=[
            pl.BlockSpec((2, R, D), lambda g: (0, 0, 0)),
            pl.BlockSpec((R, block), lambda g: (0, g)),
        ],
        out_specs=pl.BlockSpec((1, rows, block), lambda g: (g, 0, 0)),
        compiler_params=params(14),
        cost_estimate=cost(1.7e9, 9),
    )(heads, w_out)


def query_kernel(x, w, out):
    out[0] = nt(x[...], w[...]).astype(BF)


def query_partial_of(x, w_query):
    rows = x.shape[0]
    feats = w_query.shape[0]
    block = feats // 4
    return pl.pallas_call(
        query_kernel,
        out_shape=jax.ShapeDtypeStruct((4, rows, block), BF),
        grid=(4,),
        in_specs=[
            pl.BlockSpec((rows, R), lambda g: (0, 0)),
            pl.BlockSpec((block, R), lambda g: (g, 0)),
        ],
        out_specs=pl.BlockSpec((1, rows, block), lambda g: (g, 0, 0)),
        compiler_params=params(14),
        cost_estimate=cost(1.7e9, 9),
    )(x, w_query)


def last_kernel(g0, g1, g2, g3, u0, u1, u2, u3, inv, w, query_side, out):
    gs, us = (g0, g1, g2, g3), (u0, u1, u2, u3)
    mix = None
    for g, u in zip(gs, us):
        part = g[:, :D].astype(F32) * u[...].astype(F32)
        mix = part if mix is None else mix + part
    mix = jnp.sum(mix, axis=1, keepdims=True) * (1.0 / K_CHANNELS)
    total = query_side[...].astype(F32)
    for n, (g, u) in enumerate(zip(gs, us)):
        raw = (inv[...] * (g[:, :D].astype(F32) - u[...].astype(F32) * mix)).astype(BF)
        total = total + nt(jnp.concatenate([raw, g[:, D:]], axis=1), w[n])
    out[...] = total.astype(BF)


def last_of(grads, units, inv, w, query_side):
    return pl.pallas_call(
        last_kernel,
        out_shape=jax.ShapeDtypeStruct(query_side.shape, BF),
        in_specs=[VM] * 11,
        out_specs=VM,
        compiler_params=params(12),
        cost_estimate=cost(7e8, 5),
    )(*grads, *units, inv, w, query_side)

QUERY_HEADS = 20
KEY_VALUE_HEADS = 4
Q_CHANNELS = QUERY_HEADS * D
K_CHANNELS = KEY_VALUE_HEADS * D
N_Y, N_Z, N_CORE, N_TP = 4, 4, 2, 4


def ctx_index(y, z, c):
    return (y * N_Z + z) * N_CORE + c


def ctx_pairs(move):
    return [
        (ctx_index(y, z, c), ctx_index(*move(y, z, c)))
        for y in range(N_Y)
        for z in range(N_Z)
        for c in range(N_CORE)
    ]


def shift_first(x, d):
    return lax.ppermute(
        x,
        "ctx",
        ctx_pairs(lambda y, z, c: ((y + c * d) % N_Y, (z + (1 - c) * d) % N_Z, c)),
    )


def shift_second(x, d):
    return lax.ppermute(
        x,
        "ctx",
        ctx_pairs(lambda y, z, c: ((y + (1 - c) * d) % N_Y, (z + c * d) % N_Z, c)),
    )


def swap_core(x):
    return lax.ppermute(x, "ctx", ctx_pairs(lambda y, z, c: (y, z, 1 - c)))


def shift_tp(x, d):
    return lax.ppermute(x, "tp", [(i, (i + d) % N_TP) for i in range(N_TP)])


def shifts(shift, x):
    return [x] + [shift(x, d) for d in DIST[1:]]


def sum_tp(x):
    x = x + lax.ppermute(x, "tp", [(i, i ^ 1) for i in range(N_TP)])
    return x + lax.ppermute(x, "tp", [(i, 3 - i) for i in range(N_TP)])


def sum_ctx(x):
    x = x + swap_core(x)
    x = x + lax.ppermute(x, "ctx", ctx_pairs(lambda y, z, c: (y, z ^ 1, c)))
    x = x + lax.ppermute(x, "ctx", ctx_pairs(lambda y, z, c: (y, 3 - z, c)))
    x = x + lax.ppermute(x, "ctx", ctx_pairs(lambda y, z, c: (y ^ 1, z, c)))
    return x + lax.ppermute(x, "ctx", ctx_pairs(lambda y, z, c: (3 - y, z, c)))


def after(x, *others):
    return lax.optimization_barrier((x,) + others)[0]


def outgoing(x):
    rows = x.shape[0] // 4
    return [x[d * rows : (d + 1) * rows].astype(BF) for d in DIST[1:]], x[:rows]


def incoming(shift, sent, total):
    for x, d in zip(sent, DIST[1:]):
        total = total + shift(x, d).astype(F32)
    return total


def local(tokens, span_order, w_query, w_key, value_weight, w_out, gain_query, gain_key, out_grad):
    rows, feats = tokens.shape
    me = lax.axis_index("ctx")
    tp = lax.axis_index("tp")
    my_y, my_z, my_c = me // 8, (me // 2) % 4, me % 2

    with jax.named_scope("gather_tokens"):
        left = shift_tp(tokens, 1)
        right = shift_tp(tokens, 3)
    place = jnp.arange(64, dtype=jnp.int32)
    stored = jnp.sum(jnp.where(span_order[None, :] == place[:, None], place[None, :], 0), axis=1)
    src, half = stored // 2, stored % 2
    src_y, src_z, src_c = src // 8, (src // 2) % 4, src % 2
    to_y, to_z = (src_y - my_y) % 4, (src_z - my_z) % 4
    back_y, back_z = (4 - to_y) % 4, (4 - to_z) % 4
    slot_y = jnp.where(back_y >= 2, 5 - back_y, back_y)
    slot_z = jnp.where(back_z >= 2, 5 - back_z, back_z)
    table = jnp.stack(
        [
            ((slot_y * 4 + slot_z) * 2 + src_c) * 2 + half,
            ((slot_z * 4 + slot_y) * 2 + 1 - src_c) * 2 + half,
            ((to_z * 4 + to_y) * 2 + src_c) * 2 + half,
            ((to_y * 4 + to_z) * 2 + src_c) * 2 + half,
        ]
    ).astype(jnp.int32)
    own = lax.dynamic_slice_in_dim(span_order, 2 * me, 2)
    own = jnp.concatenate([own, my_c[None]]).astype(jnp.int32)

    query_pos = (own[:2, None] * SPAN + jnp.arange(SPAN)[None, :]).reshape(-1)
    frequency = jnp.exp(jnp.arange(D // 2).astype(F32) * (-2.0 * math.log(500000.0) / D))
    angles = query_pos.astype(F32)[:, None] * frequency[None, :]
    cosine, sine = jnp.cos(angles), jnp.sin(angles)
    cosine = jnp.concatenate([cosine, cosine], axis=1)
    sine = jnp.concatenate([-sine, sine], axis=1)

    offs = jnp.stack([(tp - d) % 4 for d in DIST]).astype(jnp.int32)
    with jax.named_scope("gather_tokens"):
        mid = rows // 2
        near, cosine, sine, offs, table, own = lax.optimization_barrier(
            (left[:mid], cosine, sine, offs, table, own)
        )
        far_a = shift_tp(near, 1)
        far_b = shift_tp(right[mid:], 3)
        pieces = (tokens, left, right, far_a, far_b)
    gain_q, gain_k = gain_query[None, :], gain_key[None, :]
    q_rot, q_raw, k_rot, k_raw, value, squares = project(
        offs, pieces, w_query, w_key, value_weight, cosine, sine, gain_q, gain_k
    )
    with jax.named_scope("norm_sums"):
        squares = sum_tp(squares)
    query_inv = lax.rsqrt(squares[0] / Q_CHANNELS + 1e-06)[:, None]
    key_inv = lax.rsqrt(squares[1] / K_CHANNELS + 1e-06)[:, None]
    key = (k_rot * key_inv).astype(BF)

    with jax.named_scope("gather_keys_values"):
        first_core = my_c == 0
        mine = jnp.where(first_core, key, value)
        pair = join(mine, swap_core(jnp.where(first_core, value, key)))
        plane = join(*shifts(shift_first, pair))
        mine = shifts(shift_second, plane)
        kv = (*mine, *(swap_core(x) for x in mine))

    query_unit = q_raw * query_inv
    key_unit = k_raw * key_inv
    query = (
        (q_rot.reshape(2, G, SPAN, D) * query_inv.reshape(2, 1, SPAN, 1)).astype(BF).reshape(2, R, D)
    )
    with jax.named_scope("gather_key_units"):
        key_units = shifts(shift_tp, key_unit.astype(BF))

    with jax.named_scope("gather_out_grad"):
        grad_part = lax.all_gather(after(out_grad, far_a, far_b), "tp", axis=1, tiled=True)
        head_grad = head_grad_of(grad_part, w_out)

    with jax.named_scope("weight_rows"):
        share = feats // 32
        cut = []
        for d in DIST:
            start = feats * ((tp + d) % 4) + share * me
            piece = jnp.concatenate(
                [lax.dynamic_slice_in_dim(w, start, share, 0) for w in (w_key, value_weight)],
                axis=1,
            )
            cut.append(shift_tp(piece, d) if d else piece)
        cut = after(jnp.stack(cut), grad_part)
        w_rows = lax.all_gather(cut, "ctx", axis=0, tiled=False)
        w_rows = w_rows.transpose(1, 0, 2, 3).reshape(4, feats, 2 * D)

    heads, log_total = attn_fwd(table, own, after(query, head_grad), kv)
    out_partial = out_partial_of(heads, w_out)
    attn_out = lax.psum_scatter(out_partial, "tp", scatter_dimension=0, tiled=False)

    up_query, mix_query, gain_part, mine, theirs = attn_bwd(
        table, own, after(query, out_partial), kv, head_grad, heads, log_total,
        cosine, sine, gain_q, query_unit,
    )

    with jax.named_scope("sum_key_value_grads"):
        summed = mine.astype(F32) + swap_core(theirs).astype(F32)
        sent, total = outgoing(summed)
        sent, total, up_query, mix_query = lax.optimization_barrier(
            (sent, total, up_query, mix_query)
        )
        sent, total = outgoing(incoming(shift_first, sent, total))
        total = incoming(shift_second, sent, total)
        ours, its = total[:rows], total[rows:]
        kept = jnp.where(first_core, ours, its)
        swapped = swap_core(jnp.where(first_core, its, ours))
        key_grad_rot = jnp.where(first_core, kept, swapped)
        value_grad = jnp.where(first_core, swapped, kept).astype(BF)

    with jax.named_scope("query_side"):
        mix_query = sum_tp(mix_query)[0] / Q_CHANNELS
        raw_query_grad = (query_inv * (up_query - query_unit * mix_query[:, None])).astype(BF)
        query_partial = query_partial_of(after(raw_query_grad, attn_out, w_rows), w_query)
        query_side = lax.psum_scatter(query_partial, "tp", scatter_dimension=0, tiled=False)

    with jax.named_scope("key_value_side"):
        first, second = key_grad_rot[:, : D // 2], key_grad_rot[:, D // 2 :]
        cs, sn = cosine[:, : D // 2], sine[:, D // 2 :]
        key_grad = jnp.concatenate([first * cs + second * sn, second * cs - first * sn], axis=1)
        both = jnp.concatenate([(key_grad * gain_k).astype(BF), value_grad], axis=1)
        grads = shifts(shift_tp, both)
        gain_key_part = jnp.sum(key_grad * key_unit, axis=0)[None]
        gains = sum_ctx(jnp.concatenate([gain_part, gain_key_part], axis=1))[0]
        gain_query_grad, gain_key_grad = gains[:R], gains[R:]
        input_grad = last_of(grads, key_units, key_inv, w_rows, query_side)
    return (attn_out, input_grad, gain_query_grad, gain_key_grad)


def solution(mesh):
    return jax.shard_map(
        local,
        mesh=mesh,
        in_specs=(
            P("ctx", "tp"),
            P(),
            P(None, "tp"),
            P(None, "tp"),
            P(None, "tp"),
            P("tp", None),
            P("tp"),
            P("tp"),
            P("ctx", "tp"),
        ),
        out_specs=(P("ctx", "tp"), P("ctx", "tp"), P("tp"), P("tp")),
        check_vma=False,
    )
```

```python
import math

import jax
import jax.numpy as jnp
from jax import lax
from jax.experimental import pallas as pl
from jax.experimental.pallas import tpu as pltpu
from jax.sharding import PartitionSpec as P

D = 128
SPAN = 128
G = 5
R = G * SPAN
CH = 8
KC = CH * SPAN
SCALE = D**-0.5
LOG2E = math.log2(math.e)
NEG = -1e30
BF = jnp.bfloat16
F32 = jnp.float32
DIST = (0, 1, 3, 2)
PIECES = 8


def nt(a, b):
    return lax.dot_general(a, b, (((1,), (1,)), ((), ())), preferred_element_type=F32)


def tn(a, b):
    return lax.dot_general(a, b, (((0,), (0,)), ((), ())), preferred_element_type=F32)


def nn(a, b):
    return lax.dot_general(a, b, (((1,), (0,)), ((), ())), preferred_element_type=F32)


VM = pl.BlockSpec(memory_space=pltpu.VMEM)
HB = pl.BlockSpec(memory_space=pl.ANY)


def params(mib):
    return pltpu.CompilerParams(vmem_limit_bytes=mib * 2**20)


def cost(flops, mib, exps=0):
    return pl.CostEstimate(
        flops=int(flops), bytes_accessed=int(mib * 2**20), transcendentals=int(exps)
    )


def turn(x, cosine, sine):
    return x * cosine + pltpu.roll(x, D // 2, 1) * sine


def lane_sums(x):
    return jnp.sum(x.T, axis=0, keepdims=True)


def project_kernel(
    off, x0, x1, x2, xa, xb, wq, wk, wv, cosine, sine, gain_q, gain_k,
    q_rot, q_raw, k_rot, k_raw, v_out, squares, acc,
):
    g = pl.program_id(0)

    def add(x, rows, first):
        for w, at in ((wq, slice(0, R)), (wk, slice(R, R + D)), (wv, slice(R + D, R + 2 * D))):
            part = nn(x, w[...])
            if first:
                acc[rows, at] = part
            else:
                acc[rows, at] += part

    @pl.when(g == 0)
    def _():
        add(x0[...], slice(0, 256), True)

    @pl.when(g == 1)
    def _():
        add(x1[...], slice(0, 256), False)

    @pl.when(g == 2)
    def _():
        add(x2[...], slice(0, 256), False)

    @pl.when(g == 3)
    def _():
        add(jnp.concatenate([xa[...], xb[...]], axis=0), slice(0, 256), False)
        cs, sn = cosine[...], sine[...]
        k = acc[:, R : R + D]
        k_raw[...] = k
        k_rot[...] = turn(k * gain_k[...], cs, sn)
        v_out[...] = acc[:, R + D :].astype(BF)
        squares[1:2, :] = lane_sums(k * k)
        total = None
        for h in range(G):
            q = acc[:, h * D : (h + 1) * D]
            total = q * q if total is None else total + q * q
            rotated = turn(q * gain_q[:, h * D : (h + 1) * D], cs, sn)
            for i in range(2):
                q_rot[i, h * SPAN : (h + 1) * SPAN, :] = rotated[i * SPAN : (i + 1) * SPAN]
        q_raw[...] = acc[:, :R]
        squares[0:1, :] = lane_sums(total)


def project(off, pieces, w_query, w_key, value_weight, cosine, sine, gain_q, gain_k):
    feats = pieces[0].shape[1]
    rows = 2 * SPAN

    def full(x):
        return pl.BlockSpec(x.shape, lambda g, off: (0,) * len(x.shape))

    def wspec(w):
        return pl.BlockSpec((feats, w.shape[1]), lambda g, off: (off[g], 0))

    outs = (
        jax.ShapeDtypeStruct((2, R, D), F32),
        jax.ShapeDtypeStruct((rows, R), F32),
        jax.ShapeDtypeStruct((rows, D), F32),
        jax.ShapeDtypeStruct((rows, D), F32),
        jax.ShapeDtypeStruct((rows, D), BF),
        jax.ShapeDtypeStruct((2, rows), F32),
    )
    rest = (cosine, sine, gain_q, gain_k)
    return pl.pallas_call(
        project_kernel,
        out_shape=outs,
        grid_spec=pltpu.PrefetchScalarGridSpec(
            num_scalar_prefetch=1,
            grid=(4,),
            in_specs=[full(x) for x in pieces]
            + [wspec(w) for w in (w_query, w_key, value_weight)]
            + [full(x) for x in rest],
            out_specs=tuple(full(o) for o in outs),
            scratch_shapes=[pltpu.VMEM((rows, R + 2 * D), F32)],
        ),
        compiler_params=params(20),
        cost_estimate=cost(2.4e9, 14),
    )(off, *pieces, w_query, w_key, value_weight, *rest)


def join_kernel(*refs):
    at = 0
    for ref in refs[:-1]:
        n = ref.shape[0]
        refs[-1][at : at + n, :] = ref[...]
        at += n


def join(*xs):
    rows = sum(x.shape[0] for x in xs)
    return pl.pallas_call(
        join_kernel,
        out_shape=jax.ShapeDtypeStruct((rows,) + xs[0].shape[1:], xs[0].dtype),
        in_specs=[VM] * len(xs),
        out_specs=VM,
        compiler_params=params(8),
        cost_estimate=cost(0, 1),
    )(*xs)


def spans_at(ref, loc, which, j):
    return jnp.concatenate(
        [
            ref[pl.ds(pl.multiple_of(loc[which, CH * j + t] * SPAN, SPAN), SPAN), :]
            for t in range(CH)
        ],
        axis=0,
    )


def load_pieces(refs, whole, core, sems):
    count = len(refs) // 2
    copies = []
    for n, src in enumerate(refs):
        rows = src.shape[0]
        to = core if n < count else 1 - core
        copy = pltpu.make_async_copy(
            src, whole.at[to, pl.ds((n % count) * rows, rows), :], sems.at[n]
        )
        copy.start()
        copies.append(copy)
    for copy in copies:
        copy.wait()


def fwd_kernel(loc, own, q_ref, *refs):
    kv_refs, (o_ref, lse_ref, kv, m_s, acc_s, sems) = refs[:PIECES], refs[PIECES:]
    load_pieces(kv_refs, kv, own[2], sems)
    k_ref, v_ref = kv.at[0], kv.at[1]
    ones = (lax.broadcasted_iota(jnp.int32, (KC, D), 1) == 0).astype(BF)
    for i in range(2):
        c = own[i]
        m_s[...] = jnp.full_like(m_s, NEG)
        acc_s[...] = jnp.zeros_like(acc_s)

        def step(j, masked):
            kk = spans_at(k_ref, loc, 0, j)
            vv = jnp.concatenate([spans_at(v_ref, loc, 1, j), ones], axis=1)
            for h in range(G):
                at = slice(h * SPAN, (h + 1) * SPAN)
                s = nt(q_ref[i, at, :], kk)
                if masked:
                    key = j * KC + lax.broadcasted_iota(jnp.int32, (SPAN, KC), 1)
                    row = c * SPAN + lax.broadcasted_iota(jnp.int32, (SPAN, KC), 0)
                    s = jnp.where(key <= row, s, NEG)
                m = m_s[at, :]
                new = jnp.maximum(m, jnp.max(s, axis=1, keepdims=True))
                shrink = jnp.exp2((m - new) * (SCALE * LOG2E))
                p = jnp.exp2((s - new[:, :1]) * (SCALE * LOG2E))
                m_s[at, :] = new
                acc_s[at, :] = acc_s[at, :] * shrink[:, :1] + nn(p.astype(BF), vv)

        last = c // CH

        def body(j, _):
            step(j, False)
            return 0

        lax.fori_loop(0, last, body, 0)
        step(last, True)
        total = acc_s[:, D : D + 1]
        o_ref[i] = (acc_s[:, :D] / total).astype(BF)
        lse = m_s[...] * (SCALE * LOG2E) + jnp.log2(jnp.broadcast_to(total, (R, D)))
        lse_ref[i] = lse.T[0:1, :]


def attn_fwd(table, own, q, kv):
    n = sum(x.shape[0] for x in kv) // 2
    return pl.pallas_call(
        fwd_kernel,
        out_shape=(
            jax.ShapeDtypeStruct((2, R, D), BF),
            jax.ShapeDtypeStruct((2, 1, R), F32),
            jax.ShapeDtypeStruct((2, n, D), BF),
        ),
        grid_spec=pltpu.PrefetchScalarGridSpec(
            num_scalar_prefetch=2,
            grid=(),
            in_specs=[VM] + [HB] * PIECES,
            out_specs=(VM, VM, VM),
            scratch_shapes=[
                pltpu.VMEM((R, D), F32),
                pltpu.VMEM((R, 2 * D), F32),
                pltpu.SemaphoreType.DMA((PIECES,)),
            ],
        ),
        compiler_params=params(24),
        cost_estimate=cost(1.6e10, 6, 6e6),
    )(table, own, q, *kv)


def bwd_kernel(
    loc, own, q_ref, kv, do_ref, o_ref, lse_ref, cosine, sine, gain_q, unit_ref,
    up_ref, mix_ref, gain_ref, mine_ref, theirs_ref, dkv, dqa,
):
    core = own[2]
    k_ref, v_ref = kv.at[0], kv.at[1]
    dkv[...] = jnp.zeros_like(dkv)
    dqa[...] = jnp.zeros_like(dqa)
    for i in range(2):
        c = own[i]
        q, do, lse = q_ref[i], do_ref[i], lse_ref[i]
        delta = lane_sums(do.astype(F32) * o_ref[i].astype(F32))

        def step(j, masked):
            kk = spans_at(k_ref, loc, 0, j)
            vv = spans_at(v_ref, loc, 1, j)
            p = jnp.exp2(nt(kk, q) * (SCALE * LOG2E) - lse)
            if masked:
                key = j * KC + lax.broadcasted_iota(jnp.int32, (KC, R), 0)
                row = c * SPAN + lax.rem(lax.broadcasted_iota(jnp.int32, (KC, R), 1), SPAN)
                p = jnp.where(key <= row, p, 0.0)
            ds = (p * (nt(vv, do) - delta)).astype(BF)
            dqa[i] += tn(kk, ds)
            dv = nn(p.astype(BF), do)
            dk = nn(ds, q) * SCALE
            for t in range(CH):
                part = slice(t * SPAN, (t + 1) * SPAN)
                at = pl.ds(pl.multiple_of(loc[2, CH * j + t] * SPAN, SPAN), SPAN)
                dkv[0, at, :] += dk[part]
                at = pl.ds(pl.multiple_of(loc[3, CH * j + t] * SPAN, SPAN), SPAN)
                dkv[1, at, :] += dv[part]

        last = c // CH

        def body(j, _):
            step(j, False)
            return 0

        lax.fori_loop(0, last, body, 0)
        step(last, True)
    mine_ref[...] = dkv[core].astype(BF)
    theirs_ref[...] = dkv[1 - core].astype(BF)
    for i in range(2):
        rows = slice(i * SPAN, (i + 1) * SPAN)
        cs, sn = cosine[rows, :], -sine[rows, :]
        mix = None
        for h in range(G):
            cols = slice(h * D, (h + 1) * D)
            grad = turn((dqa[i, :, cols] * SCALE).T, cs, sn)
            unit = unit_ref[rows, cols]
            up = grad * gain_q[:, cols]
            up_ref[rows, cols] = up
            mix = up * unit if mix is None else mix + up * unit
            gain = jnp.sum(grad * unit, axis=0, keepdims=True)
            if i == 0:
                gain_ref[:, cols] = gain
            else:
                gain_ref[:, cols] += gain
        mix_ref[:, rows] = lane_sums(mix)


def attn_bwd(table, own, q, kv, do, o, lse, cosine, sine, gain_q, unit):
    n = kv.shape[1]
    rows = 2 * SPAN
    return pl.pallas_call(
        bwd_kernel,
        out_shape=(
            jax.ShapeDtypeStruct((rows, R), F32),
            jax.ShapeDtypeStruct((1, rows), F32),
            jax.ShapeDtypeStruct((1, R), F32),
            jax.ShapeDtypeStruct((n, D), BF),
            jax.ShapeDtypeStruct((n, D), BF),
        ),
        grid_spec=pltpu.PrefetchScalarGridSpec(
            num_scalar_prefetch=2,
            grid=(),
            in_specs=[VM] * 9,
            out_specs=(VM,) * 5,
            scratch_shapes=[
                pltpu.VMEM((2, n, D), F32),
                pltpu.VMEM((2, D, R), F32),
            ],
        ),
        compiler_params=params(36),
        cost_estimate=cost(2.2e10, 12, 6e6),
    )(table, own, q, kv, do, o, lse, cosine, sine, gain_q, unit)


def head_grad_kernel(x, w, out, acc):
    g = pl.program_id(0)
    part = nt(x[...], w[...])

    @pl.when(g == 0)
    def _():
        acc[...] = part

    @pl.when(g > 0)
    def _():
        acc[...] += part

    @pl.when(g == pl.num_programs(0) - 1)
    def _():
        for i in range(2):
            for h in range(G):
                out[i, h * SPAN : (h + 1) * SPAN, :] = acc[
                    i * SPAN : (i + 1) * SPAN, h * D : (h + 1) * D
                ].astype(BF)


def head_grad_of(x, w_out):
    rows, feats = x.shape
    block = feats // 4
    return pl.pallas_call(
        head_grad_kernel,
        out_shape=jax.ShapeDtypeStruct((2, R, D), BF),
        grid=(4,),
        in_specs=[
            pl.BlockSpec((rows, block), lambda g: (0, g)),
            pl.BlockSpec((R, block), lambda g: (0, g)),
        ],
        out_specs=pl.BlockSpec((2, R, D), lambda g: (0, 0, 0)),
        scratch_shapes=[pltpu.VMEM((rows, R), F32)],
        compiler_params=params(14),
        cost_estimate=cost(1.7e9, 9),
    )(x, w_out)


def out_kernel(heads, w, out):
    x = jnp.concatenate(
        [
            jnp.concatenate(
                [heads[i, h * SPAN : (h + 1) * SPAN, :] for h in range(G)], axis=1
            )
            for i in range(2)
        ],
        axis=0,
    )
    out[0] = nn(x, w[...]).astype(BF)


def out_partial_of(heads, w_out):
    feats = w_out.shape[1]
    block = feats // 4
    rows = 2 * SPAN
    return pl.pallas_call(
        out_kernel,
        out_shape=jax.ShapeDtypeStruct((4, rows, block), BF),
        grid=(4,),
        in_specs=[
            pl.BlockSpec((2, R, D), lambda g: (0, 0, 0)),
            pl.BlockSpec((R, block), lambda g: (0, g)),
        ],
        out_specs=pl.BlockSpec((1, rows, block), lambda g: (g, 0, 0)),
        compiler_params=params(14),
        cost_estimate=cost(1.7e9, 9),
    )(heads, w_out)


def query_kernel(x, w, out):
    out[0] = nt(x[...], w[...]).astype(BF)


def query_partial_of(x, w_query):
    rows = x.shape[0]
    feats = w_query.shape[0]
    block = feats // 4
    return pl.pallas_call(
        query_kernel,
        out_shape=jax.ShapeDtypeStruct((4, rows, block), BF),
        grid=(4,),
        in_specs=[
            pl.BlockSpec((rows, R), lambda g: (0, 0)),
            pl.BlockSpec((block, R), lambda g: (g, 0)),
        ],
        out_specs=pl.BlockSpec((1, rows, block), lambda g: (g, 0, 0)),
        compiler_params=params(14),
        cost_estimate=cost(1.7e9, 9),
    )(x, w_query)


def last_kernel(g0, g1, g2, g3, u0, u1, u2, u3, inv, w, query_side, out):
    gs, us = (g0, g1, g2, g3), (u0, u1, u2, u3)
    mix = None
    for g, u in zip(gs, us):
        part = g[:, :D].astype(F32) * u[...].astype(F32)
        mix = part if mix is None else mix + part
    mix = jnp.sum(mix, axis=1, keepdims=True) * (1.0 / K_CHANNELS)
    total = query_side[...].astype(F32)
    for n, (g, u) in enumerate(zip(gs, us)):
        raw = (inv[...] * (g[:, :D].astype(F32) - u[...].astype(F32) * mix)).astype(BF)
        total = total + nt(jnp.concatenate([raw, g[:, D:]], axis=1), w[n])
    out[...] = total.astype(BF)


def last_of(grads, units, inv, w, query_side):
    return pl.pallas_call(
        last_kernel,
        out_shape=jax.ShapeDtypeStruct(query_side.shape, BF),
        in_specs=[VM] * 11,
        out_specs=VM,
        compiler_params=params(12),
        cost_estimate=cost(7e8, 5),
    )(*grads, *units, inv, w, query_side)

QUERY_HEADS = 20
KEY_VALUE_HEADS = 4
Q_CHANNELS = QUERY_HEADS * D
K_CHANNELS = KEY_VALUE_HEADS * D
N_Y, N_Z, N_CORE, N_TP = 4, 4, 2, 4


def ctx_index(y, z, c):
    return (y * N_Z + z) * N_CORE + c


def ctx_pairs(move):
    return [
        (ctx_index(y, z, c), ctx_index(*move(y, z, c)))
        for y in range(N_Y)
        for z in range(N_Z)
        for c in range(N_CORE)
    ]


def shift_first(x, d):
    return lax.ppermute(
        x,
        "ctx",
        ctx_pairs(lambda y, z, c: ((y + c * d) % N_Y, (z + (1 - c) * d) % N_Z, c)),
    )


def shift_second(x, d):
    return lax.ppermute(
        x,
        "ctx",
        ctx_pairs(lambda y, z, c: ((y + (1 - c) * d) % N_Y, (z + c * d) % N_Z, c)),
    )


def swap_core(x):
    return lax.ppermute(x, "ctx", ctx_pairs(lambda y, z, c: (y, z, 1 - c)))


def shift_tp(x, d):
    return lax.ppermute(x, "tp", [(i, (i + d) % N_TP) for i in range(N_TP)])


def shifts(shift, x):
    return [x] + [shift(x, d) for d in DIST[1:]]


def sum_tp(x):
    x = x + lax.ppermute(x, "tp", [(i, i ^ 1) for i in range(N_TP)])
    return x + lax.ppermute(x, "tp", [(i, 3 - i) for i in range(N_TP)])


def sum_ctx(x):
    x = x + swap_core(x)
    x = x + lax.ppermute(x, "ctx", ctx_pairs(lambda y, z, c: (y, z ^ 1, c)))
    x = x + lax.ppermute(x, "ctx", ctx_pairs(lambda y, z, c: (y, 3 - z, c)))
    x = x + lax.ppermute(x, "ctx", ctx_pairs(lambda y, z, c: (y ^ 1, z, c)))
    return x + lax.ppermute(x, "ctx", ctx_pairs(lambda y, z, c: (3 - y, z, c)))


def after(x, *others):
    return lax.optimization_barrier((x,) + others)[0]


def outgoing(x):
    rows = x.shape[0] // 4
    return [x[d * rows : (d + 1) * rows].astype(BF) for d in DIST[1:]], x[:rows]


def add_up(total, arrived):
    for x in arrived:
        total = total + x.astype(F32)
    return total


def local(tokens, span_order, w_query, w_key, value_weight, w_out, gain_query, gain_key, out_grad):
    rows, feats = tokens.shape
    me = lax.axis_index("ctx")
    tp = lax.axis_index("tp")
    my_y, my_z, my_c = me // 8, (me // 2) % 4, me % 2

    with jax.named_scope("gather_tokens"):
        left = shift_tp(tokens, 1)
        right = shift_tp(tokens, 3)
    place = jnp.arange(64, dtype=jnp.int32)
    stored = jnp.sum(jnp.where(span_order[None, :] == place[:, None], place[None, :], 0), axis=1)
    src, half = stored // 2, stored % 2
    src_y, src_z, src_c = src // 8, (src // 2) % 4, src % 2
    to_y, to_z = (src_y - my_y) % 4, (src_z - my_z) % 4
    back_y, back_z = (4 - to_y) % 4, (4 - to_z) % 4
    slot_y = jnp.where(back_y >= 2, 5 - back_y, back_y)
    slot_z = jnp.where(back_z >= 2, 5 - back_z, back_z)
    table = jnp.stack(
        [
            ((slot_y * 4 + slot_z) * 2 + src_c) * 2 + half,
            ((slot_z * 4 + slot_y) * 2 + 1 - src_c) * 2 + half,
            ((to_z * 4 + to_y) * 2 + src_c) * 2 + half,
            ((to_y * 4 + to_z) * 2 + src_c) * 2 + half,
        ]
    ).astype(jnp.int32)
    own = lax.dynamic_slice_in_dim(span_order, 2 * me, 2)
    own = jnp.concatenate([own, my_c[None]]).astype(jnp.int32)

    query_pos = (own[:2, None] * SPAN + jnp.arange(SPAN)[None, :]).reshape(-1)
    frequency = jnp.exp(jnp.arange(D // 2).astype(F32) * (-2.0 * math.log(500000.0) / D))
    angles = query_pos.astype(F32)[:, None] * frequency[None, :]
    cosine, sine = jnp.cos(angles), jnp.sin(angles)
    cosine = jnp.concatenate([cosine, cosine], axis=1)
    sine = jnp.concatenate([-sine, sine], axis=1)

    with jax.named_scope("weight_rows"):
        share = feats // 32
        cut = []
        for d in DIST:
            start = feats * ((tp + d) % 4) + share * me
            piece = jnp.concatenate(
                [lax.dynamic_slice_in_dim(w, start, share, 0) for w in (w_key, value_weight)],
                axis=1,
            )
            cut.append(shift_tp(piece, d) if d else piece)
        cut = jnp.stack(cut)

    offs = jnp.stack([(tp - d) % 4 for d in DIST]).astype(jnp.int32)
    with jax.named_scope("gather_tokens"):
        mid = rows // 2
        near, cosine, sine, offs, table, own, cut = lax.optimization_barrier(
            (left[:mid], cosine, sine, offs, table, own, cut)
        )
        far_a = shift_tp(near, 1)
        far_b = shift_tp(right[mid:], 3)
        pieces = (tokens, left, right, far_a, far_b)
    gain_q, gain_k = gain_query[None, :], gain_key[None, :]
    q_rot, q_raw, k_rot, k_raw, value, squares = project(
        offs, pieces, w_query, w_key, value_weight, cosine, sine, gain_q, gain_k
    )
    with jax.named_scope("norm_sums"):
        squares = sum_tp(squares)
    query_inv = lax.rsqrt(squares[0] / Q_CHANNELS + 1e-06)[:, None]
    key_inv = lax.rsqrt(squares[1] / K_CHANNELS + 1e-06)[:, None]
    key = (k_rot * key_inv).astype(BF)

    with jax.named_scope("gather_keys_values"):
        first_core = my_c == 0
        mine = jnp.where(first_core, key, value)
        pair = join(mine, swap_core(jnp.where(first_core, value, key)))
        plane = join(*shifts(shift_first, pair))
        mine = shifts(shift_second, plane)
    with jax.named_scope("weight_rows"):
        w_rows = lax.all_gather(after(cut, pair), "ctx", axis=0, tiled=False)

    query_unit = q_raw * query_inv
    key_unit = k_raw * key_inv
    query = (
        (q_rot.reshape(2, G, SPAN, D) * query_inv.reshape(2, 1, SPAN, 1)).astype(BF).reshape(2, R, D)
    )
    with jax.named_scope("gather_key_units"):
        key_units = shifts(shift_tp, key_unit.astype(BF))

    with jax.named_scope("gather_out_grad"):
        grad_part = lax.all_gather(after(out_grad, far_a, far_b), "tp", axis=1, tiled=True)
        head_grad = head_grad_of(grad_part, w_out)

    with jax.named_scope("swap_keys_values"):
        last, query, query_unit, head_grad = lax.optimization_barrier(
            (mine[3], query, query_unit, head_grad)
        )
        mine = mine[:3] + [last]
        pieces = (*mine, *(swap_core(x) for x in mine))

    heads, log_total, kv = attn_fwd(table, own, query, pieces)
    out_partial = out_partial_of(heads, w_out)
    attn_out = lax.psum_scatter(out_partial, "tp", scatter_dimension=0, tiled=False)

    query, out_partial, *key_units = lax.optimization_barrier((query, out_partial, *key_units))
    up_query, mix_query, gain_part, mine, theirs = attn_bwd(
        table, own, query, kv, head_grad, heads, log_total,
        cosine, sine, gain_q, query_unit,
    )

    with jax.named_scope("sum_key_value_grads"):
        summed = mine.astype(F32) + swap_core(theirs).astype(F32)
        sent, total = outgoing(summed)
        arrived = [shift_first(x, d) for x, d in zip(sent, DIST[1:])]
        arrived[0], up_query, w_rows = lax.optimization_barrier((arrived[0], up_query, w_rows))
        sent, total = outgoing(add_up(total, arrived))
        total = add_up(total, [shift_second(x, d) for x, d in zip(sent, DIST[1:])])
        ours, its = total[:rows], total[rows:]
        kept = jnp.where(first_core, ours, its)
        swapped = swap_core(jnp.where(first_core, its, ours))
        key_grad_rot = jnp.where(first_core, kept, swapped)
        value_grad = jnp.where(first_core, swapped, kept).astype(BF)

    with jax.named_scope("query_side"):
        mix_query = sum_tp(mix_query)[0] / Q_CHANNELS
        raw_query_grad = (query_inv * (up_query - query_unit * mix_query[:, None])).astype(BF)
        query_partial = query_partial_of(after(raw_query_grad, attn_out), w_query)
        query_side = lax.psum_scatter(query_partial, "tp", scatter_dimension=0, tiled=False)

    with jax.named_scope("key_value_side"):
        first, second = key_grad_rot[:, : D // 2], key_grad_rot[:, D // 2 :]
        cs, sn = cosine[:, : D // 2], sine[:, D // 2 :]
        key_grad = jnp.concatenate([first * cs + second * sn, second * cs - first * sn], axis=1)
        w_rows = after(w_rows, query_partial).transpose(1, 0, 2, 3).reshape(4, feats, 2 * D)
        key_grad, w_rows = lax.optimization_barrier((key_grad, w_rows))
        both = jnp.concatenate([(key_grad * gain_k).astype(BF), value_grad], axis=1)
        grads = shifts(shift_tp, both)
        gain_key_part = jnp.sum(key_grad * key_unit, axis=0)[None]
        gains = sum_ctx(jnp.concatenate([gain_part, gain_key_part], axis=1))[0]
        gain_query_grad, gain_key_grad = gains[:R], gains[R:]
        input_grad = last_of(grads, key_units, key_inv, w_rows, query_side)
    return (attn_out, input_grad, gain_query_grad, gain_key_grad)


def solution(mesh):
    return jax.shard_map(
        local,
        mesh=mesh,
        in_specs=(
            P("ctx", "tp"),
            P(),
            P(None, "tp"),
            P(None, "tp"),
            P(None, "tp"),
            P("tp", None),
            P("tp"),
            P("tp"),
            P("ctx", "tp"),
        ),
        out_specs=(P("ctx", "tp"), P("ctx", "tp"), P("tp"), P("tp")),
        check_vma=False,
    )
```

```python
import math

import jax
import jax.numpy as jnp
from jax import lax
from jax.experimental import pallas as pl
from jax.experimental.pallas import tpu as pltpu
from jax.sharding import PartitionSpec as P

D = 128
SPAN = 128
G = 5
R = G * SPAN
CH = 8
KC = CH * SPAN
SCALE = D**-0.5
LOG2E = math.log2(math.e)
NEG = -1e30
BF = jnp.bfloat16
F32 = jnp.float32
DIST = (0, 1, 3, 2)
PIECES = 8


def nt(a, b):
    return lax.dot_general(a, b, (((1,), (1,)), ((), ())), preferred_element_type=F32)


def tn(a, b):
    return lax.dot_general(a, b, (((0,), (0,)), ((), ())), preferred_element_type=F32)


def nn(a, b):
    return lax.dot_general(a, b, (((1,), (0,)), ((), ())), preferred_element_type=F32)


VM = pl.BlockSpec(memory_space=pltpu.VMEM)
HB = pl.BlockSpec(memory_space=pl.ANY)


def params(mib):
    return pltpu.CompilerParams(vmem_limit_bytes=mib * 2**20)


def cost(flops, mib, exps=0):
    return pl.CostEstimate(
        flops=int(flops), bytes_accessed=int(mib * 2**20), transcendentals=int(exps)
    )


def turn(x, cosine, sine):
    return x * cosine + pltpu.roll(x, D // 2, 1) * sine


def lane_sums(x):
    return jnp.sum(x.T, axis=0, keepdims=True)


def add_piece(acc, x, weights, first):
    at = 0
    for w in weights:
        cols = slice(at, at + w.shape[1])
        at += w.shape[1]
        part = nn(x, w[...])
        if first:
            acc[:, cols] = part
        else:
            acc[:, cols] += part


def project_kernel(off, *refs, count, first):
    xs, weights = refs[:count], refs[count : count + 3]
    out = refs[-1]
    g = pl.program_id(0)
    for n in range(count):

        @pl.when(g == n)
        def _(n=n):
            if n == 0 and not first:
                out[...] = refs[count + 3][...]
            add_piece(out, xs[n][...], weights, first and n == 0)


def project(off, pieces, weights, acc=None):
    rows, feats = pieces[0].shape
    width = sum(w.shape[1] for w in weights)

    def full(x):
        return pl.BlockSpec(x.shape, lambda g, off: (0,) * len(x.shape))

    def wspec(w):
        return pl.BlockSpec((feats, w.shape[1]), lambda g, off: (off[g], 0))

    out = jax.ShapeDtypeStruct((rows, width), F32)
    more = () if acc is None else (acc,)
    return pl.pallas_call(
        lambda *refs: project_kernel(*refs, count=len(pieces), first=acc is None),
        out_shape=out,
        grid_spec=pltpu.PrefetchScalarGridSpec(
            num_scalar_prefetch=1,
            grid=(len(pieces),),
            in_specs=[full(x) for x in pieces]
            + [wspec(w) for w in weights]
            + [full(x) for x in more],
            out_specs=full(out),
        ),
        compiler_params=params(16),
        cost_estimate=cost(6e8 * len(pieces), 4 * len(pieces)),
    )(off, *pieces, *weights, *more)


def project_end_kernel(
    off, xa, xb, wq, wk, wv, acc_in, cosine, sine, gain_q, gain_k,
    q_rot, q_raw, k_rot, k_raw, v_out, squares, acc,
):
    acc[...] = acc_in[...]
    add_piece(acc, jnp.concatenate([xa[...], xb[...]], axis=0), (wq, wk, wv), False)
    cs, sn = cosine[...], sine[...]
    k = acc[:, R : R + D]
    k_raw[...] = k
    k_rot[...] = turn(k * gain_k[...], cs, sn)
    v_out[...] = acc[:, R + D :].astype(BF)
    squares[1:2, :] = lane_sums(k * k)
    total = None
    for h in range(G):
        q = acc[:, h * D : (h + 1) * D]
        total = q * q if total is None else total + q * q
        rotated = turn(q * gain_q[:, h * D : (h + 1) * D], cs, sn)
        for i in range(2):
            q_rot[i, h * SPAN : (h + 1) * SPAN, :] = rotated[i * SPAN : (i + 1) * SPAN]
    q_raw[...] = acc[:, :R]
    squares[0:1, :] = lane_sums(total)


def project_end(off, xa, xb, weights, acc, cosine, sine, gain_q, gain_k):
    rows = acc.shape[0]
    feats = xa.shape[1]

    def full(x):
        return pl.BlockSpec(x.shape, lambda g, off: (0,) * len(x.shape))

    def wspec(w):
        return pl.BlockSpec((feats, w.shape[1]), lambda g, off: (off[0], 0))

    outs = (
        jax.ShapeDtypeStruct((2, R, D), F32),
        jax.ShapeDtypeStruct((rows, R), F32),
        jax.ShapeDtypeStruct((rows, D), F32),
        jax.ShapeDtypeStruct((rows, D), F32),
        jax.ShapeDtypeStruct((rows, D), BF),
        jax.ShapeDtypeStruct((2, rows), F32),
    )
    rest = (acc, cosine, sine, gain_q, gain_k)
    return pl.pallas_call(
        project_end_kernel,
        out_shape=outs,
        grid_spec=pltpu.PrefetchScalarGridSpec(
            num_scalar_prefetch=1,
            grid=(1,),
            in_specs=[full(xa), full(xb)]
            + [wspec(w) for w in weights]
            + [full(x) for x in rest],
            out_specs=tuple(full(o) for o in outs),
            scratch_shapes=[pltpu.VMEM((rows, R + 2 * D), F32)],
        ),
        compiler_params=params(24),
        cost_estimate=cost(6e8, 6),
    )(off, xa, xb, *weights, *rest)


def join_kernel(*refs):
    at = 0
    for ref in refs[:-1]:
        n = ref.shape[0]
        refs[-1][at : at + n, :] = ref[...]
        at += n


def join(*xs):
    rows = sum(x.shape[0] for x in xs)
    return pl.pallas_call(
        join_kernel,
        out_shape=jax.ShapeDtypeStruct((rows,) + xs[0].shape[1:], xs[0].dtype),
        in_specs=[VM] * len(xs),
        out_specs=VM,
        compiler_params=params(8),
        cost_estimate=cost(0, 1),
    )(*xs)


def spans_at(ref, loc, which, j):
    return jnp.concatenate(
        [
            ref[pl.ds(pl.multiple_of(loc[which, CH * j + t] * SPAN, SPAN), SPAN), :]
            for t in range(CH)
        ],
        axis=0,
    )


def load_pieces(refs, whole, core, sems):
    count = len(refs) // 2
    copies = []
    for n, src in enumerate(refs):
        rows = src.shape[0]
        to = core if n < count else 1 - core
        copy = pltpu.make_async_copy(
            src, whole.at[to, pl.ds((n % count) * rows, rows), :], sems.at[n]
        )
        copy.start()
        copies.append(copy)
    for copy in copies:
        copy.wait()


def fwd_kernel(loc, own, q_ref, *refs):
    kv_refs, (o_ref, lse_ref, kv, m_s, acc_s, sems) = refs[:PIECES], refs[PIECES:]
    load_pieces(kv_refs, kv, own[2], sems)
    k_ref, v_ref = kv.at[0], kv.at[1]
    ones = (lax.broadcasted_iota(jnp.int32, (KC, D), 1) == 0).astype(BF)
    for i in range(2):
        c = own[i]
        m_s[...] = jnp.full_like(m_s, NEG)
        acc_s[...] = jnp.zeros_like(acc_s)

        def step(j, masked):
            kk = spans_at(k_ref, loc, 0, j)
            vv = jnp.concatenate([spans_at(v_ref, loc, 1, j), ones], axis=1)
            for h in range(G):
                at = slice(h * SPAN, (h + 1) * SPAN)
                s = nt(q_ref[i, at, :], kk)
                if masked:
                    key = j * KC + lax.broadcasted_iota(jnp.int32, (SPAN, KC), 1)
                    row = c * SPAN + lax.broadcasted_iota(jnp.int32, (SPAN, KC), 0)
                    s = jnp.where(key <= row, s, NEG)
                m = m_s[at, :]
                new = jnp.maximum(m, jnp.max(s, axis=1, keepdims=True))
                shrink = jnp.exp2((m - new) * (SCALE * LOG2E))
                p = jnp.exp2((s - new[:, :1]) * (SCALE * LOG2E))
                m_s[at, :] = new
                acc_s[at, :] = acc_s[at, :] * shrink[:, :1] + nn(p.astype(BF), vv)

        last = c // CH

        def body(j, _):
            step(j, False)
            return 0

        lax.fori_loop(0, last, body, 0)
        step(last, True)
        total = acc_s[:, D : D + 1]
        o_ref[i] = (acc_s[:, :D] / total).astype(BF)
        lse = m_s[...] * (SCALE * LOG2E) + jnp.log2(jnp.broadcast_to(total, (R, D)))
        lse_ref[i] = lse.T[0:1, :]


def attn_fwd(table, own, q, kv):
    n = sum(x.shape[0] for x in kv) // 2
    return pl.pallas_call(
        fwd_kernel,
        out_shape=(
            jax.ShapeDtypeStruct((2, R, D), BF),
            jax.ShapeDtypeStruct((2, 1, R), F32),
            jax.ShapeDtypeStruct((2, n, D), BF),
        ),
        grid_spec=pltpu.PrefetchScalarGridSpec(
            num_scalar_prefetch=2,
            grid=(),
            in_specs=[VM] + [HB] * PIECES,
            out_specs=(VM, VM, VM),
            scratch_shapes=[
                pltpu.VMEM((R, D), F32),
                pltpu.VMEM((R, 2 * D), F32),
                pltpu.SemaphoreType.DMA((PIECES,)),
            ],
        ),
        compiler_params=params(16),
        cost_estimate=cost(1.6e10, 6, 6e6),
    )(table, own, q, *kv)


def bwd_kernel(
    loc, own, q_ref, kv, do_ref, o_ref, lse_ref, cosine, sine, gain_q, unit_ref,
    up_ref, mix_ref, gain_ref, mine_ref, theirs_ref, dkv, dqa,
):
    core = own[2]
    k_ref, v_ref = kv.at[0], kv.at[1]
    dkv[...] = jnp.zeros_like(dkv)
    dqa[...] = jnp.zeros_like(dqa)
    for i in range(2):
        c = own[i]
        q, do, lse = q_ref[i], do_ref[i], lse_ref[i]
        delta = lane_sums(do.astype(F32) * o_ref[i].astype(F32))

        def step(j, masked):
            kk = spans_at(k_ref, loc, 0, j)
            vv = spans_at(v_ref, loc, 1, j)
            p = jnp.exp2(nt(kk, q) * (SCALE * LOG2E) - lse)
            if masked:
                key = j * KC + lax.broadcasted_iota(jnp.int32, (KC, R), 0)
                row = c * SPAN + lax.rem(lax.broadcasted_iota(jnp.int32, (KC, R), 1), SPAN)
                p = jnp.where(key <= row, p, 0.0)
            ds = (p * (nt(vv, do) - delta)).astype(BF)
            dqa[i] += tn(kk, ds)
            dv = nn(p.astype(BF), do)
            dk = nn(ds, q) * SCALE
            for t in range(CH):
                part = slice(t * SPAN, (t + 1) * SPAN)
                at = pl.ds(pl.multiple_of(loc[2, CH * j + t] * SPAN, SPAN), SPAN)
                dkv[0, at, :] += dk[part]
                at = pl.ds(pl.multiple_of(loc[3, CH * j + t] * SPAN, SPAN), SPAN)
                dkv[1, at, :] += dv[part]

        last = c // CH

        def body(j, _):
            step(j, False)
            return 0

        lax.fori_loop(0, last, body, 0)
        step(last, True)
    mine_ref[...] = dkv[core].astype(BF)
    theirs_ref[...] = dkv[1 - core].astype(BF)
    for i in range(2):
        rows = slice(i * SPAN, (i + 1) * SPAN)
        cs, sn = cosine[rows, :], -sine[rows, :]
        mix = None
        for h in range(G):
            cols = slice(h * D, (h + 1) * D)
            grad = turn((dqa[i, :, cols] * SCALE).T, cs, sn)
            unit = unit_ref[rows, cols]
            up = grad * gain_q[:, cols]
            up_ref[rows, cols] = up
            mix = up * unit if mix is None else mix + up * unit
            gain = jnp.sum(grad * unit, axis=0, keepdims=True)
            if i == 0:
                gain_ref[:, cols] = gain
            else:
                gain_ref[:, cols] += gain
        mix_ref[:, rows] = lane_sums(mix)


def attn_bwd(table, own, q, kv, do, o, lse, cosine, sine, gain_q, unit):
    n = kv.shape[1]
    rows = 2 * SPAN
    return pl.pallas_call(
        bwd_kernel,
        out_shape=(
            jax.ShapeDtypeStruct((rows, R), F32),
            jax.ShapeDtypeStruct((1, rows), F32),
            jax.ShapeDtypeStruct((1, R), F32),
            jax.ShapeDtypeStruct((n, D), BF),
            jax.ShapeDtypeStruct((n, D), BF),
        ),
        grid_spec=pltpu.PrefetchScalarGridSpec(
            num_scalar_prefetch=2,
            grid=(),
            in_specs=[VM] * 9,
            out_specs=(VM,) * 5,
            scratch_shapes=[
                pltpu.VMEM((2, n, D), F32),
                pltpu.VMEM((2, D, R), F32),
            ],
        ),
        compiler_params=params(26),
        cost_estimate=cost(2.2e10, 12, 6e6),
    )(table, own, q, kv, do, o, lse, cosine, sine, gain_q, unit)


def head_grad_kernel(x, w, out, acc):
    g = pl.program_id(0)
    part = nt(x[...], w[...])

    @pl.when(g == 0)
    def _():
        acc[...] = part

    @pl.when(g > 0)
    def _():
        acc[...] += part

    @pl.when(g == pl.num_programs(0) - 1)
    def _():
        for i in range(2):
            for h in range(G):
                out[i, h * SPAN : (h + 1) * SPAN, :] = acc[
                    i * SPAN : (i + 1) * SPAN, h * D : (h + 1) * D
                ].astype(BF)


def head_grad_of(x, w_out):
    rows, feats = x.shape
    block = feats // 4
    return pl.pallas_call(
        head_grad_kernel,
        out_shape=jax.ShapeDtypeStruct((2, R, D), BF),
        grid=(4,),
        in_specs=[
            pl.BlockSpec((rows, block), lambda g: (0, g)),
            pl.BlockSpec((R, block), lambda g: (0, g)),
        ],
        out_specs=pl.BlockSpec((2, R, D), lambda g: (0, 0, 0)),
        scratch_shapes=[pltpu.VMEM((rows, R), F32)],
        compiler_params=params(14),
        cost_estimate=cost(1.7e9, 9),
    )(x, w_out)


def out_kernel(heads, w, *outs):
    x = jnp.concatenate(
        [
            jnp.concatenate(
                [heads[i, h * SPAN : (h + 1) * SPAN, :] for h in range(G)], axis=1
            )
            for i in range(2)
        ],
        axis=0,
    )
    y = nn(x, w[...]).astype(BF)
    for i in range(2):
        outs[i][0] = y[i * SPAN : (i + 1) * SPAN]


def out_partial_of(heads, w_out):
    feats = w_out.shape[1]
    block = feats // 4
    return pl.pallas_call(
        out_kernel,
        out_shape=(jax.ShapeDtypeStruct((4, SPAN, block), BF),) * 2,
        grid=(4,),
        in_specs=[
            pl.BlockSpec((2, R, D), lambda g: (0, 0, 0)),
            pl.BlockSpec((R, block), lambda g: (0, g)),
        ],
        out_specs=(pl.BlockSpec((1, SPAN, block), lambda g: (g, 0, 0)),) * 2,
        compiler_params=params(14),
        cost_estimate=cost(1.7e9, 9),
    )(heads, w_out)


def query_kernel(x, w, out):
    out[0] = nt(x[...], w[...]).astype(BF)


def query_partial_of(x, w_query):
    rows = x.shape[0]
    feats = w_query.shape[0]
    block = feats // 4
    return pl.pallas_call(
        query_kernel,
        out_shape=jax.ShapeDtypeStruct((4, rows, block), BF),
        grid=(4,),
        in_specs=[
            pl.BlockSpec((rows, R), lambda g: (0, 0)),
            pl.BlockSpec((block, R), lambda g: (g, 0)),
        ],
        out_specs=pl.BlockSpec((1, rows, block), lambda g: (g, 0, 0)),
        compiler_params=params(14),
        cost_estimate=cost(1.7e9, 9),
    )(x, w_query)


def last_kernel(g0, g1, g2, g3, u0, u1, u2, u3, inv, w, query_side, out):
    gs, us = (g0, g1, g2, g3), (u0, u1, u2, u3)
    mix = None
    for g, u in zip(gs, us):
        part = g[:, :D].astype(F32) * u[...].astype(F32)
        mix = part if mix is None else mix + part
    mix = jnp.sum(mix, axis=1, keepdims=True) * (1.0 / K_CHANNELS)
    total = query_side[...].astype(F32)
    for n, (g, u) in enumerate(zip(gs, us)):
        raw = (inv[...] * (g[:, :D].astype(F32) - u[...].astype(F32) * mix)).astype(BF)
        total = total + nt(jnp.concatenate([raw, g[:, D:]], axis=1), w[n])
    out[...] = total.astype(BF)


def last_of(grads, units, inv, w, query_side):
    return pl.pallas_call(
        last_kernel,
        out_shape=jax.ShapeDtypeStruct(query_side.shape, BF),
        in_specs=[VM] * 11,
        out_specs=VM,
        compiler_params=params(12),
        cost_estimate=cost(7e8, 5),
    )(*grads, *units, inv, w, query_side)

QUERY_HEADS = 20
KEY_VALUE_HEADS = 4
Q_CHANNELS = QUERY_HEADS * D
K_CHANNELS = KEY_VALUE_HEADS * D
N_Y, N_Z, N_CORE, N_TP = 4, 4, 2, 4


def ctx_index(y, z, c):
    return (y * N_Z + z) * N_CORE + c


def ctx_pairs(move):
    return [
        (ctx_index(y, z, c), ctx_index(*move(y, z, c)))
        for y in range(N_Y)
        for z in range(N_Z)
        for c in range(N_CORE)
    ]


def shift_first(x, d):
    return lax.ppermute(
        x,
        "ctx",
        ctx_pairs(lambda y, z, c: ((y + c * d) % N_Y, (z + (1 - c) * d) % N_Z, c)),
    )


def shift_second(x, d):
    return lax.ppermute(
        x,
        "ctx",
        ctx_pairs(lambda y, z, c: ((y + (1 - c) * d) % N_Y, (z + c * d) % N_Z, c)),
    )


def swap_core(x):
    return lax.ppermute(x, "ctx", ctx_pairs(lambda y, z, c: (y, z, 1 - c)))


def shift_tp(x, d):
    return lax.ppermute(x, "tp", [(i, (i + d) % N_TP) for i in range(N_TP)])


def shifts(shift, x):
    return [x] + [shift(x, d) for d in DIST[1:]]


def sum_tp(x):
    x = x + lax.ppermute(x, "tp", [(i, i ^ 1) for i in range(N_TP)])
    return x + lax.ppermute(x, "tp", [(i, 3 - i) for i in range(N_TP)])


def sum_ctx(x):
    x = x + swap_core(x)
    x = x + lax.ppermute(x, "ctx", ctx_pairs(lambda y, z, c: (y, z ^ 1, c)))
    x = x + lax.ppermute(x, "ctx", ctx_pairs(lambda y, z, c: (y, 3 - z, c)))
    x = x + lax.ppermute(x, "ctx", ctx_pairs(lambda y, z, c: (y ^ 1, z, c)))
    return x + lax.ppermute(x, "ctx", ctx_pairs(lambda y, z, c: (3 - y, z, c)))


def after(x, *others):
    return lax.optimization_barrier((x,) + others)[0]


def outgoing(x):
    rows = x.shape[0] // 4
    return [x[d * rows : (d + 1) * rows].astype(BF) for d in DIST[1:]], x[:rows]


def add_up(total, arrived):
    for x in arrived:
        total = total + x.astype(F32)
    return total


def local(tokens, span_order, w_query, w_key, value_weight, w_out, gain_query, gain_key, out_grad):
    rows, feats = tokens.shape
    me = lax.axis_index("ctx")
    tp = lax.axis_index("tp")
    my_y, my_z, my_c = me // 8, (me // 2) % 4, me % 2

    with jax.named_scope("gather_tokens"):
        left = shift_tp(tokens, 1)
        right = shift_tp(tokens, 3)
    place = jnp.arange(64, dtype=jnp.int32)
    stored = jnp.sum(jnp.where(span_order[None, :] == place[:, None], place[None, :], 0), axis=1)
    src, half = stored // 2, stored % 2
    src_y, src_z, src_c = src // 8, (src // 2) % 4, src % 2
    to_y, to_z = (src_y - my_y) % 4, (src_z - my_z) % 4
    back_y, back_z = (4 - to_y) % 4, (4 - to_z) % 4
    slot_y = jnp.where(back_y >= 2, 5 - back_y, back_y)
    slot_z = jnp.where(back_z >= 2, 5 - back_z, back_z)
    table = jnp.stack(
        [
            ((slot_y * 4 + slot_z) * 2 + src_c) * 2 + half,
            ((slot_z * 4 + slot_y) * 2 + 1 - src_c) * 2 + half,
            ((to_z * 4 + to_y) * 2 + src_c) * 2 + half,
            ((to_y * 4 + to_z) * 2 + src_c) * 2 + half,
        ]
    ).astype(jnp.int32)
    own = lax.dynamic_slice_in_dim(span_order, 2 * me, 2)
    own = jnp.concatenate([own, my_c[None]]).astype(jnp.int32)

    query_pos = (own[:2, None] * SPAN + jnp.arange(SPAN)[None, :]).reshape(-1)
    frequency = jnp.exp(jnp.arange(D // 2).astype(F32) * (-2.0 * math.log(500000.0) / D))
    angles = query_pos.astype(F32)[:, None] * frequency[None, :]
    cosine, sine = jnp.cos(angles), jnp.sin(angles)
    cosine = jnp.concatenate([cosine, cosine], axis=1)
    sine = jnp.concatenate([-sine, sine], axis=1)

    with jax.named_scope("weight_rows"):
        share = feats // 32
        cut = []
        for d in DIST:
            start = feats * ((tp + d) % 4) + share * me
            piece = jnp.concatenate(
                [lax.dynamic_slice_in_dim(w, start, share, 0) for w in (w_key, value_weight)],
                axis=1,
            )
            cut.append(shift_tp(piece, d) if d else piece)
        cut = jnp.stack(cut)

    offs = jnp.stack([(tp - d) % 4 for d in DIST]).astype(jnp.int32)
    with jax.named_scope("gather_tokens"):
        mid = rows // 2
        weights = (w_query, w_key, value_weight)
        acc = project(offs[:1], (tokens,), weights)
        near, cosine, sine, offs, table, own, cut, acc = lax.optimization_barrier(
            (left[:mid], cosine, sine, offs, table, own, cut, acc)
        )
        far_a = shift_tp(near, 1)
        far_b = shift_tp(right[mid:], 3)
        acc = project(offs[1:3], (left, right), weights, acc)
        far_a, far_b, acc = lax.optimization_barrier((far_a, far_b, acc))
    gain_q, gain_k = gain_query[None, :], gain_key[None, :]
    q_rot, q_raw, k_rot, k_raw, value, squares = project_end(
        offs[3:], far_a, far_b, weights, acc, cosine, sine, gain_q, gain_k
    )
    with jax.named_scope("norm_sums"):
        squares = sum_tp(squares)
    query_inv = lax.rsqrt(squares[0] / Q_CHANNELS + 1e-06)[:, None]
    key_inv = lax.rsqrt(squares[1] / K_CHANNELS + 1e-06)[:, None]
    key = (k_rot * key_inv).astype(BF)

    with jax.named_scope("gather_keys_values"):
        first_core = my_c == 0
        mine = jnp.where(first_core, key, value)
        pair = join(mine, swap_core(jnp.where(first_core, value, key)))
        plane = join(*shifts(shift_first, pair))
        mine = shifts(shift_second, plane)
    with jax.named_scope("weight_rows"):
        w_rows = lax.all_gather(after(cut, pair), "ctx", axis=0, tiled=False)

    query_unit = q_raw * query_inv
    key_unit = k_raw * key_inv
    query = (
        (q_rot.reshape(2, G, SPAN, D) * query_inv.reshape(2, 1, SPAN, 1)).astype(BF).reshape(2, R, D)
    )
    with jax.named_scope("gather_key_units"):
        key_units = shifts(shift_tp, key_unit.astype(BF))

    with jax.named_scope("gather_out_grad"):
        grad_part = lax.all_gather(after(out_grad, far_a, far_b), "tp", axis=1, tiled=True)
        head_grad = head_grad_of(grad_part, w_out)

    with jax.named_scope("swap_keys_values"):
        last, query, query_unit, head_grad = lax.optimization_barrier(
            (mine[3], query, query_unit, head_grad)
        )
        mine = mine[:3] + [last]
        pieces = (*mine, *(swap_core(x) for x in mine))

    heads, log_total, kv = attn_fwd(table, own, query, pieces)
    out_partial = out_partial_of(heads, w_out)
    attn_out = [
        lax.psum_scatter(x, "tp", scatter_dimension=0, tiled=False) for x in out_partial
    ]

    query, _, _, *key_units = lax.optimization_barrier((query, *out_partial, *key_units))
    up_query, mix_query, gain_part, mine, theirs = attn_bwd(
        table, own, query, kv, head_grad, heads, log_total,
        cosine, sine, gain_q, query_unit,
    )

    with jax.named_scope("sum_key_value_grads"):
        theirs, mix_query, attn_out[0], w_rows = lax.optimization_barrier(
            (theirs, mix_query, attn_out[0], w_rows)
        )
        mix_query = sum_tp(mix_query)[0] / Q_CHANNELS
        received, mix_query = lax.optimization_barrier((swap_core(theirs), mix_query))
        summed = mine.astype(F32) + received.astype(F32)
        sent, total = outgoing(summed)
        arrived = [shift_first(x, d) for x, d in zip(sent, DIST[1:])]
        sent, total = outgoing(add_up(total, arrived))
        total = add_up(total, [shift_second(x, d) for x, d in zip(sent, DIST[1:])])
        ours, its = total[:rows], total[rows:]
        kept = jnp.where(first_core, ours, its)
        swapped = swap_core(jnp.where(first_core, its, ours))
        key_grad_rot = jnp.where(first_core, kept, swapped)
        value_grad = jnp.where(first_core, swapped, kept).astype(BF)

    with jax.named_scope("query_side"):
        raw_query_grad = (query_inv * (up_query - query_unit * mix_query[:, None])).astype(BF)
        query_partial = query_partial_of(raw_query_grad, w_query)
        query_side = lax.psum_scatter(query_partial, "tp", scatter_dimension=0, tiled=False)

    with jax.named_scope("key_value_side"):
        first, second = key_grad_rot[:, : D // 2], key_grad_rot[:, D // 2 :]
        cs, sn = cosine[:, : D // 2], sine[:, D // 2 :]
        key_grad = jnp.concatenate([first * cs + second * sn, second * cs - first * sn], axis=1)
        w_rows = after(w_rows, query_partial).transpose(1, 0, 2, 3).reshape(4, feats, 2 * D)
        key_grad, w_rows = lax.optimization_barrier((key_grad, w_rows))
        both = jnp.concatenate([(key_grad * gain_k).astype(BF), value_grad], axis=1)
        grads = shifts(shift_tp, both)
        key_grad = after(key_grad, *grads)
        gain_key_part = jnp.sum(key_grad * key_unit, axis=0)[None]
        gains = sum_ctx(jnp.concatenate([gain_part, gain_key_part], axis=1))[0]
        gain_query_grad, gain_key_grad = gains[:R], gains[R:]
        input_grad = last_of(grads, key_units, key_inv, w_rows, query_side)
    attn_out = jnp.concatenate(attn_out, axis=0)
    return (attn_out, input_grad, gain_query_grad, gain_key_grad)


def solution(mesh):
    return jax.shard_map(
        local,
        mesh=mesh,
        in_specs=(
            P("ctx", "tp"),
            P(),
            P(None, "tp"),
            P(None, "tp"),
            P(None, "tp"),
            P("tp", None),
            P("tp"),
            P("tp"),
            P("ctx", "tp"),
        ),
        out_specs=(P("ctx", "tp"), P("ctx", "tp"), P("tp"), P("tp")),
        check_vma=False,
    )
```

```python
import math

import jax
import jax.numpy as jnp
from jax import lax
from jax.experimental import pallas as pl
from jax.experimental.pallas import tpu as pltpu
from jax.sharding import PartitionSpec as P

D = 128
SPAN = 128
G = 5
R = G * SPAN
CH = 8
KC = CH * SPAN
SCALE = D**-0.5
LOG2E = math.log2(math.e)
NEG = -1e30
BF = jnp.bfloat16
F32 = jnp.float32
DIST = (0, 1, 3, 2)
PIECES = 8


def nt(a, b):
    return lax.dot_general(a, b, (((1,), (1,)), ((), ())), preferred_element_type=F32)


def tn(a, b):
    return lax.dot_general(a, b, (((0,), (0,)), ((), ())), preferred_element_type=F32)


def nn(a, b):
    return lax.dot_general(a, b, (((1,), (0,)), ((), ())), preferred_element_type=F32)


VM = pl.BlockSpec(memory_space=pltpu.VMEM)
HB = pl.BlockSpec(memory_space=pl.ANY)
FAR = pl.BlockSpec(memory_space=pltpu.HBM)


def params(mib):
    return pltpu.CompilerParams(vmem_limit_bytes=mib * 2**20)


def cost(flops, mib, exps=0):
    return pl.CostEstimate(
        flops=int(flops), bytes_accessed=int(mib * 2**20), transcendentals=int(exps)
    )


def turn(x, cosine, sine):
    return x * cosine + pltpu.roll(x, D // 2, 1) * sine


def lane_sums(x):
    return jnp.sum(x.T, axis=0, keepdims=True)


def fetch(pairs, sems):
    copies = [pltpu.make_async_copy(src, dst, sems.at[n]) for n, (src, dst) in enumerate(pairs)]
    for copy in copies:
        copy.start()
    return copies


def fetch_rows(off, weights, stages, sems):
    pairs = []
    for n in range(stages[0].shape[0]):
        rows = stages[0].shape[1]
        at = pl.ds(pl.multiple_of(off[n] * rows, rows), rows)
        pairs += [(w.at[at, :], s.at[n]) for w, s in zip(weights, stages)]
    return fetch(pairs, sems)


def product_of(x, stages, n):
    return jnp.concatenate([nn(x, s[n]) for s in stages], axis=1)


def project_kernel(off, *refs, count, first):
    xs, weights = refs[:count], refs[count : count + 3]
    stages, sems, out = refs[-4:-1], refs[-1], refs[-5]
    copies = fetch_rows(off, weights, stages, sems)
    total = None if first else refs[count + 3][...]
    for n in range(count):
        for copy in copies[3 * n : 3 * n + 3]:
            copy.wait()
        part = product_of(xs[n][...], stages, n)
        total = part if total is None else total + part
    out[...] = total


def stages_of(weights, count, feats):
    return [pltpu.VMEM((count, feats, w.shape[1]), BF) for w in weights] + [
        pltpu.SemaphoreType.DMA((3 * count,))
    ]


def project(off, pieces, weights, acc=None):
    rows, feats = pieces[0].shape
    width = sum(w.shape[1] for w in weights)
    count = len(pieces)
    more = () if acc is None else (acc,)
    return pl.pallas_call(
        lambda *refs: project_kernel(*refs, count=count, first=acc is None),
        out_shape=jax.ShapeDtypeStruct((rows, width), F32),
        grid_spec=pltpu.PrefetchScalarGridSpec(
            num_scalar_prefetch=1,
            grid=(),
            in_specs=[VM] * count + [FAR] * 3 + [VM] * len(more),
            out_specs=VM,
            scratch_shapes=stages_of(weights, count, feats),
        ),
        compiler_params=params(14),
        cost_estimate=cost(6e8 * count, 4 * count),
    )(off, *pieces, *weights, *more)


def project_end_kernel(
    off, xa, xb, wq, wk, wv, acc_in, cosine, sine, gain_q, gain_k,
    q_rot, q_raw, k_rot, k_raw, v_out, squares, sq, sk, sv, sems,
):
    stages = (sq, sk, sv)
    copies = fetch_rows(off, (wq, wk, wv), stages, sems)
    x = jnp.concatenate([xa[...], xb[...]], axis=0)
    cs, sn = cosine[...], sine[...]
    for copy in copies:
        copy.wait()
    raw = acc_in[...] + product_of(x, stages, 0)
    k = raw[:, R : R + D]
    k_raw[...] = k
    k_rot[...] = turn(k * gain_k[...], cs, sn)
    v_out[...] = raw[:, R + D :].astype(BF)
    squares[1:2, :] = lane_sums(k * k)
    total = None
    for h in range(G):
        q = raw[:, h * D : (h + 1) * D]
        total = q * q if total is None else total + q * q
        rotated = turn(q * gain_q[:, h * D : (h + 1) * D], cs, sn)
        for i in range(2):
            q_rot[i, h * SPAN : (h + 1) * SPAN, :] = rotated[i * SPAN : (i + 1) * SPAN]
    q_raw[...] = raw[:, :R]
    squares[0:1, :] = lane_sums(total)


def project_end(off, xa, xb, weights, acc, cosine, sine, gain_q, gain_k):
    rows = acc.shape[0]
    feats = xa.shape[1]
    outs = (
        jax.ShapeDtypeStruct((2, R, D), F32),
        jax.ShapeDtypeStruct((rows, R), F32),
        jax.ShapeDtypeStruct((rows, D), F32),
        jax.ShapeDtypeStruct((rows, D), F32),
        jax.ShapeDtypeStruct((rows, D), BF),
        jax.ShapeDtypeStruct((2, rows), F32),
    )
    return pl.pallas_call(
        project_end_kernel,
        out_shape=outs,
        grid_spec=pltpu.PrefetchScalarGridSpec(
            num_scalar_prefetch=1,
            grid=(),
            in_specs=[VM, VM] + [FAR] * 3 + [VM] * 5,
            out_specs=(VM,) * 6,
            scratch_shapes=stages_of(weights, 1, feats),
        ),
        compiler_params=params(14),
        cost_estimate=cost(6e8, 6),
    )(off, xa, xb, *weights, acc, cosine, sine, gain_q, gain_k)


def join_kernel(*refs):
    at = 0
    for ref in refs[:-1]:
        n = ref.shape[0]
        refs[-1][at : at + n, :] = ref[...]
        at += n


def join(*xs):
    rows = sum(x.shape[0] for x in xs)
    return pl.pallas_call(
        join_kernel,
        out_shape=jax.ShapeDtypeStruct((rows,) + xs[0].shape[1:], xs[0].dtype),
        in_specs=[VM] * len(xs),
        out_specs=VM,
        compiler_params=params(8),
        cost_estimate=cost(0, 1),
    )(*xs)


def spans_at(ref, loc, which, j):
    return jnp.concatenate(
        [
            ref[pl.ds(pl.multiple_of(loc[which, CH * j + t] * SPAN, SPAN), SPAN), :]
            for t in range(CH)
        ],
        axis=0,
    )


def load_pieces(refs, whole, core, sems):
    count = len(refs) // 2
    copies = []
    for n, src in enumerate(refs):
        rows = src.shape[0]
        to = core if n < count else 1 - core
        copy = pltpu.make_async_copy(
            src, whole.at[to, pl.ds((n % count) * rows, rows), :], sems.at[n]
        )
        copy.start()
        copies.append(copy)
    for copy in copies:
        copy.wait()


def fwd_kernel(loc, own, q_ref, *refs):
    kv_refs, w_ref, (lse_ref, o_ref, kv_out, outa, outb) = (
        refs[:PIECES], refs[PIECES], refs[PIECES + 1 : PIECES + 6],
    )
    kv, w_s, y_s, m_s, acc_s, sems, wsems, kvsem, ysems = refs[PIECES + 6 :]
    load_pieces(kv_refs, kv, own[2], sems)
    keep = fetch([(kv, kv_out)], kvsem)
    block = y_s.shape[2]
    w_copies = fetch(
        [(w_ref.at[:, pl.ds(b * block, block)], w_s.at[b]) for b in range(4)], wsems
    )
    k_ref, v_ref = kv.at[0], kv.at[1]
    ones = (lax.broadcasted_iota(jnp.int32, (KC, D), 1) == 0).astype(BF)
    for i in range(2):
        c = own[i]
        m_s[...] = jnp.full_like(m_s, NEG)
        acc_s[...] = jnp.zeros_like(acc_s)

        def step(j, masked):
            kk = spans_at(k_ref, loc, 0, j)
            vv = jnp.concatenate([spans_at(v_ref, loc, 1, j), ones], axis=1)
            for h in range(G):
                at = slice(h * SPAN, (h + 1) * SPAN)
                s = nt(q_ref[i, at, :], kk)
                if masked:
                    key = j * KC + lax.broadcasted_iota(jnp.int32, (SPAN, KC), 1)
                    row = c * SPAN + lax.broadcasted_iota(jnp.int32, (SPAN, KC), 0)
                    s = jnp.where(key <= row, s, NEG)
                m = m_s[at, :]
                new = jnp.maximum(m, jnp.max(s, axis=1, keepdims=True))
                shrink = jnp.exp2((m - new) * (SCALE * LOG2E))
                p = jnp.exp2((s - new[:, :1]) * (SCALE * LOG2E))
                m_s[at, :] = new
                acc_s[at, :] = acc_s[at, :] * shrink[:, :1] + nn(p.astype(BF), vv)

        last = c // CH

        def body(j, _):
            step(j, False)
            return 0

        lax.fori_loop(0, last, body, 0)
        step(last, True)
        total = acc_s[:, D : D + 1]
        o_ref[i] = (acc_s[:, :D] / total).astype(BF)
        lse = m_s[...] * (SCALE * LOG2E) + jnp.log2(jnp.broadcast_to(total, (R, D)))
        lse_ref[i] = lse.T[0:1, :]
    x = jnp.concatenate(
        [
            jnp.concatenate(
                [o_ref[i, h * SPAN : (h + 1) * SPAN, :] for h in range(G)], axis=1
            )
            for i in range(2)
        ],
        axis=0,
    )
    y_copies = []
    for b in range(4):
        w_copies[b].wait()
        y_s[b] = nn(x, w_s[b]).astype(BF)
        for i, out in enumerate((outa, outb)):
            copy = pltpu.make_async_copy(
                y_s.at[b, pl.ds(i * SPAN, SPAN), :], out.at[b], ysems.at[2 * b + i]
            )
            copy.start()
            y_copies.append(copy)
    for copy in keep + y_copies:
        copy.wait()


def attn_fwd(table, own, q, pieces, w_out):
    n = sum(x.shape[0] for x in pieces) // 2
    block = w_out.shape[1] // 4
    return pl.pallas_call(
        fwd_kernel,
        out_shape=(
            jax.ShapeDtypeStruct((2, 1, R), F32),
            jax.ShapeDtypeStruct((2, R, D), BF),
            jax.ShapeDtypeStruct((2, n, D), BF),
            jax.ShapeDtypeStruct((4, SPAN, block), BF),
            jax.ShapeDtypeStruct((4, SPAN, block), BF),
        ),
        grid_spec=pltpu.PrefetchScalarGridSpec(
            num_scalar_prefetch=2,
            grid=(),
            in_specs=[VM] + [HB] * PIECES + [FAR],
            out_specs=(VM, VM, FAR, FAR, FAR),
            scratch_shapes=[
                pltpu.VMEM((2, n, D), BF),
                pltpu.VMEM((4, R, block), BF),
                pltpu.VMEM((4, 2 * SPAN, block), BF),
                pltpu.VMEM((R, D), F32),
                pltpu.VMEM((R, 2 * D), F32),
                pltpu.SemaphoreType.DMA((PIECES,)),
                pltpu.SemaphoreType.DMA((4,)),
                pltpu.SemaphoreType.DMA((1,)),
                pltpu.SemaphoreType.DMA((8,)),
            ],
        ),
        compiler_params=params(30),
        cost_estimate=cost(1.8e10, 12, 6e6),
    )(table, own, q, *pieces, w_out)


def bwd_kernel(
    loc, own, q_ref, kv_in, do_ref, o_ref, lse_ref, cosine, sine, gain_q, unit_ref,
    up_ref, mix_ref, gain_ref, mine_ref, theirs_ref, kv, dkv, dqa, sems,
):
    core = own[2]
    copies = fetch([(kv_in.at[0], kv.at[0]), (kv_in.at[1], kv.at[1])], sems)
    k_ref, v_ref = kv.at[0], kv.at[1]
    dkv[...] = jnp.zeros_like(dkv)
    dqa[...] = jnp.zeros_like(dqa)
    for copy in copies:
        copy.wait()
    for i in range(2):
        c = own[i]
        q, do, lse = q_ref[i], do_ref[i], lse_ref[i]
        delta = lane_sums(do.astype(F32) * o_ref[i].astype(F32))

        def step(j, masked):
            kk = spans_at(k_ref, loc, 0, j)
            vv = spans_at(v_ref, loc, 1, j)
            p = jnp.exp2(nt(kk, q) * (SCALE * LOG2E) - lse)
            if masked:
                key = j * KC + lax.broadcasted_iota(jnp.int32, (KC, R), 0)
                row = c * SPAN + lax.rem(lax.broadcasted_iota(jnp.int32, (KC, R), 1), SPAN)
                p = jnp.where(key <= row, p, 0.0)
            ds = (p * (nt(vv, do) - delta)).astype(BF)
            dqa[i] += tn(kk, ds)
            dv = nn(p.astype(BF), do)
            dk = nn(ds, q) * SCALE
            for t in range(CH):
                part = slice(t * SPAN, (t + 1) * SPAN)
                at = pl.ds(pl.multiple_of(loc[2, CH * j + t] * SPAN, SPAN), SPAN)
                dkv[0, at, :] += dk[part]
                at = pl.ds(pl.multiple_of(loc[3, CH * j + t] * SPAN, SPAN), SPAN)
                dkv[1, at, :] += dv[part]

        last = c // CH

        def body(j, _):
            step(j, False)
            return 0

        lax.fori_loop(0, last, body, 0)
        step(last, True)
    mine_ref[...] = dkv[core].astype(BF)
    theirs_ref[...] = dkv[1 - core].astype(BF)
    for i in range(2):
        rows = slice(i * SPAN, (i + 1) * SPAN)
        cs, sn = cosine[rows, :], -sine[rows, :]
        mix = None
        for h in range(G):
            cols = slice(h * D, (h + 1) * D)
            grad = turn((dqa[i, :, cols] * SCALE).T, cs, sn)
            unit = unit_ref[rows, cols]
            up = grad * gain_q[:, cols]
            up_ref[rows, cols] = up
            mix = up * unit if mix is None else mix + up * unit
            gain = jnp.sum(grad * unit, axis=0, keepdims=True)
            if i == 0:
                gain_ref[:, cols] = gain
            else:
                gain_ref[:, cols] += gain
        mix_ref[:, rows] = lane_sums(mix)


def attn_bwd(table, own, q, kv, do, o, lse, cosine, sine, gain_q, unit):
    n = kv.shape[1]
    rows = 2 * SPAN
    return pl.pallas_call(
        bwd_kernel,
        out_shape=(
            jax.ShapeDtypeStruct((rows, R), F32),
            jax.ShapeDtypeStruct((1, rows), F32),
            jax.ShapeDtypeStruct((1, R), F32),
            jax.ShapeDtypeStruct((n, D), BF),
            jax.ShapeDtypeStruct((n, D), BF),
        ),
        grid_spec=pltpu.PrefetchScalarGridSpec(
            num_scalar_prefetch=2,
            grid=(),
            in_specs=[VM, FAR] + [VM] * 7,
            out_specs=(VM,) * 5,
            scratch_shapes=[
                pltpu.VMEM((2, n, D), BF),
                pltpu.VMEM((2, n, D), F32),
                pltpu.VMEM((2, D, R), F32),
                pltpu.SemaphoreType.DMA((2,)),
            ],
        ),
        compiler_params=params(34),
        cost_estimate=cost(2.2e10, 12, 6e6),
    )(table, own, q, kv, do, o, lse, cosine, sine, gain_q, unit)


def head_grad_kernel(x_ref, w_ref, out, x_s, w_s, sems):
    block = x_s.shape[2]
    pairs = []
    for b in range(4):
        cols = pl.ds(b * block, block)
        pairs += [(w_ref.at[:, cols], w_s.at[b]), (x_ref.at[:, cols], x_s.at[b])]
    copies = fetch(pairs, sems)
    total = None
    for b in range(4):
        copies[2 * b].wait()
        copies[2 * b + 1].wait()
        part = nt(x_s[b], w_s[b])
        total = part if total is None else total + part
    for i in range(2):
        for h in range(G):
            out[i, h * SPAN : (h + 1) * SPAN, :] = total[
                i * SPAN : (i + 1) * SPAN, h * D : (h + 1) * D
            ].astype(BF)


def head_grad_of(x, w_out):
    rows, feats = x.shape
    block = feats // 4
    return pl.pallas_call(
        head_grad_kernel,
        out_shape=jax.ShapeDtypeStruct((2, R, D), BF),
        in_specs=[FAR, FAR],
        out_specs=VM,
        scratch_shapes=[
            pltpu.VMEM((4, rows, block), BF),
            pltpu.VMEM((4, R, block), BF),
            pltpu.SemaphoreType.DMA((8,)),
        ],
        compiler_params=params(18),
        cost_estimate=cost(1.7e9, 9),
    )(x, w_out)


def query_kernel(up, unit, mix, inv, w_ref, out, w_s, y_s, sems, ysems):
    block = w_s.shape[1]
    copies = fetch([(w_ref.at[pl.ds(b * block, block), :], w_s.at[b]) for b in range(4)], sems)
    rows = up.shape[0]

    def column(ref):
        return jnp.broadcast_to(ref[...], (D, rows)).T[:, :1]

    x = (column(inv) * (up[...] - unit[...] * (column(mix) * (1.0 / Q_CHANNELS)))).astype(BF)
    y_copies = []
    for b in range(4):
        copies[b].wait()
        y_s[b] = nt(x, w_s[b]).astype(BF)
        copy = pltpu.make_async_copy(y_s.at[b], out.at[b], ysems.at[b])
        copy.start()
        y_copies.append(copy)
    for copy in y_copies:
        copy.wait()


def query_partial_of(up, unit, mix, inv, w_query):
    rows = up.shape[0]
    feats = w_query.shape[0]
    block = feats // 4
    return pl.pallas_call(
        query_kernel,
        out_shape=jax.ShapeDtypeStruct((4, rows, block), BF),
        in_specs=[VM] * 4 + [FAR],
        out_specs=FAR,
        scratch_shapes=[
            pltpu.VMEM((4, block, R), BF),
            pltpu.VMEM((4, rows, block), BF),
            pltpu.SemaphoreType.DMA((4,)),
            pltpu.SemaphoreType.DMA((4,)),
        ],
        compiler_params=params(18),
        cost_estimate=cost(1.7e9, 9),
    )(up, unit, mix, inv, w_query)


def last_kernel(g0, g1, g2, g3, u0, u1, u2, u3, inv, w, query_side, out):
    gs, us = (g0, g1, g2, g3), (u0, u1, u2, u3)
    mix = None
    for g, u in zip(gs, us):
        part = g[:, :D].astype(F32) * u[...].astype(F32)
        mix = part if mix is None else mix + part
    mix = jnp.sum(mix, axis=1, keepdims=True) * (1.0 / K_CHANNELS)
    total = query_side[...].astype(F32)
    for n, (g, u) in enumerate(zip(gs, us)):
        raw = (inv[...] * (g[:, :D].astype(F32) - u[...].astype(F32) * mix)).astype(BF)
        total = total + nt(jnp.concatenate([raw, g[:, D:]], axis=1), w[n])
    out[...] = total.astype(BF)


def last_of(grads, units, inv, w, query_side):
    return pl.pallas_call(
        last_kernel,
        out_shape=jax.ShapeDtypeStruct(query_side.shape, BF),
        in_specs=[VM] * 11,
        out_specs=VM,
        compiler_params=params(12),
        cost_estimate=cost(7e8, 5),
    )(*grads, *units, inv, w, query_side)

QUERY_HEADS = 20
KEY_VALUE_HEADS = 4
Q_CHANNELS = QUERY_HEADS * D
K_CHANNELS = KEY_VALUE_HEADS * D
N_Y, N_Z, N_CORE, N_TP = 4, 4, 2, 4


def ctx_index(y, z, c):
    return (y * N_Z + z) * N_CORE + c


def ctx_pairs(move):
    return [
        (ctx_index(y, z, c), ctx_index(*move(y, z, c)))
        for y in range(N_Y)
        for z in range(N_Z)
        for c in range(N_CORE)
    ]


def shift_first(x, d):
    return lax.ppermute(
        x,
        "ctx",
        ctx_pairs(lambda y, z, c: ((y + c * d) % N_Y, (z + (1 - c) * d) % N_Z, c)),
    )


def shift_second(x, d):
    return lax.ppermute(
        x,
        "ctx",
        ctx_pairs(lambda y, z, c: ((y + (1 - c) * d) % N_Y, (z + c * d) % N_Z, c)),
    )


def swap_core(x):
    return lax.ppermute(x, "ctx", ctx_pairs(lambda y, z, c: (y, z, 1 - c)))


def shift_tp(x, d):
    return lax.ppermute(x, "tp", [(i, (i + d) % N_TP) for i in range(N_TP)])


def shifts(shift, x):
    return [x] + [shift(x, d) for d in DIST[1:]]


def sum_tp(x):
    x = x + lax.ppermute(x, "tp", [(i, i ^ 1) for i in range(N_TP)])
    return x + lax.ppermute(x, "tp", [(i, 3 - i) for i in range(N_TP)])


def sum_ctx(x):
    x = x + swap_core(x)
    x = x + lax.ppermute(x, "ctx", ctx_pairs(lambda y, z, c: (y, z ^ 1, c)))
    x = x + lax.ppermute(x, "ctx", ctx_pairs(lambda y, z, c: (y, 3 - z, c)))
    x = x + lax.ppermute(x, "ctx", ctx_pairs(lambda y, z, c: (y ^ 1, z, c)))
    return x + lax.ppermute(x, "ctx", ctx_pairs(lambda y, z, c: (3 - y, z, c)))


def after(x, *others):
    return lax.optimization_barrier((x,) + others)[0]


def outgoing(x):
    rows = x.shape[0] // 4
    return [x[d * rows : (d + 1) * rows].astype(BF) for d in DIST[1:]], x[:rows]


def add_up(total, arrived):
    for x in arrived:
        total = total + x.astype(F32)
    return total


def local(tokens, span_order, w_query, w_key, value_weight, w_out, gain_query, gain_key, out_grad):
    rows, feats = tokens.shape
    me = lax.axis_index("ctx")
    tp = lax.axis_index("tp")
    my_y, my_z, my_c = me // 8, (me // 2) % 4, me % 2

    with jax.named_scope("gather_tokens"):
        left = shift_tp(tokens, 1)
        right = shift_tp(tokens, 3)
    place = jnp.arange(64, dtype=jnp.int32)
    stored = jnp.sum(jnp.where(span_order[None, :] == place[:, None], place[None, :], 0), axis=1)
    src, half = stored // 2, stored % 2
    src_y, src_z, src_c = src // 8, (src // 2) % 4, src % 2
    to_y, to_z = (src_y - my_y) % 4, (src_z - my_z) % 4
    back_y, back_z = (4 - to_y) % 4, (4 - to_z) % 4
    slot_y = jnp.where(back_y >= 2, 5 - back_y, back_y)
    slot_z = jnp.where(back_z >= 2, 5 - back_z, back_z)
    table = jnp.stack(
        [
            ((slot_y * 4 + slot_z) * 2 + src_c) * 2 + half,
            ((slot_z * 4 + slot_y) * 2 + 1 - src_c) * 2 + half,
            ((to_z * 4 + to_y) * 2 + src_c) * 2 + half,
            ((to_y * 4 + to_z) * 2 + src_c) * 2 + half,
        ]
    ).astype(jnp.int32)
    own = lax.dynamic_slice_in_dim(span_order, 2 * me, 2)
    own = jnp.concatenate([own, my_c[None]]).astype(jnp.int32)

    query_pos = (own[:2, None] * SPAN + jnp.arange(SPAN)[None, :]).reshape(-1)
    frequency = jnp.exp(jnp.arange(D // 2).astype(F32) * (-2.0 * math.log(500000.0) / D))
    angles = query_pos.astype(F32)[:, None] * frequency[None, :]
    cosine, sine = jnp.cos(angles), jnp.sin(angles)
    cosine = jnp.concatenate([cosine, cosine], axis=1)
    sine = jnp.concatenate([-sine, sine], axis=1)

    with jax.named_scope("weight_rows"):
        share = feats // 32
        cut = []
        for d in DIST:
            start = feats * ((tp + d) % 4) + share * me
            piece = jnp.concatenate(
                [lax.dynamic_slice_in_dim(w, start, share, 0) for w in (w_key, value_weight)],
                axis=1,
            )
            cut.append(shift_tp(piece, d) if d else piece)
        cut = jnp.stack(cut)

    offs = jnp.stack([(tp - d) % 4 for d in DIST]).astype(jnp.int32)
    with jax.named_scope("gather_tokens"):
        mid = rows // 2
        weights = (w_query, w_key, value_weight)
        acc = project(offs[:1], (tokens,), weights)
        near, cosine, sine, offs, table, own, cut, acc = lax.optimization_barrier(
            (left[:mid], cosine, sine, offs, table, own, cut, acc)
        )
        far_a = shift_tp(near, 1)
        far_b = shift_tp(right[mid:], 3)
        acc = project(offs[1:3], (left, right), weights, acc)
        far_a, far_b, acc = lax.optimization_barrier((far_a, far_b, acc))
    gain_q, gain_k = gain_query[None, :], gain_key[None, :]
    q_rot, q_raw, k_rot, k_raw, value, squares = project_end(
        offs[3:], far_a, far_b, weights, acc, cosine, sine, gain_q, gain_k
    )
    with jax.named_scope("norm_sums"):
        squares = sum_tp(squares)
    query_inv = lax.rsqrt(squares[0] / Q_CHANNELS + 1e-06)[:, None]
    key_inv = lax.rsqrt(squares[1] / K_CHANNELS + 1e-06)[:, None]
    key = (k_rot * key_inv).astype(BF)

    with jax.named_scope("gather_keys_values"):
        first_core = my_c == 0
        mine = jnp.where(first_core, key, value)
        pair = join(mine, swap_core(jnp.where(first_core, value, key)))
        plane = join(*shifts(shift_first, pair))
        mine = shifts(shift_second, plane)
    with jax.named_scope("weight_rows"):
        w_rows = lax.all_gather(after(cut, pair), "ctx", axis=0, tiled=False)

    query_unit = q_raw * query_inv
    key_unit = k_raw * key_inv
    query = (
        (q_rot.reshape(2, G, SPAN, D) * query_inv.reshape(2, 1, SPAN, 1)).astype(BF).reshape(2, R, D)
    )
    with jax.named_scope("gather_key_units"):
        key_units = shifts(shift_tp, key_unit.astype(BF))

    with jax.named_scope("gather_out_grad"):
        grad_part = lax.all_gather(after(out_grad, far_a, far_b), "tp", axis=1, tiled=True)
        head_grad = head_grad_of(grad_part, w_out)

    with jax.named_scope("swap_keys_values"):
        last, query, query_unit, head_grad = lax.optimization_barrier(
            (mine[3], query, query_unit, head_grad)
        )
        mine = mine[:3] + [last]
        pieces = (*mine, *(swap_core(x) for x in mine))

    log_total, heads, kv, *out_partial = attn_fwd(table, own, query, pieces, w_out)
    attn_out = [
        lax.psum_scatter(x, "tp", scatter_dimension=0, tiled=False) for x in out_partial
    ]

    query, _, _, *key_units = lax.optimization_barrier((query, *out_partial, *key_units))
    up_query, mix_query, gain_part, mine, theirs = attn_bwd(
        table, own, query, kv, head_grad, heads, log_total,
        cosine, sine, gain_q, query_unit,
    )

    with jax.named_scope("sum_key_value_grads"):
        theirs, mix_query, attn_out[0], w_rows = lax.optimization_barrier(
            (theirs, mix_query, attn_out[0], w_rows)
        )
        mix_query = sum_tp(mix_query)
        received, mix_query = lax.optimization_barrier((swap_core(theirs), mix_query))
        summed = mine.astype(F32) + received.astype(F32)
        sent, total = outgoing(summed)
        arrived = [shift_first(x, d) for x, d in zip(sent, DIST[1:])]
        sent, total = outgoing(add_up(total, arrived))
        total = add_up(total, [shift_second(x, d) for x, d in zip(sent, DIST[1:])])
        ours, its = total[:rows], total[rows:]
        kept = jnp.where(first_core, ours, its)
        swapped = swap_core(jnp.where(first_core, its, ours))
        key_grad_rot = jnp.where(first_core, kept, swapped)
        value_grad = jnp.where(first_core, swapped, kept).astype(BF)

    with jax.named_scope("query_side"):
        query_partial = query_partial_of(
            up_query, query_unit, mix_query, query_inv.reshape(1, rows), w_query
        )
        query_side = lax.psum_scatter(query_partial, "tp", scatter_dimension=0, tiled=False)

    with jax.named_scope("key_value_side"):
        first, second = key_grad_rot[:, : D // 2], key_grad_rot[:, D // 2 :]
        cs, sn = cosine[:, : D // 2], sine[:, D // 2 :]
        key_grad = jnp.concatenate([first * cs + second * sn, second * cs - first * sn], axis=1)
        w_rows = after(w_rows, query_partial).transpose(1, 0, 2, 3).reshape(4, feats, 2 * D)
        key_grad, w_rows = lax.optimization_barrier((key_grad, w_rows))
        both = jnp.concatenate([(key_grad * gain_k).astype(BF), value_grad], axis=1)
        grads = shifts(shift_tp, both)
        key_grad = after(key_grad, *grads)
        gain_key_part = jnp.sum(key_grad * key_unit, axis=0)[None]
        gains = sum_ctx(jnp.concatenate([gain_part, gain_key_part], axis=1))[0]
        gain_query_grad, gain_key_grad = gains[:R], gains[R:]
        input_grad = last_of(grads, key_units, key_inv, w_rows, query_side)
    attn_out = jnp.concatenate(attn_out, axis=0)
    return (attn_out, input_grad, gain_query_grad, gain_key_grad)


def solution(mesh):
    return jax.shard_map(
        local,
        mesh=mesh,
        in_specs=(
            P("ctx", "tp"),
            P(),
            P(None, "tp"),
            P(None, "tp"),
            P(None, "tp"),
            P("tp", None),
            P("tp"),
            P("tp"),
            P("ctx", "tp"),
        ),
        out_specs=(P("ctx", "tp"), P("ctx", "tp"), P("tp"), P("tp")),
        check_vma=False,
    )
```

```python
import math

import jax
import jax.numpy as jnp
from jax import lax
from jax.experimental import pallas as pl
from jax.experimental.pallas import tpu as pltpu
from jax.sharding import PartitionSpec as P

D = 128
SPAN = 128
G = 5
R = G * SPAN
CH = 8
KC = CH * SPAN
SCALE = D**-0.5
LOG2E = math.log2(math.e)
NEG = -1e30
BF = jnp.bfloat16
F32 = jnp.float32
DIST = (0, 1, 3, 2)
PIECES = 8


def nt(a, b):
    return lax.dot_general(a, b, (((1,), (1,)), ((), ())), preferred_element_type=F32)


def tn(a, b):
    return lax.dot_general(a, b, (((0,), (0,)), ((), ())), preferred_element_type=F32)


def nn(a, b):
    return lax.dot_general(a, b, (((1,), (0,)), ((), ())), preferred_element_type=F32)


VM = pl.BlockSpec(memory_space=pltpu.VMEM)
HB = pl.BlockSpec(memory_space=pl.ANY)
FAR = pl.BlockSpec(memory_space=pltpu.HBM)


def params(mib):
    return pltpu.CompilerParams(vmem_limit_bytes=mib * 2**20)


def cost(flops, mib, exps=0):
    return pl.CostEstimate(
        flops=int(flops), bytes_accessed=int(mib * 2**20), transcendentals=int(exps)
    )


def turn(x, cosine, sine):
    return x * cosine + pltpu.roll(x, D // 2, 1) * sine


def lane_sums(x):
    return jnp.sum(x.T, axis=0, keepdims=True)


def fetch(pairs, sems):
    copies = [pltpu.make_async_copy(src, dst, sems.at[n]) for n, (src, dst) in enumerate(pairs)]
    for copy in copies:
        copy.start()
    return copies


def fetch_rows(off, weights, stages, sems):
    pairs = []
    for n in range(stages[0].shape[0]):
        rows = stages[0].shape[1]
        at = pl.ds(pl.multiple_of(off[n] * rows, rows), rows)
        pairs += [(w.at[at, :], s.at[n]) for w, s in zip(weights, stages)]
    return fetch(pairs, sems)


def product_of(x, stages, n):
    return jnp.concatenate([nn(x, s[n]) for s in stages], axis=1)


def project_kernel(off, *refs, count, parts, first):
    xs, weights = refs[: count * parts], refs[count * parts : count * parts + 3]
    stages, sems, out = refs[-4:-1], refs[-1], refs[-5]
    copies = fetch_rows(off, weights, stages, sems)
    total = None if first else refs[count * parts + 3][...]
    for n in range(count):
        for copy in copies[3 * n : 3 * n + 3]:
            copy.wait()
        x = jnp.concatenate([r[...] for r in xs[n * parts : (n + 1) * parts]], axis=0)
        part = product_of(x, stages, n)
        total = part if total is None else total + part
    out[...] = total


def stages_of(weights, count, feats):
    return [pltpu.VMEM((count, feats, w.shape[1]), BF) for w in weights] + [
        pltpu.SemaphoreType.DMA((3 * count,))
    ]


def project(off, pieces, weights, acc=None):
    parts = len(pieces[0])
    rows, feats = sum(x.shape[0] for x in pieces[0]), pieces[0][0].shape[1]
    width = sum(w.shape[1] for w in weights)
    count = len(pieces)
    xs = [x for piece in pieces for x in piece]
    more = () if acc is None else (acc,)
    return pl.pallas_call(
        lambda *refs: project_kernel(*refs, count=count, parts=parts, first=acc is None),
        out_shape=jax.ShapeDtypeStruct((rows, width), F32),
        grid_spec=pltpu.PrefetchScalarGridSpec(
            num_scalar_prefetch=1,
            grid=(),
            in_specs=[VM] * len(xs) + [FAR] * 3 + [VM] * len(more),
            out_specs=VM,
            scratch_shapes=stages_of(weights, count, feats),
        ),
        compiler_params=params(56),
        cost_estimate=cost(6e8 * count, 4 * count),
    )(off, *xs, *weights, *more)


def project_end_kernel(
    off, xa, xb, wq, wk, wv, acc_in, cosine, sine, gain_q, gain_k,
    q_rot, q_raw, k_rot, k_raw, v_out, squares, sq, sk, sv, sems,
):
    stages = (sq, sk, sv)
    copies = fetch_rows(off, (wq, wk, wv), stages, sems)
    x = jnp.concatenate([xa[...], xb[...]], axis=0)
    cs, sn = cosine[...], sine[...]
    for copy in copies:
        copy.wait()
    raw = acc_in[...] + product_of(x, stages, 0)
    k = raw[:, R : R + D]
    k_raw[...] = k
    k_rot[...] = turn(k * gain_k[...], cs, sn)
    v_out[...] = raw[:, R + D :].astype(BF)
    squares[1:2, :] = lane_sums(k * k)
    total = None
    for h in range(G):
        q = raw[:, h * D : (h + 1) * D]
        total = q * q if total is None else total + q * q
        rotated = turn(q * gain_q[:, h * D : (h + 1) * D], cs, sn)
        for i in range(2):
            q_rot[i, h * SPAN : (h + 1) * SPAN, :] = rotated[i * SPAN : (i + 1) * SPAN]
    q_raw[...] = raw[:, :R]
    squares[0:1, :] = lane_sums(total)


def project_end(off, xa, xb, weights, acc, cosine, sine, gain_q, gain_k):
    rows = acc.shape[0]
    feats = xa.shape[1]
    outs = (
        jax.ShapeDtypeStruct((2, R, D), F32),
        jax.ShapeDtypeStruct((rows, R), F32),
        jax.ShapeDtypeStruct((rows, D), F32),
        jax.ShapeDtypeStruct((rows, D), F32),
        jax.ShapeDtypeStruct((rows, D), BF),
        jax.ShapeDtypeStruct((2, rows), F32),
    )
    return pl.pallas_call(
        project_end_kernel,
        out_shape=outs,
        grid_spec=pltpu.PrefetchScalarGridSpec(
            num_scalar_prefetch=1,
            grid=(),
            in_specs=[VM, VM] + [FAR] * 3 + [VM] * 5,
            out_specs=(VM,) * 6,
            scratch_shapes=stages_of(weights, 1, feats),
        ),
        compiler_params=params(56),
        cost_estimate=cost(6e8, 6),
    )(off, xa, xb, *weights, acc, cosine, sine, gain_q, gain_k)


def join_kernel(*refs):
    at = 0
    for ref in refs[:-1]:
        n = ref.shape[0]
        refs[-1][at : at + n, :] = ref[...]
        at += n


def join(*xs):
    rows = sum(x.shape[0] for x in xs)
    return pl.pallas_call(
        join_kernel,
        out_shape=jax.ShapeDtypeStruct((rows,) + xs[0].shape[1:], xs[0].dtype),
        in_specs=[VM] * len(xs),
        out_specs=VM,
        compiler_params=params(8),
        cost_estimate=cost(0, 1),
    )(*xs)


def spans_at(ref, loc, which, j):
    return jnp.concatenate(
        [
            ref[pl.ds(pl.multiple_of(loc[which, CH * j + t] * SPAN, SPAN), SPAN), :]
            for t in range(CH)
        ],
        axis=0,
    )


def load_pieces(refs, whole, core, sems):
    count = len(refs) // 2
    copies = []
    for n, src in enumerate(refs):
        rows = src.shape[0]
        to = core if n < count else 1 - core
        copy = pltpu.make_async_copy(
            src, whole.at[to, pl.ds((n % count) * rows, rows), :], sems.at[n]
        )
        copy.start()
        copies.append(copy)
    for copy in copies:
        copy.wait()


def fwd_kernel(loc, own, q_ref, *refs):
    kv_refs, w_ref, (lse_ref, o_ref, kv_out, outa, outb) = (
        refs[:PIECES], refs[PIECES], refs[PIECES + 1 : PIECES + 6],
    )
    kv, w_s, y_s, m_s, acc_s, sems, wsems, kvsem, ysems = refs[PIECES + 6 :]
    load_pieces(kv_refs, kv, own[2], sems)
    keep = fetch([(kv, kv_out)], kvsem)
    block = y_s.shape[2]
    w_copies = fetch(
        [(w_ref.at[:, pl.ds(b * block, block)], w_s.at[b]) for b in range(4)], wsems
    )
    k_ref, v_ref = kv.at[0], kv.at[1]
    ones = (lax.broadcasted_iota(jnp.int32, (KC, D), 1) == 0).astype(BF)
    for i in range(2):
        c = own[i]
        m_s[...] = jnp.full_like(m_s, NEG)
        acc_s[...] = jnp.zeros_like(acc_s)

        def step(j, masked):
            kk = spans_at(k_ref, loc, 0, j)
            vv = jnp.concatenate([spans_at(v_ref, loc, 1, j), ones], axis=1)
            for h in range(G):
                at = slice(h * SPAN, (h + 1) * SPAN)
                s = nt(q_ref[i, at, :], kk)
                if masked:
                    key = j * KC + lax.broadcasted_iota(jnp.int32, (SPAN, KC), 1)
                    row = c * SPAN + lax.broadcasted_iota(jnp.int32, (SPAN, KC), 0)
                    s = jnp.where(key <= row, s, NEG)
                m = m_s[at, :]
                new = jnp.maximum(m, jnp.max(s, axis=1, keepdims=True))
                shrink = jnp.exp2((m - new) * (SCALE * LOG2E))
                p = jnp.exp2((s - new[:, :1]) * (SCALE * LOG2E))
                m_s[at, :] = new
                acc_s[at, :] = acc_s[at, :] * shrink[:, :1] + nn(p.astype(BF), vv)

        last = c // CH

        def body(j, _):
            step(j, False)
            return 0

        lax.fori_loop(0, last, body, 0)
        step(last, True)
        total = acc_s[:, D : D + 1]
        o_ref[i] = (acc_s[:, :D] / total).astype(BF)
        lse = m_s[...] * (SCALE * LOG2E) + jnp.log2(jnp.broadcast_to(total, (R, D)))
        lse_ref[i] = lse.T[0:1, :]
    x = jnp.concatenate(
        [
            jnp.concatenate(
                [o_ref[i, h * SPAN : (h + 1) * SPAN, :] for h in range(G)], axis=1
            )
            for i in range(2)
        ],
        axis=0,
    )
    y_copies = []
    for b in range(4):
        w_copies[b].wait()
        y_s[b] = nn(x, w_s[b]).astype(BF)
        for i, out in enumerate((outa, outb)):
            copy = pltpu.make_async_copy(
                y_s.at[b, pl.ds(i * SPAN, SPAN), :], out.at[b], ysems.at[2 * b + i]
            )
            copy.start()
            y_copies.append(copy)
    for copy in keep + y_copies:
        copy.wait()


def attn_fwd(table, own, q, pieces, w_out):
    n = sum(x.shape[0] for x in pieces) // 2
    block = w_out.shape[1] // 4
    return pl.pallas_call(
        fwd_kernel,
        out_shape=(
            jax.ShapeDtypeStruct((2, 1, R), F32),
            jax.ShapeDtypeStruct((2, R, D), BF),
            jax.ShapeDtypeStruct((2, n, D), BF),
            jax.ShapeDtypeStruct((4, SPAN, block), BF),
            jax.ShapeDtypeStruct((4, SPAN, block), BF),
        ),
        grid_spec=pltpu.PrefetchScalarGridSpec(
            num_scalar_prefetch=2,
            grid=(),
            in_specs=[VM] + [HB] * PIECES + [FAR],
            out_specs=(VM, VM, FAR, FAR, FAR),
            scratch_shapes=[
                pltpu.VMEM((2, n, D), BF),
                pltpu.VMEM((4, R, block), BF),
                pltpu.VMEM((4, 2 * SPAN, block), BF),
                pltpu.VMEM((R, D), F32),
                pltpu.VMEM((R, 2 * D), F32),
                pltpu.SemaphoreType.DMA((PIECES,)),
                pltpu.SemaphoreType.DMA((4,)),
                pltpu.SemaphoreType.DMA((1,)),
                pltpu.SemaphoreType.DMA((8,)),
            ],
        ),
        compiler_params=params(56),
        cost_estimate=cost(1.8e10, 12, 6e6),
    )(table, own, q, *pieces, w_out)


def bwd_kernel(
    loc, own, q_ref, kv_in, do_ref, o_ref, lse_ref, cosine, sine, gain_q, unit_ref,
    up_ref, mix_ref, gain_ref, mine_ref, theirs_ref, kv, dkv, dqa, sems,
):
    core = own[2]
    copies = fetch([(kv_in.at[0], kv.at[0]), (kv_in.at[1], kv.at[1])], sems)
    k_ref, v_ref = kv.at[0], kv.at[1]
    dkv[...] = jnp.zeros_like(dkv)
    dqa[...] = jnp.zeros_like(dqa)
    for copy in copies:
        copy.wait()
    for i in range(2):
        c = own[i]
        q, do, lse = q_ref[i], do_ref[i], lse_ref[i]
        delta = lane_sums(do.astype(F32) * o_ref[i].astype(F32))

        def step(j, masked):
            kk = spans_at(k_ref, loc, 0, j)
            vv = spans_at(v_ref, loc, 1, j)
            p = jnp.exp2(nt(kk, q) * (SCALE * LOG2E) - lse)
            if masked:
                key = j * KC + lax.broadcasted_iota(jnp.int32, (KC, R), 0)
                row = c * SPAN + lax.rem(lax.broadcasted_iota(jnp.int32, (KC, R), 1), SPAN)
                p = jnp.where(key <= row, p, 0.0)
            ds = (p * (nt(vv, do) - delta)).astype(BF)
            dqa[i] += tn(kk, ds)
            dv = nn(p.astype(BF), do)
            dk = nn(ds, q) * SCALE
            for t in range(CH):
                part = slice(t * SPAN, (t + 1) * SPAN)
                at = pl.ds(pl.multiple_of(loc[2, CH * j + t] * SPAN, SPAN), SPAN)
                dkv[0, at, :] += dk[part]
                at = pl.ds(pl.multiple_of(loc[3, CH * j + t] * SPAN, SPAN), SPAN)
                dkv[1, at, :] += dv[part]

        last = c // CH

        def body(j, _):
            step(j, False)
            return 0

        lax.fori_loop(0, last, body, 0)
        step(last, True)
    mine_ref[...] = dkv[core].astype(BF)
    theirs_ref[...] = dkv[1 - core].astype(BF)
    for i in range(2):
        rows = slice(i * SPAN, (i + 1) * SPAN)
        cs, sn = cosine[rows, :], -sine[rows, :]
        mix = None
        for h in range(G):
            cols = slice(h * D, (h + 1) * D)
            grad = turn((dqa[i, :, cols] * SCALE).T, cs, sn)
            unit = unit_ref[rows, cols]
            up = grad * gain_q[:, cols]
            up_ref[rows, cols] = up
            mix = up * unit if mix is None else mix + up * unit
            gain = jnp.sum(grad * unit, axis=0, keepdims=True)
            if i == 0:
                gain_ref[:, cols] = gain
            else:
                gain_ref[:, cols] += gain
        mix_ref[:, rows] = lane_sums(mix)


def attn_bwd(table, own, q, kv, do, o, lse, cosine, sine, gain_q, unit):
    n = kv.shape[1]
    rows = 2 * SPAN
    return pl.pallas_call(
        bwd_kernel,
        out_shape=(
            jax.ShapeDtypeStruct((rows, R), F32),
            jax.ShapeDtypeStruct((1, rows), F32),
            jax.ShapeDtypeStruct((1, R), F32),
            jax.ShapeDtypeStruct((n, D), BF),
            jax.ShapeDtypeStruct((n, D), BF),
        ),
        grid_spec=pltpu.PrefetchScalarGridSpec(
            num_scalar_prefetch=2,
            grid=(),
            in_specs=[VM, FAR] + [VM] * 7,
            out_specs=(VM,) * 5,
            scratch_shapes=[
                pltpu.VMEM((2, n, D), BF),
                pltpu.VMEM((2, n, D), F32),
                pltpu.VMEM((2, D, R), F32),
                pltpu.SemaphoreType.DMA((2,)),
            ],
        ),
        compiler_params=params(56),
        cost_estimate=cost(2.2e10, 12, 6e6),
    )(table, own, q, kv, do, o, lse, cosine, sine, gain_q, unit)


def key_gain_kernel(
    loc, own, kv_in, mine_in, theirs_in, cos_r, sin_r, cos_s, sin_s, out, k_s, g_s, sems
):
    core = own[2]
    key_copy = pltpu.make_async_copy(kv_in.at[0], k_s, sems.at[0])
    key_copy.start()

    @pl.when(core == 0)
    def _():
        pltpu.make_async_copy(mine_in, g_s, sems.at[1]).start()

    @pl.when(core != 0)
    def _():
        pltpu.make_async_copy(theirs_in, g_s, sems.at[1]).start()

    key_copy.wait()
    pltpu.make_async_copy(mine_in, g_s, sems.at[1]).wait()
    cr, sr = cos_r[...], sin_r[...]

    def body(s, sums):
        plain, by_cos, by_sin = sums
        k = k_s[pl.ds(pl.multiple_of(loc[0, s] * SPAN, SPAN), SPAN), :].astype(F32)
        g = g_s[pl.ds(pl.multiple_of(loc[2, s] * SPAN, SPAN), SPAN), :].astype(F32)
        cs, sn = cos_s[pl.ds(s, 1), :], sin_s[pl.ds(s, 1), :]
        same = k * g
        cross = g * pltpu.roll(k, D // 2, 1)
        return (
            plain + same,
            by_cos + same * (cs * cr - sn * sr),
            by_sin + cross * (sn * cr + cs * sr),
        )

    zero = jnp.zeros((SPAN, D), F32)
    plain, by_cos, by_sin = lax.fori_loop(0, loc.shape[1], body, (zero, zero, zero))

    def over_rows(x):
        return jnp.broadcast_to(jnp.sum(x, axis=0, keepdims=True), (8, D))

    plain, by_cos, by_sin = over_rows(plain), over_rows(by_cos), over_rows(by_sin)
    half = D // 2
    sign = jnp.where(lax.broadcasted_iota(jnp.int32, (8, D), 1) < half, 1.0, -1.0)
    total = (
        plain
        + pltpu.roll(plain, half, 1)
        + by_cos
        - pltpu.roll(by_cos, half, 1)
        + sign * (by_sin + pltpu.roll(by_sin, half, 1))
    )
    out[...] = 0.5 * total[0:1]


def key_gain_of(table, own, kv, mine, theirs, tables):
    n = kv.shape[1]
    return pl.pallas_call(
        key_gain_kernel,
        out_shape=jax.ShapeDtypeStruct((1, D), F32),
        grid_spec=pltpu.PrefetchScalarGridSpec(
            num_scalar_prefetch=2,
            grid=(),
            in_specs=[HB] * 3 + [VM] * 4,
            out_specs=VM,
            scratch_shapes=[
                pltpu.VMEM((n, D), BF),
                pltpu.VMEM((n, D), BF),
                pltpu.SemaphoreType.DMA((2,)),
            ],
        ),
        compiler_params=params(56),
        cost_estimate=cost(1e9, 6),
    )(table, own, kv, mine, theirs, *tables)


def head_grad_kernel(x_ref, w_ref, out, x_s, w_s, sems):
    block = x_s.shape[2]
    pairs = []
    for b in range(4):
        cols = pl.ds(b * block, block)
        pairs += [(w_ref.at[:, cols], w_s.at[b]), (x_ref.at[:, cols], x_s.at[b])]
    copies = fetch(pairs, sems)
    total = None
    for b in range(4):
        copies[2 * b].wait()
        copies[2 * b + 1].wait()
        part = nt(x_s[b], w_s[b])
        total = part if total is None else total + part
    for i in range(2):
        for h in range(G):
            out[i, h * SPAN : (h + 1) * SPAN, :] = total[
                i * SPAN : (i + 1) * SPAN, h * D : (h + 1) * D
            ].astype(BF)


def head_grad_of(x, w_out):
    rows, feats = x.shape
    block = feats // 4
    return pl.pallas_call(
        head_grad_kernel,
        out_shape=jax.ShapeDtypeStruct((2, R, D), BF),
        in_specs=[FAR, FAR],
        out_specs=VM,
        scratch_shapes=[
            pltpu.VMEM((4, rows, block), BF),
            pltpu.VMEM((4, R, block), BF),
            pltpu.SemaphoreType.DMA((8,)),
        ],
        compiler_params=params(56),
        cost_estimate=cost(1.7e9, 9),
    )(x, w_out)


def query_kernel(up, unit, mix, inv, w_ref, out, w_s, y_s, sems, ysems):
    block = w_s.shape[1]
    copies = fetch([(w_ref.at[pl.ds(b * block, block), :], w_s.at[b]) for b in range(4)], sems)
    rows = up.shape[0]

    def column(ref):
        return jnp.broadcast_to(ref[...], (D, rows)).T[:, :1]

    x = (column(inv) * (up[...] - unit[...] * (column(mix) * (1.0 / Q_CHANNELS)))).astype(BF)
    y_copies = []
    for b in range(4):
        copies[b].wait()
        y_s[b] = nt(x, w_s[b]).astype(BF)
        copy = pltpu.make_async_copy(y_s.at[b], out.at[b], ysems.at[b])
        copy.start()
        y_copies.append(copy)
    for copy in y_copies:
        copy.wait()


def query_partial_of(up, unit, mix, inv, w_query):
    rows = up.shape[0]
    feats = w_query.shape[0]
    block = feats // 4
    return pl.pallas_call(
        query_kernel,
        out_shape=jax.ShapeDtypeStruct((4, rows, block), BF),
        in_specs=[VM] * 4 + [FAR],
        out_specs=FAR,
        scratch_shapes=[
            pltpu.VMEM((4, block, R), BF),
            pltpu.VMEM((4, rows, block), BF),
            pltpu.SemaphoreType.DMA((4,)),
            pltpu.SemaphoreType.DMA((4,)),
        ],
        compiler_params=params(56),
        cost_estimate=cost(1.7e9, 9),
    )(up, unit, mix, inv, w_query)


def last_kernel(g0, g1, g2, g3, u0, u1, u2, u3, inv, w, query_side, out):
    gs, us = (g0, g1, g2, g3), (u0, u1, u2, u3)
    mix = None
    for g, u in zip(gs, us):
        part = g[:, :D].astype(F32) * u[...].astype(F32)
        mix = part if mix is None else mix + part
    mix = jnp.sum(mix, axis=1, keepdims=True) * (1.0 / K_CHANNELS)
    total = query_side[...].astype(F32)
    for n, (g, u) in enumerate(zip(gs, us)):
        raw = (inv[...] * (g[:, :D].astype(F32) - u[...].astype(F32) * mix)).astype(BF)
        total = total + nt(jnp.concatenate([raw, g[:, D:]], axis=1), w[n])
    out[...] = total.astype(BF)


def last_of(grads, units, inv, w, query_side):
    return pl.pallas_call(
        last_kernel,
        out_shape=jax.ShapeDtypeStruct(query_side.shape, BF),
        in_specs=[VM] * 11,
        out_specs=VM,
        compiler_params=params(56),
        cost_estimate=cost(7e8, 5),
    )(*grads, *units, inv, w, query_side)

QUERY_HEADS = 20
KEY_VALUE_HEADS = 4
Q_CHANNELS = QUERY_HEADS * D
K_CHANNELS = KEY_VALUE_HEADS * D
N_Y, N_Z, N_CORE, N_TP = 4, 4, 2, 4


def ctx_index(y, z, c):
    return (y * N_Z + z) * N_CORE + c


def ctx_pairs(move):
    return [
        (ctx_index(y, z, c), ctx_index(*move(y, z, c)))
        for y in range(N_Y)
        for z in range(N_Z)
        for c in range(N_CORE)
    ]


def shift_first(x, d):
    return lax.ppermute(
        x,
        "ctx",
        ctx_pairs(lambda y, z, c: ((y + c * d) % N_Y, (z + (1 - c) * d) % N_Z, c)),
    )


def shift_second(x, d):
    return lax.ppermute(
        x,
        "ctx",
        ctx_pairs(lambda y, z, c: ((y + (1 - c) * d) % N_Y, (z + c * d) % N_Z, c)),
    )


def swap_core(x):
    return lax.ppermute(x, "ctx", ctx_pairs(lambda y, z, c: (y, z, 1 - c)))


def shift_tp(x, d):
    return lax.ppermute(x, "tp", [(i, (i + d) % N_TP) for i in range(N_TP)])


def shifts(shift, x):
    return [x] + [shift(x, d) for d in DIST[1:]]


def sum_tp(x):
    x = x + lax.ppermute(x, "tp", [(i, i ^ 1) for i in range(N_TP)])
    return x + lax.ppermute(x, "tp", [(i, 3 - i) for i in range(N_TP)])


def sum_core_z(x):
    x = x + swap_core(x)
    x = x + lax.ppermute(x, "ctx", ctx_pairs(lambda y, z, c: (y, z ^ 1, c)))
    return x + lax.ppermute(x, "ctx", ctx_pairs(lambda y, z, c: (y, 3 - z, c)))


def sum_y(x):
    x = x + lax.ppermute(x, "ctx", ctx_pairs(lambda y, z, c: (y ^ 1, z, c)))
    return x + lax.ppermute(x, "ctx", ctx_pairs(lambda y, z, c: (3 - y, z, c)))


def after(x, *others):
    return lax.optimization_barrier((x,) + others)[0]


def outgoing(x):
    rows = x.shape[0] // 4
    return [x[d * rows : (d + 1) * rows].astype(BF) for d in DIST[1:]], x[:rows]


def add_up(total, arrived):
    for x in arrived:
        total = total + x.astype(F32)
    return total


def local(tokens, span_order, w_query, w_key, value_weight, w_out, gain_query, gain_key, out_grad):
    rows, feats = tokens.shape
    me = lax.axis_index("ctx")
    tp = lax.axis_index("tp")
    my_y, my_z, my_c = me // 8, (me // 2) % 4, me % 2

    mid = rows // 2
    with jax.named_scope("gather_tokens"):
        upper, lower = tokens[:mid], tokens[mid:]
        left_a = shift_tp(upper, 1)
        right_b = shift_tp(lower, 3)
        left_b = shift_tp(lower, 1)
        right_a = shift_tp(upper, 3)

    place = jnp.arange(64, dtype=jnp.int32)
    stored = jnp.sum(jnp.where(span_order[None, :] == place[:, None], place[None, :], 0), axis=1)
    src, half = stored // 2, stored % 2
    src_y, src_z, src_c = src // 8, (src // 2) % 4, src % 2
    to_y, to_z = (src_y - my_y) % 4, (src_z - my_z) % 4
    back_y, back_z = (4 - to_y) % 4, (4 - to_z) % 4
    slot_y = jnp.where(back_y >= 2, 5 - back_y, back_y)
    slot_z = jnp.where(back_z >= 2, 5 - back_z, back_z)
    table = jnp.stack(
        [
            ((slot_y * 4 + slot_z) * 2 + src_c) * 2 + half,
            ((slot_z * 4 + slot_y) * 2 + 1 - src_c) * 2 + half,
            ((to_z * 4 + to_y) * 2 + src_c) * 2 + half,
            ((to_y * 4 + to_z) * 2 + src_c) * 2 + half,
        ]
    ).astype(jnp.int32)
    own = lax.dynamic_slice_in_dim(span_order, 2 * me, 2)
    own = jnp.concatenate([own, my_c[None]]).astype(jnp.int32)

    query_pos = (own[:2, None] * SPAN + jnp.arange(SPAN)[None, :]).reshape(-1)
    frequency = jnp.exp(jnp.arange(D // 2).astype(F32) * (-2.0 * math.log(500000.0) / D))
    angles = query_pos.astype(F32)[:, None] * frequency[None, :]
    cosine, sine = jnp.cos(angles), jnp.sin(angles)
    cosine = jnp.concatenate([cosine, cosine], axis=1)
    sine = jnp.concatenate([-sine, sine], axis=1)

    with jax.named_scope("weight_rows"):
        share = feats // 32
        cut = []
        for d in DIST:
            start = feats * ((tp + d) % 4) + share * me
            piece = jnp.concatenate(
                [lax.dynamic_slice_in_dim(w, start, share, 0) for w in (w_key, value_weight)],
                axis=1,
            )
            cut.append(shift_tp(piece, d) if d else piece)
        cut = jnp.stack(cut)

    offs = jnp.stack([(tp - d) % 4 for d in DIST]).astype(jnp.int32)
    twice = 2.0 * jnp.concatenate([frequency, frequency])[None, :]
    by_row = jnp.arange(SPAN).astype(F32)[:, None] * twice
    by_span = (SPAN * jnp.arange(64)).astype(F32)[:, None] * twice
    tables = (jnp.cos(by_row), jnp.sin(by_row), jnp.cos(by_span), jnp.sin(by_span))

    with jax.named_scope("gather_tokens"):
        weights = (w_query, w_key, value_weight)
        acc = project(offs[:1], ((tokens,),), weights)
        left_a, right_b, cosine, sine, offs, table, own, cut, acc, *tables = lax.optimization_barrier(
            (left_a, right_b, cosine, sine, offs, table, own, cut, acc, *tables)
        )
        far_a = shift_tp(left_a, 1)
        far_b = shift_tp(right_b, 3)
        acc = project(offs[1:3], ((left_a, left_b), (right_a, right_b)), weights, acc)
        far_a, far_b, acc = lax.optimization_barrier((far_a, far_b, acc))
    gain_q, gain_k = gain_query[None, :], gain_key[None, :]
    q_rot, q_raw, k_rot, k_raw, value, squares = project_end(
        offs[3:], far_a, far_b, weights, acc, cosine, sine, gain_q, gain_k
    )
    with jax.named_scope("norm_sums"):
        squares = sum_tp(squares)
    query_inv = lax.rsqrt(squares[0] / Q_CHANNELS + 1e-06)[:, None]
    key_inv = lax.rsqrt(squares[1] / K_CHANNELS + 1e-06)[:, None]
    key = (k_rot * key_inv).astype(BF)

    with jax.named_scope("gather_keys_values"):
        first_core = my_c == 0
        mine = jnp.where(first_core, key, value)
        pair = join(mine, swap_core(jnp.where(first_core, value, key)))
        plane = join(*shifts(shift_first, pair))
        mine = shifts(shift_second, plane)
    with jax.named_scope("weight_rows"):
        w_rows = lax.all_gather(after(cut, pair), "ctx", axis=0, tiled=False)

    query_unit = q_raw * query_inv
    key_unit = (k_raw * key_inv).astype(BF)
    query = (
        (q_rot.reshape(2, G, SPAN, D) * query_inv.reshape(2, 1, SPAN, 1)).astype(BF).reshape(2, R, D)
    )
    with jax.named_scope("gather_key_units"):
        key_units = shifts(shift_tp, key_unit)

    with jax.named_scope("gather_out_grad"):
        grad_part = lax.all_gather(after(out_grad, far_a, far_b), "tp", axis=1, tiled=True)
        head_grad = head_grad_of(grad_part, w_out)

    with jax.named_scope("swap_keys_values"):
        last, query, query_unit, head_grad = lax.optimization_barrier(
            (mine[3], query, query_unit, head_grad)
        )
        mine = mine[:3] + [last]
        pieces = (*mine, *(swap_core(x) for x in mine))

    log_total, heads, kv, *out_partial = attn_fwd(table, own, query, pieces, w_out)
    attn_out = [
        lax.psum_scatter(x, "tp", scatter_dimension=0, tiled=False) for x in out_partial
    ]

    query, _, _, *key_units = lax.optimization_barrier((query, *out_partial, *key_units))
    up_query, mix_query, gain_part, mine, theirs = attn_bwd(
        table, own, query, kv, head_grad, heads, log_total,
        cosine, sine, gain_q, query_unit,
    )

    with jax.named_scope("sum_key_value_grads"):
        theirs, mix_query, attn_out[0], w_rows = lax.optimization_barrier(
            (theirs, mix_query, attn_out[0], w_rows)
        )
        mix_query = sum_tp(mix_query)
        received, mix_query = lax.optimization_barrier((swap_core(theirs), mix_query))
        summed = mine.astype(F32) + received.astype(F32)
        sent, total = outgoing(summed)
        arrived = [shift_first(x, d) for x, d in zip(sent, DIST[1:])]
        gain_key_part = key_gain_of(table, own, kv, mine, theirs, tables) / gain_k
        gains = sum_core_z(jnp.concatenate([gain_part, gain_key_part], axis=1))
        *arrived, gains = lax.optimization_barrier((*arrived, gains))
        sent, total = outgoing(add_up(total, arrived))
        arrived = [shift_second(x, d) for x, d in zip(sent, DIST[1:])]
        *arrived, gains = lax.optimization_barrier((*arrived, sum_y(gains)))
        gain_query_grad, gain_key_grad = gains[0, :R], gains[0, R:]
        total = add_up(total, arrived)
        ours, its = total[:rows], total[rows:]
        kept = jnp.where(first_core, ours, its)
        swapped = swap_core(jnp.where(first_core, its, ours))
        key_grad_rot = jnp.where(first_core, kept, swapped)
        value_grad = jnp.where(first_core, swapped, kept).astype(BF)

    with jax.named_scope("query_side"):
        query_partial = query_partial_of(
            up_query, query_unit, mix_query, query_inv.reshape(1, rows), w_query
        )
        query_side = lax.psum_scatter(query_partial, "tp", scatter_dimension=0, tiled=False)

    with jax.named_scope("key_value_side"):
        first, second = key_grad_rot[:, : D // 2], key_grad_rot[:, D // 2 :]
        cs, sn = cosine[:, : D // 2], sine[:, D // 2 :]
        key_grad = jnp.concatenate([first * cs + second * sn, second * cs - first * sn], axis=1)
        w_rows = after(w_rows, query_partial).transpose(1, 0, 2, 3).reshape(4, feats, 2 * D)
        key_grad, w_rows = lax.optimization_barrier((key_grad, w_rows))
        both = jnp.concatenate([(key_grad * gain_k).astype(BF), value_grad], axis=1)
        grads = shifts(shift_tp, both)
        input_grad = last_of(grads, key_units, key_inv, w_rows, query_side)
    attn_out = jnp.concatenate(attn_out, axis=0)
    return (attn_out, input_grad, gain_query_grad, gain_key_grad)


def solution(mesh):
    return jax.shard_map(
        local,
        mesh=mesh,
        in_specs=(
            P("ctx", "tp"),
            P(),
            P(None, "tp"),
            P(None, "tp"),
            P(None, "tp"),
            P("tp", None),
            P("tp"),
            P("tp"),
            P("ctx", "tp"),
        ),
        out_specs=(P("ctx", "tp"), P("ctx", "tp"), P("tp"), P("tp")),
        check_vma=False,
    )
```

```python
import math

import jax
import jax.numpy as jnp
from jax import lax
from jax.experimental import pallas as pl
from jax.experimental.pallas import tpu as pltpu
from jax.sharding import PartitionSpec as P

D = 128
SPAN = 128
G = 5
R = G * SPAN
CH = 8
KC = CH * SPAN
SCALE = D**-0.5
LOG2E = math.log2(math.e)
NEG = -1e30
BF = jnp.bfloat16
F32 = jnp.float32
DIST = (0, 1, 3, 2)
PIECES = 8


def nt(a, b):
    return lax.dot_general(a, b, (((1,), (1,)), ((), ())), preferred_element_type=F32)


def tn(a, b):
    return lax.dot_general(a, b, (((0,), (0,)), ((), ())), preferred_element_type=F32)


def nn(a, b):
    return lax.dot_general(a, b, (((1,), (0,)), ((), ())), preferred_element_type=F32)


VM = pl.BlockSpec(memory_space=pltpu.VMEM)
HB = pl.BlockSpec(memory_space=pl.ANY)
FAR = pl.BlockSpec(memory_space=pltpu.HBM)


def params(mib):
    return pltpu.CompilerParams(vmem_limit_bytes=mib * 2**20)


def cost(flops, mib, exps=0):
    return pl.CostEstimate(
        flops=int(flops), bytes_accessed=int(mib * 2**20), transcendentals=int(exps)
    )


def turn(x, cosine, sine):
    return x * cosine + pltpu.roll(x, D // 2, 1) * sine


def lane_sums(x):
    return jnp.sum(x.T, axis=0, keepdims=True)


def fetch(pairs, sems):
    copies = [pltpu.make_async_copy(src, dst, sems.at[n]) for n, (src, dst) in enumerate(pairs)]
    for copy in copies:
        copy.start()
    return copies


def fetch_rows(off, weights, stages, sems):
    pairs = []
    for n in range(stages[0].shape[0]):
        rows = stages[0].shape[1]
        at = pl.ds(pl.multiple_of(off[n] * rows, rows), rows)
        pairs += [(w.at[at, :], s.at[n]) for w, s in zip(weights, stages)]
    return fetch(pairs, sems)


def product_of(x, stages, n):
    return jnp.concatenate([nn(x, s[n]) for s in stages], axis=1)


def project_kernel(off, *refs, count, parts, first):
    xs, weights = refs[: count * parts], refs[count * parts : count * parts + 3]
    stages, sems, x_s, isems, out = refs[-6:-3], refs[-3], refs[-2], refs[-1], refs[-7]
    part_rows = x_s.shape[1] // parts
    inputs = fetch(
        [
            (xs[n * parts + m], x_s.at[n, pl.ds(m * part_rows, part_rows), :])
            for n in range(count)
            for m in range(parts)
        ]
        + ([] if first else [(refs[count * parts + 3], out)]),
        isems,
    )
    copies = fetch_rows(off, weights, stages, sems)
    for copy in inputs:
        copy.wait()
    total = None if first else out[...]
    for n in range(count):
        for copy in copies[3 * n : 3 * n + 3]:
            copy.wait()
        part = product_of(x_s[n], stages, n)
        total = part if total is None else total + part
    out[...] = total


def stages_of(weights, count, feats):
    return [pltpu.VMEM((count, feats, w.shape[1]), BF) for w in weights] + [
        pltpu.SemaphoreType.DMA((3 * count,))
    ]


def project(off, pieces, weights, acc=None):
    parts = len(pieces[0])
    rows, feats = sum(x.shape[0] for x in pieces[0]), pieces[0][0].shape[1]
    width = sum(w.shape[1] for w in weights)
    count = len(pieces)
    xs = [x for piece in pieces for x in piece]
    more = () if acc is None else (acc,)
    return pl.pallas_call(
        lambda *refs: project_kernel(*refs, count=count, parts=parts, first=acc is None),
        out_shape=jax.ShapeDtypeStruct((rows, width), F32),
        grid_spec=pltpu.PrefetchScalarGridSpec(
            num_scalar_prefetch=1,
            grid=(),
            in_specs=[HB] * (len(xs) + 3 + len(more)),
            out_specs=VM,
            scratch_shapes=stages_of(weights, count, feats)
            + [pltpu.VMEM((count, rows, feats), BF), pltpu.SemaphoreType.DMA((len(xs) + 1,))],
        ),
        compiler_params=params(56),
        cost_estimate=cost(6e8 * count, 4 * count),
    )(off, *xs, *weights, *more)


def project_end_kernel(
    off, xa, xb, wq, wk, wv, acc_in, cosine, sine, gain_q, gain_k,
    q_rot, q_raw, k_rot, k_raw, v_out, squares, sq, sk, sv, sems, x_s, a_s, c_s, s_s, gq_s, gk_s, isems,
):
    stages = (sq, sk, sv)
    copies = fetch(
        [
            (xa, x_s.at[pl.ds(0, SPAN), :]), (xb, x_s.at[pl.ds(SPAN, SPAN), :]), (acc_in, a_s),
            (cosine, c_s), (sine, s_s), (gain_q, gq_s), (gain_k, gk_s),
        ],
        isems,
    )
    copies += fetch_rows(off, (wq, wk, wv), stages, sems)
    for copy in copies:
        copy.wait()
    cs, sn, gain_q, gain_k = c_s[...], s_s[...], gq_s, gk_s
    raw = a_s[...] + product_of(x_s[...], stages, 0)
    k = raw[:, R : R + D]
    k_raw[...] = k
    k_rot[...] = turn(k * gain_k[...], cs, sn)
    v_out[...] = raw[:, R + D :].astype(BF)
    squares[1:2, :] = lane_sums(k * k)
    total = None
    for h in range(G):
        q = raw[:, h * D : (h + 1) * D]
        total = q * q if total is None else total + q * q
        rotated = turn(q * gain_q[:, h * D : (h + 1) * D], cs, sn)
        for i in range(2):
            q_rot[i, h * SPAN : (h + 1) * SPAN, :] = rotated[i * SPAN : (i + 1) * SPAN]
    q_raw[...] = raw[:, :R]
    squares[0:1, :] = lane_sums(total)


def project_end(off, xa, xb, weights, acc, cosine, sine, gain_q, gain_k):
    rows = acc.shape[0]
    feats = xa.shape[1]
    outs = (
        jax.ShapeDtypeStruct((2, R, D), F32),
        jax.ShapeDtypeStruct((rows, R), F32),
        jax.ShapeDtypeStruct((rows, D), F32),
        jax.ShapeDtypeStruct((rows, D), F32),
        jax.ShapeDtypeStruct((rows, D), BF),
        jax.ShapeDtypeStruct((2, rows), F32),
    )
    return pl.pallas_call(
        project_end_kernel,
        out_shape=outs,
        grid_spec=pltpu.PrefetchScalarGridSpec(
            num_scalar_prefetch=1,
            grid=(),
            in_specs=[HB] * 10,
            out_specs=(VM,) * 6,
            scratch_shapes=stages_of(weights, 1, feats)
            + [
                pltpu.VMEM((rows, feats), BF),
                pltpu.VMEM(acc.shape, F32),
                pltpu.VMEM(cosine.shape, F32),
                pltpu.VMEM(sine.shape, F32),
                pltpu.VMEM(gain_q.shape, F32),
                pltpu.VMEM(gain_k.shape, F32),
                pltpu.SemaphoreType.DMA((7,)),
            ],
        ),
        compiler_params=params(56),
        cost_estimate=cost(6e8, 6),
    )(off, xa, xb, *weights, acc, cosine, sine, gain_q, gain_k)


def join_kernel(*refs):
    at = 0
    for ref in refs[:-1]:
        n = ref.shape[0]
        refs[-1][at : at + n, :] = ref[...]
        at += n


def join(*xs):
    rows = sum(x.shape[0] for x in xs)
    return pl.pallas_call(
        join_kernel,
        out_shape=jax.ShapeDtypeStruct((rows,) + xs[0].shape[1:], xs[0].dtype),
        in_specs=[VM] * len(xs),
        out_specs=VM,
        compiler_params=params(8),
        cost_estimate=cost(0, 1),
    )(*xs)


def spans_at(ref, loc, which, j):
    return jnp.concatenate(
        [
            ref[pl.ds(pl.multiple_of(loc[which, CH * j + t] * SPAN, SPAN), SPAN), :]
            for t in range(CH)
        ],
        axis=0,
    )


def load_pieces(refs, whole, core, sems):
    count = len(refs) // 2
    copies = []
    for n, src in enumerate(refs):
        rows = src.shape[0]
        to = core if n < count else 1 - core
        copy = pltpu.make_async_copy(
            src, whole.at[to, pl.ds((n % count) * rows, rows), :], sems.at[n]
        )
        copy.start()
        copies.append(copy)
    for copy in copies:
        copy.wait()


def fwd_kernel(loc, own, q_in, *refs):
    kv_refs, (w_ref, g_ref), (lse_ref, o_ref, kv_out, outa, outb, do_ref) = (
        refs[:PIECES], refs[PIECES : PIECES + 2], refs[PIECES + 2 : PIECES + 8],
    )
    kv, w_s, g_s, y_s, m_s, acc_s, q_ref, sems, wsems, gsems, kvsem, ysems, qsem = refs[PIECES + 8 :]
    q_copies = fetch([(q_in, q_ref)], qsem)
    load_pieces(kv_refs, kv, own[2], sems)
    keep = fetch([(kv, kv_out)], kvsem)
    block = y_s.shape[2]
    w_copies = fetch(
        [(w_ref.at[:, pl.ds(b * block, block)], w_s.at[b]) for b in range(4)], wsems
    )
    g_copies = fetch(
        [(g_ref.at[:, pl.ds(b * block, block)], g_s.at[b]) for b in range(4)], gsems
    )
    for copy in q_copies:
        copy.wait()
    k_ref, v_ref = kv.at[0], kv.at[1]
    ones = (lax.broadcasted_iota(jnp.int32, (KC, D), 1) == 0).astype(BF)
    for i in range(2):
        c = own[i]
        m_s[...] = jnp.full_like(m_s, NEG)
        acc_s[...] = jnp.zeros_like(acc_s)

        def step(j, masked):
            kk = spans_at(k_ref, loc, 0, j)
            vv = jnp.concatenate([spans_at(v_ref, loc, 1, j), ones], axis=1)
            for h in range(G):
                at = slice(h * SPAN, (h + 1) * SPAN)
                s = nt(q_ref[i, at, :], kk)
                if masked:
                    key = j * KC + lax.broadcasted_iota(jnp.int32, (SPAN, KC), 1)
                    row = c * SPAN + lax.broadcasted_iota(jnp.int32, (SPAN, KC), 0)
                    s = jnp.where(key <= row, s, NEG)
                m = m_s[at, :]
                new = jnp.maximum(m, jnp.max(s, axis=1, keepdims=True))
                shrink = jnp.exp2((m - new) * (SCALE * LOG2E))
                p = jnp.exp2((s - new[:, :1]) * (SCALE * LOG2E))
                m_s[at, :] = new
                acc_s[at, :] = acc_s[at, :] * shrink[:, :1] + nn(p.astype(BF), vv)

        last = c // CH

        def body(j, _):
            step(j, False)
            return 0

        lax.fori_loop(0, last, body, 0)
        step(last, True)
        total = acc_s[:, D : D + 1]
        o_ref[i] = (acc_s[:, :D] / total).astype(BF)
        lse = m_s[...] * (SCALE * LOG2E) + jnp.log2(jnp.broadcast_to(total, (R, D)))
        lse_ref[i] = lse.T[0:1, :]
    x = jnp.concatenate(
        [
            jnp.concatenate(
                [o_ref[i, h * SPAN : (h + 1) * SPAN, :] for h in range(G)], axis=1
            )
            for i in range(2)
        ],
        axis=0,
    )
    y_copies = []
    for b in range(4):
        w_copies[b].wait()
        y_s[b] = nn(x, w_s[b]).astype(BF)
        for i, out in enumerate((outa, outb)):
            copy = pltpu.make_async_copy(
                y_s.at[b, pl.ds(i * SPAN, SPAN), :], out.at[b], ysems.at[2 * b + i]
            )
            copy.start()
            y_copies.append(copy)
    grad = None
    for b in range(4):
        g_copies[b].wait()
        part = nt(g_s[b], w_s[b])
        grad = part if grad is None else grad + part
    for i in range(2):
        for h in range(G):
            do_ref[i, h * SPAN : (h + 1) * SPAN, :] = grad[
                i * SPAN : (i + 1) * SPAN, h * D : (h + 1) * D
            ].astype(BF)
    for copy in keep + y_copies:
        copy.wait()


def attn_fwd(table, own, q, pieces, w_out, grad_part):
    n = sum(x.shape[0] for x in pieces) // 2
    block = w_out.shape[1] // 4
    return pl.pallas_call(
        fwd_kernel,
        out_shape=(
            jax.ShapeDtypeStruct((2, 1, R), F32),
            jax.ShapeDtypeStruct((2, R, D), BF),
            jax.ShapeDtypeStruct((2, n, D), BF),
            jax.ShapeDtypeStruct((4, SPAN, block), BF),
            jax.ShapeDtypeStruct((4, SPAN, block), BF),
            jax.ShapeDtypeStruct((2, R, D), BF),
        ),
        grid_spec=pltpu.PrefetchScalarGridSpec(
            num_scalar_prefetch=2,
            grid=(),
            in_specs=[HB] * (PIECES + 3),
            out_specs=(VM, VM, FAR, FAR, FAR, VM),
            scratch_shapes=[
                pltpu.VMEM((2, n, D), BF),
                pltpu.VMEM((4, R, block), BF),
                pltpu.VMEM((4, 2 * SPAN, block), BF),
                pltpu.VMEM((4, 2 * SPAN, block), BF),
                pltpu.VMEM((R, D), F32),
                pltpu.VMEM((R, 2 * D), F32),
                pltpu.VMEM((2, R, D), BF),
                pltpu.SemaphoreType.DMA((PIECES,)),
                pltpu.SemaphoreType.DMA((4,)),
                pltpu.SemaphoreType.DMA((4,)),
                pltpu.SemaphoreType.DMA((1,)),
                pltpu.SemaphoreType.DMA((8,)),
                pltpu.SemaphoreType.DMA((1,)),
            ],
        ),
        compiler_params=params(56),
        cost_estimate=cost(1.8e10, 12, 6e6),
    )(table, own, q, *pieces, w_out, grad_part)


def bwd_kernel(
    loc, own, *refs,
):
    ins, (up_ref, mix_ref, gain_ref, mine_ref, theirs_ref) = refs[:9], refs[9:14]
    stages, (dkv, dqa, sems) = refs[14:23], refs[23:]
    q_ref, kv, do_ref, o_ref, lse_ref, cosine, sine, gain_q, unit_ref = stages
    core = own[2]
    copies = fetch(list(zip(ins, stages)), sems)
    late = copies[5:]
    copies = copies[:5]
    k_ref, v_ref = kv.at[0], kv.at[1]
    dkv[...] = jnp.zeros_like(dkv)
    dqa[...] = jnp.zeros_like(dqa)
    for copy in copies:
        copy.wait()
    for i in range(2):
        c = own[i]
        q, do, lse = q_ref[i], do_ref[i], lse_ref[i]
        delta = lane_sums(do.astype(F32) * o_ref[i].astype(F32))

        def step(j, masked):
            kk = spans_at(k_ref, loc, 0, j)
            vv = spans_at(v_ref, loc, 1, j)
            p = jnp.exp2(nt(kk, q) * (SCALE * LOG2E) - lse)
            if masked:
                key = j * KC + lax.broadcasted_iota(jnp.int32, (KC, R), 0)
                row = c * SPAN + lax.rem(lax.broadcasted_iota(jnp.int32, (KC, R), 1), SPAN)
                p = jnp.where(key <= row, p, 0.0)
            ds = (p * (nt(vv, do) - delta)).astype(BF)
            dqa[i] += tn(kk, ds)
            dv = nn(p.astype(BF), do)
            dk = nn(ds, q) * SCALE
            for t in range(CH):
                part = slice(t * SPAN, (t + 1) * SPAN)
                at = pl.ds(pl.multiple_of(loc[2, CH * j + t] * SPAN, SPAN), SPAN)
                dkv[0, at, :] += dk[part]
                at = pl.ds(pl.multiple_of(loc[3, CH * j + t] * SPAN, SPAN), SPAN)
                dkv[1, at, :] += dv[part]

        last = c // CH

        def body(j, _):
            step(j, False)
            return 0

        lax.fori_loop(0, last, body, 0)
        step(last, True)
    for copy in late:
        copy.wait()
    mine_ref[...] = dkv[core].astype(BF)
    theirs_ref[...] = dkv[1 - core].astype(BF)
    for i in range(2):
        rows = slice(i * SPAN, (i + 1) * SPAN)
        cs, sn = cosine[rows, :], -sine[rows, :]
        mix = None
        for h in range(G):
            cols = slice(h * D, (h + 1) * D)
            grad = turn((dqa[i, :, cols] * SCALE).T, cs, sn)
            unit = unit_ref[rows, cols]
            up = grad * gain_q[:, cols]
            up_ref[rows, cols] = up
            mix = up * unit if mix is None else mix + up * unit
            gain = jnp.sum(grad * unit, axis=0, keepdims=True)
            if i == 0:
                gain_ref[:, cols] = gain
            else:
                gain_ref[:, cols] += gain
        mix_ref[:, rows] = lane_sums(mix)


def attn_bwd(table, own, q, kv, do, o, lse, cosine, sine, gain_q, unit):
    n = kv.shape[1]
    rows = 2 * SPAN
    return pl.pallas_call(
        bwd_kernel,
        out_shape=(
            jax.ShapeDtypeStruct((rows, R), F32),
            jax.ShapeDtypeStruct((1, rows), F32),
            jax.ShapeDtypeStruct((1, R), F32),
            jax.ShapeDtypeStruct((n, D), BF),
            jax.ShapeDtypeStruct((n, D), BF),
        ),
        grid_spec=pltpu.PrefetchScalarGridSpec(
            num_scalar_prefetch=2,
            grid=(),
            in_specs=[HB] * 9,
            out_specs=(VM,) * 5,
            scratch_shapes=[
                pltpu.VMEM(x.shape, x.dtype)
                for x in (q, kv, do, o, lse, cosine, sine, gain_q, unit)
            ]
            + [
                pltpu.VMEM((2, n, D), F32),
                pltpu.VMEM((2, D, R), F32),
                pltpu.SemaphoreType.DMA((9,)),
            ],
        ),
        compiler_params=params(56),
        cost_estimate=cost(2.2e10, 12, 6e6),
    )(table, own, q, kv, do, o, lse, cosine, sine, gain_q, unit)


def key_gain_kernel(
    loc, own, kv_in, mine_in, theirs_in, cos_r, sin_r, cos_s, sin_s, out, k_s, g_s, sems
):
    core = own[2]
    key_copy = pltpu.make_async_copy(kv_in.at[0], k_s, sems.at[0])
    key_copy.start()

    @pl.when(core == 0)
    def _():
        pltpu.make_async_copy(mine_in, g_s, sems.at[1]).start()

    @pl.when(core != 0)
    def _():
        pltpu.make_async_copy(theirs_in, g_s, sems.at[1]).start()

    key_copy.wait()
    pltpu.make_async_copy(mine_in, g_s, sems.at[1]).wait()
    cr, sr = cos_r[...], sin_r[...]

    def body(s, sums):
        plain, by_cos, by_sin = sums
        k = k_s[pl.ds(pl.multiple_of(loc[0, s] * SPAN, SPAN), SPAN), :].astype(F32)
        g = g_s[pl.ds(pl.multiple_of(loc[2, s] * SPAN, SPAN), SPAN), :].astype(F32)
        cs, sn = cos_s[pl.ds(s, 1), :], sin_s[pl.ds(s, 1), :]
        same = k * g
        cross = g * pltpu.roll(k, D // 2, 1)
        return (
            plain + same,
            by_cos + same * (cs * cr - sn * sr),
            by_sin + cross * (sn * cr + cs * sr),
        )

    zero = jnp.zeros((SPAN, D), F32)
    plain, by_cos, by_sin = lax.fori_loop(0, loc.shape[1], body, (zero, zero, zero), unroll=4)

    def over_rows(x):
        return jnp.broadcast_to(jnp.sum(x, axis=0, keepdims=True), (8, D))

    plain, by_cos, by_sin = over_rows(plain), over_rows(by_cos), over_rows(by_sin)
    half = D // 2
    sign = jnp.where(lax.broadcasted_iota(jnp.int32, (8, D), 1) < half, 1.0, -1.0)
    total = (
        plain
        + pltpu.roll(plain, half, 1)
        + by_cos
        - pltpu.roll(by_cos, half, 1)
        + sign * (by_sin + pltpu.roll(by_sin, half, 1))
    )
    out[...] = 0.5 * total[0:1]


def key_gain_of(table, own, kv, mine, theirs, tables):
    n = kv.shape[1]
    return pl.pallas_call(
        key_gain_kernel,
        out_shape=jax.ShapeDtypeStruct((1, D), F32),
        grid_spec=pltpu.PrefetchScalarGridSpec(
            num_scalar_prefetch=2,
            grid=(),
            in_specs=[HB] * 3 + [VM] * 4,
            out_specs=VM,
            scratch_shapes=[
                pltpu.VMEM((n, D), BF),
                pltpu.VMEM((n, D), BF),
                pltpu.SemaphoreType.DMA((2,)),
            ],
        ),
        compiler_params=params(56),
        cost_estimate=cost(1e9, 6),
    )(table, own, kv, mine, theirs, *tables)


def query_kernel(*refs):
    ins, w_ref, out, stages = refs[:4], refs[4], refs[5], refs[6:10]
    w_s, y_s, sems, ysems, isems = refs[10:]
    block = w_s.shape[1]
    inputs = fetch(list(zip(ins, stages)), isems)
    up, unit, mix, inv = stages
    copies = fetch([(w_ref.at[pl.ds(b * block, block), :], w_s.at[b]) for b in range(4)], sems)
    rows = up.shape[0]

    for copy in inputs:
        copy.wait()

    def column(ref):
        return jnp.broadcast_to(ref[...], (D, rows)).T[:, :1]

    x = (column(inv) * (up[...] - unit[...] * (column(mix) * (1.0 / Q_CHANNELS)))).astype(BF)
    y_copies = []
    for b in range(4):
        copies[b].wait()
        y_s[b] = nt(x, w_s[b]).astype(BF)
        copy = pltpu.make_async_copy(y_s.at[b], out.at[b], ysems.at[b])
        copy.start()
        y_copies.append(copy)
    for copy in y_copies:
        copy.wait()


def query_partial_of(up, unit, mix, inv, w_query):
    rows = up.shape[0]
    feats = w_query.shape[0]
    block = feats // 4
    return pl.pallas_call(
        query_kernel,
        out_shape=jax.ShapeDtypeStruct((4, rows, block), BF),
        in_specs=[HB] * 5,
        out_specs=FAR,
        scratch_shapes=[pltpu.VMEM(x.shape, x.dtype) for x in (up, unit, mix, inv)]
        + [
            pltpu.VMEM((4, block, R), BF),
            pltpu.VMEM((4, rows, block), BF),
            pltpu.SemaphoreType.DMA((4,)),
            pltpu.SemaphoreType.DMA((4,)),
            pltpu.SemaphoreType.DMA((4,)),
        ],
        compiler_params=params(56),
        cost_estimate=cost(1.7e9, 9),
    )(up, unit, mix, inv, w_query)


def last_kernel(g0, g1, g2, g3, u0, u1, u2, u3, inv, w, query_side, out):
    gs, us = (g0, g1, g2, g3), (u0, u1, u2, u3)
    mix = None
    for g, u in zip(gs, us):
        part = g[:, :D].astype(F32) * u[...].astype(F32)
        mix = part if mix is None else mix + part
    mix = jnp.sum(mix, axis=1, keepdims=True) * (1.0 / K_CHANNELS)
    total = query_side[...].astype(F32)
    for n, (g, u) in enumerate(zip(gs, us)):
        raw = (inv[...] * (g[:, :D].astype(F32) - u[...].astype(F32) * mix)).astype(BF)
        total = total + nt(jnp.concatenate([raw, g[:, D:]], axis=1), w[n])
    out[...] = total.astype(BF)


def last_of(grads, units, inv, w, query_side):
    return pl.pallas_call(
        last_kernel,
        out_shape=jax.ShapeDtypeStruct(query_side.shape, BF),
        in_specs=[VM] * 11,
        out_specs=VM,
        compiler_params=params(56),
        cost_estimate=cost(7e8, 5),
    )(*grads, *units, inv, w, query_side)

QUERY_HEADS = 20
KEY_VALUE_HEADS = 4
Q_CHANNELS = QUERY_HEADS * D
K_CHANNELS = KEY_VALUE_HEADS * D
N_Y, N_Z, N_CORE, N_TP = 4, 4, 2, 4


def ctx_index(y, z, c):
    return (y * N_Z + z) * N_CORE + c


def ctx_pairs(move):
    return [
        (ctx_index(y, z, c), ctx_index(*move(y, z, c)))
        for y in range(N_Y)
        for z in range(N_Z)
        for c in range(N_CORE)
    ]


def shift_first(x, d):
    return lax.ppermute(
        x,
        "ctx",
        ctx_pairs(lambda y, z, c: ((y + c * d) % N_Y, (z + (1 - c) * d) % N_Z, c)),
    )


def shift_second(x, d):
    return lax.ppermute(
        x,
        "ctx",
        ctx_pairs(lambda y, z, c: ((y + (1 - c) * d) % N_Y, (z + c * d) % N_Z, c)),
    )


def swap_core(x):
    return lax.ppermute(x, "ctx", ctx_pairs(lambda y, z, c: (y, z, 1 - c)))


def shift_tp(x, d):
    return lax.ppermute(x, "tp", [(i, (i + d) % N_TP) for i in range(N_TP)])


def shifts(shift, x):
    return [x] + [shift(x, d) for d in DIST[1:]]


def sum_tp(x):
    x = x + lax.ppermute(x, "tp", [(i, i ^ 1) for i in range(N_TP)])
    return x + lax.ppermute(x, "tp", [(i, 3 - i) for i in range(N_TP)])


def sum_core_z(x):
    x = x + swap_core(x)
    x = x + lax.ppermute(x, "ctx", ctx_pairs(lambda y, z, c: (y, z ^ 1, c)))
    return x + lax.ppermute(x, "ctx", ctx_pairs(lambda y, z, c: (y, 3 - z, c)))


def sum_y(x):
    x = x + lax.ppermute(x, "ctx", ctx_pairs(lambda y, z, c: (y ^ 1, z, c)))
    return x + lax.ppermute(x, "ctx", ctx_pairs(lambda y, z, c: (3 - y, z, c)))


def after(x, *others):
    return lax.optimization_barrier((x,) + others)[0]


def outgoing(x):
    rows = x.shape[0] // 4
    return [x[d * rows : (d + 1) * rows].astype(BF) for d in DIST[1:]], x[:rows]


def add_up(total, arrived):
    for x in arrived:
        total = total + x.astype(F32)
    return total


def local(tokens, span_order, w_query, w_key, value_weight, w_out, gain_query, gain_key, out_grad):
    rows, feats = tokens.shape
    me = lax.axis_index("ctx")
    tp = lax.axis_index("tp")
    my_y, my_z, my_c = me // 8, (me // 2) % 4, me % 2

    mid = rows // 2
    with jax.named_scope("gather_tokens"):
        upper, lower = tokens[:mid], tokens[mid:]
        left_a = shift_tp(upper, 1)
        right_b = shift_tp(lower, 3)
        left_b = shift_tp(lower, 1)
        right_a = shift_tp(upper, 3)

    place = jnp.arange(64, dtype=jnp.int32)
    stored = jnp.sum(jnp.where(span_order[None, :] == place[:, None], place[None, :], 0), axis=1)
    src, half = stored // 2, stored % 2
    src_y, src_z, src_c = src // 8, (src // 2) % 4, src % 2
    to_y, to_z = (src_y - my_y) % 4, (src_z - my_z) % 4
    back_y, back_z = (4 - to_y) % 4, (4 - to_z) % 4
    slot_y = jnp.where(back_y >= 2, 5 - back_y, back_y)
    slot_z = jnp.where(back_z >= 2, 5 - back_z, back_z)
    table = jnp.stack(
        [
            ((slot_y * 4 + slot_z) * 2 + src_c) * 2 + half,
            ((slot_z * 4 + slot_y) * 2 + 1 - src_c) * 2 + half,
            ((to_z * 4 + to_y) * 2 + src_c) * 2 + half,
            ((to_y * 4 + to_z) * 2 + src_c) * 2 + half,
        ]
    ).astype(jnp.int32)
    own = lax.dynamic_slice_in_dim(span_order, 2 * me, 2)
    own = jnp.concatenate([own, my_c[None]]).astype(jnp.int32)

    query_pos = (own[:2, None] * SPAN + jnp.arange(SPAN)[None, :]).reshape(-1)
    frequency = jnp.exp(jnp.arange(D // 2).astype(F32) * (-2.0 * math.log(500000.0) / D))
    angles = query_pos.astype(F32)[:, None] * frequency[None, :]
    cosine, sine = jnp.cos(angles), jnp.sin(angles)
    cosine = jnp.concatenate([cosine, cosine], axis=1)
    sine = jnp.concatenate([-sine, sine], axis=1)

    offs = jnp.stack([(tp - d) % 4 for d in DIST]).astype(jnp.int32)
    twice = 2.0 * jnp.concatenate([frequency, frequency])[None, :]
    by_row = jnp.arange(SPAN).astype(F32)[:, None] * twice
    by_span = (SPAN * jnp.arange(64)).astype(F32)[:, None] * twice
    tables = (jnp.cos(by_row), jnp.sin(by_row), jnp.cos(by_span), jnp.sin(by_span))

    with jax.named_scope("gather_tokens"):
        weights = (w_query, w_key, value_weight)
        acc = project(offs[:1], ((tokens,),), weights)
        left_a, right_b, left_b, right_a, cosine, sine, offs, table, own, acc, *tables = (
            lax.optimization_barrier(
                (left_a, right_b, left_b, right_a, cosine, sine, offs, table, own, acc, *tables)
            )
        )
        far_a = shift_tp(left_a, 1)
        far_b = shift_tp(right_b, 3)
        acc = project(offs[1:3], ((left_a, left_b), (right_a, right_b)), weights, acc)
        far_a, far_b, acc = lax.optimization_barrier((far_a, far_b, acc))
    with jax.named_scope("weight_rows"):
        share = feats // 32
        cut = []
        key_rows, value_rows, _ = lax.optimization_barrier((w_key, value_weight, left_a))
        for d in DIST:
            start = feats * ((tp + d) % 4) + share * me
            piece = jnp.concatenate(
                [lax.dynamic_slice_in_dim(w, start, share, 0) for w in (key_rows, value_rows)],
                axis=1,
            )
            cut.append(shift_tp(piece, d) if d else piece)
        cut = jnp.stack(cut)

    gain_q, gain_k = gain_query[None, :], gain_key[None, :]
    q_rot, q_raw, k_rot, k_raw, value, squares = project_end(
        offs[3:], far_a, far_b, weights, acc, cosine, sine, gain_q, gain_k
    )
    with jax.named_scope("norm_sums"):
        squares = sum_tp(squares)
    query_inv = lax.rsqrt(squares[0] / Q_CHANNELS + 1e-06)[:, None]
    key_inv = lax.rsqrt(squares[1] / K_CHANNELS + 1e-06)[:, None]
    key = (k_rot * key_inv).astype(BF)

    with jax.named_scope("gather_keys_values"):
        first_core = my_c == 0
        mine = jnp.where(first_core, key, value)
        pair = join(mine, swap_core(jnp.where(first_core, value, key)))
        plane = join(*shifts(shift_first, pair))
        mine = shifts(shift_second, plane)
    with jax.named_scope("weight_rows"):
        w_rows = lax.all_gather(after(cut, pair), "ctx", axis=0, tiled=False)

    query_unit = q_raw * query_inv
    key_unit = (k_raw * key_inv).astype(BF)
    query = (
        (q_rot.reshape(2, G, SPAN, D) * query_inv.reshape(2, 1, SPAN, 1)).astype(BF).reshape(2, R, D)
    )
    with jax.named_scope("gather_key_units"):
        key_units = shifts(shift_tp, key_unit)

    with jax.named_scope("gather_out_grad"):
        grad_part = lax.all_gather(after(out_grad, far_a, far_b), "tp", axis=1, tiled=True)

    with jax.named_scope("swap_keys_values"):
        last, query, query_unit, *key_units = lax.optimization_barrier(
            (mine[3], query, query_unit, *key_units)
        )
        mine = mine[:3] + [last]
        pieces = (*mine, *(swap_core(x) for x in mine))

    log_total, heads, kv, *out_partial, head_grad = attn_fwd(
        table, own, query, pieces, w_out, grad_part
    )
    attn_out = [
        lax.psum_scatter(x, "tp", scatter_dimension=0, tiled=False) for x in out_partial
    ]

    up_query, mix_query, gain_part, mine, theirs = attn_bwd(
        table, own, query, kv, head_grad, heads, log_total,
        cosine, sine, gain_q, query_unit,
    )

    with jax.named_scope("sum_key_value_grads"):
        theirs, mix_query, attn_out[0], w_rows = lax.optimization_barrier(
            (theirs, mix_query, attn_out[0], w_rows)
        )
        mix_query = sum_tp(mix_query)
        received, mix_query = lax.optimization_barrier((swap_core(theirs), mix_query))
        summed = mine.astype(F32) + received.astype(F32)
        sent, total = outgoing(summed)
        arrived = [shift_first(x, d) for x, d in zip(sent, DIST[1:])]
        sent, total = outgoing(add_up(total, arrived))
        *sent, mine, theirs = lax.optimization_barrier((*sent, mine, theirs))
        arrived = [shift_second(x, d) for x, d in zip(sent, DIST[1:])]
        gain_key_part = key_gain_of(table, own, kv, mine, theirs, tables) / gain_k
        gains = sum_y(sum_core_z(jnp.concatenate([gain_part, gain_key_part], axis=1)))
        total = add_up(total, arrived)
        ours, its = total[:rows], total[rows:]
        kept = jnp.where(first_core, ours, its)
        swapped = swap_core(jnp.where(first_core, its, ours))
        key_grad_rot = jnp.where(first_core, kept, swapped)
        value_grad = jnp.where(first_core, swapped, kept).astype(BF)

    with jax.named_scope("query_side"):
        query_partial = query_partial_of(
            up_query, query_unit, mix_query, query_inv.reshape(1, rows), w_query
        )
        query_side = lax.psum_scatter(query_partial, "tp", scatter_dimension=0, tiled=False)

    with jax.named_scope("key_value_side"):
        first, second = key_grad_rot[:, : D // 2], key_grad_rot[:, D // 2 :]
        cs, sn = cosine[:, : D // 2], sine[:, D // 2 :]
        key_grad = jnp.concatenate([first * cs + second * sn, second * cs - first * sn], axis=1)
        w_rows = after(w_rows, query_partial).transpose(1, 0, 2, 3).reshape(4, feats, 2 * D)
        key_grad, w_rows = lax.optimization_barrier((key_grad, w_rows))
        both = jnp.concatenate([(key_grad * gain_k).astype(BF), value_grad], axis=1)
        grads = shifts(shift_tp, both)
        *grads, gains = lax.optimization_barrier((*grads, gains))
        gain_query_grad, gain_key_grad = gains[0, :R], gains[0, R:]
        input_grad = last_of(grads, key_units, key_inv, w_rows, query_side)
    attn_out = jnp.concatenate(attn_out, axis=0)
    return (attn_out, input_grad, gain_query_grad, gain_key_grad)


def solution(mesh):
    return jax.shard_map(
        local,
        mesh=mesh,
        in_specs=(
            P("ctx", "tp"),
            P(),
            P(None, "tp"),
            P(None, "tp"),
            P(None, "tp"),
            P("tp", None),
            P("tp"),
            P("tp"),
            P("ctx", "tp"),
        ),
        out_specs=(P("ctx", "tp"), P("ctx", "tp"), P("tp"), P("tp")),
        check_vma=False,
    )
```

```python
import math

import jax
import jax.numpy as jnp
from jax import lax
from jax.experimental import pallas as pl
from jax.experimental.pallas import tpu as pltpu
from jax.sharding import PartitionSpec as P

D = 128
SPAN = 128
G = 5
R = G * SPAN
CH = 8
KC = CH * SPAN
SCALE = D**-0.5
LOG2E = math.log2(math.e)
NEG = -1e30
BF = jnp.bfloat16
F32 = jnp.float32
DIST = (0, 1, 3, 2)
PIECES = 8


def nt(a, b):
    return lax.dot_general(a, b, (((1,), (1,)), ((), ())), preferred_element_type=F32)


def tn(a, b):
    return lax.dot_general(a, b, (((0,), (0,)), ((), ())), preferred_element_type=F32)


def nn(a, b):
    return lax.dot_general(a, b, (((1,), (0,)), ((), ())), preferred_element_type=F32)


VM = pl.BlockSpec(memory_space=pltpu.VMEM)
HB = pl.BlockSpec(memory_space=pl.ANY)
FAR = pl.BlockSpec(memory_space=pltpu.HBM)


def params(mib):
    return pltpu.CompilerParams(vmem_limit_bytes=mib * 2**20)


def cost(flops, mib, exps=0):
    return pl.CostEstimate(
        flops=int(flops), bytes_accessed=int(mib * 2**20), transcendentals=int(exps)
    )


def turn(x, cosine, sine):
    return x * cosine + pltpu.roll(x, D // 2, 1) * sine


def lane_sums(x):
    return jnp.sum(x.T, axis=0, keepdims=True)


def fetch(pairs, sems):
    copies = [pltpu.make_async_copy(src, dst, sems.at[n]) for n, (src, dst) in enumerate(pairs)]
    for copy in copies:
        copy.start()
    return copies


def fetch_rows(off, weights, stages, sems):
    pairs = []
    for n in range(stages[0].shape[0]):
        rows = stages[0].shape[1]
        at = pl.ds(pl.multiple_of(off[n] * rows, rows), rows)
        pairs += [(w.at[at, :], s.at[n]) for w, s in zip(weights, stages)]
    return fetch(pairs, sems)


def product_of(x, stages, n):
    return jnp.concatenate([nn(x, s[n]) for s in stages], axis=1)


def project_kernel(off, *refs, count, parts, first):
    xs, weights = refs[: count * parts], refs[count * parts : count * parts + 3]
    stages, sems, x_s, isems, out = refs[-6:-3], refs[-3], refs[-2], refs[-1], refs[-7]
    part_rows = x_s.shape[1] // parts
    inputs = fetch(
        [
            (xs[n * parts + m], x_s.at[n, pl.ds(m * part_rows, part_rows), :])
            for n in range(count)
            for m in range(parts)
        ]
        + ([] if first else [(refs[count * parts + 3], out)]),
        isems,
    )
    copies = fetch_rows(off, weights, stages, sems)
    for copy in inputs:
        copy.wait()
    total = None if first else out[...]
    for n in range(count):
        for copy in copies[3 * n : 3 * n + 3]:
            copy.wait()
        part = product_of(x_s[n], stages, n)
        total = part if total is None else total + part
    out[...] = total


def stages_of(weights, count, feats):
    return [pltpu.VMEM((count, feats, w.shape[1]), BF) for w in weights] + [
        pltpu.SemaphoreType.DMA((3 * count,))
    ]


def project(off, pieces, weights, acc=None):
    parts = len(pieces[0])
    rows, feats = sum(x.shape[0] for x in pieces[0]), pieces[0][0].shape[1]
    width = sum(w.shape[1] for w in weights)
    count = len(pieces)
    xs = [x for piece in pieces for x in piece]
    more = () if acc is None else (acc,)
    return pl.pallas_call(
        lambda *refs: project_kernel(*refs, count=count, parts=parts, first=acc is None),
        out_shape=jax.ShapeDtypeStruct((rows, width), F32),
        grid_spec=pltpu.PrefetchScalarGridSpec(
            num_scalar_prefetch=1,
            grid=(),
            in_specs=[HB] * (len(xs) + 3 + len(more)),
            out_specs=VM,
            scratch_shapes=stages_of(weights, count, feats)
            + [pltpu.VMEM((count, rows, feats), BF), pltpu.SemaphoreType.DMA((len(xs) + 1,))],
        ),
        compiler_params=params(56),
        cost_estimate=cost(6e8 * count, 4 * count),
    )(off, *xs, *weights, *more)


def project_end_kernel(
    off, xa, xb, wq, wk, wv, acc_in, cosine, sine, gain_q, gain_k,
    q_rot, q_raw, k_rot, k_raw, v_out, squares, sq, sk, sv, sems, x_s, a_s, c_s, s_s, gq_s, gk_s, isems,
):
    stages = (sq, sk, sv)
    copies = fetch(
        [
            (xa, x_s.at[pl.ds(0, SPAN), :]), (xb, x_s.at[pl.ds(SPAN, SPAN), :]), (acc_in, a_s),
            (cosine, c_s), (sine, s_s), (gain_q, gq_s), (gain_k, gk_s),
        ],
        isems,
    )
    copies += fetch_rows(off, (wq, wk, wv), stages, sems)
    for copy in copies:
        copy.wait()
    cs, sn, gain_q, gain_k = c_s[...], s_s[...], gq_s, gk_s
    raw = a_s[...] + product_of(x_s[...], stages, 0)
    k = raw[:, R : R + D]
    k_raw[...] = k
    k_rot[...] = turn(k * gain_k[...], cs, sn)
    v_out[...] = raw[:, R + D :].astype(BF)
    squares[1:2, :] = lane_sums(k * k)
    total = None
    for h in range(G):
        q = raw[:, h * D : (h + 1) * D]
        total = q * q if total is None else total + q * q
        rotated = turn(q * gain_q[:, h * D : (h + 1) * D], cs, sn)
        for i in range(2):
            q_rot[i, h * SPAN : (h + 1) * SPAN, :] = rotated[i * SPAN : (i + 1) * SPAN]
    q_raw[...] = raw[:, :R]
    squares[0:1, :] = lane_sums(total)


def project_end(off, xa, xb, weights, acc, cosine, sine, gain_q, gain_k):
    rows = acc.shape[0]
    feats = xa.shape[1]
    outs = (
        jax.ShapeDtypeStruct((2, R, D), F32),
        jax.ShapeDtypeStruct((rows, R), F32),
        jax.ShapeDtypeStruct((rows, D), F32),
        jax.ShapeDtypeStruct((rows, D), F32),
        jax.ShapeDtypeStruct((rows, D), BF),
        jax.ShapeDtypeStruct((2, rows), F32),
    )
    return pl.pallas_call(
        project_end_kernel,
        out_shape=outs,
        grid_spec=pltpu.PrefetchScalarGridSpec(
            num_scalar_prefetch=1,
            grid=(),
            in_specs=[HB] * 10,
            out_specs=(VM,) * 6,
            scratch_shapes=stages_of(weights, 1, feats)
            + [
                pltpu.VMEM((rows, feats), BF),
                pltpu.VMEM(acc.shape, F32),
                pltpu.VMEM(cosine.shape, F32),
                pltpu.VMEM(sine.shape, F32),
                pltpu.VMEM(gain_q.shape, F32),
                pltpu.VMEM(gain_k.shape, F32),
                pltpu.SemaphoreType.DMA((7,)),
            ],
        ),
        compiler_params=params(56),
        cost_estimate=cost(6e8, 6),
    )(off, xa, xb, *weights, acc, cosine, sine, gain_q, gain_k)


def join_kernel(*refs):
    at = 0
    for ref in refs[:-1]:
        n = ref.shape[0]
        refs[-1][at : at + n, :] = ref[...]
        at += n


def join(*xs):
    rows = sum(x.shape[0] for x in xs)
    return pl.pallas_call(
        join_kernel,
        out_shape=jax.ShapeDtypeStruct((rows,) + xs[0].shape[1:], xs[0].dtype),
        in_specs=[VM] * len(xs),
        out_specs=VM,
        compiler_params=params(8),
        cost_estimate=cost(0, 1),
    )(*xs)


def spans_at(ref, loc, which, j):
    return jnp.concatenate(
        [
            ref[pl.ds(pl.multiple_of(loc[which, CH * j + t] * SPAN, SPAN), SPAN), :]
            for t in range(CH)
        ],
        axis=0,
    )


def load_pieces(refs, whole, core, sems):
    count = len(refs) // 2
    copies = []
    for n, src in enumerate(refs):
        rows = src.shape[0]
        to = core if n < count else 1 - core
        copy = pltpu.make_async_copy(
            src, whole.at[to, pl.ds((n % count) * rows, rows), :], sems.at[n]
        )
        copy.start()
        copies.append(copy)
    for copy in copies:
        copy.wait()


def fwd_kernel(loc, own, q_in, *refs):
    kv_refs, (w_ref, g_ref), (lse_ref, o_ref, kv_out, outa, outb, do_ref) = (
        refs[:PIECES], refs[PIECES : PIECES + 2], refs[PIECES + 2 : PIECES + 8],
    )
    kv, w_s, g_s, y_s, m_s, acc_s, q_ref, sems, wsems, gsems, kvsem, ysems, qsem = refs[PIECES + 8 :]
    q_copies = fetch([(q_in, q_ref)], qsem)
    load_pieces(kv_refs, kv, own[2], sems)
    keep = fetch([(kv, kv_out)], kvsem)
    block = y_s.shape[2]
    w_copies = fetch(
        [(w_ref.at[:, pl.ds(b * block, block)], w_s.at[b]) for b in range(4)], wsems
    )
    g_copies = fetch(
        [(g_ref.at[:, pl.ds(b * block, block)], g_s.at[b]) for b in range(4)], gsems
    )
    for copy in q_copies:
        copy.wait()
    k_ref, v_ref = kv.at[0], kv.at[1]
    ones = (lax.broadcasted_iota(jnp.int32, (KC, D), 1) == 0).astype(BF)
    for i in range(2):
        c = own[i]
        m_s[...] = jnp.full_like(m_s, NEG)
        acc_s[...] = jnp.zeros_like(acc_s)

        def step(j, masked):
            kk = spans_at(k_ref, loc, 0, j)
            vv = jnp.concatenate([spans_at(v_ref, loc, 1, j), ones], axis=1)
            for h in range(G):
                at = slice(h * SPAN, (h + 1) * SPAN)
                s = nt(q_ref[i, at, :], kk)
                if masked:
                    key = j * KC + lax.broadcasted_iota(jnp.int32, (SPAN, KC), 1)
                    row = c * SPAN + lax.broadcasted_iota(jnp.int32, (SPAN, KC), 0)
                    s = jnp.where(key <= row, s, NEG)
                m = m_s[at, :]
                new = jnp.maximum(m, jnp.max(s, axis=1, keepdims=True))
                shrink = jnp.exp2((m - new) * (SCALE * LOG2E))
                p = jnp.exp2((s - new[:, :1]) * (SCALE * LOG2E))
                m_s[at, :] = new
                acc_s[at, :] = acc_s[at, :] * shrink[:, :1] + nn(p.astype(BF), vv)

        last = c // CH

        def body(j, _):
            step(j, False)
            return 0

        lax.fori_loop(0, last, body, 0)
        step(last, True)
        total = acc_s[:, D : D + 1]
        o_ref[i] = (acc_s[:, :D] / total).astype(BF)
        lse = m_s[...] * (SCALE * LOG2E) + jnp.log2(jnp.broadcast_to(total, (R, D)))
        lse_ref[i] = lse.T[0:1, :]
    x = jnp.concatenate(
        [
            jnp.concatenate(
                [o_ref[i, h * SPAN : (h + 1) * SPAN, :] for h in range(G)], axis=1
            )
            for i in range(2)
        ],
        axis=0,
    )
    y_copies = []
    for b in range(4):
        w_copies[b].wait()
        y_s[b] = nn(x, w_s[b]).astype(BF)
        for i, out in enumerate((outa, outb)):
            copy = pltpu.make_async_copy(
                y_s.at[b, pl.ds(i * SPAN, SPAN), :], out.at[b], ysems.at[2 * b + i]
            )
            copy.start()
            y_copies.append(copy)
    grad = None
    for b in range(4):
        g_copies[b].wait()
        part = nt(g_s[b], w_s[b])
        grad = part if grad is None else grad + part
    for i in range(2):
        for h in range(G):
            do_ref[i, h * SPAN : (h + 1) * SPAN, :] = grad[
                i * SPAN : (i + 1) * SPAN, h * D : (h + 1) * D
            ].astype(BF)
    for copy in keep + y_copies:
        copy.wait()


def attn_fwd(table, own, q, pieces, w_out, grad_part):
    n = sum(x.shape[0] for x in pieces) // 2
    block = w_out.shape[1] // 4
    return pl.pallas_call(
        fwd_kernel,
        out_shape=(
            jax.ShapeDtypeStruct((2, 1, R), F32),
            jax.ShapeDtypeStruct((2, R, D), BF),
            jax.ShapeDtypeStruct((2, n, D), BF),
            jax.ShapeDtypeStruct((4, SPAN, block), BF),
            jax.ShapeDtypeStruct((4, SPAN, block), BF),
            jax.ShapeDtypeStruct((2, R, D), BF),
        ),
        grid_spec=pltpu.PrefetchScalarGridSpec(
            num_scalar_prefetch=2,
            grid=(),
            in_specs=[HB] * (PIECES + 3),
            out_specs=(VM, VM, FAR, FAR, FAR, VM),
            scratch_shapes=[
                pltpu.VMEM((2, n, D), BF),
                pltpu.VMEM((4, R, block), BF),
                pltpu.VMEM((4, 2 * SPAN, block), BF),
                pltpu.VMEM((4, 2 * SPAN, block), BF),
                pltpu.VMEM((R, D), F32),
                pltpu.VMEM((R, 2 * D), F32),
                pltpu.VMEM((2, R, D), BF),
                pltpu.SemaphoreType.DMA((PIECES,)),
                pltpu.SemaphoreType.DMA((4,)),
                pltpu.SemaphoreType.DMA((4,)),
                pltpu.SemaphoreType.DMA((1,)),
                pltpu.SemaphoreType.DMA((8,)),
                pltpu.SemaphoreType.DMA((1,)),
            ],
        ),
        compiler_params=params(56),
        cost_estimate=cost(1.8e10, 12, 6e6),
    )(table, own, q, *pieces, w_out, grad_part)


def bwd_kernel(
    loc, own, *refs,
):
    ins, (up_ref, mix_ref, gain_ref, mine_ref, theirs_ref) = refs[:9], refs[9:14]
    stages, (dkv, dqa, sems) = refs[14:23], refs[23:]
    q_ref, kv, do_ref, o_ref, lse_ref, cosine, sine, gain_q, unit_ref = stages
    core = own[2]
    copies = fetch(list(zip(ins, stages)), sems)
    late = copies[5:]
    copies = copies[:5]
    k_ref, v_ref = kv.at[0], kv.at[1]
    dkv[...] = jnp.zeros_like(dkv)
    dqa[...] = jnp.zeros_like(dqa)
    for copy in copies:
        copy.wait()
    for i in range(2):
        c = own[i]
        q, do, lse = q_ref[i], do_ref[i], lse_ref[i]
        delta = lane_sums(do.astype(F32) * o_ref[i].astype(F32))

        def step(j, masked):
            kk = spans_at(k_ref, loc, 0, j)
            vv = spans_at(v_ref, loc, 1, j)
            p = jnp.exp2(nt(kk, q) * (SCALE * LOG2E) - lse)
            if masked:
                key = j * KC + lax.broadcasted_iota(jnp.int32, (KC, R), 0)
                row = c * SPAN + lax.rem(lax.broadcasted_iota(jnp.int32, (KC, R), 1), SPAN)
                p = jnp.where(key <= row, p, 0.0)
            ds = (p * (nt(vv, do) - delta)).astype(BF)
            dqa[i] += tn(kk, ds)
            dv = nn(p.astype(BF), do)
            dk = nn(ds, q) * SCALE
            for t in range(CH):
                part = slice(t * SPAN, (t + 1) * SPAN)
                at = pl.ds(pl.multiple_of(loc[2, CH * j + t] * SPAN, SPAN), SPAN)
                dkv[0, at, :] += dk[part]
                at = pl.ds(pl.multiple_of(loc[3, CH * j + t] * SPAN, SPAN), SPAN)
                dkv[1, at, :] += dv[part]

        last = c // CH

        def body(j, _):
            step(j, False)
            return 0

        lax.fori_loop(0, last, body, 0)
        step(last, True)
    for copy in late:
        copy.wait()
    mine_ref[...] = dkv[core].astype(BF)
    theirs_ref[...] = dkv[1 - core].astype(BF)
    for i in range(2):
        rows = slice(i * SPAN, (i + 1) * SPAN)
        cs, sn = cosine[rows, :], -sine[rows, :]
        mix = None
        for h in range(G):
            cols = slice(h * D, (h + 1) * D)
            grad = turn((dqa[i, :, cols] * SCALE).T, cs, sn)
            unit = unit_ref[rows, cols]
            up = grad * gain_q[:, cols]
            up_ref[rows, cols] = up
            mix = up * unit if mix is None else mix + up * unit
            gain = jnp.sum(grad * unit, axis=0, keepdims=True)
            if i == 0:
                gain_ref[:, cols] = gain
            else:
                gain_ref[:, cols] += gain
        mix_ref[:, rows] = lane_sums(mix)


def attn_bwd(table, own, q, kv, do, o, lse, cosine, sine, gain_q, unit):
    n = kv.shape[1]
    rows = 2 * SPAN
    return pl.pallas_call(
        bwd_kernel,
        out_shape=(
            jax.ShapeDtypeStruct((rows, R), F32),
            jax.ShapeDtypeStruct((1, rows), F32),
            jax.ShapeDtypeStruct((1, R), F32),
            jax.ShapeDtypeStruct((n, D), BF),
            jax.ShapeDtypeStruct((n, D), BF),
        ),
        grid_spec=pltpu.PrefetchScalarGridSpec(
            num_scalar_prefetch=2,
            grid=(),
            in_specs=[HB] * 9,
            out_specs=(VM,) * 5,
            scratch_shapes=[
                pltpu.VMEM(x.shape, x.dtype)
                for x in (q, kv, do, o, lse, cosine, sine, gain_q, unit)
            ]
            + [
                pltpu.VMEM((2, n, D), F32),
                pltpu.VMEM((2, D, R), F32),
                pltpu.SemaphoreType.DMA((9,)),
            ],
        ),
        compiler_params=params(56),
        cost_estimate=cost(2.2e10, 12, 6e6),
    )(table, own, q, kv, do, o, lse, cosine, sine, gain_q, unit)


def key_gain_kernel(
    loc, own, kv_in, mine_in, theirs_in, cos_r, sin_r, cos_s, sin_s, out, k_s, g_s, sems
):
    core = own[2]
    key_copy = pltpu.make_async_copy(kv_in.at[0], k_s, sems.at[0])
    key_copy.start()

    @pl.when(core == 0)
    def _():
        pltpu.make_async_copy(mine_in, g_s, sems.at[1]).start()

    @pl.when(core != 0)
    def _():
        pltpu.make_async_copy(theirs_in, g_s, sems.at[1]).start()

    key_copy.wait()
    pltpu.make_async_copy(mine_in, g_s, sems.at[1]).wait()
    cr, sr = cos_r[...], sin_r[...]

    def body(s, sums):
        plain, by_cos, by_sin = sums
        k = k_s[pl.ds(pl.multiple_of(loc[0, s] * SPAN, SPAN), SPAN), :].astype(F32)
        g = g_s[pl.ds(pl.multiple_of(loc[2, s] * SPAN, SPAN), SPAN), :].astype(F32)
        cs, sn = cos_s[pl.ds(s, 1), :], sin_s[pl.ds(s, 1), :]
        same = k * g
        cross = g * pltpu.roll(k, D // 2, 1)
        return (
            plain + same,
            by_cos + same * (cs * cr - sn * sr),
            by_sin + cross * (sn * cr + cs * sr),
        )

    zero = jnp.zeros((SPAN, D), F32)
    plain, by_cos, by_sin = lax.fori_loop(0, loc.shape[1], body, (zero, zero, zero), unroll=4)

    def over_rows(x):
        return jnp.broadcast_to(jnp.sum(x, axis=0, keepdims=True), (8, D))

    plain, by_cos, by_sin = over_rows(plain), over_rows(by_cos), over_rows(by_sin)
    half = D // 2
    sign = jnp.where(lax.broadcasted_iota(jnp.int32, (8, D), 1) < half, 1.0, -1.0)
    total = (
        plain
        + pltpu.roll(plain, half, 1)
        + by_cos
        - pltpu.roll(by_cos, half, 1)
        + sign * (by_sin + pltpu.roll(by_sin, half, 1))
    )
    out[...] = 0.5 * total[0:1]


def key_gain_of(table, own, kv, mine, theirs, tables):
    n = kv.shape[1]
    return pl.pallas_call(
        key_gain_kernel,
        out_shape=jax.ShapeDtypeStruct((1, D), F32),
        grid_spec=pltpu.PrefetchScalarGridSpec(
            num_scalar_prefetch=2,
            grid=(),
            in_specs=[HB] * 3 + [VM] * 4,
            out_specs=VM,
            scratch_shapes=[
                pltpu.VMEM((n, D), BF),
                pltpu.VMEM((n, D), BF),
                pltpu.SemaphoreType.DMA((2,)),
            ],
        ),
        compiler_params=params(56),
        cost_estimate=cost(1e9, 6),
    )(table, own, kv, mine, theirs, *tables)


def query_kernel(*refs):
    ins, w_ref, out, stages = refs[:4], refs[4], refs[5], refs[6:10]
    w_s, y_s, sems, ysems, isems = refs[10:]
    block = w_s.shape[1]
    inputs = fetch(list(zip(ins, stages)), isems)
    up, unit, mix, inv = stages
    copies = fetch([(w_ref.at[pl.ds(b * block, block), :], w_s.at[b]) for b in range(4)], sems)
    rows = up.shape[0]

    for copy in inputs:
        copy.wait()

    def column(ref):
        return jnp.broadcast_to(ref[...], (D, rows)).T[:, :1]

    x = (column(inv) * (up[...] - unit[...] * (column(mix) * (1.0 / Q_CHANNELS)))).astype(BF)
    y_copies = []
    for b in range(4):
        copies[b].wait()
        y_s[b] = nt(x, w_s[b]).astype(BF)
        copy = pltpu.make_async_copy(y_s.at[b], out.at[b], ysems.at[b])
        copy.start()
        y_copies.append(copy)
    for copy in y_copies:
        copy.wait()


def query_partial_of(up, unit, mix, inv, w_query):
    rows = up.shape[0]
    feats = w_query.shape[0]
    block = feats // 4
    return pl.pallas_call(
        query_kernel,
        out_shape=jax.ShapeDtypeStruct((4, rows, block), BF),
        in_specs=[HB] * 5,
        out_specs=FAR,
        scratch_shapes=[pltpu.VMEM(x.shape, x.dtype) for x in (up, unit, mix, inv)]
        + [
            pltpu.VMEM((4, block, R), BF),
            pltpu.VMEM((4, rows, block), BF),
            pltpu.SemaphoreType.DMA((4,)),
            pltpu.SemaphoreType.DMA((4,)),
            pltpu.SemaphoreType.DMA((4,)),
        ],
        compiler_params=params(56),
        cost_estimate=cost(1.7e9, 9),
    )(up, unit, mix, inv, w_query)


def last_kernel(g0, g1, g2, g3, u0, u1, u2, u3, inv, w, query_side, out):
    gs, us = (g0, g1, g2, g3), (u0, u1, u2, u3)
    mix = None
    for g, u in zip(gs, us):
        part = g[:, :D].astype(F32) * u[...].astype(F32)
        mix = part if mix is None else mix + part
    mix = jnp.sum(mix, axis=1, keepdims=True) * (1.0 / K_CHANNELS)
    total = query_side[...].astype(F32)
    for n, (g, u) in enumerate(zip(gs, us)):
        raw = (inv[...] * (g[:, :D].astype(F32) - u[...].astype(F32) * mix)).astype(BF)
        total = total + nt(jnp.concatenate([raw, g[:, D:]], axis=1), w[n])
    out[...] = total.astype(BF)


def last_of(grads, units, inv, w, query_side):
    return pl.pallas_call(
        last_kernel,
        out_shape=jax.ShapeDtypeStruct(query_side.shape, BF),
        in_specs=[VM] * 11,
        out_specs=VM,
        compiler_params=params(56),
        cost_estimate=cost(7e8, 5),
    )(*grads, *units, inv, w, query_side)

QUERY_HEADS = 20
KEY_VALUE_HEADS = 4
Q_CHANNELS = QUERY_HEADS * D
K_CHANNELS = KEY_VALUE_HEADS * D
N_Y, N_Z, N_CORE, N_TP = 4, 4, 2, 4


def ctx_index(y, z, c):
    return (y * N_Z + z) * N_CORE + c


def ctx_pairs(move):
    return [
        (ctx_index(y, z, c), ctx_index(*move(y, z, c)))
        for y in range(N_Y)
        for z in range(N_Z)
        for c in range(N_CORE)
    ]


def shift_first(x, d):
    return lax.ppermute(
        x,
        "ctx",
        ctx_pairs(lambda y, z, c: ((y + c * d) % N_Y, (z + (1 - c) * d) % N_Z, c)),
    )


def shift_second(x, d):
    return lax.ppermute(
        x,
        "ctx",
        ctx_pairs(lambda y, z, c: ((y + (1 - c) * d) % N_Y, (z + c * d) % N_Z, c)),
    )


def swap_core(x):
    return lax.ppermute(x, "ctx", ctx_pairs(lambda y, z, c: (y, z, 1 - c)))


def shift_tp(x, d):
    return lax.ppermute(x, "tp", [(i, (i + d) % N_TP) for i in range(N_TP)])


def shifts(shift, x):
    return [x] + [shift(x, d) for d in DIST[1:]]


def sum_tp(x):
    one, three, two = (shift_tp(x, d) for d in DIST[1:])
    return (x + one) + (three + two)


def sum_core_z(x):
    x = x + swap_core(x)
    x = x + lax.ppermute(x, "ctx", ctx_pairs(lambda y, z, c: (y, z ^ 1, c)))
    return x + lax.ppermute(x, "ctx", ctx_pairs(lambda y, z, c: (y, 3 - z, c)))


def sum_y(x):
    x = x + lax.ppermute(x, "ctx", ctx_pairs(lambda y, z, c: (y ^ 1, z, c)))
    return x + lax.ppermute(x, "ctx", ctx_pairs(lambda y, z, c: (3 - y, z, c)))


def after(x, *others):
    return lax.optimization_barrier((x,) + others)[0]


def outgoing(x):
    rows = x.shape[0] // 4
    return [x[d * rows : (d + 1) * rows].astype(BF) for d in DIST[1:]], x[:rows]


def add_up(total, arrived):
    for x in arrived:
        total = total + x.astype(F32)
    return total


def local(tokens, span_order, w_query, w_key, value_weight, w_out, gain_query, gain_key, out_grad):
    rows, feats = tokens.shape
    me = lax.axis_index("ctx")
    tp = lax.axis_index("tp")
    my_y, my_z, my_c = me // 8, (me // 2) % 4, me % 2

    mid = rows // 2
    with jax.named_scope("gather_tokens"):
        upper, lower = tokens[:mid], tokens[mid:]
        left_a = shift_tp(upper, 1)
        right_b = shift_tp(lower, 3)
        left_b = shift_tp(lower, 1)
        right_a = shift_tp(upper, 3)

    place = jnp.arange(64, dtype=jnp.int32)
    stored = jnp.sum(jnp.where(span_order[None, :] == place[:, None], place[None, :], 0), axis=1)
    src, half = stored // 2, stored % 2
    src_y, src_z, src_c = src // 8, (src // 2) % 4, src % 2
    to_y, to_z = (src_y - my_y) % 4, (src_z - my_z) % 4
    back_y, back_z = (4 - to_y) % 4, (4 - to_z) % 4
    slot_y = jnp.where(back_y >= 2, 5 - back_y, back_y)
    slot_z = jnp.where(back_z >= 2, 5 - back_z, back_z)
    table = jnp.stack(
        [
            ((slot_y * 4 + slot_z) * 2 + src_c) * 2 + half,
            ((slot_z * 4 + slot_y) * 2 + 1 - src_c) * 2 + half,
            ((to_z * 4 + to_y) * 2 + src_c) * 2 + half,
            ((to_y * 4 + to_z) * 2 + src_c) * 2 + half,
        ]
    ).astype(jnp.int32)
    own = lax.dynamic_slice_in_dim(span_order, 2 * me, 2)
    own = jnp.concatenate([own, my_c[None]]).astype(jnp.int32)

    query_pos = (own[:2, None] * SPAN + jnp.arange(SPAN)[None, :]).reshape(-1)
    frequency = jnp.exp(jnp.arange(D // 2).astype(F32) * (-2.0 * math.log(500000.0) / D))
    angles = query_pos.astype(F32)[:, None] * frequency[None, :]
    cosine, sine = jnp.cos(angles), jnp.sin(angles)
    cosine = jnp.concatenate([cosine, cosine], axis=1)
    sine = jnp.concatenate([-sine, sine], axis=1)

    offs = jnp.stack([(tp - d) % 4 for d in DIST]).astype(jnp.int32)
    twice = 2.0 * jnp.concatenate([frequency, frequency])[None, :]
    by_row = jnp.arange(SPAN).astype(F32)[:, None] * twice
    by_span = (SPAN * jnp.arange(64)).astype(F32)[:, None] * twice
    tables = (jnp.cos(by_row), jnp.sin(by_row), jnp.cos(by_span), jnp.sin(by_span))

    with jax.named_scope("weight_rows"):
        share = feats // 32
        cut = []
        key_rows, value_rows, _ = lax.optimization_barrier((w_key, value_weight, cosine))
        for d in DIST:
            start = feats * ((tp + d) % 4) + share * me
            piece = jnp.concatenate(
                [lax.dynamic_slice_in_dim(w, start, share, 0) for w in (key_rows, value_rows)],
                axis=1,
            )
            cut.append(shift_tp(piece, d) if d else piece)
        cut = jnp.stack(cut)

    with jax.named_scope("gather_tokens"):
        weights = (w_query, w_key, value_weight)
        acc = project(offs[:1], ((tokens,),), weights)
        left_a, right_b, left_b, right_a, cosine, sine, offs, table, own, cut, acc, *tables = (
            lax.optimization_barrier(
                (left_a, right_b, left_b, right_a, cosine, sine, offs, table, own, cut, acc, *tables)
            )
        )
        far_a = shift_tp(left_a, 1)
        far_b = shift_tp(right_b, 3)
        acc = project(offs[1:3], ((left_a, left_b), (right_a, right_b)), weights, acc)
        far_a, far_b, acc = lax.optimization_barrier((far_a, far_b, acc))
    gain_q, gain_k = gain_query[None, :], gain_key[None, :]
    q_rot, q_raw, k_rot, k_raw, value, squares = project_end(
        offs[3:], far_a, far_b, weights, acc, cosine, sine, gain_q, gain_k
    )
    with jax.named_scope("norm_sums"):
        squares = sum_tp(squares)
    query_inv = lax.rsqrt(squares[0] / Q_CHANNELS + 1e-06)[:, None]
    key_inv = lax.rsqrt(squares[1] / K_CHANNELS + 1e-06)[:, None]
    key = (k_rot * key_inv).astype(BF)

    with jax.named_scope("gather_keys_values"):
        first_core = my_c == 0
        mine = jnp.where(first_core, key, value)
        pair = join(mine, swap_core(jnp.where(first_core, value, key)))
        plane = join(*shifts(shift_first, pair))
        mine = shifts(shift_second, plane)
    with jax.named_scope("weight_rows"):
        w_rows = lax.all_gather(after(cut, pair), "ctx", axis=0, tiled=False)

    query_unit = q_raw * query_inv
    key_unit = (k_raw * key_inv).astype(BF)
    query = (
        (q_rot.reshape(2, G, SPAN, D) * query_inv.reshape(2, 1, SPAN, 1)).astype(BF).reshape(2, R, D)
    )
    with jax.named_scope("gather_key_units"):
        key_units = shifts(shift_tp, key_unit)

    with jax.named_scope("gather_out_grad"):
        grad_part = lax.all_gather(after(out_grad, far_a, far_b), "tp", axis=1, tiled=True)

    with jax.named_scope("swap_keys_values"):
        last, query, query_unit, *key_units = lax.optimization_barrier(
            (mine[3], query, query_unit, *key_units)
        )
        mine = mine[:3] + [last]
        pieces = (*mine, *(swap_core(x) for x in mine))

    log_total, heads, kv, *out_partial, head_grad = attn_fwd(
        table, own, query, pieces, w_out, grad_part
    )
    attn_out = [
        lax.psum_scatter(x, "tp", scatter_dimension=0, tiled=False) for x in out_partial
    ]

    up_query, mix_query, gain_part, mine, theirs = attn_bwd(
        table, own, query, kv, head_grad, heads, log_total,
        cosine, sine, gain_q, query_unit,
    )

    with jax.named_scope("sum_key_value_grads"):
        mix_query = sum_tp(mix_query)
        received, mix_query, attn_out[0], w_rows = lax.optimization_barrier(
            (swap_core(theirs), mix_query, attn_out[0], w_rows)
        )
        summed = mine.astype(F32) + received.astype(F32)
        sent, total = outgoing(summed)
        *sent, mine, theirs = lax.optimization_barrier((*sent, mine, theirs))
        arrived = [shift_first(x, d) for x, d in zip(sent, DIST[1:])]
        gain_key_part = key_gain_of(table, own, kv, mine, theirs, tables) / gain_k
        gains = jnp.concatenate([gain_part, gain_key_part], axis=1)
        *arrived, gains = lax.optimization_barrier((*arrived, gains))
        sent, total = outgoing(add_up(total, arrived))
        *sent, gains = lax.optimization_barrier((*sent, gains))
        arrived = [shift_second(x, d) for x, d in zip(sent, DIST[1:])]
        *arrived, gains = lax.optimization_barrier((*arrived, sum_core_z(gains)))
        total = add_up(total, arrived)
        ours, its = total[:rows], total[rows:]
        kept = jnp.where(first_core, ours, its)
        swapped = swap_core(jnp.where(first_core, its, ours))
        key_grad_rot = jnp.where(first_core, kept, swapped)
        value_grad = jnp.where(first_core, swapped, kept).astype(BF)

    with jax.named_scope("query_side"):
        query_partial = query_partial_of(
            up_query, query_unit, mix_query, query_inv.reshape(1, rows), w_query
        )
        query_side = lax.psum_scatter(query_partial, "tp", scatter_dimension=0, tiled=False)

    with jax.named_scope("key_value_side"):
        first, second = key_grad_rot[:, : D // 2], key_grad_rot[:, D // 2 :]
        cs, sn = cosine[:, : D // 2], sine[:, D // 2 :]
        key_grad = jnp.concatenate([first * cs + second * sn, second * cs - first * sn], axis=1)
        w_rows = after(w_rows, query_partial).transpose(1, 0, 2, 3).reshape(4, feats, 2 * D)
        key_grad, w_rows = lax.optimization_barrier((key_grad, w_rows))
        both = jnp.concatenate([(key_grad * gain_k).astype(BF), value_grad], axis=1)
        grads = shifts(shift_tp, both)
        *grads, gains = lax.optimization_barrier((*grads, sum_y(gains)))
        gain_query_grad, gain_key_grad = gains[0, :R], gains[0, R:]
        input_grad = last_of(grads, key_units, key_inv, w_rows, query_side)
    attn_out = jnp.concatenate(attn_out, axis=0)
    return (attn_out, input_grad, gain_query_grad, gain_key_grad)


def solution(mesh):
    return jax.shard_map(
        local,
        mesh=mesh,
        in_specs=(
            P("ctx", "tp"),
            P(),
            P(None, "tp"),
            P(None, "tp"),
            P(None, "tp"),
            P("tp", None),
            P("tp"),
            P("tp"),
            P("ctx", "tp"),
        ),
        out_specs=(P("ctx", "tp"), P("ctx", "tp"), P("tp"), P("tp")),
        check_vma=False,
    )
```

```python
import math

import jax
import jax.numpy as jnp
from jax import lax
from jax.experimental import pallas as pl
from jax.experimental.pallas import tpu as pltpu
from jax.sharding import PartitionSpec as P

D = 128
SPAN = 128
G = 5
R = G * SPAN
CH = 8
KC = CH * SPAN
SCALE = D**-0.5
LOG2E = math.log2(math.e)
NEG = -1e30
BF = jnp.bfloat16
F32 = jnp.float32
DIST = (0, 1, 3, 2)
PIECES = 8


def nt(a, b):
    return lax.dot_general(a, b, (((1,), (1,)), ((), ())), preferred_element_type=F32)


def tn(a, b):
    return lax.dot_general(a, b, (((0,), (0,)), ((), ())), preferred_element_type=F32)


def nn(a, b):
    return lax.dot_general(a, b, (((1,), (0,)), ((), ())), preferred_element_type=F32)


VM = pl.BlockSpec(memory_space=pltpu.VMEM)
HB = pl.BlockSpec(memory_space=pl.ANY)
FAR = pl.BlockSpec(memory_space=pltpu.HBM)


def params(mib):
    return pltpu.CompilerParams(vmem_limit_bytes=mib * 2**20)


def cost(flops, mib, exps=0):
    return pl.CostEstimate(
        flops=int(flops), bytes_accessed=int(mib * 2**20), transcendentals=int(exps)
    )


def turn(x, cosine, sine):
    return x * cosine + pltpu.roll(x, D // 2, 1) * sine


def lane_sums(x):
    return jnp.sum(x.T, axis=0, keepdims=True)


def fetch(pairs, sems):
    copies = [pltpu.make_async_copy(src, dst, sems.at[n]) for n, (src, dst) in enumerate(pairs)]
    for copy in copies:
        copy.start()
    return copies


def fetch_rows(off, weights, stages, sems):
    pairs = []
    for n in range(stages[0].shape[0]):
        rows = stages[0].shape[1]
        at = pl.ds(pl.multiple_of(off[n] * rows, rows), rows)
        pairs += [(w.at[at, :], s.at[n]) for w, s in zip(weights, stages)]
    return fetch(pairs, sems)


def product_of(x, stages, n):
    return jnp.concatenate([nn(x, s[n]) for s in stages], axis=1)


def project_kernel(off, *refs, count, parts, first):
    xs, weights = refs[: count * parts], refs[count * parts : count * parts + 3]
    stages, sems, x_s, isems, out = refs[-6:-3], refs[-3], refs[-2], refs[-1], refs[-7]
    part_rows = x_s.shape[1] // parts
    inputs = fetch(
        [
            (xs[n * parts + m], x_s.at[n, pl.ds(m * part_rows, part_rows), :])
            for n in range(count)
            for m in range(parts)
        ]
        + ([] if first else [(refs[count * parts + 3], out)]),
        isems,
    )
    copies = fetch_rows(off, weights, stages, sems)
    for copy in inputs:
        copy.wait()
    total = None if first else out[...]
    for n in range(count):
        for copy in copies[3 * n : 3 * n + 3]:
            copy.wait()
        part = product_of(x_s[n], stages, n)
        total = part if total is None else total + part
    out[...] = total


def stages_of(weights, count, feats):
    return [pltpu.VMEM((count, feats, w.shape[1]), BF) for w in weights] + [
        pltpu.SemaphoreType.DMA((3 * count,))
    ]


def project(off, pieces, weights, acc=None):
    parts = len(pieces[0])
    rows, feats = sum(x.shape[0] for x in pieces[0]), pieces[0][0].shape[1]
    width = sum(w.shape[1] for w in weights)
    count = len(pieces)
    xs = [x for piece in pieces for x in piece]
    more = () if acc is None else (acc,)
    return pl.pallas_call(
        lambda *refs: project_kernel(*refs, count=count, parts=parts, first=acc is None),
        out_shape=jax.ShapeDtypeStruct((rows, width), F32),
        grid_spec=pltpu.PrefetchScalarGridSpec(
            num_scalar_prefetch=1,
            grid=(),
            in_specs=[HB] * (len(xs) + 3 + len(more)),
            out_specs=VM,
            scratch_shapes=stages_of(weights, count, feats)
            + [pltpu.VMEM((count, rows, feats), BF), pltpu.SemaphoreType.DMA((len(xs) + 1,))],
        ),
        compiler_params=params(56),
        cost_estimate=cost(6e8 * count, 4 * count),
    )(off, *xs, *weights, *more)


def project_end_kernel(
    off, xa, xb, wq, wk, wv, acc_in, cosine, sine, gain_q, gain_k,
    q_rot, q_raw, k_rot, k_raw, v_out, squares, sq, sk, sv, sems, x_s, a_s, c_s, s_s, gq_s, gk_s, isems,
):
    stages = (sq, sk, sv)
    copies = fetch(
        [
            (xa, x_s.at[pl.ds(0, SPAN), :]), (xb, x_s.at[pl.ds(SPAN, SPAN), :]), (acc_in, a_s),
            (cosine, c_s), (sine, s_s), (gain_q, gq_s), (gain_k, gk_s),
        ],
        isems,
    )
    copies += fetch_rows(off, (wq, wk, wv), stages, sems)
    for copy in copies:
        copy.wait()
    cs, sn, gain_q, gain_k = c_s[...], s_s[...], gq_s, gk_s
    raw = a_s[...] + product_of(x_s[...], stages, 0)
    k = raw[:, R : R + D]
    k_raw[...] = k
    k_rot[...] = turn(k * gain_k[...], cs, sn)
    v_out[...] = raw[:, R + D :].astype(BF)
    squares[1:2, :] = lane_sums(k * k)
    total = None
    for h in range(G):
        q = raw[:, h * D : (h + 1) * D]
        total = q * q if total is None else total + q * q
        rotated = turn(q * gain_q[:, h * D : (h + 1) * D], cs, sn)
        for i in range(2):
            q_rot[i, h * SPAN : (h + 1) * SPAN, :] = rotated[i * SPAN : (i + 1) * SPAN]
    q_raw[...] = raw[:, :R]
    squares[0:1, :] = lane_sums(total)


def project_end(off, xa, xb, weights, acc, cosine, sine, gain_q, gain_k):
    rows = acc.shape[0]
    feats = xa.shape[1]
    outs = (
        jax.ShapeDtypeStruct((2, R, D), F32),
        jax.ShapeDtypeStruct((rows, R), F32),
        jax.ShapeDtypeStruct((rows, D), F32),
        jax.ShapeDtypeStruct((rows, D), F32),
        jax.ShapeDtypeStruct((rows, D), BF),
        jax.ShapeDtypeStruct((2, rows), F32),
    )
    return pl.pallas_call(
        project_end_kernel,
        out_shape=outs,
        grid_spec=pltpu.PrefetchScalarGridSpec(
            num_scalar_prefetch=1,
            grid=(),
            in_specs=[HB] * 10,
            out_specs=(VM,) * 6,
            scratch_shapes=stages_of(weights, 1, feats)
            + [
                pltpu.VMEM((rows, feats), BF),
                pltpu.VMEM(acc.shape, F32),
                pltpu.VMEM(cosine.shape, F32),
                pltpu.VMEM(sine.shape, F32),
                pltpu.VMEM(gain_q.shape, F32),
                pltpu.VMEM(gain_k.shape, F32),
                pltpu.SemaphoreType.DMA((7,)),
            ],
        ),
        compiler_params=params(56),
        cost_estimate=cost(6e8, 6),
    )(off, xa, xb, *weights, acc, cosine, sine, gain_q, gain_k)


def join_kernel(*refs):
    at = 0
    for ref in refs[:-1]:
        n = ref.shape[0]
        refs[-1][at : at + n, :] = ref[...]
        at += n


def join(*xs):
    rows = sum(x.shape[0] for x in xs)
    return pl.pallas_call(
        join_kernel,
        out_shape=jax.ShapeDtypeStruct((rows,) + xs[0].shape[1:], xs[0].dtype),
        in_specs=[VM] * len(xs),
        out_specs=VM,
        compiler_params=params(8),
        cost_estimate=cost(0, 1),
    )(*xs)


def spans_at(ref, loc, which, j):
    return jnp.concatenate(
        [
            ref[pl.ds(pl.multiple_of(loc[which, CH * j + t] * SPAN, SPAN), SPAN), :]
            for t in range(CH)
        ],
        axis=0,
    )


def load_pieces(refs, whole, core, sems):
    count = len(refs) // 2
    copies = []
    for n, src in enumerate(refs):
        rows = src.shape[0]
        to = core if n < count else 1 - core
        copy = pltpu.make_async_copy(
            src, whole.at[to, pl.ds((n % count) * rows, rows), :], sems.at[n]
        )
        copy.start()
        copies.append(copy)
    for copy in copies:
        copy.wait()


def fwd_kernel(loc, own, q_in, *refs):
    kv_refs, w_ref, (lse_ref, o_ref, kv_out, out) = (
        refs[:PIECES], refs[PIECES], refs[PIECES + 1 : PIECES + 5],
    )
    kv, w_s, y_s, m_s, acc_s, q_ref, sems, wsems, kvsem, ysems, qsem = refs[PIECES + 5 :]
    q_copies = fetch([(q_in, q_ref)], qsem)
    load_pieces(kv_refs, kv, own[2], sems)
    keep = fetch([(kv, kv_out)], kvsem)
    block = y_s.shape[2]
    w_copies = fetch(
        [(w_ref.at[:, pl.ds(b * block, block)], w_s.at[b]) for b in range(4)], wsems
    )
    for copy in q_copies:
        copy.wait()
    k_ref, v_ref = kv.at[0], kv.at[1]
    ones = (lax.broadcasted_iota(jnp.int32, (KC, D), 1) == 0).astype(BF)
    for i in range(2):
        c = own[i]
        m_s[...] = jnp.full_like(m_s, NEG)
        acc_s[...] = jnp.zeros_like(acc_s)

        def step(j, masked):
            kk = spans_at(k_ref, loc, 0, j)
            vv = jnp.concatenate([spans_at(v_ref, loc, 1, j), ones], axis=1)
            for h in range(G):
                at = slice(h * SPAN, (h + 1) * SPAN)
                s = nt(q_ref[i, at, :], kk)
                if masked:
                    key = j * KC + lax.broadcasted_iota(jnp.int32, (SPAN, KC), 1)
                    row = c * SPAN + lax.broadcasted_iota(jnp.int32, (SPAN, KC), 0)
                    s = jnp.where(key <= row, s, NEG)
                m = m_s[at, :]
                new = jnp.maximum(m, jnp.max(s, axis=1, keepdims=True))
                shrink = jnp.exp2((m - new) * (SCALE * LOG2E))
                p = jnp.exp2((s - new[:, :1]) * (SCALE * LOG2E))
                m_s[at, :] = new
                acc_s[at, :] = acc_s[at, :] * shrink[:, :1] + nn(p.astype(BF), vv)

        last = c // CH

        def body(j, _):
            step(j, False)
            return 0

        lax.fori_loop(0, last, body, 0)
        step(last, True)
        total = acc_s[:, D : D + 1]
        o_ref[i] = (acc_s[:, :D] / total).astype(BF)
        lse = m_s[...] * (SCALE * LOG2E) + jnp.log2(jnp.broadcast_to(total, (R, D)))
        lse_ref[i] = lse.T[0:1, :]
    x = jnp.concatenate(
        [
            jnp.concatenate(
                [o_ref[i, h * SPAN : (h + 1) * SPAN, :] for h in range(G)], axis=1
            )
            for i in range(2)
        ],
        axis=0,
    )
    y_copies = []
    for b in range(4):
        w_copies[b].wait()
        y_s[b] = nn(x, w_s[b]).astype(BF)
        copy = pltpu.make_async_copy(y_s.at[b], out.at[b], ysems.at[b])
        copy.start()
        y_copies.append(copy)
    for copy in keep + y_copies:
        copy.wait()


def attn_fwd(table, own, q, pieces, w_out):
    n = sum(x.shape[0] for x in pieces) // 2
    block = w_out.shape[1] // 4
    return pl.pallas_call(
        fwd_kernel,
        out_shape=(
            jax.ShapeDtypeStruct((2, 1, R), F32),
            jax.ShapeDtypeStruct((2, R, D), BF),
            jax.ShapeDtypeStruct((2, n, D), BF),
            jax.ShapeDtypeStruct((4, 2 * SPAN, block), BF),
        ),
        grid_spec=pltpu.PrefetchScalarGridSpec(
            num_scalar_prefetch=2,
            grid=(),
            in_specs=[HB] * (PIECES + 2),
            out_specs=(VM, VM, FAR, FAR),
            scratch_shapes=[
                pltpu.VMEM((2, n, D), BF),
                pltpu.VMEM((4, R, block), BF),
                pltpu.VMEM((4, 2 * SPAN, block), BF),
                pltpu.VMEM((R, D), F32),
                pltpu.VMEM((R, 2 * D), F32),
                pltpu.VMEM((2, R, D), BF),
                pltpu.SemaphoreType.DMA((PIECES,)),
                pltpu.SemaphoreType.DMA((4,)),
                pltpu.SemaphoreType.DMA((1,)),
                pltpu.SemaphoreType.DMA((4,)),
                pltpu.SemaphoreType.DMA((1,)),
            ],
        ),
        compiler_params=params(56),
        cost_estimate=cost(1.8e10, 12, 6e6),
    )(table, own, q, *pieces, w_out)


def bwd_kernel(
    loc, own, *refs,
):
    ins, g_ref, w_ref, (up_ref, mix_ref, gain_ref, mine_ref, theirs_ref) = (
        refs[:8], refs[8], refs[9], refs[10:15],
    )
    stages, (do_ref, g_s, w_s, dkv, dqa, gsems, sems) = refs[15:23], refs[23:]
    q_ref, kv, o_ref, lse_ref, cosine, sine, gain_q, unit_ref = stages
    core = own[2]
    block = g_s.shape[2]
    g_pairs = []
    for b in range(4):
        cols = pl.ds(b * block, block)
        g_pairs += [(w_ref.at[:, cols], w_s.at[b]), (g_ref.at[:, cols], g_s.at[b])]
    g_copies = fetch(g_pairs, gsems)
    copies = fetch(list(zip(ins, stages)), sems)
    late = copies[4:]
    copies = copies[:4]
    k_ref, v_ref = kv.at[0], kv.at[1]
    dkv[...] = jnp.zeros_like(dkv)
    dqa[...] = jnp.zeros_like(dqa)
    grad = None
    for b in range(4):
        g_copies[2 * b].wait()
        g_copies[2 * b + 1].wait()
        part = nt(g_s[b], w_s[b])
        grad = part if grad is None else grad + part
    for i in range(2):
        for h in range(G):
            do_ref[i, h * SPAN : (h + 1) * SPAN, :] = grad[
                i * SPAN : (i + 1) * SPAN, h * D : (h + 1) * D
            ].astype(BF)
    for copy in copies:
        copy.wait()
    for i in range(2):
        c = own[i]
        q, do, lse = q_ref[i], do_ref[i], lse_ref[i]
        delta = lane_sums(do.astype(F32) * o_ref[i].astype(F32))

        def step(j, masked):
            kk = spans_at(k_ref, loc, 0, j)
            vv = spans_at(v_ref, loc, 1, j)
            p = jnp.exp2(nt(kk, q) * (SCALE * LOG2E) - lse)
            if masked:
                key = j * KC + lax.broadcasted_iota(jnp.int32, (KC, R), 0)
                row = c * SPAN + lax.rem(lax.broadcasted_iota(jnp.int32, (KC, R), 1), SPAN)
                p = jnp.where(key <= row, p, 0.0)
            ds = (p * (nt(vv, do) - delta)).astype(BF)
            dqa[i] += tn(kk, ds)
            dv = nn(p.astype(BF), do)
            dk = nn(ds, q) * SCALE
            for t in range(CH):
                part = slice(t * SPAN, (t + 1) * SPAN)
                at = pl.ds(pl.multiple_of(loc[2, CH * j + t] * SPAN, SPAN), SPAN)
                dkv[0, at, :] += dk[part]
                at = pl.ds(pl.multiple_of(loc[3, CH * j + t] * SPAN, SPAN), SPAN)
                dkv[1, at, :] += dv[part]

        last = c // CH

        def body(j, _):
            step(j, False)
            return 0

        lax.fori_loop(0, last, body, 0)
        step(last, True)
    for copy in late:
        copy.wait()
    mine_ref[...] = dkv[core].astype(BF)
    theirs_ref[...] = dkv[1 - core].astype(BF)
    for i in range(2):
        rows = slice(i * SPAN, (i + 1) * SPAN)
        cs, sn = cosine[rows, :], -sine[rows, :]
        mix = None
        for h in range(G):
            cols = slice(h * D, (h + 1) * D)
            grad = turn((dqa[i, :, cols] * SCALE).T, cs, sn)
            unit = unit_ref[rows, cols]
            up = grad * gain_q[:, cols]
            up_ref[rows, cols] = up
            mix = up * unit if mix is None else mix + up * unit
            gain = jnp.sum(grad * unit, axis=0, keepdims=True)
            if i == 0:
                gain_ref[:, cols] = gain
            else:
                gain_ref[:, cols] += gain
        mix_ref[:, rows] = lane_sums(mix)


def attn_bwd(table, own, q, kv, grad_part, w_out, o, lse, cosine, sine, gain_q, unit):
    block = w_out.shape[1] // 4
    n = kv.shape[1]
    rows = 2 * SPAN
    return pl.pallas_call(
        bwd_kernel,
        out_shape=(
            jax.ShapeDtypeStruct((rows, R), F32),
            jax.ShapeDtypeStruct((1, rows), F32),
            jax.ShapeDtypeStruct((1, R), F32),
            jax.ShapeDtypeStruct((n, D), BF),
            jax.ShapeDtypeStruct((n, D), BF),
        ),
        grid_spec=pltpu.PrefetchScalarGridSpec(
            num_scalar_prefetch=2,
            grid=(),
            in_specs=[HB] * 10,
            out_specs=(VM,) * 5,
            scratch_shapes=[
                pltpu.VMEM(x.shape, x.dtype)
                for x in (q, kv, o, lse, cosine, sine, gain_q, unit)
            ]
            + [
                pltpu.VMEM((2, R, D), BF),
                pltpu.VMEM((4, rows, block), BF),
                pltpu.VMEM((4, R, block), BF),
                pltpu.VMEM((2, n, D), F32),
                pltpu.VMEM((2, D, R), F32),
                pltpu.SemaphoreType.DMA((8,)),
                pltpu.SemaphoreType.DMA((8,)),
            ],
        ),
        compiler_params=params(56),
        cost_estimate=cost(2.2e10, 12, 6e6),
    )(table, own, q, kv, o, lse, cosine, sine, gain_q, unit, grad_part, w_out)


def key_gain_kernel(
    loc, own, kv_in, mine_in, theirs_in, cos_r, sin_r, cos_s, sin_s, out, k_s, g_s, sems
):
    core = own[2]
    key_copy = pltpu.make_async_copy(kv_in.at[0], k_s, sems.at[0])
    key_copy.start()

    @pl.when(core == 0)
    def _():
        pltpu.make_async_copy(mine_in, g_s, sems.at[1]).start()

    @pl.when(core != 0)
    def _():
        pltpu.make_async_copy(theirs_in, g_s, sems.at[1]).start()

    key_copy.wait()
    pltpu.make_async_copy(mine_in, g_s, sems.at[1]).wait()
    cr, sr = cos_r[...], sin_r[...]

    def body(s, sums):
        plain, by_cos, by_sin = sums
        k = k_s[pl.ds(pl.multiple_of(loc[0, s] * SPAN, SPAN), SPAN), :].astype(F32)
        g = g_s[pl.ds(pl.multiple_of(loc[2, s] * SPAN, SPAN), SPAN), :].astype(F32)
        cs, sn = cos_s[pl.ds(s, 1), :], sin_s[pl.ds(s, 1), :]
        same = k * g
        cross = g * pltpu.roll(k, D // 2, 1)
        return (
            plain + same,
            by_cos + same * (cs * cr - sn * sr),
            by_sin + cross * (sn * cr + cs * sr),
        )

    zero = jnp.zeros((SPAN, D), F32)
    plain, by_cos, by_sin = lax.fori_loop(0, loc.shape[1], body, (zero, zero, zero), unroll=4)

    def over_rows(x):
        return jnp.broadcast_to(jnp.sum(x, axis=0, keepdims=True), (8, D))

    plain, by_cos, by_sin = over_rows(plain), over_rows(by_cos), over_rows(by_sin)
    half = D // 2
    sign = jnp.where(lax.broadcasted_iota(jnp.int32, (8, D), 1) < half, 1.0, -1.0)
    total = (
        plain
        + pltpu.roll(plain, half, 1)
        + by_cos
        - pltpu.roll(by_cos, half, 1)
        + sign * (by_sin + pltpu.roll(by_sin, half, 1))
    )
    out[...] = 0.5 * total[0:1]


def key_gain_of(table, own, kv, mine, theirs, tables):
    n = kv.shape[1]
    return pl.pallas_call(
        key_gain_kernel,
        out_shape=jax.ShapeDtypeStruct((1, D), F32),
        grid_spec=pltpu.PrefetchScalarGridSpec(
            num_scalar_prefetch=2,
            grid=(),
            in_specs=[HB] * 3 + [VM] * 4,
            out_specs=VM,
            scratch_shapes=[
                pltpu.VMEM((n, D), BF),
                pltpu.VMEM((n, D), BF),
                pltpu.SemaphoreType.DMA((2,)),
            ],
        ),
        compiler_params=params(56),
        cost_estimate=cost(1e9, 6),
    )(table, own, kv, mine, theirs, *tables)


def query_kernel(*refs):
    ins, w_ref, out, stages = refs[:4], refs[4], refs[5], refs[6:10]
    w_s, y_s, sems, ysems, isems = refs[10:]
    block = w_s.shape[1]
    inputs = fetch(list(zip(ins, stages)), isems)
    up, unit, mix, inv = stages
    copies = fetch([(w_ref.at[pl.ds(b * block, block), :], w_s.at[b]) for b in range(4)], sems)
    rows = up.shape[0]

    for copy in inputs:
        copy.wait()

    def column(ref):
        return jnp.broadcast_to(ref[...], (D, rows)).T[:, :1]

    x = (column(inv) * (up[...] - unit[...] * (column(mix) * (1.0 / Q_CHANNELS)))).astype(BF)
    y_copies = []
    for b in range(4):
        copies[b].wait()
        y_s[b] = nt(x, w_s[b]).astype(BF)
        copy = pltpu.make_async_copy(y_s.at[b], out.at[b], ysems.at[b])
        copy.start()
        y_copies.append(copy)
    for copy in y_copies:
        copy.wait()


def query_partial_of(up, unit, mix, inv, w_query):
    rows = up.shape[0]
    feats = w_query.shape[0]
    block = feats // 4
    return pl.pallas_call(
        query_kernel,
        out_shape=jax.ShapeDtypeStruct((4, rows, block), BF),
        in_specs=[HB] * 5,
        out_specs=FAR,
        scratch_shapes=[pltpu.VMEM(x.shape, x.dtype) for x in (up, unit, mix, inv)]
        + [
            pltpu.VMEM((4, block, R), BF),
            pltpu.VMEM((4, rows, block), BF),
            pltpu.SemaphoreType.DMA((4,)),
            pltpu.SemaphoreType.DMA((4,)),
            pltpu.SemaphoreType.DMA((4,)),
        ],
        compiler_params=params(56),
        cost_estimate=cost(1.7e9, 9),
    )(up, unit, mix, inv, w_query)


def last_kernel(g0, g1, g2, g3, u0, u1, u2, u3, inv, w, query_side, out):
    gs, us = (g0, g1, g2, g3), (u0, u1, u2, u3)
    mix = None
    for g, u in zip(gs, us):
        part = g[:, :D].astype(F32) * u[...].astype(F32)
        mix = part if mix is None else mix + part
    mix = jnp.sum(mix, axis=1, keepdims=True) * (1.0 / K_CHANNELS)
    total = query_side[...].astype(F32)
    for n, (g, u) in enumerate(zip(gs, us)):
        raw = (inv[...] * (g[:, :D].astype(F32) - u[...].astype(F32) * mix)).astype(BF)
        total = total + nt(jnp.concatenate([raw, g[:, D:]], axis=1), w[n])
    out[...] = total.astype(BF)


def last_of(grads, units, inv, w, query_side):
    return pl.pallas_call(
        last_kernel,
        out_shape=jax.ShapeDtypeStruct(query_side.shape, BF),
        in_specs=[VM] * 11,
        out_specs=VM,
        compiler_params=params(56),
        cost_estimate=cost(7e8, 5),
    )(*grads, *units, inv, w, query_side)

QUERY_HEADS = 20
KEY_VALUE_HEADS = 4
Q_CHANNELS = QUERY_HEADS * D
K_CHANNELS = KEY_VALUE_HEADS * D
N_Y, N_Z, N_CORE, N_TP = 4, 4, 2, 4


def ctx_index(y, z, c):
    return (y * N_Z + z) * N_CORE + c


def ctx_pairs(move):
    return [
        (ctx_index(y, z, c), ctx_index(*move(y, z, c)))
        for y in range(N_Y)
        for z in range(N_Z)
        for c in range(N_CORE)
    ]


def shift_first(x, d):
    return lax.ppermute(
        x,
        "ctx",
        ctx_pairs(lambda y, z, c: ((y + c * d) % N_Y, (z + (1 - c) * d) % N_Z, c)),
    )


def shift_second(x, d):
    return lax.ppermute(
        x,
        "ctx",
        ctx_pairs(lambda y, z, c: ((y + (1 - c) * d) % N_Y, (z + c * d) % N_Z, c)),
    )


def swap_core(x):
    return lax.ppermute(x, "ctx", ctx_pairs(lambda y, z, c: (y, z, 1 - c)))


def shift_tp(x, d):
    return lax.ppermute(x, "tp", [(i, (i + d) % N_TP) for i in range(N_TP)])


def shifts(shift, x):
    return [x] + [shift(x, d) for d in DIST[1:]]


def sum_tp(x):
    one, three, two = (shift_tp(x, d) for d in DIST[1:])
    return (x + one) + (three + two)


def sum_core_z(x):
    x = x + swap_core(x)
    x = x + lax.ppermute(x, "ctx", ctx_pairs(lambda y, z, c: (y, z ^ 1, c)))
    return x + lax.ppermute(x, "ctx", ctx_pairs(lambda y, z, c: (y, 3 - z, c)))


def sum_y(x):
    x = x + lax.ppermute(x, "ctx", ctx_pairs(lambda y, z, c: (y ^ 1, z, c)))
    return x + lax.ppermute(x, "ctx", ctx_pairs(lambda y, z, c: (3 - y, z, c)))


def after(x, *others):
    return lax.optimization_barrier((x,) + others)[0]


def outgoing(x):
    rows = x.shape[0] // 4
    return [x[d * rows : (d + 1) * rows].astype(BF) for d in DIST[1:]], x[:rows]


def add_up(total, arrived):
    for x in arrived:
        total = total + x.astype(F32)
    return total


def local(tokens, span_order, w_query, w_key, value_weight, w_out, gain_query, gain_key, out_grad):
    rows, feats = tokens.shape
    me = lax.axis_index("ctx")
    tp = lax.axis_index("tp")
    my_y, my_z, my_c = me // 8, (me // 2) % 4, me % 2

    mid = rows // 2
    with jax.named_scope("gather_tokens"):
        upper, lower = tokens[:mid], tokens[mid:]
        left_a = shift_tp(upper, 1)
        right_b = shift_tp(lower, 3)
        left_b = shift_tp(lower, 1)
        right_a = shift_tp(upper, 3)

    place = jnp.arange(64, dtype=jnp.int32)
    stored = jnp.sum(jnp.where(span_order[None, :] == place[:, None], place[None, :], 0), axis=1)
    src, half = stored // 2, stored % 2
    src_y, src_z, src_c = src // 8, (src // 2) % 4, src % 2
    to_y, to_z = (src_y - my_y) % 4, (src_z - my_z) % 4
    back_y, back_z = (4 - to_y) % 4, (4 - to_z) % 4
    slot_y = jnp.where(back_y >= 2, 5 - back_y, back_y)
    slot_z = jnp.where(back_z >= 2, 5 - back_z, back_z)
    table = jnp.stack(
        [
            ((slot_y * 4 + slot_z) * 2 + src_c) * 2 + half,
            ((slot_z * 4 + slot_y) * 2 + 1 - src_c) * 2 + half,
            ((to_z * 4 + to_y) * 2 + src_c) * 2 + half,
            ((to_y * 4 + to_z) * 2 + src_c) * 2 + half,
        ]
    ).astype(jnp.int32)
    own = lax.dynamic_slice_in_dim(span_order, 2 * me, 2)
    own = jnp.concatenate([own, my_c[None]]).astype(jnp.int32)

    query_pos = (own[:2, None] * SPAN + jnp.arange(SPAN)[None, :]).reshape(-1)
    frequency = jnp.exp(jnp.arange(D // 2).astype(F32) * (-2.0 * math.log(500000.0) / D))
    angles = query_pos.astype(F32)[:, None] * frequency[None, :]
    cosine, sine = jnp.cos(angles), jnp.sin(angles)
    cosine = jnp.concatenate([cosine, cosine], axis=1)
    sine = jnp.concatenate([-sine, sine], axis=1)

    offs = jnp.stack([(tp - d) % 4 for d in DIST]).astype(jnp.int32)
    twice = 2.0 * jnp.concatenate([frequency, frequency])[None, :]
    by_row = jnp.arange(SPAN).astype(F32)[:, None] * twice
    by_span = (SPAN * jnp.arange(64)).astype(F32)[:, None] * twice
    tables = (jnp.cos(by_row), jnp.sin(by_row), jnp.cos(by_span), jnp.sin(by_span))

    with jax.named_scope("weight_rows"):
        share = feats // 32
        cut = jnp.concatenate(
            [
                lax.dynamic_slice_in_dim(w.reshape(N_TP, feats, D), share * me, share, 1)
                for w in (w_key, value_weight)
            ],
            axis=2,
        )
        cut = lax.all_gather(cut, "tp", axis=0, tiled=False)
        ours = lax.dynamic_index_in_dim(cut, tp, 1, keepdims=False)
        cut = jnp.stack(
            [lax.dynamic_index_in_dim(ours, (tp - d) % 4, 0, keepdims=False) for d in DIST]
        )
        w_rows = lax.all_gather(cut, "ctx", axis=0, tiled=False)

    with jax.named_scope("gather_tokens"):
        weights = (w_query, w_key, value_weight)
        acc = project(offs[:1], ((tokens,),), weights)
        left_a, right_b, left_b, right_a, cosine, sine, offs, table, own, acc, *tables = (
            lax.optimization_barrier(
                (left_a, right_b, left_b, right_a, cosine, sine, offs, table, own, acc, *tables)
            )
        )
        far_a = shift_tp(left_a, 1)
        far_b = shift_tp(right_b, 3)
        acc = project(offs[1:3], ((left_a, left_b), (right_a, right_b)), weights, acc)
        far_a, far_b, acc = lax.optimization_barrier((far_a, far_b, acc))
    gain_q, gain_k = gain_query[None, :], gain_key[None, :]
    q_rot, q_raw, k_rot, k_raw, value, squares = project_end(
        offs[3:], far_a, far_b, weights, acc, cosine, sine, gain_q, gain_k
    )
    with jax.named_scope("norm_sums"):
        squares = sum_tp(squares)
    query_inv = lax.rsqrt(squares[0] / Q_CHANNELS + 1e-06)[:, None]
    key_inv = lax.rsqrt(squares[1] / K_CHANNELS + 1e-06)[:, None]
    key = (k_rot * key_inv).astype(BF)

    with jax.named_scope("gather_keys_values"):
        first_core = my_c == 0
        mine = jnp.where(first_core, key, value)
        pair = join(mine, swap_core(jnp.where(first_core, value, key)))
        plane = join(*shifts(shift_first, pair))
        mine = shifts(shift_second, plane)
    query_unit = q_raw * query_inv
    key_unit = (k_raw * key_inv).astype(BF)
    query = (
        (q_rot.reshape(2, G, SPAN, D) * query_inv.reshape(2, 1, SPAN, 1)).astype(BF).reshape(2, R, D)
    )
    with jax.named_scope("gather_key_units"):
        key_units = shifts(shift_tp, key_unit)

    with jax.named_scope("gather_out_grad"):
        grad_part = lax.all_gather(after(out_grad, far_a, far_b, cut), "tp", axis=1, tiled=True)

    with jax.named_scope("swap_keys_values"):
        last, query, query_unit, *key_units = lax.optimization_barrier(
            (mine[3], query, query_unit, *key_units)
        )
        mine = mine[:3] + [last]
        pieces = (*mine, *(swap_core(x) for x in mine))

    log_total, heads, kv, out_partial = attn_fwd(table, own, query, pieces, w_out)
    attn_out = lax.psum_scatter(out_partial, "tp", scatter_dimension=0, tiled=False)

    up_query, mix_query, gain_part, mine, theirs = attn_bwd(
        table, own, query, kv, grad_part, w_out, heads, log_total,
        cosine, sine, gain_q, query_unit,
    )

    with jax.named_scope("sum_key_value_grads"):
        mix_query = sum_tp(mix_query)
        received, mix_query, w_rows = lax.optimization_barrier(
            (swap_core(theirs), mix_query, w_rows)
        )
        summed = mine.astype(F32) + received.astype(F32)
        sent, total = outgoing(summed)
        *sent, mine, theirs, attn_out = lax.optimization_barrier((*sent, mine, theirs, attn_out))
        arrived = [shift_first(x, d) for x, d in zip(sent, DIST[1:])]
        gain_key_part = key_gain_of(table, own, kv, mine, theirs, tables) / gain_k
        gains = jnp.concatenate([gain_part, gain_key_part], axis=1)
        *arrived, gains = lax.optimization_barrier((*arrived, gains))
        sent, total = outgoing(add_up(total, arrived))
        *sent, gains = lax.optimization_barrier((*sent, gains))
        arrived = [shift_second(x, d) for x, d in zip(sent, DIST[1:])]
        *arrived, gains = lax.optimization_barrier((*arrived, sum_core_z(gains)))
        total = add_up(total, arrived)
        ours, its = total[:rows], total[rows:]
        kept = jnp.where(first_core, ours, its)
        swapped = swap_core(jnp.where(first_core, its, ours))
        key_grad_rot = jnp.where(first_core, kept, swapped)
        value_grad = jnp.where(first_core, swapped, kept).astype(BF)

    with jax.named_scope("query_side"):
        query_partial = query_partial_of(
            up_query, query_unit, mix_query, query_inv.reshape(1, rows), w_query
        )
        query_side = lax.psum_scatter(query_partial, "tp", scatter_dimension=0, tiled=False)

    with jax.named_scope("key_value_side"):
        first, second = key_grad_rot[:, : D // 2], key_grad_rot[:, D // 2 :]
        cs, sn = cosine[:, : D // 2], sine[:, D // 2 :]
        key_grad = jnp.concatenate([first * cs + second * sn, second * cs - first * sn], axis=1)
        w_rows = after(w_rows, query_partial).transpose(1, 0, 2, 3).reshape(4, feats, 2 * D)
        key_grad, w_rows = lax.optimization_barrier((key_grad, w_rows))
        both = jnp.concatenate([(key_grad * gain_k).astype(BF), value_grad], axis=1)
        grads = shifts(shift_tp, both)
        *grads, gains = lax.optimization_barrier((*grads, sum_y(gains)))
        gain_query_grad, gain_key_grad = gains[0, :R], gains[0, R:]
        input_grad = last_of(grads, key_units, key_inv, w_rows, query_side)
    return (attn_out, input_grad, gain_query_grad, gain_key_grad)


def solution(mesh):
    return jax.shard_map(
        local,
        mesh=mesh,
        in_specs=(
            P("ctx", "tp"),
            P(),
            P(None, "tp"),
            P(None, "tp"),
            P(None, "tp"),
            P("tp", None),
            P("tp"),
            P("tp"),
            P("ctx", "tp"),
        ),
        out_specs=(P("ctx", "tp"), P("ctx", "tp"), P("tp"), P("tp")),
        check_vma=False,
    )
```

```python
import math

import jax
import jax.numpy as jnp
from jax import lax
from jax.experimental import pallas as pl
from jax.experimental.pallas import tpu as pltpu
from jax.sharding import PartitionSpec as P

D = 128
SPAN = 128
G = 5
R = G * SPAN
CH = 8
KC = CH * SPAN
SCALE = D**-0.5
LOG2E = math.log2(math.e)
NEG = -1e30
BF = jnp.bfloat16
F32 = jnp.float32
DIST = (0, 1, 3, 2)
PIECES = 8


def nt(a, b):
    return lax.dot_general(a, b, (((1,), (1,)), ((), ())), preferred_element_type=F32)


def tn(a, b):
    return lax.dot_general(a, b, (((0,), (0,)), ((), ())), preferred_element_type=F32)


def nn(a, b):
    return lax.dot_general(a, b, (((1,), (0,)), ((), ())), preferred_element_type=F32)


VM = pl.BlockSpec(memory_space=pltpu.VMEM)
HB = pl.BlockSpec(memory_space=pl.ANY)
FAR = pl.BlockSpec(memory_space=pltpu.HBM)


def params(mib):
    return pltpu.CompilerParams(vmem_limit_bytes=mib * 2**20)


def cost(flops, mib, exps=0):
    return pl.CostEstimate(
        flops=int(flops), bytes_accessed=int(mib * 2**20), transcendentals=int(exps)
    )


def turn(x, cosine, sine):
    return x * cosine + pltpu.roll(x, D // 2, 1) * sine


def lane_sums(x):
    return jnp.sum(x.T, axis=0, keepdims=True)


def fetch(pairs, sems):
    copies = [pltpu.make_async_copy(src, dst, sems.at[n]) for n, (src, dst) in enumerate(pairs)]
    for copy in copies:
        copy.start()
    return copies


def fetch_rows(off, weights, stages, sems):
    pairs = []
    for n in range(stages[0].shape[0]):
        rows = stages[0].shape[1]
        at = pl.ds(pl.multiple_of(off[n] * rows, rows), rows)
        pairs += [(w.at[at, :], s.at[n]) for w, s in zip(weights, stages)]
    return fetch(pairs, sems)


def product_of(x, stages, n):
    return jnp.concatenate([nn(x, s[n]) for s in stages], axis=1)


def project_kernel(off, *refs, count, parts, first):
    xs, weights = refs[: count * parts], refs[count * parts : count * parts + 3]
    stages, sems, x_s, isems, out = refs[-6:-3], refs[-3], refs[-2], refs[-1], refs[-7]
    part_rows = x_s.shape[1] // parts
    inputs = fetch(
        [
            (xs[n * parts + m], x_s.at[n, pl.ds(m * part_rows, part_rows), :])
            for n in range(count)
            for m in range(parts)
        ]
        + ([] if first else [(refs[count * parts + 3], out)]),
        isems,
    )
    copies = fetch_rows(off, weights, stages, sems)
    for copy in inputs:
        copy.wait()
    total = None if first else out[...]
    for n in range(count):
        for copy in copies[3 * n : 3 * n + 3]:
            copy.wait()
        part = product_of(x_s[n], stages, n)
        total = part if total is None else total + part
    out[...] = total


def stages_of(weights, count, feats):
    return [pltpu.VMEM((count, feats, w.shape[1]), BF) for w in weights] + [
        pltpu.SemaphoreType.DMA((3 * count,))
    ]


def project(off, pieces, weights, acc=None):
    parts = len(pieces[0])
    rows, feats = sum(x.shape[0] for x in pieces[0]), pieces[0][0].shape[1]
    width = sum(w.shape[1] for w in weights)
    count = len(pieces)
    xs = [x for piece in pieces for x in piece]
    more = () if acc is None else (acc,)
    return pl.pallas_call(
        lambda *refs: project_kernel(*refs, count=count, parts=parts, first=acc is None),
        out_shape=jax.ShapeDtypeStruct((rows, width), F32),
        grid_spec=pltpu.PrefetchScalarGridSpec(
            num_scalar_prefetch=1,
            grid=(),
            in_specs=[HB] * (len(xs) + 3 + len(more)),
            out_specs=VM,
            scratch_shapes=stages_of(weights, count, feats)
            + [pltpu.VMEM((count, rows, feats), BF), pltpu.SemaphoreType.DMA((len(xs) + 1,))],
        ),
        compiler_params=params(56),
        cost_estimate=cost(6e8 * count, 4 * count),
    )(off, *xs, *weights, *more)


def project_end_kernel(
    off, xa, xb, wq, wk, wv, acc_in, cosine, sine, gain_q, gain_k,
    q_rot, q_raw, k_rot, k_raw, v_out, squares, sq, sk, sv, sems, x_s, a_s, c_s, s_s, gq_s, gk_s, isems,
):
    stages = (sq, sk, sv)
    copies = fetch(
        [
            (xa, x_s.at[pl.ds(0, SPAN), :]), (xb, x_s.at[pl.ds(SPAN, SPAN), :]), (acc_in, a_s),
            (cosine, c_s), (sine, s_s), (gain_q, gq_s), (gain_k, gk_s),
        ],
        isems,
    )
    copies += fetch_rows(off, (wq, wk, wv), stages, sems)
    for copy in copies:
        copy.wait()
    cs, sn, gain_q, gain_k = c_s[...], s_s[...], gq_s, gk_s
    raw = a_s[...] + product_of(x_s[...], stages, 0)
    k = raw[:, R : R + D]
    k_raw[...] = k
    k_rot[...] = turn(k * gain_k[...], cs, sn)
    v_out[...] = raw[:, R + D :].astype(BF)
    squares[1:2, :] = lane_sums(k * k)
    total = None
    for h in range(G):
        q = raw[:, h * D : (h + 1) * D]
        total = q * q if total is None else total + q * q
        rotated = turn(q * gain_q[:, h * D : (h + 1) * D], cs, sn)
        for i in range(2):
            q_rot[i, h * SPAN : (h + 1) * SPAN, :] = rotated[i * SPAN : (i + 1) * SPAN]
    q_raw[...] = raw[:, :R]
    squares[0:1, :] = lane_sums(total)


def project_end(off, xa, xb, weights, acc, cosine, sine, gain_q, gain_k):
    rows = acc.shape[0]
    feats = xa.shape[1]
    outs = (
        jax.ShapeDtypeStruct((2, R, D), F32),
        jax.ShapeDtypeStruct((rows, R), F32),
        jax.ShapeDtypeStruct((rows, D), F32),
        jax.ShapeDtypeStruct((rows, D), F32),
        jax.ShapeDtypeStruct((rows, D), BF),
        jax.ShapeDtypeStruct((2, rows), F32),
    )
    return pl.pallas_call(
        project_end_kernel,
        out_shape=outs,
        grid_spec=pltpu.PrefetchScalarGridSpec(
            num_scalar_prefetch=1,
            grid=(),
            in_specs=[HB] * 10,
            out_specs=(VM,) * 6,
            scratch_shapes=stages_of(weights, 1, feats)
            + [
                pltpu.VMEM((rows, feats), BF),
                pltpu.VMEM(acc.shape, F32),
                pltpu.VMEM(cosine.shape, F32),
                pltpu.VMEM(sine.shape, F32),
                pltpu.VMEM(gain_q.shape, F32),
                pltpu.VMEM(gain_k.shape, F32),
                pltpu.SemaphoreType.DMA((7,)),
            ],
        ),
        compiler_params=params(56),
        cost_estimate=cost(6e8, 6),
    )(off, xa, xb, *weights, acc, cosine, sine, gain_q, gain_k)


def join_kernel(*refs):
    at = 0
    for ref in refs[:-1]:
        n = ref.shape[0]
        refs[-1][at : at + n, :] = ref[...]
        at += n


def join(*xs):
    rows = sum(x.shape[0] for x in xs)
    return pl.pallas_call(
        join_kernel,
        out_shape=jax.ShapeDtypeStruct((rows,) + xs[0].shape[1:], xs[0].dtype),
        in_specs=[VM] * len(xs),
        out_specs=VM,
        compiler_params=params(8),
        cost_estimate=cost(0, 1),
    )(*xs)


def spans_at(ref, loc, which, j):
    return jnp.concatenate(
        [
            ref[pl.ds(pl.multiple_of(loc[which, CH * j + t] * SPAN, SPAN), SPAN), :]
            for t in range(CH)
        ],
        axis=0,
    )


def load_pieces(refs, whole, core, sems):
    count = len(refs) // 2
    copies = []
    for n, src in enumerate(refs):
        rows = src.shape[0]
        to = core if n < count else 1 - core
        copy = pltpu.make_async_copy(
            src, whole.at[to, pl.ds((n % count) * rows, rows), :], sems.at[n]
        )
        copy.start()
        copies.append(copy)
    for copy in copies:
        copy.wait()


def fwd_kernel(loc, own, q_in, *refs):
    kv_refs, w_ref, (lse_ref, o_ref, kv_out, out) = (
        refs[:PIECES], refs[PIECES], refs[PIECES + 1 : PIECES + 5],
    )
    kv, w_s, y_s, m_s, acc_s, q_ref, sems, wsems, kvsem, ysems, qsem = refs[PIECES + 5 :]
    q_copies = fetch([(q_in, q_ref)], qsem)
    load_pieces(kv_refs, kv, own[2], sems)
    keep = fetch([(kv, kv_out)], kvsem)
    block = y_s.shape[2]
    w_copies = fetch(
        [(w_ref.at[:, pl.ds(b * block, block)], w_s.at[b]) for b in range(4)], wsems
    )
    for copy in q_copies:
        copy.wait()
    k_ref, v_ref = kv.at[0], kv.at[1]
    ones = (lax.broadcasted_iota(jnp.int32, (KC, D), 1) == 0).astype(BF)
    for i in range(2):
        c = own[i]
        m_s[...] = jnp.full_like(m_s, NEG)
        acc_s[...] = jnp.zeros_like(acc_s)

        def step(j, masked):
            kk = spans_at(k_ref, loc, 0, j)
            vv = jnp.concatenate([spans_at(v_ref, loc, 1, j), ones], axis=1)
            for h in range(G):
                at = slice(h * SPAN, (h + 1) * SPAN)
                s = nt(q_ref[i, at, :], kk)
                if masked:
                    key = j * KC + lax.broadcasted_iota(jnp.int32, (SPAN, KC), 1)
                    row = c * SPAN + lax.broadcasted_iota(jnp.int32, (SPAN, KC), 0)
                    s = jnp.where(key <= row, s, NEG)
                m = m_s[at, :]
                new = jnp.maximum(m, jnp.max(s, axis=1, keepdims=True))
                shrink = jnp.exp2((m - new) * (SCALE * LOG2E))
                p = jnp.exp2((s - new[:, :1]) * (SCALE * LOG2E))
                m_s[at, :] = new
                acc_s[at, :] = acc_s[at, :] * shrink[:, :1] + nn(p.astype(BF), vv)

        last = c // CH

        def body(j, _):
            step(j, False)
            return 0

        lax.fori_loop(0, last, body, 0)
        step(last, True)
        total = acc_s[:, D : D + 1]
        o_ref[i] = (acc_s[:, :D] / total).astype(BF)
        lse = m_s[...] * (SCALE * LOG2E) + jnp.log2(jnp.broadcast_to(total, (R, D)))
        lse_ref[i] = lse.T[0:1, :]
    x = jnp.concatenate(
        [
            jnp.concatenate(
                [o_ref[i, h * SPAN : (h + 1) * SPAN, :] for h in range(G)], axis=1
            )
            for i in range(2)
        ],
        axis=0,
    )
    y_copies = []
    for b in range(4):
        w_copies[b].wait()
        y_s[b] = nn(x, w_s[b]).astype(BF)
        copy = pltpu.make_async_copy(y_s.at[b], out.at[b], ysems.at[b])
        copy.start()
        y_copies.append(copy)
    for copy in keep + y_copies:
        copy.wait()


def attn_fwd(table, own, q, pieces, w_out):
    n = sum(x.shape[0] for x in pieces) // 2
    block = w_out.shape[1] // 4
    return pl.pallas_call(
        fwd_kernel,
        out_shape=(
            jax.ShapeDtypeStruct((2, 1, R), F32),
            jax.ShapeDtypeStruct((2, R, D), BF),
            jax.ShapeDtypeStruct((2, n, D), BF),
            jax.ShapeDtypeStruct((4, 2 * SPAN, block), BF),
        ),
        grid_spec=pltpu.PrefetchScalarGridSpec(
            num_scalar_prefetch=2,
            grid=(),
            in_specs=[HB] * (PIECES + 2),
            out_specs=(VM, VM, FAR, FAR),
            scratch_shapes=[
                pltpu.VMEM((2, n, D), BF),
                pltpu.VMEM((4, R, block), BF),
                pltpu.VMEM((4, 2 * SPAN, block), BF),
                pltpu.VMEM((R, D), F32),
                pltpu.VMEM((R, 2 * D), F32),
                pltpu.VMEM((2, R, D), BF),
                pltpu.SemaphoreType.DMA((PIECES,)),
                pltpu.SemaphoreType.DMA((4,)),
                pltpu.SemaphoreType.DMA((1,)),
                pltpu.SemaphoreType.DMA((4,)),
                pltpu.SemaphoreType.DMA((1,)),
            ],
        ),
        compiler_params=params(56),
        cost_estimate=cost(1.8e10, 12, 6e6),
    )(table, own, q, *pieces, w_out)


def bwd_kernel(
    loc, own, *refs,
):
    ins, g_ref, w_ref, (up_ref, mix_ref, gain_ref, mine_ref, theirs_ref) = (
        refs[:8], refs[8], refs[9], refs[10:15],
    )
    stages, (do_ref, g_s, w_s, dkv, dqa, gsems, sems) = refs[15:23], refs[23:]
    q_ref, kv, o_ref, lse_ref, cosine, sine, gain_q, unit_ref = stages
    core = own[2]
    block = g_s.shape[2]
    g_pairs = []
    for b in range(4):
        cols = pl.ds(b * block, block)
        g_pairs += [(w_ref.at[:, cols], w_s.at[b]), (g_ref.at[:, cols], g_s.at[b])]
    g_copies = fetch(g_pairs, gsems)
    copies = fetch(list(zip(ins, stages)), sems)
    late = copies[4:]
    copies = copies[:4]
    k_ref, v_ref = kv.at[0], kv.at[1]
    dkv[...] = jnp.zeros_like(dkv)
    dqa[...] = jnp.zeros_like(dqa)
    grad = None
    for b in range(4):
        g_copies[2 * b].wait()
        g_copies[2 * b + 1].wait()
        part = nt(g_s[b], w_s[b])
        grad = part if grad is None else grad + part
    for i in range(2):
        for h in range(G):
            do_ref[i, h * SPAN : (h + 1) * SPAN, :] = grad[
                i * SPAN : (i + 1) * SPAN, h * D : (h + 1) * D
            ].astype(BF)
    for copy in copies:
        copy.wait()
    for i in range(2):
        c = own[i]
        q, do, lse = q_ref[i], do_ref[i], lse_ref[i]
        delta = lane_sums(do.astype(F32) * o_ref[i].astype(F32))

        def step(j, masked):
            kk = spans_at(k_ref, loc, 0, j)
            vv = spans_at(v_ref, loc, 1, j)
            p = jnp.exp2(nt(kk, q) * (SCALE * LOG2E) - lse)
            if masked:
                key = j * KC + lax.broadcasted_iota(jnp.int32, (KC, R), 0)
                row = c * SPAN + lax.rem(lax.broadcasted_iota(jnp.int32, (KC, R), 1), SPAN)
                p = jnp.where(key <= row, p, 0.0)
            ds = (p * (nt(vv, do) - delta)).astype(BF)
            dqa[i] += tn(kk, ds)
            dv = nn(p.astype(BF), do)
            dk = nn(ds, q) * SCALE
            for t in range(CH):
                part = slice(t * SPAN, (t + 1) * SPAN)
                at = pl.ds(pl.multiple_of(loc[2, CH * j + t] * SPAN, SPAN), SPAN)
                dkv[0, at, :] += dk[part]
                at = pl.ds(pl.multiple_of(loc[3, CH * j + t] * SPAN, SPAN), SPAN)
                dkv[1, at, :] += dv[part]

        last = c // CH

        def body(j, _):
            step(j, False)
            return 0

        lax.fori_loop(0, last, body, 0)
        step(last, True)
    for copy in late:
        copy.wait()
    mine_ref[...] = dkv[core].astype(BF)
    theirs_ref[...] = dkv[1 - core].astype(BF)
    for i in range(2):
        rows = slice(i * SPAN, (i + 1) * SPAN)
        cs, sn = cosine[rows, :], -sine[rows, :]
        mix = None
        for h in range(G):
            cols = slice(h * D, (h + 1) * D)
            grad = turn((dqa[i, :, cols] * SCALE).T, cs, sn)
            unit = unit_ref[rows, cols]
            up = grad * gain_q[:, cols]
            up_ref[rows, cols] = up
            mix = up * unit if mix is None else mix + up * unit
            gain = jnp.sum(grad * unit, axis=0, keepdims=True)
            if i == 0:
                gain_ref[:, cols] = gain
            else:
                gain_ref[:, cols] += gain
        mix_ref[:, rows] = lane_sums(mix)


def attn_bwd(table, own, q, kv, grad_part, w_out, o, lse, cosine, sine, gain_q, unit):
    block = w_out.shape[1] // 4
    n = kv.shape[1]
    rows = 2 * SPAN
    return pl.pallas_call(
        bwd_kernel,
        out_shape=(
            jax.ShapeDtypeStruct((rows, R), F32),
            jax.ShapeDtypeStruct((1, rows), F32),
            jax.ShapeDtypeStruct((1, R), F32),
            jax.ShapeDtypeStruct((n, D), BF),
            jax.ShapeDtypeStruct((n, D), BF),
        ),
        grid_spec=pltpu.PrefetchScalarGridSpec(
            num_scalar_prefetch=2,
            grid=(),
            in_specs=[HB] * 10,
            out_specs=(VM,) * 5,
            scratch_shapes=[
                pltpu.VMEM(x.shape, x.dtype)
                for x in (q, kv, o, lse, cosine, sine, gain_q, unit)
            ]
            + [
                pltpu.VMEM((2, R, D), BF),
                pltpu.VMEM((4, rows, block), BF),
                pltpu.VMEM((4, R, block), BF),
                pltpu.VMEM((2, n, D), F32),
                pltpu.VMEM((2, D, R), F32),
                pltpu.SemaphoreType.DMA((8,)),
                pltpu.SemaphoreType.DMA((8,)),
            ],
        ),
        compiler_params=params(56),
        cost_estimate=cost(2.2e10, 12, 6e6),
    )(table, own, q, kv, o, lse, cosine, sine, gain_q, unit, grad_part, w_out)


def key_gain_kernel(
    loc, own, kv_in, mine_in, theirs_in, cos_r, sin_r, cos_s, sin_s, out, k_s, g_s, sems
):
    core = own[2]
    key_copy = pltpu.make_async_copy(kv_in.at[0], k_s, sems.at[0])
    key_copy.start()

    @pl.when(core == 0)
    def _():
        pltpu.make_async_copy(mine_in, g_s, sems.at[1]).start()

    @pl.when(core != 0)
    def _():
        pltpu.make_async_copy(theirs_in, g_s, sems.at[1]).start()

    key_copy.wait()
    pltpu.make_async_copy(mine_in, g_s, sems.at[1]).wait()
    cr, sr = cos_r[...], sin_r[...]

    def body(s, sums):
        plain, by_cos, by_sin = sums
        k = k_s[pl.ds(pl.multiple_of(loc[0, s] * SPAN, SPAN), SPAN), :].astype(F32)
        g = g_s[pl.ds(pl.multiple_of(loc[2, s] * SPAN, SPAN), SPAN), :].astype(F32)
        cs, sn = cos_s[pl.ds(s, 1), :], sin_s[pl.ds(s, 1), :]
        same = k * g
        cross = g * pltpu.roll(k, D // 2, 1)
        return (
            plain + same,
            by_cos + same * (cs * cr - sn * sr),
            by_sin + cross * (sn * cr + cs * sr),
        )

    zero = jnp.zeros((SPAN, D), F32)
    plain, by_cos, by_sin = lax.fori_loop(0, loc.shape[1], body, (zero, zero, zero), unroll=4)

    def over_rows(x):
        return jnp.broadcast_to(jnp.sum(x, axis=0, keepdims=True), (8, D))

    plain, by_cos, by_sin = over_rows(plain), over_rows(by_cos), over_rows(by_sin)
    half = D // 2
    sign = jnp.where(lax.broadcasted_iota(jnp.int32, (8, D), 1) < half, 1.0, -1.0)
    total = (
        plain
        + pltpu.roll(plain, half, 1)
        + by_cos
        - pltpu.roll(by_cos, half, 1)
        + sign * (by_sin + pltpu.roll(by_sin, half, 1))
    )
    out[...] = 0.5 * total[0:1]


def key_gain_of(table, own, kv, mine, theirs, tables):
    n = kv.shape[1]
    return pl.pallas_call(
        key_gain_kernel,
        out_shape=jax.ShapeDtypeStruct((1, D), F32),
        grid_spec=pltpu.PrefetchScalarGridSpec(
            num_scalar_prefetch=2,
            grid=(),
            in_specs=[HB] * 3 + [VM] * 4,
            out_specs=VM,
            scratch_shapes=[
                pltpu.VMEM((n, D), BF),
                pltpu.VMEM((n, D), BF),
                pltpu.SemaphoreType.DMA((2,)),
            ],
        ),
        compiler_params=params(56),
        cost_estimate=cost(1e9, 6),
    )(table, own, kv, mine, theirs, *tables)


def query_kernel(*refs):
    ins, w_ref, out, stages = refs[:4], refs[4], refs[5], refs[6:10]
    w_s, y_s, sems, ysems, isems = refs[10:]
    block = w_s.shape[1]
    inputs = fetch(list(zip(ins, stages)), isems)
    up, unit, mix, inv = stages
    copies = fetch([(w_ref.at[pl.ds(b * block, block), :], w_s.at[b]) for b in range(4)], sems)
    rows = up.shape[0]

    for copy in inputs:
        copy.wait()

    def column(ref):
        return jnp.broadcast_to(ref[...], (D, rows)).T[:, :1]

    x = (column(inv) * (up[...] - unit[...] * (column(mix) * (1.0 / Q_CHANNELS)))).astype(BF)
    y_copies = []
    for b in range(4):
        copies[b].wait()
        y_s[b] = nt(x, w_s[b]).astype(BF)
        copy = pltpu.make_async_copy(y_s.at[b], out.at[b], ysems.at[b])
        copy.start()
        y_copies.append(copy)
    for copy in y_copies:
        copy.wait()


def query_partial_of(up, unit, mix, inv, w_query):
    rows = up.shape[0]
    feats = w_query.shape[0]
    block = feats // 4
    return pl.pallas_call(
        query_kernel,
        out_shape=jax.ShapeDtypeStruct((4, rows, block), BF),
        in_specs=[HB] * 5,
        out_specs=FAR,
        scratch_shapes=[pltpu.VMEM(x.shape, x.dtype) for x in (up, unit, mix, inv)]
        + [
            pltpu.VMEM((4, block, R), BF),
            pltpu.VMEM((4, rows, block), BF),
            pltpu.SemaphoreType.DMA((4,)),
            pltpu.SemaphoreType.DMA((4,)),
            pltpu.SemaphoreType.DMA((4,)),
        ],
        compiler_params=params(56),
        cost_estimate=cost(1.7e9, 9),
    )(up, unit, mix, inv, w_query)


def last_kernel(g0, g1, g2, g3, u0, u1, u2, u3, inv, w, query_side, out):
    gs, us = (g0, g1, g2, g3), (u0, u1, u2, u3)
    mix = None
    for g, u in zip(gs, us):
        part = g[:, :D].astype(F32) * u[...].astype(F32)
        mix = part if mix is None else mix + part
    mix = jnp.sum(mix, axis=1, keepdims=True) * (1.0 / K_CHANNELS)
    total = query_side[...].astype(F32)
    for n, (g, u) in enumerate(zip(gs, us)):
        raw = (inv[...] * (g[:, :D].astype(F32) - u[...].astype(F32) * mix)).astype(BF)
        total = total + nt(jnp.concatenate([raw, g[:, D:]], axis=1), w[n])
    out[...] = total.astype(BF)


def last_of(grads, units, inv, w, query_side):
    return pl.pallas_call(
        last_kernel,
        out_shape=jax.ShapeDtypeStruct(query_side.shape, BF),
        in_specs=[VM] * 11,
        out_specs=VM,
        compiler_params=params(56),
        cost_estimate=cost(7e8, 5),
    )(*grads, *units, inv, w, query_side)

QUERY_HEADS = 20
KEY_VALUE_HEADS = 4
Q_CHANNELS = QUERY_HEADS * D
K_CHANNELS = KEY_VALUE_HEADS * D
N_Y, N_Z, N_CORE, N_TP = 4, 4, 2, 4


def ctx_index(y, z, c):
    return (y * N_Z + z) * N_CORE + c


def ctx_pairs(move):
    return [
        (ctx_index(y, z, c), ctx_index(*move(y, z, c)))
        for y in range(N_Y)
        for z in range(N_Z)
        for c in range(N_CORE)
    ]


def shift_first(x, d):
    return lax.ppermute(
        x,
        "ctx",
        ctx_pairs(lambda y, z, c: ((y + c * d) % N_Y, (z + (1 - c) * d) % N_Z, c)),
    )


def shift_second(x, d):
    return lax.ppermute(
        x,
        "ctx",
        ctx_pairs(lambda y, z, c: ((y + (1 - c) * d) % N_Y, (z + c * d) % N_Z, c)),
    )


def swap_core(x):
    return lax.ppermute(x, "ctx", ctx_pairs(lambda y, z, c: (y, z, 1 - c)))


def shift_tp(x, d):
    return lax.ppermute(x, "tp", [(i, (i + d) % N_TP) for i in range(N_TP)])


def shifts(shift, x):
    return [x] + [shift(x, d) for d in DIST[1:]]


def sum_tp(x):
    one, three, two = (shift_tp(x, d) for d in DIST[1:])
    return (x + one) + (three + two)


def sum_core_z(x):
    x = x + swap_core(x)
    x = x + lax.ppermute(x, "ctx", ctx_pairs(lambda y, z, c: (y, z ^ 1, c)))
    return x + lax.ppermute(x, "ctx", ctx_pairs(lambda y, z, c: (y, 3 - z, c)))


def sum_y(x):
    x = x + lax.ppermute(x, "ctx", ctx_pairs(lambda y, z, c: (y ^ 1, z, c)))
    return x + lax.ppermute(x, "ctx", ctx_pairs(lambda y, z, c: (3 - y, z, c)))


def after(x, *others):
    return lax.optimization_barrier((x,) + others)[0]


def outgoing(x):
    rows = x.shape[0] // 4
    return [x[d * rows : (d + 1) * rows].astype(BF) for d in DIST[1:]], x[:rows]


def add_up(total, arrived):
    for x in arrived:
        total = total + x.astype(F32)
    return total


def local(tokens, span_order, w_query, w_key, value_weight, w_out, gain_query, gain_key, out_grad):
    rows, feats = tokens.shape
    me = lax.axis_index("ctx")
    tp = lax.axis_index("tp")
    my_y, my_z, my_c = me // 8, (me // 2) % 4, me % 2

    mid = rows // 2
    with jax.named_scope("gather_tokens"):
        upper, lower = tokens[:mid], tokens[mid:]
        left_a = shift_tp(upper, 1)
        right_b = shift_tp(lower, 3)
        left_b = shift_tp(lower, 1)
        right_a = shift_tp(upper, 3)

    place = jnp.arange(64, dtype=jnp.int32)
    stored = jnp.sum(jnp.where(span_order[None, :] == place[:, None], place[None, :], 0), axis=1)
    src, half = stored // 2, stored % 2
    src_y, src_z, src_c = src // 8, (src // 2) % 4, src % 2
    to_y, to_z = (src_y - my_y) % 4, (src_z - my_z) % 4
    back_y, back_z = (4 - to_y) % 4, (4 - to_z) % 4
    slot_y = jnp.where(back_y >= 2, 5 - back_y, back_y)
    slot_z = jnp.where(back_z >= 2, 5 - back_z, back_z)
    table = jnp.stack(
        [
            ((slot_y * 4 + slot_z) * 2 + src_c) * 2 + half,
            ((slot_z * 4 + slot_y) * 2 + 1 - src_c) * 2 + half,
            ((to_z * 4 + to_y) * 2 + src_c) * 2 + half,
            ((to_y * 4 + to_z) * 2 + src_c) * 2 + half,
        ]
    ).astype(jnp.int32)
    own = lax.dynamic_slice_in_dim(span_order, 2 * me, 2)
    own = jnp.concatenate([own, my_c[None]]).astype(jnp.int32)

    query_pos = (own[:2, None] * SPAN + jnp.arange(SPAN)[None, :]).reshape(-1)
    frequency = jnp.exp(jnp.arange(D // 2).astype(F32) * (-2.0 * math.log(500000.0) / D))
    angles = query_pos.astype(F32)[:, None] * frequency[None, :]
    cosine, sine = jnp.cos(angles), jnp.sin(angles)
    cosine = jnp.concatenate([cosine, cosine], axis=1)
    sine = jnp.concatenate([-sine, sine], axis=1)

    offs = jnp.stack([(tp - d) % 4 for d in DIST]).astype(jnp.int32)
    twice = 2.0 * jnp.concatenate([frequency, frequency])[None, :]
    by_row = jnp.arange(SPAN).astype(F32)[:, None] * twice
    by_span = (SPAN * jnp.arange(64)).astype(F32)[:, None] * twice
    tables = (jnp.cos(by_row), jnp.sin(by_row), jnp.cos(by_span), jnp.sin(by_span))

    with jax.named_scope("gather_tokens"):
        weights = (w_query, w_key, value_weight)
        acc = project(offs[:1], ((tokens,),), weights)
        left_a, right_b, left_b, right_a, cosine, sine, offs, table, own, acc, *tables = (
            lax.optimization_barrier(
                (left_a, right_b, left_b, right_a, cosine, sine, offs, table, own, acc, *tables)
            )
        )
        far_a = shift_tp(left_a, 1)
        far_b = shift_tp(right_b, 3)
        acc = project(offs[1:3], ((left_a, left_b), (right_a, right_b)), weights, acc)
        far_a, far_b, acc = lax.optimization_barrier((far_a, far_b, acc))
    gain_q, gain_k = gain_query[None, :], gain_key[None, :]
    q_rot, q_raw, k_rot, k_raw, value, squares = project_end(
        offs[3:], far_a, far_b, weights, acc, cosine, sine, gain_q, gain_k
    )
    with jax.named_scope("norm_sums"):
        squares = sum_tp(squares)
    query_inv = lax.rsqrt(squares[0] / Q_CHANNELS + 1e-06)[:, None]
    key_inv = lax.rsqrt(squares[1] / K_CHANNELS + 1e-06)[:, None]
    key = (k_rot * key_inv).astype(BF)

    with jax.named_scope("gather_keys_values"):
        first_core = my_c == 0
        mine = jnp.where(first_core, key, value)
        pair = join(mine, swap_core(jnp.where(first_core, value, key)))
        plane = join(*shifts(shift_first, pair))
        mine = shifts(shift_second, plane)
    with jax.named_scope("weight_rows"):
        share = feats // 32
        mine[1], key_rows, value_rows = lax.optimization_barrier((mine[1], w_key, value_weight))
        cut = []
        for d in DIST:
            start = feats * ((tp + d) % 4) + share * me
            piece = jnp.concatenate(
                [lax.dynamic_slice_in_dim(w, start, share, 0) for w in (key_rows, value_rows)],
                axis=1,
            )
            cut.append(shift_tp(piece, d) if d else piece)
        w_rows = lax.all_gather(jnp.stack(cut), "ctx", axis=0, tiled=False)

    query_unit = q_raw * query_inv
    key_unit = (k_raw * key_inv).astype(BF)
    query = (
        (q_rot.reshape(2, G, SPAN, D) * query_inv.reshape(2, 1, SPAN, 1)).astype(BF).reshape(2, R, D)
    )
    with jax.named_scope("gather_key_units"):
        key_units = shifts(shift_tp, key_unit)

    with jax.named_scope("gather_out_grad"):
        grad_part = lax.all_gather(after(out_grad, far_a, far_b), "tp", axis=1, tiled=True)

    with jax.named_scope("swap_keys_values"):
        last, query, query_unit, *key_units = lax.optimization_barrier(
            (mine[3], query, query_unit, *key_units)
        )
        mine = mine[:3] + [last]
        pieces = (*mine, *(swap_core(x) for x in mine))

    log_total, heads, kv, out_partial = attn_fwd(table, own, query, pieces, w_out)
    attn_out = lax.psum_scatter(out_partial, "tp", scatter_dimension=0, tiled=False)

    up_query, mix_query, gain_part, mine, theirs = attn_bwd(
        table, own, query, kv, grad_part, w_out, heads, log_total,
        cosine, sine, gain_q, query_unit,
    )

    with jax.named_scope("sum_key_value_grads"):
        mix_query = sum_tp(mix_query)
        received, mix_query, w_rows = lax.optimization_barrier(
            (swap_core(theirs), mix_query, w_rows)
        )
        summed = mine.astype(F32) + received.astype(F32)
        sent, total = outgoing(summed)
        *sent, mine, theirs = lax.optimization_barrier((*sent, mine, theirs))
        arrived = [shift_first(x, d) for x, d in zip(sent, DIST[1:])]
        gain_key_part = key_gain_of(table, own, kv, mine, theirs, tables) / gain_k
        gains = jnp.concatenate([gain_part, gain_key_part], axis=1)
        *arrived, gains, attn_out = lax.optimization_barrier((*arrived, gains, attn_out))
        sent, total = outgoing(add_up(total, arrived))
        arrived = [shift_second(x, d) for x, d in zip(sent, DIST[1:])]
        total = add_up(total, arrived)
        ours, its = total[:rows], total[rows:]
        kept = jnp.where(first_core, ours, its)
        swapped = swap_core(jnp.where(first_core, its, ours))
        key_grad_rot = jnp.where(first_core, kept, swapped)
        value_grad = jnp.where(first_core, swapped, kept).astype(BF)

    with jax.named_scope("query_side"):
        query_partial = query_partial_of(
            up_query, query_unit, mix_query, query_inv.reshape(1, rows), w_query
        )
        query_side = lax.psum_scatter(query_partial, "tp", scatter_dimension=0, tiled=False)

    with jax.named_scope("key_value_side"):
        first, second = key_grad_rot[:, : D // 2], key_grad_rot[:, D // 2 :]
        cs, sn = cosine[:, : D // 2], sine[:, D // 2 :]
        key_grad = jnp.concatenate([first * cs + second * sn, second * cs - first * sn], axis=1)
        w_rows = after(w_rows, query_partial).transpose(1, 0, 2, 3).reshape(4, feats, 2 * D)
        key_grad, w_rows = lax.optimization_barrier((key_grad, w_rows))
        both = jnp.concatenate([(key_grad * gain_k).astype(BF), value_grad], axis=1)
        both, gains = lax.optimization_barrier((both, gains))
        grads = shifts(shift_tp, both)
        gains = sum_y(sum_core_z(gains))
        gain_query_grad, gain_key_grad = gains[0, :R], gains[0, R:]
        input_grad = last_of(grads, key_units, key_inv, w_rows, query_side)
    return (attn_out, input_grad, gain_query_grad, gain_key_grad)


def solution(mesh):
    return jax.shard_map(
        local,
        mesh=mesh,
        in_specs=(
            P("ctx", "tp"),
            P(),
            P(None, "tp"),
            P(None, "tp"),
            P(None, "tp"),
            P("tp", None),
            P("tp"),
            P("tp"),
            P("ctx", "tp"),
        ),
        out_specs=(P("ctx", "tp"), P("ctx", "tp"), P("tp"), P("tp")),
        check_vma=False,
    )
```

```python
import math

import jax
import jax.numpy as jnp
from jax import lax
from jax.experimental import pallas as pl
from jax.experimental.pallas import tpu as pltpu
from jax.sharding import PartitionSpec as P

D = 128
SPAN = 128
G = 5
R = G * SPAN
CH = 8
KC = CH * SPAN
SCALE = D**-0.5
LOG2E = math.log2(math.e)
NEG = -1e30
BF = jnp.bfloat16
F32 = jnp.float32
DIST = (0, 1, 3, 2)
PIECES = 8


def nt(a, b):
    return lax.dot_general(a, b, (((1,), (1,)), ((), ())), preferred_element_type=F32)


def tn(a, b):
    return lax.dot_general(a, b, (((0,), (0,)), ((), ())), preferred_element_type=F32)


def nn(a, b):
    return lax.dot_general(a, b, (((1,), (0,)), ((), ())), preferred_element_type=F32)


VM = pl.BlockSpec(memory_space=pltpu.VMEM)
HB = pl.BlockSpec(memory_space=pl.ANY)
FAR = pl.BlockSpec(memory_space=pltpu.HBM)


def params(mib):
    return pltpu.CompilerParams(vmem_limit_bytes=mib * 2**20)


def cost(flops, mib, exps=0):
    return pl.CostEstimate(
        flops=int(flops), bytes_accessed=int(mib * 2**20), transcendentals=int(exps)
    )


def turn(x, cosine, sine):
    return x * cosine + pltpu.roll(x, D // 2, 1) * sine


def lane_sums(x):
    return jnp.sum(x.T, axis=0, keepdims=True)


def fetch(pairs, sems):
    copies = [pltpu.make_async_copy(src, dst, sems.at[n]) for n, (src, dst) in enumerate(pairs)]
    for copy in copies:
        copy.start()
    return copies


def fetch_rows(off, weights, stages, sems):
    pairs = []
    for n in range(stages[0].shape[0]):
        rows = stages[0].shape[1]
        at = pl.ds(pl.multiple_of(off[n] * rows, rows), rows)
        pairs += [(w.at[at, :], s.at[n]) for w, s in zip(weights, stages)]
    return fetch(pairs, sems)


def product_of(x, stages, n):
    return jnp.concatenate([nn(x, s[n]) for s in stages], axis=1)


def project_kernel(off, *refs, count, parts, first):
    xs, weights = refs[: count * parts], refs[count * parts : count * parts + 3]
    stages, sems, x_s, isems, out = refs[-6:-3], refs[-3], refs[-2], refs[-1], refs[-7]
    part_rows = x_s.shape[1] // parts
    inputs = fetch(
        [
            (xs[n * parts + m], x_s.at[n, pl.ds(m * part_rows, part_rows), :])
            for n in range(count)
            for m in range(parts)
        ]
        + ([] if first else [(refs[count * parts + 3], out)]),
        isems,
    )
    copies = fetch_rows(off, weights, stages, sems)
    for copy in inputs:
        copy.wait()
    total = None if first else out[...]
    for n in range(count):
        for copy in copies[3 * n : 3 * n + 3]:
            copy.wait()
        part = product_of(x_s[n], stages, n)
        total = part if total is None else total + part
    out[...] = total


def stages_of(weights, count, feats):
    return [pltpu.VMEM((count, feats, w.shape[1]), BF) for w in weights] + [
        pltpu.SemaphoreType.DMA((3 * count,))
    ]


def project(off, pieces, weights, acc=None):
    parts = len(pieces[0])
    rows, feats = sum(x.shape[0] for x in pieces[0]), pieces[0][0].shape[1]
    width = sum(w.shape[1] for w in weights)
    count = len(pieces)
    xs = [x for piece in pieces for x in piece]
    more = () if acc is None else (acc,)
    return pl.pallas_call(
        lambda *refs: project_kernel(*refs, count=count, parts=parts, first=acc is None),
        out_shape=jax.ShapeDtypeStruct((rows, width), F32),
        grid_spec=pltpu.PrefetchScalarGridSpec(
            num_scalar_prefetch=1,
            grid=(),
            in_specs=[HB] * (len(xs) + 3 + len(more)),
            out_specs=VM,
            scratch_shapes=stages_of(weights, count, feats)
            + [pltpu.VMEM((count, rows, feats), BF), pltpu.SemaphoreType.DMA((len(xs) + 1,))],
        ),
        compiler_params=params(56),
        cost_estimate=cost(6e8 * count, 4 * count),
    )(off, *xs, *weights, *more)


def project_end_kernel(
    off, xa, xb, wq, wk, wv, acc_in, cosine, sine, gain_q, gain_k,
    q_rot, q_raw, k_rot, k_raw, v_out, squares, sq, sk, sv, sems, x_s, a_s, c_s, s_s, gq_s, gk_s, isems,
):
    stages = (sq, sk, sv)
    copies = fetch(
        [
            (xa, x_s.at[pl.ds(0, SPAN), :]), (xb, x_s.at[pl.ds(SPAN, SPAN), :]), (acc_in, a_s),
            (cosine, c_s), (sine, s_s), (gain_q, gq_s), (gain_k, gk_s),
        ],
        isems,
    )
    copies += fetch_rows(off, (wq, wk, wv), stages, sems)
    for copy in copies:
        copy.wait()
    cs, sn, gain_q, gain_k = c_s[...], s_s[...], gq_s, gk_s
    raw = a_s[...] + product_of(x_s[...], stages, 0)
    k = raw[:, R : R + D]
    k_raw[...] = k
    k_rot[...] = turn(k * gain_k[...], cs, sn)
    v_out[...] = raw[:, R + D :].astype(BF)
    squares[1:2, :] = lane_sums(k * k)
    total = None
    for h in range(G):
        q = raw[:, h * D : (h + 1) * D]
        total = q * q if total is None else total + q * q
        rotated = turn(q * gain_q[:, h * D : (h + 1) * D], cs, sn)
        for i in range(2):
            q_rot[i, h * SPAN : (h + 1) * SPAN, :] = rotated[i * SPAN : (i + 1) * SPAN]
    q_raw[...] = raw[:, :R]
    squares[0:1, :] = lane_sums(total)


def project_end(off, xa, xb, weights, acc, cosine, sine, gain_q, gain_k):
    rows = acc.shape[0]
    feats = xa.shape[1]
    outs = (
        jax.ShapeDtypeStruct((2, R, D), F32),
        jax.ShapeDtypeStruct((rows, R), F32),
        jax.ShapeDtypeStruct((rows, D), F32),
        jax.ShapeDtypeStruct((rows, D), F32),
        jax.ShapeDtypeStruct((rows, D), BF),
        jax.ShapeDtypeStruct((2, rows), F32),
    )
    return pl.pallas_call(
        project_end_kernel,
        out_shape=outs,
        grid_spec=pltpu.PrefetchScalarGridSpec(
            num_scalar_prefetch=1,
            grid=(),
            in_specs=[HB] * 10,
            out_specs=(VM,) * 6,
            scratch_shapes=stages_of(weights, 1, feats)
            + [
                pltpu.VMEM((rows, feats), BF),
                pltpu.VMEM(acc.shape, F32),
                pltpu.VMEM(cosine.shape, F32),
                pltpu.VMEM(sine.shape, F32),
                pltpu.VMEM(gain_q.shape, F32),
                pltpu.VMEM(gain_k.shape, F32),
                pltpu.SemaphoreType.DMA((7,)),
            ],
        ),
        compiler_params=params(56),
        cost_estimate=cost(6e8, 6),
    )(off, xa, xb, *weights, acc, cosine, sine, gain_q, gain_k)


def join_kernel(*refs):
    at = 0
    for ref in refs[:-1]:
        n = ref.shape[0]
        refs[-1][at : at + n, :] = ref[...]
        at += n


def join(*xs):
    rows = sum(x.shape[0] for x in xs)
    return pl.pallas_call(
        join_kernel,
        out_shape=jax.ShapeDtypeStruct((rows,) + xs[0].shape[1:], xs[0].dtype),
        in_specs=[VM] * len(xs),
        out_specs=VM,
        compiler_params=params(8),
        cost_estimate=cost(0, 1),
    )(*xs)


def spans_at(ref, loc, which, j):
    return jnp.concatenate(
        [
            ref[pl.ds(pl.multiple_of(loc[which, CH * j + t] * SPAN, SPAN), SPAN), :]
            for t in range(CH)
        ],
        axis=0,
    )


def load_pieces(refs, whole, core, sems):
    count = len(refs) // 2
    copies = []
    for n, src in enumerate(refs):
        rows = src.shape[0]
        to = core if n < count else 1 - core
        copy = pltpu.make_async_copy(
            src, whole.at[to, pl.ds((n % count) * rows, rows), :], sems.at[n]
        )
        copy.start()
        copies.append(copy)
    for copy in copies:
        copy.wait()


def fwd_kernel(loc, own, q_in, *refs):
    kv_refs, w_ref, (lse_ref, o_ref, kv_out, out) = (
        refs[:PIECES], refs[PIECES], refs[PIECES + 1 : PIECES + 5],
    )
    kv, w_s, y_s, m_s, acc_s, q_ref, sems, wsems, kvsem, ysems, qsem = refs[PIECES + 5 :]
    q_copies = fetch([(q_in, q_ref)], qsem)
    load_pieces(kv_refs, kv, own[2], sems)
    keep = fetch([(kv, kv_out)], kvsem)
    block = y_s.shape[2]
    w_copies = fetch(
        [(w_ref.at[:, pl.ds(b * block, block)], w_s.at[b]) for b in range(4)], wsems
    )
    for copy in q_copies:
        copy.wait()
    k_ref, v_ref = kv.at[0], kv.at[1]
    ones = (lax.broadcasted_iota(jnp.int32, (KC, D), 1) == 0).astype(BF)
    for i in range(2):
        c = own[i]
        m_s[...] = jnp.full_like(m_s, NEG)
        acc_s[...] = jnp.zeros_like(acc_s)

        def step(j, masked):
            kk = spans_at(k_ref, loc, 0, j)
            vv = jnp.concatenate([spans_at(v_ref, loc, 1, j), ones], axis=1)
            for h in range(G):
                at = slice(h * SPAN, (h + 1) * SPAN)
                s = nt(q_ref[i, at, :], kk)
                if masked:
                    key = j * KC + lax.broadcasted_iota(jnp.int32, (SPAN, KC), 1)
                    row = c * SPAN + lax.broadcasted_iota(jnp.int32, (SPAN, KC), 0)
                    s = jnp.where(key <= row, s, NEG)
                m = m_s[at, :]
                new = jnp.maximum(m, jnp.max(s, axis=1, keepdims=True))
                shrink = jnp.exp2((m - new) * (SCALE * LOG2E))
                p = jnp.exp2((s - new[:, :1]) * (SCALE * LOG2E))
                m_s[at, :] = new
                acc_s[at, :] = acc_s[at, :] * shrink[:, :1] + nn(p.astype(BF), vv)

        last = c // CH

        def body(j, _):
            step(j, False)
            return 0

        lax.fori_loop(0, last, body, 0)
        step(last, True)
        total = acc_s[:, D : D + 1]
        o_ref[i] = (acc_s[:, :D] / total).astype(BF)
        lse = m_s[...] * (SCALE * LOG2E) + jnp.log2(jnp.broadcast_to(total, (R, D)))
        lse_ref[i] = lse.T[0:1, :]
    x = jnp.concatenate(
        [
            jnp.concatenate(
                [o_ref[i, h * SPAN : (h + 1) * SPAN, :] for h in range(G)], axis=1
            )
            for i in range(2)
        ],
        axis=0,
    )
    y_copies = []
    for b in range(4):
        w_copies[b].wait()
        y_s[b] = nn(x, w_s[b]).astype(BF)
        copy = pltpu.make_async_copy(y_s.at[b], out.at[b], ysems.at[b])
        copy.start()
        y_copies.append(copy)
    for copy in keep + y_copies:
        copy.wait()


def attn_fwd(table, own, q, pieces, w_out):
    n = sum(x.shape[0] for x in pieces) // 2
    block = w_out.shape[1] // 4
    return pl.pallas_call(
        fwd_kernel,
        out_shape=(
            jax.ShapeDtypeStruct((2, 1, R), F32),
            jax.ShapeDtypeStruct((2, R, D), BF),
            jax.ShapeDtypeStruct((2, n, D), BF),
            jax.ShapeDtypeStruct((4, 2 * SPAN, block), BF),
        ),
        grid_spec=pltpu.PrefetchScalarGridSpec(
            num_scalar_prefetch=2,
            grid=(),
            in_specs=[HB] * (PIECES + 2),
            out_specs=(VM, VM, FAR, FAR),
            scratch_shapes=[
                pltpu.VMEM((2, n, D), BF),
                pltpu.VMEM((4, R, block), BF),
                pltpu.VMEM((4, 2 * SPAN, block), BF),
                pltpu.VMEM((R, D), F32),
                pltpu.VMEM((R, 2 * D), F32),
                pltpu.VMEM((2, R, D), BF),
                pltpu.SemaphoreType.DMA((PIECES,)),
                pltpu.SemaphoreType.DMA((4,)),
                pltpu.SemaphoreType.DMA((1,)),
                pltpu.SemaphoreType.DMA((4,)),
                pltpu.SemaphoreType.DMA((1,)),
            ],
        ),
        compiler_params=params(56),
        cost_estimate=cost(1.8e10, 12, 6e6),
    )(table, own, q, *pieces, w_out)


def bwd_kernel(
    loc, own, *refs,
):
    ins, g_ref, w_ref, (up_ref, mix_ref, gain_ref, mine_ref, theirs_ref) = (
        refs[:8], refs[8], refs[9], refs[10:15],
    )
    stages, (do_ref, g_s, w_s, dkv, dqa, gsems, sems) = refs[15:23], refs[23:]
    q_ref, kv, o_ref, lse_ref, cosine, sine, gain_q, unit_ref = stages
    core = own[2]
    block = g_s.shape[2]
    g_pairs = []
    for b in range(4):
        cols = pl.ds(b * block, block)
        g_pairs += [(w_ref.at[:, cols], w_s.at[b]), (g_ref.at[:, cols], g_s.at[b])]
    g_copies = fetch(g_pairs, gsems)
    copies = fetch(list(zip(ins, stages)), sems)
    late = copies[4:]
    copies = copies[:4]
    k_ref, v_ref = kv.at[0], kv.at[1]
    dkv[...] = jnp.zeros_like(dkv)
    dqa[...] = jnp.zeros_like(dqa)
    grad = None
    for b in range(4):
        g_copies[2 * b].wait()
        g_copies[2 * b + 1].wait()
        part = nt(g_s[b], w_s[b])
        grad = part if grad is None else grad + part
    for i in range(2):
        for h in range(G):
            do_ref[i, h * SPAN : (h + 1) * SPAN, :] = grad[
                i * SPAN : (i + 1) * SPAN, h * D : (h + 1) * D
            ].astype(BF)
    for copy in copies:
        copy.wait()
    for i in range(2):
        c = own[i]
        q, do, lse = q_ref[i], do_ref[i], lse_ref[i]
        delta = lane_sums(do.astype(F32) * o_ref[i].astype(F32))

        def step(j, masked):
            kk = spans_at(k_ref, loc, 0, j)
            vv = spans_at(v_ref, loc, 1, j)
            p = jnp.exp2(nt(kk, q) * (SCALE * LOG2E) - lse)
            if masked:
                key = j * KC + lax.broadcasted_iota(jnp.int32, (KC, R), 0)
                row = c * SPAN + lax.rem(lax.broadcasted_iota(jnp.int32, (KC, R), 1), SPAN)
                p = jnp.where(key <= row, p, 0.0)
            ds = (p * (nt(vv, do) - delta)).astype(BF)
            dqa[i] += tn(kk, ds)
            dv = nn(p.astype(BF), do)
            dk = nn(ds, q) * SCALE
            for t in range(CH):
                part = slice(t * SPAN, (t + 1) * SPAN)
                at = pl.ds(pl.multiple_of(loc[2, CH * j + t] * SPAN, SPAN), SPAN)
                dkv[0, at, :] += dk[part]
                at = pl.ds(pl.multiple_of(loc[3, CH * j + t] * SPAN, SPAN), SPAN)
                dkv[1, at, :] += dv[part]

        last = c // CH

        def body(j, _):
            step(j, False)
            return 0

        lax.fori_loop(0, last, body, 0)
        step(last, True)
    for copy in late:
        copy.wait()
    mine_ref[...] = dkv[core].astype(BF)
    theirs_ref[...] = dkv[1 - core].astype(BF)
    for i in range(2):
        rows = slice(i * SPAN, (i + 1) * SPAN)
        cs, sn = cosine[rows, :], -sine[rows, :]
        mix = None
        for h in range(G):
            cols = slice(h * D, (h + 1) * D)
            grad = turn((dqa[i, :, cols] * SCALE).T, cs, sn)
            unit = unit_ref[rows, cols]
            up = grad * gain_q[:, cols]
            up_ref[rows, cols] = up
            mix = up * unit if mix is None else mix + up * unit
            gain = jnp.sum(grad * unit, axis=0, keepdims=True)
            if i == 0:
                gain_ref[:, cols] = gain
            else:
                gain_ref[:, cols] += gain
        mix_ref[:, rows] = lane_sums(mix)


def attn_bwd(table, own, q, kv, grad_part, w_out, o, lse, cosine, sine, gain_q, unit):
    block = w_out.shape[1] // 4
    n = kv.shape[1]
    rows = 2 * SPAN
    return pl.pallas_call(
        bwd_kernel,
        out_shape=(
            jax.ShapeDtypeStruct((rows, R), F32),
            jax.ShapeDtypeStruct((1, rows), F32),
            jax.ShapeDtypeStruct((1, R), F32),
            jax.ShapeDtypeStruct((n, D), BF),
            jax.ShapeDtypeStruct((n, D), BF),
        ),
        grid_spec=pltpu.PrefetchScalarGridSpec(
            num_scalar_prefetch=2,
            grid=(),
            in_specs=[HB] * 10,
            out_specs=(VM,) * 5,
            scratch_shapes=[
                pltpu.VMEM(x.shape, x.dtype)
                for x in (q, kv, o, lse, cosine, sine, gain_q, unit)
            ]
            + [
                pltpu.VMEM((2, R, D), BF),
                pltpu.VMEM((4, rows, block), BF),
                pltpu.VMEM((4, R, block), BF),
                pltpu.VMEM((2, n, D), F32),
                pltpu.VMEM((2, D, R), F32),
                pltpu.SemaphoreType.DMA((8,)),
                pltpu.SemaphoreType.DMA((8,)),
            ],
        ),
        compiler_params=params(56),
        cost_estimate=cost(2.2e10, 12, 6e6),
    )(table, own, q, kv, o, lse, cosine, sine, gain_q, unit, grad_part, w_out)


def key_gain_kernel(
    loc, own, kv_in, mine_in, theirs_in, cos_r, sin_r, cos_s, sin_s, out, k_s, g_s, sems
):
    core = own[2]
    key_copy = pltpu.make_async_copy(kv_in.at[0], k_s, sems.at[0])
    key_copy.start()

    @pl.when(core == 0)
    def _():
        pltpu.make_async_copy(mine_in, g_s, sems.at[1]).start()

    @pl.when(core != 0)
    def _():
        pltpu.make_async_copy(theirs_in, g_s, sems.at[1]).start()

    key_copy.wait()
    pltpu.make_async_copy(mine_in, g_s, sems.at[1]).wait()
    cr, sr = cos_r[...], sin_r[...]

    def body(s, sums):
        plain, by_cos, by_sin = sums
        k = k_s[pl.ds(pl.multiple_of(loc[0, s] * SPAN, SPAN), SPAN), :].astype(F32)
        g = g_s[pl.ds(pl.multiple_of(loc[2, s] * SPAN, SPAN), SPAN), :].astype(F32)
        cs, sn = cos_s[pl.ds(s, 1), :], sin_s[pl.ds(s, 1), :]
        same = k * g
        cross = g * pltpu.roll(k, D // 2, 1)
        return (
            plain + same,
            by_cos + same * (cs * cr - sn * sr),
            by_sin + cross * (sn * cr + cs * sr),
        )

    zero = jnp.zeros((SPAN, D), F32)
    plain, by_cos, by_sin = lax.fori_loop(0, loc.shape[1], body, (zero, zero, zero), unroll=4)

    def over_rows(x):
        return jnp.broadcast_to(jnp.sum(x, axis=0, keepdims=True), (8, D))

    plain, by_cos, by_sin = over_rows(plain), over_rows(by_cos), over_rows(by_sin)
    half = D // 2
    sign = jnp.where(lax.broadcasted_iota(jnp.int32, (8, D), 1) < half, 1.0, -1.0)
    total = (
        plain
        + pltpu.roll(plain, half, 1)
        + by_cos
        - pltpu.roll(by_cos, half, 1)
        + sign * (by_sin + pltpu.roll(by_sin, half, 1))
    )
    out[...] = 0.5 * total[0:1]


def key_gain_of(table, own, kv, mine, theirs, tables):
    n = kv.shape[1]
    return pl.pallas_call(
        key_gain_kernel,
        out_shape=jax.ShapeDtypeStruct((1, D), F32),
        grid_spec=pltpu.PrefetchScalarGridSpec(
            num_scalar_prefetch=2,
            grid=(),
            in_specs=[HB] * 3 + [VM] * 4,
            out_specs=VM,
            scratch_shapes=[
                pltpu.VMEM((n, D), BF),
                pltpu.VMEM((n, D), BF),
                pltpu.SemaphoreType.DMA((2,)),
            ],
        ),
        compiler_params=params(56),
        cost_estimate=cost(1e9, 6),
    )(table, own, kv, mine, theirs, *tables)


def query_kernel(*refs):
    ins, w_ref, out, stages = refs[:4], refs[4], refs[5], refs[6:10]
    w_s, y_s, sems, ysems, isems = refs[10:]
    block = w_s.shape[1]
    inputs = fetch(list(zip(ins, stages)), isems)
    up, unit, mix, inv = stages
    copies = fetch([(w_ref.at[pl.ds(b * block, block), :], w_s.at[b]) for b in range(4)], sems)
    rows = up.shape[0]

    for copy in inputs:
        copy.wait()

    def column(ref):
        return jnp.broadcast_to(ref[...], (D, rows)).T[:, :1]

    x = (column(inv) * (up[...] - unit[...] * (column(mix) * (1.0 / Q_CHANNELS)))).astype(BF)
    y_copies = []
    for b in range(4):
        copies[b].wait()
        y_s[b] = nt(x, w_s[b]).astype(BF)
        copy = pltpu.make_async_copy(y_s.at[b], out.at[b], ysems.at[b])
        copy.start()
        y_copies.append(copy)
    for copy in y_copies:
        copy.wait()


def query_partial_of(up, unit, mix, inv, w_query):
    rows = up.shape[0]
    feats = w_query.shape[0]
    block = feats // 4
    return pl.pallas_call(
        query_kernel,
        out_shape=jax.ShapeDtypeStruct((4, rows, block), BF),
        in_specs=[HB] * 5,
        out_specs=FAR,
        scratch_shapes=[pltpu.VMEM(x.shape, x.dtype) for x in (up, unit, mix, inv)]
        + [
            pltpu.VMEM((4, block, R), BF),
            pltpu.VMEM((4, rows, block), BF),
            pltpu.SemaphoreType.DMA((4,)),
            pltpu.SemaphoreType.DMA((4,)),
            pltpu.SemaphoreType.DMA((4,)),
        ],
        compiler_params=params(56),
        cost_estimate=cost(1.7e9, 9),
    )(up, unit, mix, inv, w_query)


def last_kernel(g0, g1, g2, g3, u0, u1, u2, u3, inv, w, query_side, out):
    gs, us = (g0, g1, g2, g3), (u0, u1, u2, u3)
    mix = None
    for g, u in zip(gs, us):
        part = g[:, :D].astype(F32) * u[...].astype(F32)
        mix = part if mix is None else mix + part
    mix = jnp.sum(mix, axis=1, keepdims=True) * (1.0 / K_CHANNELS)
    total = query_side[...].astype(F32)
    for n, (g, u) in enumerate(zip(gs, us)):
        raw = (inv[...] * (g[:, :D].astype(F32) - u[...].astype(F32) * mix)).astype(BF)
        total = total + nt(jnp.concatenate([raw, g[:, D:]], axis=1), w[n])
    out[...] = total.astype(BF)


def last_of(grads, units, inv, w, query_side):
    return pl.pallas_call(
        last_kernel,
        out_shape=jax.ShapeDtypeStruct(query_side.shape, BF),
        in_specs=[VM] * 11,
        out_specs=VM,
        compiler_params=params(56),
        cost_estimate=cost(7e8, 5),
    )(*grads, *units, inv, w, query_side)

QUERY_HEADS = 20
KEY_VALUE_HEADS = 4
Q_CHANNELS = QUERY_HEADS * D
K_CHANNELS = KEY_VALUE_HEADS * D
N_Y, N_Z, N_CORE, N_TP = 4, 4, 2, 4


def ctx_index(y, z, c):
    return (y * N_Z + z) * N_CORE + c


def ctx_pairs(move):
    return [
        (ctx_index(y, z, c), ctx_index(*move(y, z, c)))
        for y in range(N_Y)
        for z in range(N_Z)
        for c in range(N_CORE)
    ]


def shift_first(x, d):
    return lax.ppermute(
        x,
        "ctx",
        ctx_pairs(lambda y, z, c: ((y + c * d) % N_Y, (z + (1 - c) * d) % N_Z, c)),
    )


def shift_second(x, d):
    return lax.ppermute(
        x,
        "ctx",
        ctx_pairs(lambda y, z, c: ((y + (1 - c) * d) % N_Y, (z + c * d) % N_Z, c)),
    )


def swap_core(x):
    return lax.ppermute(x, "ctx", ctx_pairs(lambda y, z, c: (y, z, 1 - c)))


def shift_tp(x, d):
    return lax.ppermute(x, "tp", [(i, (i + d) % N_TP) for i in range(N_TP)])


def shifts(shift, x):
    return [x] + [shift(x, d) for d in DIST[1:]]


def sum_tp(x):
    one, three, two = (shift_tp(x, d) for d in DIST[1:])
    return (x + one) + (three + two)


def sum_core_z(x):
    x = x + swap_core(x)
    x = x + lax.ppermute(x, "ctx", ctx_pairs(lambda y, z, c: (y, z ^ 1, c)))
    return x + lax.ppermute(x, "ctx", ctx_pairs(lambda y, z, c: (y, 3 - z, c)))


def sum_y(x):
    x = x + lax.ppermute(x, "ctx", ctx_pairs(lambda y, z, c: (y ^ 1, z, c)))
    return x + lax.ppermute(x, "ctx", ctx_pairs(lambda y, z, c: (3 - y, z, c)))


def after(x, *others):
    return lax.optimization_barrier((x,) + others)[0]


def outgoing(x):
    rows = x.shape[0] // 4
    return [x[d * rows : (d + 1) * rows].astype(BF) for d in DIST[1:]], x[:rows]


def add_up(total, arrived):
    for x in arrived:
        total = total + x.astype(F32)
    return total


def local(tokens, span_order, w_query, w_key, value_weight, w_out, gain_query, gain_key, out_grad):
    rows, feats = tokens.shape
    me = lax.axis_index("ctx")
    tp = lax.axis_index("tp")
    my_y, my_z, my_c = me // 8, (me // 2) % 4, me % 2

    mid = rows // 2
    with jax.named_scope("gather_tokens"):
        upper, lower = tokens[:mid], tokens[mid:]
        left_a = shift_tp(upper, 1)
        right_b = shift_tp(lower, 3)
        left_b = shift_tp(lower, 1)
        right_a = shift_tp(upper, 3)

    place = jnp.arange(64, dtype=jnp.int32)
    stored = jnp.sum(jnp.where(span_order[None, :] == place[:, None], place[None, :], 0), axis=1)
    src, half = stored // 2, stored % 2
    src_y, src_z, src_c = src // 8, (src // 2) % 4, src % 2
    to_y, to_z = (src_y - my_y) % 4, (src_z - my_z) % 4
    back_y, back_z = (4 - to_y) % 4, (4 - to_z) % 4
    slot_y = jnp.where(back_y >= 2, 5 - back_y, back_y)
    slot_z = jnp.where(back_z >= 2, 5 - back_z, back_z)
    table = jnp.stack(
        [
            ((slot_y * 4 + slot_z) * 2 + src_c) * 2 + half,
            ((slot_z * 4 + slot_y) * 2 + 1 - src_c) * 2 + half,
            ((to_z * 4 + to_y) * 2 + src_c) * 2 + half,
            ((to_y * 4 + to_z) * 2 + src_c) * 2 + half,
        ]
    ).astype(jnp.int32)
    own = lax.dynamic_slice_in_dim(span_order, 2 * me, 2)
    own = jnp.concatenate([own, my_c[None]]).astype(jnp.int32)

    query_pos = (own[:2, None] * SPAN + jnp.arange(SPAN)[None, :]).reshape(-1)
    frequency = jnp.exp(jnp.arange(D // 2).astype(F32) * (-2.0 * math.log(500000.0) / D))
    angles = query_pos.astype(F32)[:, None] * frequency[None, :]
    cosine, sine = jnp.cos(angles), jnp.sin(angles)
    cosine = jnp.concatenate([cosine, cosine], axis=1)
    sine = jnp.concatenate([-sine, sine], axis=1)

    offs = jnp.stack([(tp - d) % 4 for d in DIST]).astype(jnp.int32)
    twice = 2.0 * jnp.concatenate([frequency, frequency])[None, :]
    by_row = jnp.arange(SPAN).astype(F32)[:, None] * twice
    by_span = (SPAN * jnp.arange(64)).astype(F32)[:, None] * twice
    tables = (jnp.cos(by_row), jnp.sin(by_row), jnp.cos(by_span), jnp.sin(by_span))

    with jax.named_scope("weight_rows"):
        share = feats // 32
        cut = []
        for d in DIST:
            start = feats * ((tp + d) % 4) + share * me
            piece = jnp.concatenate(
                [lax.dynamic_slice_in_dim(w, start, share, 0) for w in (w_key, value_weight)],
                axis=1,
            )
            cut.append(shift_tp(piece, d) if d else piece)
        cut = jnp.stack(cut)

    with jax.named_scope("gather_tokens"):
        weights = (w_query, w_key, value_weight)
        acc = project(offs[:1], ((tokens,),), weights)
        left_a, right_b, left_b, right_a, cosine, sine, offs, table, own, cut, acc, *tables = (
            lax.optimization_barrier(
                (left_a, right_b, left_b, right_a, cosine, sine, offs, table, own, cut, acc, *tables)
            )
        )
        far_a = shift_tp(left_a, 1)
        far_b = shift_tp(right_b, 3)
        acc = project(offs[1:3], ((left_a, left_b), (right_a, right_b)), weights, acc)
        far_a, far_b, acc = lax.optimization_barrier((far_a, far_b, acc))
    gain_q, gain_k = gain_query[None, :], gain_key[None, :]
    q_rot, q_raw, k_rot, k_raw, value, squares = project_end(
        offs[3:], far_a, far_b, weights, acc, cosine, sine, gain_q, gain_k
    )
    with jax.named_scope("norm_sums"):
        squares = sum_tp(squares)
    query_inv = lax.rsqrt(squares[0] / Q_CHANNELS + 1e-06)[:, None]
    key_inv = lax.rsqrt(squares[1] / K_CHANNELS + 1e-06)[:, None]
    key = (k_rot * key_inv).astype(BF)

    with jax.named_scope("gather_keys_values"):
        first_core = my_c == 0
        mine = jnp.where(first_core, key, value)
        pair = join(mine, swap_core(jnp.where(first_core, value, key)))
        plane = join(*shifts(shift_first, pair))
        mine = shifts(shift_second, plane)
    with jax.named_scope("weight_rows"):
        w_rows = lax.all_gather(after(cut, pair), "ctx", axis=0, tiled=False)

    query_unit = q_raw * query_inv
    key_unit = (k_raw * key_inv).astype(BF)
    query = (
        (q_rot.reshape(2, G, SPAN, D) * query_inv.reshape(2, 1, SPAN, 1)).astype(BF).reshape(2, R, D)
    )
    with jax.named_scope("gather_key_units"):
        key_units = shifts(shift_tp, key_unit)

    with jax.named_scope("gather_out_grad"):
        grad_part = lax.all_gather(after(out_grad, far_a, far_b), "tp", axis=1, tiled=True)

    with jax.named_scope("swap_keys_values"):
        last, query, query_unit, *key_units = lax.optimization_barrier(
            (mine[3], query, query_unit, *key_units)
        )
        mine = mine[:3] + [last]
        pieces = (*mine, *(swap_core(x) for x in mine))

    log_total, heads, kv, out_partial = attn_fwd(table, own, query, pieces, w_out)
    attn_out = lax.psum_scatter(out_partial, "tp", scatter_dimension=0, tiled=False)

    up_query, mix_query, gain_part, mine, theirs = attn_bwd(
        table, own, query, kv, grad_part, w_out, heads, log_total,
        cosine, sine, gain_q, query_unit,
    )

    with jax.named_scope("sum_key_value_grads"):
        mix_query = sum_tp(mix_query)
        gain_key_part = key_gain_of(table, own, kv, mine, theirs, tables) / gain_k
        gains = jnp.concatenate([gain_part, gain_key_part], axis=1)
        received, mix_query, w_rows, gains = lax.optimization_barrier(
            (swap_core(theirs), mix_query, w_rows, gains)
        )
        summed = mine.astype(F32) + received.astype(F32)
        sent, total = outgoing(summed)
        *sent, gains = lax.optimization_barrier((*sent, gains))
        arrived = [shift_first(x, d) for x, d in zip(sent, DIST[1:])]
        *arrived, gains, attn_out = lax.optimization_barrier(
            (*arrived, sum_core_z(gains), attn_out)
        )
        sent, total = outgoing(add_up(total, arrived))
        *sent, gains = lax.optimization_barrier((*sent, gains))
        arrived = [shift_second(x, d) for x, d in zip(sent, DIST[1:])]
        *arrived, gains = lax.optimization_barrier((*arrived, sum_y(gains)))
        total = add_up(total, arrived)
        ours, its = total[:rows], total[rows:]
        kept = jnp.where(first_core, ours, its)
        swapped = swap_core(jnp.where(first_core, its, ours))
        key_grad_rot = jnp.where(first_core, kept, swapped)
        value_grad = jnp.where(first_core, swapped, kept).astype(BF)

    with jax.named_scope("query_side"):
        query_partial = query_partial_of(
            up_query, query_unit, mix_query, query_inv.reshape(1, rows), w_query
        )
        query_side = lax.psum_scatter(query_partial, "tp", scatter_dimension=0, tiled=False)

    with jax.named_scope("key_value_side"):
        first, second = key_grad_rot[:, : D // 2], key_grad_rot[:, D // 2 :]
        cs, sn = cosine[:, : D // 2], sine[:, D // 2 :]
        key_grad = jnp.concatenate([first * cs + second * sn, second * cs - first * sn], axis=1)
        w_rows = after(w_rows, query_partial).transpose(1, 0, 2, 3).reshape(4, feats, 2 * D)
        key_grad, w_rows = lax.optimization_barrier((key_grad, w_rows))
        both = jnp.concatenate([(key_grad * gain_k).astype(BF), value_grad], axis=1)
        grads = shifts(shift_tp, both)
        gain_query_grad, gain_key_grad = gains[0, :R], gains[0, R:]
        input_grad = last_of(grads, key_units, key_inv, w_rows, query_side)
    return (attn_out, input_grad, gain_query_grad, gain_key_grad)


def solution(mesh):
    return jax.shard_map(
        local,
        mesh=mesh,
        in_specs=(
            P("ctx", "tp"),
            P(),
            P(None, "tp"),
            P(None, "tp"),
            P(None, "tp"),
            P("tp", None),
            P("tp"),
            P("tp"),
            P("ctx", "tp"),
        ),
        out_specs=(P("ctx", "tp"), P("ctx", "tp"), P("tp"), P("tp")),
        check_vma=False,
    )
```

```python
import math

import jax
import jax.numpy as jnp
from jax import lax
from jax.experimental import pallas as pl
from jax.experimental.pallas import tpu as pltpu
from jax.sharding import PartitionSpec as P

D = 128
SPAN = 128
G = 5
R = G * SPAN
CH = 8
KC = CH * SPAN
SCALE = D**-0.5
LOG2E = math.log2(math.e)
NEG = -1e30
BF = jnp.bfloat16
F32 = jnp.float32
DIST = (0, 1, 3, 2)
PIECES = 8


def nt(a, b):
    return lax.dot_general(a, b, (((1,), (1,)), ((), ())), preferred_element_type=F32)


def tn(a, b):
    return lax.dot_general(a, b, (((0,), (0,)), ((), ())), preferred_element_type=F32)


def nn(a, b):
    return lax.dot_general(a, b, (((1,), (0,)), ((), ())), preferred_element_type=F32)


VM = pl.BlockSpec(memory_space=pltpu.VMEM)
HB = pl.BlockSpec(memory_space=pl.ANY)
FAR = pl.BlockSpec(memory_space=pltpu.HBM)


def params(mib):
    return pltpu.CompilerParams(vmem_limit_bytes=mib * 2**20)


def cost(flops, mib, exps=0):
    return pl.CostEstimate(
        flops=int(flops), bytes_accessed=int(mib * 2**20), transcendentals=int(exps)
    )


def turn(x, cosine, sine):
    return x * cosine + pltpu.roll(x, D // 2, 1) * sine


def lane_sums(x):
    return jnp.sum(x.T, axis=0, keepdims=True)


def fetch(pairs, sems):
    copies = [pltpu.make_async_copy(src, dst, sems.at[n]) for n, (src, dst) in enumerate(pairs)]
    for copy in copies:
        copy.start()
    return copies


def fetch_rows(off, weights, stages, sems):
    pairs = []
    for n in range(stages[0].shape[0]):
        rows = stages[0].shape[1]
        at = pl.ds(pl.multiple_of(off[n] * rows, rows), rows)
        pairs += [(w.at[at, :], s.at[n]) for w, s in zip(weights, stages)]
    return fetch(pairs, sems)


def product_of(x, stages, n):
    return jnp.concatenate([nn(x, s[n]) for s in stages], axis=1)


def project_kernel(off, *refs, count, parts, first):
    xs, weights = refs[: count * parts], refs[count * parts : count * parts + 3]
    stages, sems, x_s, isems, out = refs[-6:-3], refs[-3], refs[-2], refs[-1], refs[-7]
    part_rows = x_s.shape[1] // parts
    inputs = fetch(
        [
            (xs[n * parts + m], x_s.at[n, pl.ds(m * part_rows, part_rows), :])
            for n in range(count)
            for m in range(parts)
        ]
        + ([] if first else [(refs[count * parts + 3], out)]),
        isems,
    )
    copies = fetch_rows(off, weights, stages, sems)
    for copy in inputs:
        copy.wait()
    total = None if first else out[...]
    for n in range(count):
        for copy in copies[3 * n : 3 * n + 3]:
            copy.wait()
        part = product_of(x_s[n], stages, n)
        total = part if total is None else total + part
    out[...] = total


def stages_of(weights, count, feats):
    return [pltpu.VMEM((count, feats, w.shape[1]), BF) for w in weights] + [
        pltpu.SemaphoreType.DMA((3 * count,))
    ]


def project(off, pieces, weights, acc=None):
    parts = len(pieces[0])
    rows, feats = sum(x.shape[0] for x in pieces[0]), pieces[0][0].shape[1]
    width = sum(w.shape[1] for w in weights)
    count = len(pieces)
    xs = [x for piece in pieces for x in piece]
    more = () if acc is None else (acc,)
    return pl.pallas_call(
        lambda *refs: project_kernel(*refs, count=count, parts=parts, first=acc is None),
        out_shape=jax.ShapeDtypeStruct((rows, width), F32),
        grid_spec=pltpu.PrefetchScalarGridSpec(
            num_scalar_prefetch=1,
            grid=(),
            in_specs=[HB] * (len(xs) + 3 + len(more)),
            out_specs=VM,
            scratch_shapes=stages_of(weights, count, feats)
            + [pltpu.VMEM((count, rows, feats), BF), pltpu.SemaphoreType.DMA((len(xs) + 1,))],
        ),
        compiler_params=params(56),
        cost_estimate=cost(6e8 * count, 4 * count),
    )(off, *xs, *weights, *more)


def project_end_kernel(
    off, xa, xb, wq, wk, wv, acc_in, cosine, sine, gain_q, gain_k,
    q_rot, q_raw, k_rot, k_raw, v_out, squares, sq, sk, sv, sems, x_s, a_s, c_s, s_s, gq_s, gk_s, isems,
):
    stages = (sq, sk, sv)
    copies = fetch(
        [
            (xa, x_s.at[pl.ds(0, SPAN), :]), (xb, x_s.at[pl.ds(SPAN, SPAN), :]), (acc_in, a_s),
            (cosine, c_s), (sine, s_s), (gain_q, gq_s), (gain_k, gk_s),
        ],
        isems,
    )
    copies += fetch_rows(off, (wq, wk, wv), stages, sems)
    for copy in copies:
        copy.wait()
    cs, sn, gain_q, gain_k = c_s[...], s_s[...], gq_s, gk_s
    raw = a_s[...] + product_of(x_s[...], stages, 0)
    k = raw[:, R : R + D]
    k_raw[...] = k
    k_rot[...] = turn(k * gain_k[...], cs, sn)
    v_out[...] = raw[:, R + D :].astype(BF)
    squares[1:2, :] = lane_sums(k * k)
    total = None
    for h in range(G):
        q = raw[:, h * D : (h + 1) * D]
        total = q * q if total is None else total + q * q
        rotated = turn(q * gain_q[:, h * D : (h + 1) * D], cs, sn)
        for i in range(2):
            q_rot[i, h * SPAN : (h + 1) * SPAN, :] = rotated[i * SPAN : (i + 1) * SPAN]
    q_raw[...] = raw[:, :R]
    squares[0:1, :] = lane_sums(total)


def project_end(off, xa, xb, weights, acc, cosine, sine, gain_q, gain_k):
    rows = acc.shape[0]
    feats = xa.shape[1]
    outs = (
        jax.ShapeDtypeStruct((2, R, D), F32),
        jax.ShapeDtypeStruct((rows, R), F32),
        jax.ShapeDtypeStruct((rows, D), F32),
        jax.ShapeDtypeStruct((rows, D), F32),
        jax.ShapeDtypeStruct((rows, D), BF),
        jax.ShapeDtypeStruct((2, rows), F32),
    )
    return pl.pallas_call(
        project_end_kernel,
        out_shape=outs,
        grid_spec=pltpu.PrefetchScalarGridSpec(
            num_scalar_prefetch=1,
            grid=(),
            in_specs=[HB] * 10,
            out_specs=(VM,) * 6,
            scratch_shapes=stages_of(weights, 1, feats)
            + [
                pltpu.VMEM((rows, feats), BF),
                pltpu.VMEM(acc.shape, F32),
                pltpu.VMEM(cosine.shape, F32),
                pltpu.VMEM(sine.shape, F32),
                pltpu.VMEM(gain_q.shape, F32),
                pltpu.VMEM(gain_k.shape, F32),
                pltpu.SemaphoreType.DMA((7,)),
            ],
        ),
        compiler_params=params(56),
        cost_estimate=cost(6e8, 6),
    )(off, xa, xb, *weights, acc, cosine, sine, gain_q, gain_k)


def join_kernel(*refs):
    at = 0
    for ref in refs[:-1]:
        n = ref.shape[0]
        refs[-1][at : at + n, :] = ref[...]
        at += n


def join(*xs):
    rows = sum(x.shape[0] for x in xs)
    return pl.pallas_call(
        join_kernel,
        out_shape=jax.ShapeDtypeStruct((rows,) + xs[0].shape[1:], xs[0].dtype),
        in_specs=[VM] * len(xs),
        out_specs=VM,
        compiler_params=params(8),
        cost_estimate=cost(0, 1),
    )(*xs)


def spans_at(ref, loc, which, j):
    return jnp.concatenate(
        [
            ref[pl.ds(pl.multiple_of(loc[which, CH * j + t] * SPAN, SPAN), SPAN), :]
            for t in range(CH)
        ],
        axis=0,
    )


def load_pieces(refs, whole, core, sems):
    count = len(refs) // 2
    copies = []
    for n, src in enumerate(refs):
        rows = src.shape[0]
        to = core if n < count else 1 - core
        copy = pltpu.make_async_copy(
            src, whole.at[to, pl.ds((n % count) * rows, rows), :], sems.at[n]
        )
        copy.start()
        copies.append(copy)
    for copy in copies:
        copy.wait()


def fwd_kernel(loc, own, q_in, *refs):
    kv_refs, w_ref, (lse_ref, o_ref, kv_out, out) = (
        refs[:PIECES], refs[PIECES], refs[PIECES + 1 : PIECES + 5],
    )
    kv, w_s, y_s, m_s, acc_s, q_ref, sems, wsems, kvsem, ysems, qsem = refs[PIECES + 5 :]
    q_copies = fetch([(q_in, q_ref)], qsem)
    load_pieces(kv_refs, kv, own[2], sems)
    keep = fetch([(kv, kv_out)], kvsem)
    block = y_s.shape[2]
    w_copies = fetch(
        [(w_ref.at[:, pl.ds(b * block, block)], w_s.at[b]) for b in range(4)], wsems
    )
    for copy in q_copies:
        copy.wait()
    k_ref, v_ref = kv.at[0], kv.at[1]
    ones = (lax.broadcasted_iota(jnp.int32, (KC, D), 1) == 0).astype(BF)
    for i in range(2):
        c = own[i]
        m_s[...] = jnp.full_like(m_s, NEG)
        acc_s[...] = jnp.zeros_like(acc_s)

        def step(j, masked):
            kk = spans_at(k_ref, loc, 0, j)
            vv = jnp.concatenate([spans_at(v_ref, loc, 1, j), ones], axis=1)
            for h in range(G):
                at = slice(h * SPAN, (h + 1) * SPAN)
                s = nt(q_ref[i, at, :], kk)
                if masked:
                    key = j * KC + lax.broadcasted_iota(jnp.int32, (SPAN, KC), 1)
                    row = c * SPAN + lax.broadcasted_iota(jnp.int32, (SPAN, KC), 0)
                    s = jnp.where(key <= row, s, NEG)
                m = m_s[at, :]
                new = jnp.maximum(m, jnp.max(s, axis=1, keepdims=True))
                shrink = jnp.exp2((m - new) * (SCALE * LOG2E))
                p = jnp.exp2((s - new[:, :1]) * (SCALE * LOG2E))
                m_s[at, :] = new
                acc_s[at, :] = acc_s[at, :] * shrink[:, :1] + nn(p.astype(BF), vv)

        last = c // CH

        def body(j, _):
            step(j, False)
            return 0

        lax.fori_loop(0, last, body, 0)
        step(last, True)
        total = acc_s[:, D : D + 1]
        o_ref[i] = (acc_s[:, :D] / total).astype(BF)
        lse = m_s[...] * (SCALE * LOG2E) + jnp.log2(jnp.broadcast_to(total, (R, D)))
        lse_ref[i] = lse.T[0:1, :]
    x = jnp.concatenate(
        [
            jnp.concatenate(
                [o_ref[i, h * SPAN : (h + 1) * SPAN, :] for h in range(G)], axis=1
            )
            for i in range(2)
        ],
        axis=0,
    )
    y_copies = []
    for b in range(4):
        w_copies[b].wait()
        y_s[b] = nn(x, w_s[b]).astype(BF)
        copy = pltpu.make_async_copy(y_s.at[b], out.at[b], ysems.at[b])
        copy.start()
        y_copies.append(copy)
    for copy in keep + y_copies:
        copy.wait()


def attn_fwd(table, own, q, pieces, w_out):
    n = sum(x.shape[0] for x in pieces) // 2
    block = w_out.shape[1] // 4
    return pl.pallas_call(
        fwd_kernel,
        out_shape=(
            jax.ShapeDtypeStruct((2, 1, R), F32),
            jax.ShapeDtypeStruct((2, R, D), BF),
            jax.ShapeDtypeStruct((2, n, D), BF),
            jax.ShapeDtypeStruct((4, 2 * SPAN, block), BF),
        ),
        grid_spec=pltpu.PrefetchScalarGridSpec(
            num_scalar_prefetch=2,
            grid=(),
            in_specs=[HB] * (PIECES + 2),
            out_specs=(VM, VM, FAR, FAR),
            scratch_shapes=[
                pltpu.VMEM((2, n, D), BF),
                pltpu.VMEM((4, R, block), BF),
                pltpu.VMEM((4, 2 * SPAN, block), BF),
                pltpu.VMEM((R, D), F32),
                pltpu.VMEM((R, 2 * D), F32),
                pltpu.VMEM((2, R, D), BF),
                pltpu.SemaphoreType.DMA((PIECES,)),
                pltpu.SemaphoreType.DMA((4,)),
                pltpu.SemaphoreType.DMA((1,)),
                pltpu.SemaphoreType.DMA((4,)),
                pltpu.SemaphoreType.DMA((1,)),
            ],
        ),
        compiler_params=params(56),
        cost_estimate=cost(1.8e10, 12, 6e6),
    )(table, own, q, *pieces, w_out)


def bwd_kernel(
    loc, own, *refs,
):
    ins, g_ref, w_ref, (up_ref, mix_ref, gain_ref, mine_ref, theirs_ref) = (
        refs[:8], refs[8], refs[9], refs[10:15],
    )
    stages, (do_ref, g_s, w_s, dkv, dqa, gsems, sems) = refs[15:23], refs[23:]
    q_ref, kv, o_ref, lse_ref, cosine, sine, gain_q, unit_ref = stages
    core = own[2]
    block = g_s.shape[2]
    g_pairs = []
    for b in range(4):
        cols = pl.ds(b * block, block)
        g_pairs += [(w_ref.at[:, cols], w_s.at[b]), (g_ref.at[:, cols], g_s.at[b])]
    g_copies = fetch(g_pairs, gsems)
    copies = fetch(list(zip(ins, stages)), sems)
    late = copies[4:]
    copies = copies[:4]
    k_ref, v_ref = kv.at[0], kv.at[1]
    dkv[...] = jnp.zeros_like(dkv)
    dqa[...] = jnp.zeros_like(dqa)
    grad = None
    for b in range(4):
        g_copies[2 * b].wait()
        g_copies[2 * b + 1].wait()
        part = nt(g_s[b], w_s[b])
        grad = part if grad is None else grad + part
    for i in range(2):
        for h in range(G):
            do_ref[i, h * SPAN : (h + 1) * SPAN, :] = grad[
                i * SPAN : (i + 1) * SPAN, h * D : (h + 1) * D
            ].astype(BF)
    for copy in copies:
        copy.wait()
    for i in range(2):
        c = own[i]
        q, do, lse = q_ref[i], do_ref[i], lse_ref[i]
        delta = lane_sums(do.astype(F32) * o_ref[i].astype(F32))

        def step(j, masked):
            kk = spans_at(k_ref, loc, 0, j)
            vv = spans_at(v_ref, loc, 1, j)
            p = jnp.exp2(nt(kk, q) * (SCALE * LOG2E) - lse)
            if masked:
                key = j * KC + lax.broadcasted_iota(jnp.int32, (KC, R), 0)
                row = c * SPAN + lax.rem(lax.broadcasted_iota(jnp.int32, (KC, R), 1), SPAN)
                p = jnp.where(key <= row, p, 0.0)
            ds = (p * (nt(vv, do) - delta)).astype(BF)
            dqa[i] += tn(kk, ds)
            dv = nn(p.astype(BF), do)
            dk = nn(ds, q) * SCALE
            for t in range(CH):
                part = slice(t * SPAN, (t + 1) * SPAN)
                at = pl.ds(pl.multiple_of(loc[2, CH * j + t] * SPAN, SPAN), SPAN)
                dkv[0, at, :] += dk[part]
                at = pl.ds(pl.multiple_of(loc[3, CH * j + t] * SPAN, SPAN), SPAN)
                dkv[1, at, :] += dv[part]

        last = c // CH

        def body(j, _):
            step(j, False)
            return 0

        lax.fori_loop(0, last, body, 0)
        step(last, True)
    for copy in late:
        copy.wait()
    mine_ref[...] = dkv[core].astype(BF)
    theirs_ref[...] = dkv[1 - core].astype(BF)
    for i in range(2):
        rows = slice(i * SPAN, (i + 1) * SPAN)
        cs, sn = cosine[rows, :], -sine[rows, :]
        mix = None
        for h in range(G):
            cols = slice(h * D, (h + 1) * D)
            grad = turn((dqa[i, :, cols] * SCALE).T, cs, sn)
            unit = unit_ref[rows, cols]
            up = grad * gain_q[:, cols]
            up_ref[rows, cols] = up
            mix = up * unit if mix is None else mix + up * unit
            gain = jnp.sum(grad * unit, axis=0, keepdims=True)
            if i == 0:
                gain_ref[:, cols] = gain
            else:
                gain_ref[:, cols] += gain
        mix_ref[:, rows] = lane_sums(mix)


def attn_bwd(table, own, q, kv, grad_part, w_out, o, lse, cosine, sine, gain_q, unit):
    block = w_out.shape[1] // 4
    n = kv.shape[1]
    rows = 2 * SPAN
    return pl.pallas_call(
        bwd_kernel,
        out_shape=(
            jax.ShapeDtypeStruct((rows, R), F32),
            jax.ShapeDtypeStruct((1, rows), F32),
            jax.ShapeDtypeStruct((1, R), F32),
            jax.ShapeDtypeStruct((n, D), BF),
            jax.ShapeDtypeStruct((n, D), BF),
        ),
        grid_spec=pltpu.PrefetchScalarGridSpec(
            num_scalar_prefetch=2,
            grid=(),
            in_specs=[HB] * 10,
            out_specs=(VM,) * 5,
            scratch_shapes=[
                pltpu.VMEM(x.shape, x.dtype)
                for x in (q, kv, o, lse, cosine, sine, gain_q, unit)
            ]
            + [
                pltpu.VMEM((2, R, D), BF),
                pltpu.VMEM((4, rows, block), BF),
                pltpu.VMEM((4, R, block), BF),
                pltpu.VMEM((2, n, D), F32),
                pltpu.VMEM((2, D, R), F32),
                pltpu.SemaphoreType.DMA((8,)),
                pltpu.SemaphoreType.DMA((8,)),
            ],
        ),
        compiler_params=params(56),
        cost_estimate=cost(2.2e10, 12, 6e6),
    )(table, own, q, kv, o, lse, cosine, sine, gain_q, unit, grad_part, w_out)


def key_gain_kernel(
    loc, own, kv_in, mine_in, theirs_in, cos_r, sin_r, cos_s, sin_s, out, k_s, g_s, sems
):
    core = own[2]
    key_copy = pltpu.make_async_copy(kv_in.at[0], k_s, sems.at[0])
    key_copy.start()

    @pl.when(core == 0)
    def _():
        pltpu.make_async_copy(mine_in, g_s, sems.at[1]).start()

    @pl.when(core != 0)
    def _():
        pltpu.make_async_copy(theirs_in, g_s, sems.at[1]).start()

    key_copy.wait()
    pltpu.make_async_copy(mine_in, g_s, sems.at[1]).wait()
    cr, sr = cos_r[...], sin_r[...]

    def body(s, sums):
        plain, by_cos, by_sin = sums
        k = k_s[pl.ds(pl.multiple_of(loc[0, s] * SPAN, SPAN), SPAN), :].astype(F32)
        g = g_s[pl.ds(pl.multiple_of(loc[2, s] * SPAN, SPAN), SPAN), :].astype(F32)
        cs, sn = cos_s[pl.ds(s, 1), :], sin_s[pl.ds(s, 1), :]
        same = k * g
        cross = g * pltpu.roll(k, D // 2, 1)
        return (
            plain + same,
            by_cos + same * (cs * cr - sn * sr),
            by_sin + cross * (sn * cr + cs * sr),
        )

    zero = jnp.zeros((SPAN, D), F32)
    plain, by_cos, by_sin = lax.fori_loop(0, loc.shape[1], body, (zero, zero, zero), unroll=4)

    def over_rows(x):
        return jnp.broadcast_to(jnp.sum(x, axis=0, keepdims=True), (8, D))

    plain, by_cos, by_sin = over_rows(plain), over_rows(by_cos), over_rows(by_sin)
    half = D // 2
    sign = jnp.where(lax.broadcasted_iota(jnp.int32, (8, D), 1) < half, 1.0, -1.0)
    total = (
        plain
        + pltpu.roll(plain, half, 1)
        + by_cos
        - pltpu.roll(by_cos, half, 1)
        + sign * (by_sin + pltpu.roll(by_sin, half, 1))
    )
    out[...] = 0.5 * total[0:1]


def key_gain_of(table, own, kv, mine, theirs, tables):
    n = kv.shape[1]
    return pl.pallas_call(
        key_gain_kernel,
        out_shape=jax.ShapeDtypeStruct((1, D), F32),
        grid_spec=pltpu.PrefetchScalarGridSpec(
            num_scalar_prefetch=2,
            grid=(),
            in_specs=[HB] * 3 + [VM] * 4,
            out_specs=VM,
            scratch_shapes=[
                pltpu.VMEM((n, D), BF),
                pltpu.VMEM((n, D), BF),
                pltpu.SemaphoreType.DMA((2,)),
            ],
        ),
        compiler_params=params(56),
        cost_estimate=cost(1e9, 6),
    )(table, own, kv, mine, theirs, *tables)


def query_kernel(*refs):
    ins, w_ref, out, stages = refs[:4], refs[4], refs[5], refs[6:10]
    w_s, y_s, sems, ysems, isems = refs[10:]
    block = w_s.shape[1]
    inputs = fetch(list(zip(ins, stages)), isems)
    up, unit, mix, inv = stages
    copies = fetch([(w_ref.at[pl.ds(b * block, block), :], w_s.at[b]) for b in range(4)], sems)
    rows = up.shape[0]

    for copy in inputs:
        copy.wait()

    def column(ref):
        return jnp.broadcast_to(ref[...], (D, rows)).T[:, :1]

    x = (column(inv) * (up[...] - unit[...] * (column(mix) * (1.0 / Q_CHANNELS)))).astype(BF)
    y_copies = []
    for b in range(4):
        copies[b].wait()
        y_s[b] = nt(x, w_s[b]).astype(BF)
        copy = pltpu.make_async_copy(y_s.at[b], out.at[b], ysems.at[b])
        copy.start()
        y_copies.append(copy)
    for copy in y_copies:
        copy.wait()


def query_partial_of(up, unit, mix, inv, w_query):
    rows = up.shape[0]
    feats = w_query.shape[0]
    block = feats // 4
    return pl.pallas_call(
        query_kernel,
        out_shape=jax.ShapeDtypeStruct((4, rows, block), BF),
        in_specs=[HB] * 5,
        out_specs=FAR,
        scratch_shapes=[pltpu.VMEM(x.shape, x.dtype) for x in (up, unit, mix, inv)]
        + [
            pltpu.VMEM((4, block, R), BF),
            pltpu.VMEM((4, rows, block), BF),
            pltpu.SemaphoreType.DMA((4,)),
            pltpu.SemaphoreType.DMA((4,)),
            pltpu.SemaphoreType.DMA((4,)),
        ],
        compiler_params=params(56),
        cost_estimate=cost(1.7e9, 9),
    )(up, unit, mix, inv, w_query)


def last_kernel(g0, g1, g2, g3, u0, u1, u2, u3, inv, w, query_side, out):
    gs, us = (g0, g1, g2, g3), (u0, u1, u2, u3)
    mix = None
    for g, u in zip(gs, us):
        part = g[:, :D].astype(F32) * u[...].astype(F32)
        mix = part if mix is None else mix + part
    mix = jnp.sum(mix, axis=1, keepdims=True) * (1.0 / K_CHANNELS)
    total = query_side[...].astype(F32)
    for n, (g, u) in enumerate(zip(gs, us)):
        raw = (inv[...] * (g[:, :D].astype(F32) - u[...].astype(F32) * mix)).astype(BF)
        total = total + nt(jnp.concatenate([raw, g[:, D:]], axis=1), w[n])
    out[...] = total.astype(BF)


def last_of(grads, units, inv, w, query_side):
    return pl.pallas_call(
        last_kernel,
        out_shape=jax.ShapeDtypeStruct(query_side.shape, BF),
        in_specs=[VM] * 11,
        out_specs=VM,
        compiler_params=params(56),
        cost_estimate=cost(7e8, 5),
    )(*grads, *units, inv, w, query_side)

QUERY_HEADS = 20
KEY_VALUE_HEADS = 4
Q_CHANNELS = QUERY_HEADS * D
K_CHANNELS = KEY_VALUE_HEADS * D
N_Y, N_Z, N_CORE, N_TP = 4, 4, 2, 4


def ctx_index(y, z, c):
    return (y * N_Z + z) * N_CORE + c


def ctx_pairs(move):
    return [
        (ctx_index(y, z, c), ctx_index(*move(y, z, c)))
        for y in range(N_Y)
        for z in range(N_Z)
        for c in range(N_CORE)
    ]


def shift_first(x, d):
    return lax.ppermute(
        x,
        "ctx",
        ctx_pairs(lambda y, z, c: ((y + c * d) % N_Y, (z + (1 - c) * d) % N_Z, c)),
    )


def shift_second(x, d):
    return lax.ppermute(
        x,
        "ctx",
        ctx_pairs(lambda y, z, c: ((y + (1 - c) * d) % N_Y, (z + c * d) % N_Z, c)),
    )


def swap_core(x):
    return lax.ppermute(x, "ctx", ctx_pairs(lambda y, z, c: (y, z, 1 - c)))


def shift_tp(x, d):
    return lax.ppermute(x, "tp", [(i, (i + d) % N_TP) for i in range(N_TP)])


def shifts(shift, x):
    return [x] + [shift(x, d) for d in DIST[1:]]


def sum_tp(x):
    one, three, two = (shift_tp(x, d) for d in DIST[1:])
    return (x + one) + (three + two)


def sum_core_z(x):
    x = x + swap_core(x)
    x = x + lax.ppermute(x, "ctx", ctx_pairs(lambda y, z, c: (y, z ^ 1, c)))
    return x + lax.ppermute(x, "ctx", ctx_pairs(lambda y, z, c: (y, 3 - z, c)))


def sum_y(x):
    x = x + lax.ppermute(x, "ctx", ctx_pairs(lambda y, z, c: (y ^ 1, z, c)))
    return x + lax.ppermute(x, "ctx", ctx_pairs(lambda y, z, c: (3 - y, z, c)))


def after(x, *others):
    return lax.optimization_barrier((x,) + others)[0]


def outgoing(x):
    rows = x.shape[0] // 4
    return [x[d * rows : (d + 1) * rows].astype(BF) for d in DIST[1:]], x[:rows]


def add_up(total, arrived):
    for x in arrived:
        total = total + x.astype(F32)
    return total


def local(tokens, span_order, w_query, w_key, value_weight, w_out, gain_query, gain_key, out_grad):
    rows, feats = tokens.shape
    me = lax.axis_index("ctx")
    tp = lax.axis_index("tp")
    my_y, my_z, my_c = me // 8, (me // 2) % 4, me % 2

    mid = rows // 2
    with jax.named_scope("gather_tokens"):
        upper, lower = tokens[:mid], tokens[mid:]
        left_a = shift_tp(upper, 1)
        right_b = shift_tp(lower, 3)
        left_b = shift_tp(lower, 1)
        right_a = shift_tp(upper, 3)

    place = jnp.arange(64, dtype=jnp.int32)
    stored = jnp.sum(jnp.where(span_order[None, :] == place[:, None], place[None, :], 0), axis=1)
    src, half = stored // 2, stored % 2
    src_y, src_z, src_c = src // 8, (src // 2) % 4, src % 2
    to_y, to_z = (src_y - my_y) % 4, (src_z - my_z) % 4
    back_y, back_z = (4 - to_y) % 4, (4 - to_z) % 4
    slot_y = jnp.where(back_y >= 2, 5 - back_y, back_y)
    slot_z = jnp.where(back_z >= 2, 5 - back_z, back_z)
    table = jnp.stack(
        [
            ((slot_y * 4 + slot_z) * 2 + src_c) * 2 + half,
            ((slot_z * 4 + slot_y) * 2 + 1 - src_c) * 2 + half,
            ((to_z * 4 + to_y) * 2 + src_c) * 2 + half,
            ((to_y * 4 + to_z) * 2 + src_c) * 2 + half,
        ]
    ).astype(jnp.int32)
    own = lax.dynamic_slice_in_dim(span_order, 2 * me, 2)
    own = jnp.concatenate([own, my_c[None]]).astype(jnp.int32)

    query_pos = (own[:2, None] * SPAN + jnp.arange(SPAN)[None, :]).reshape(-1)
    frequency = jnp.exp(jnp.arange(D // 2).astype(F32) * (-2.0 * math.log(500000.0) / D))
    angles = query_pos.astype(F32)[:, None] * frequency[None, :]
    cosine, sine = jnp.cos(angles), jnp.sin(angles)
    cosine = jnp.concatenate([cosine, cosine], axis=1)
    sine = jnp.concatenate([-sine, sine], axis=1)

    offs = jnp.stack([(tp - d) % 4 for d in DIST]).astype(jnp.int32)
    twice = 2.0 * jnp.concatenate([frequency, frequency])[None, :]
    by_row = jnp.arange(SPAN).astype(F32)[:, None] * twice
    by_span = (SPAN * jnp.arange(64)).astype(F32)[:, None] * twice
    tables = (jnp.cos(by_row), jnp.sin(by_row), jnp.cos(by_span), jnp.sin(by_span))

    with jax.named_scope("gather_tokens"):
        weights = (w_query, w_key, value_weight)
        acc = project(offs[:1], ((tokens,),), weights)
        left_a, right_b, left_b, right_a, cosine, sine, offs, table, own, acc, *tables = (
            lax.optimization_barrier(
                (left_a, right_b, left_b, right_a, cosine, sine, offs, table, own, acc, *tables)
            )
        )
        far_a = shift_tp(left_a, 1)
        far_b = shift_tp(right_b, 3)
        acc = project(offs[1:3], ((left_a, left_b), (right_a, right_b)), weights, acc)

    with jax.named_scope("weight_rows"):
        share = feats // 32
        key_rows, value_rows, _ = lax.optimization_barrier((w_key, value_weight, left_a))
        cut = []
        for d in DIST:
            start = feats * ((tp + d) % 4) + share * me
            piece = jnp.concatenate(
                [lax.dynamic_slice_in_dim(w, start, share, 0) for w in (key_rows, value_rows)],
                axis=1,
            )
            cut.append(shift_tp(piece, d) if d else piece)
        cut = jnp.stack(cut)

    far_a, far_b, acc, cut = lax.optimization_barrier((far_a, far_b, acc, cut))
    gain_q, gain_k = gain_query[None, :], gain_key[None, :]
    q_rot, q_raw, k_rot, k_raw, value, squares = project_end(
        offs[3:], far_a, far_b, weights, acc, cosine, sine, gain_q, gain_k
    )
    with jax.named_scope("norm_sums"):
        squares = sum_tp(squares)
    query_inv = lax.rsqrt(squares[0] / Q_CHANNELS + 1e-06)[:, None]
    key_inv = lax.rsqrt(squares[1] / K_CHANNELS + 1e-06)[:, None]
    key = (k_rot * key_inv).astype(BF)

    with jax.named_scope("gather_keys_values"):
        first_core = my_c == 0
        mine = jnp.where(first_core, key, value)
        pair = join(mine, swap_core(jnp.where(first_core, value, key)))
        plane = join(*shifts(shift_first, pair))
        mine = shifts(shift_second, plane)
    with jax.named_scope("weight_rows"):
        w_rows = lax.all_gather(after(cut, pair), "ctx", axis=0, tiled=False)

    query_unit = q_raw * query_inv
    key_unit = (k_raw * key_inv).astype(BF)
    query = (
        (q_rot.reshape(2, G, SPAN, D) * query_inv.reshape(2, 1, SPAN, 1)).astype(BF).reshape(2, R, D)
    )
    with jax.named_scope("gather_key_units"):
        key_units = shifts(shift_tp, key_unit)

    with jax.named_scope("gather_out_grad"):
        grad_part = lax.all_gather(after(out_grad, far_a, far_b), "tp", axis=1, tiled=True)

    with jax.named_scope("swap_keys_values"):
        last, query, query_unit, *key_units = lax.optimization_barrier(
            (mine[3], query, query_unit, *key_units)
        )
        mine = mine[:3] + [last]
        pieces = (*mine, *(swap_core(x) for x in mine))

    log_total, heads, kv, out_partial = attn_fwd(table, own, query, pieces, w_out)
    attn_out = lax.psum_scatter(out_partial, "tp", scatter_dimension=0, tiled=False)

    up_query, mix_query, gain_part, mine, theirs = attn_bwd(
        table, own, query, kv, grad_part, w_out, heads, log_total,
        cosine, sine, gain_q, query_unit,
    )

    with jax.named_scope("sum_key_value_grads"):
        mix_query = sum_tp(mix_query)
        gain_key_part = key_gain_of(table, own, kv, mine, theirs, tables) / gain_k
        gains = jnp.concatenate([gain_part, gain_key_part], axis=1)
        received, mix_query, w_rows, gains = lax.optimization_barrier(
            (swap_core(theirs), mix_query, w_rows, gains)
        )
        summed = mine.astype(F32) + received.astype(F32)
        sent, total = outgoing(summed)
        *sent, gains = lax.optimization_barrier((*sent, gains))
        arrived = [shift_first(x, d) for x, d in zip(sent, DIST[1:])]
        *arrived, gains, attn_out = lax.optimization_barrier(
            (*arrived, sum_core_z(gains), attn_out)
        )
        sent, total = outgoing(add_up(total, arrived))
        *sent, gains = lax.optimization_barrier((*sent, gains))
        arrived = [shift_second(x, d) for x, d in zip(sent, DIST[1:])]
        *arrived, gains = lax.optimization_barrier((*arrived, sum_y(gains)))
        total = add_up(total, arrived)
        ours, its = total[:rows], total[rows:]
        kept = jnp.where(first_core, ours, its)
        swapped = swap_core(jnp.where(first_core, its, ours))
        key_grad_rot = jnp.where(first_core, kept, swapped)
        value_grad = jnp.where(first_core, swapped, kept).astype(BF)

    with jax.named_scope("query_side"):
        query_partial = query_partial_of(
            up_query, query_unit, mix_query, query_inv.reshape(1, rows), w_query
        )
        query_side = lax.psum_scatter(query_partial, "tp", scatter_dimension=0, tiled=False)

    with jax.named_scope("key_value_side"):
        first, second = key_grad_rot[:, : D // 2], key_grad_rot[:, D // 2 :]
        cs, sn = cosine[:, : D // 2], sine[:, D // 2 :]
        key_grad = jnp.concatenate([first * cs + second * sn, second * cs - first * sn], axis=1)
        w_rows = after(w_rows, query_partial).transpose(1, 0, 2, 3).reshape(4, feats, 2 * D)
        key_grad, w_rows = lax.optimization_barrier((key_grad, w_rows))
        both = jnp.concatenate([(key_grad * gain_k).astype(BF), value_grad], axis=1)
        grads = shifts(shift_tp, both)
        gain_query_grad, gain_key_grad = gains[0, :R], gains[0, R:]
        input_grad = last_of(grads, key_units, key_inv, w_rows, query_side)
    return (attn_out, input_grad, gain_query_grad, gain_key_grad)


def solution(mesh):
    return jax.shard_map(
        local,
        mesh=mesh,
        in_specs=(
            P("ctx", "tp"),
            P(),
            P(None, "tp"),
            P(None, "tp"),
            P(None, "tp"),
            P("tp", None),
            P("tp"),
            P("tp"),
            P("ctx", "tp"),
        ),
        out_specs=(P("ctx", "tp"), P("ctx", "tp"), P("tp"), P("tp")),
        check_vma=False,
    )
```

```python
import math

import jax
import jax.numpy as jnp
from jax import lax
from jax.experimental import pallas as pl
from jax.experimental.pallas import tpu as pltpu
from jax.sharding import PartitionSpec as P

D = 128
SPAN = 128
G = 5
R = G * SPAN
CH = 8
KC = CH * SPAN
SCALE = D**-0.5
LOG2E = math.log2(math.e)
NEG = -1e30
BF = jnp.bfloat16
F32 = jnp.float32
DIST = (0, 1, 3, 2)
PIECES = 8


def nt(a, b):
    return lax.dot_general(a, b, (((1,), (1,)), ((), ())), preferred_element_type=F32)


def tn(a, b):
    return lax.dot_general(a, b, (((0,), (0,)), ((), ())), preferred_element_type=F32)


def nn(a, b):
    return lax.dot_general(a, b, (((1,), (0,)), ((), ())), preferred_element_type=F32)


VM = pl.BlockSpec(memory_space=pltpu.VMEM)
HB = pl.BlockSpec(memory_space=pl.ANY)
FAR = pl.BlockSpec(memory_space=pltpu.HBM)


def params(mib):
    return pltpu.CompilerParams(vmem_limit_bytes=mib * 2**20)


def cost(flops, mib, exps=0):
    return pl.CostEstimate(
        flops=int(flops), bytes_accessed=int(mib * 2**20), transcendentals=int(exps)
    )


def turn(x, cosine, sine):
    return x * cosine + pltpu.roll(x, D // 2, 1) * sine


def lane_sums(x):
    return jnp.sum(x.T, axis=0, keepdims=True)


def fetch(pairs, sems):
    copies = [pltpu.make_async_copy(src, dst, sems.at[n]) for n, (src, dst) in enumerate(pairs)]
    for copy in copies:
        copy.start()
    return copies


def fetch_rows(off, weights, stages, sems):
    pairs = []
    for n in range(stages[0].shape[0]):
        rows = stages[0].shape[1]
        at = pl.ds(pl.multiple_of(off[n] * rows, rows), rows)
        pairs += [(w.at[at, :], s.at[n]) for w, s in zip(weights, stages)]
    return fetch(pairs, sems)


def product_of(x, stages, n):
    return jnp.concatenate([nn(x, s[n]) for s in stages], axis=1)


def project_kernel(off, *refs, count, parts, first):
    xs, weights = refs[: count * parts], refs[count * parts : count * parts + 3]
    stages, sems, x_s, isems, out = refs[-6:-3], refs[-3], refs[-2], refs[-1], refs[-7]
    part_rows = x_s.shape[1] // parts
    inputs = fetch(
        [
            (xs[n * parts + m], x_s.at[n, pl.ds(m * part_rows, part_rows), :])
            for n in range(count)
            for m in range(parts)
        ]
        + ([] if first else [(refs[count * parts + 3], out)]),
        isems,
    )
    copies = fetch_rows(off, weights, stages, sems)
    for copy in inputs:
        copy.wait()
    total = None if first else out[...]
    for n in range(count):
        for copy in copies[3 * n : 3 * n + 3]:
            copy.wait()
        part = product_of(x_s[n], stages, n)
        total = part if total is None else total + part
    out[...] = total


def stages_of(weights, count, feats):
    return [pltpu.VMEM((count, feats, w.shape[1]), BF) for w in weights] + [
        pltpu.SemaphoreType.DMA((3 * count,))
    ]


def project(off, pieces, weights, acc=None):
    parts = len(pieces[0])
    rows, feats = sum(x.shape[0] for x in pieces[0]), pieces[0][0].shape[1]
    width = sum(w.shape[1] for w in weights)
    count = len(pieces)
    xs = [x for piece in pieces for x in piece]
    more = () if acc is None else (acc,)
    return pl.pallas_call(
        lambda *refs: project_kernel(*refs, count=count, parts=parts, first=acc is None),
        out_shape=jax.ShapeDtypeStruct((rows, width), F32),
        grid_spec=pltpu.PrefetchScalarGridSpec(
            num_scalar_prefetch=1,
            grid=(),
            in_specs=[HB] * (len(xs) + 3 + len(more)),
            out_specs=VM,
            scratch_shapes=stages_of(weights, count, feats)
            + [pltpu.VMEM((count, rows, feats), BF), pltpu.SemaphoreType.DMA((len(xs) + 1,))],
        ),
        compiler_params=params(56),
        cost_estimate=cost(6e8 * count, 4 * count),
    )(off, *xs, *weights, *more)


def project_end_kernel(
    off, xa, xb, wq, wk, wv, acc_in, cosine, sine, gain_q, gain_k,
    q_rot, q_raw, k_rot, k_raw, v_out, squares, sq, sk, sv, sems, x_s, a_s, c_s, s_s, gq_s, gk_s, isems,
):
    stages = (sq, sk, sv)
    copies = fetch(
        [
            (xa, x_s.at[pl.ds(0, SPAN), :]), (xb, x_s.at[pl.ds(SPAN, SPAN), :]), (acc_in, a_s),
            (cosine, c_s), (sine, s_s), (gain_q, gq_s), (gain_k, gk_s),
        ],
        isems,
    )
    copies += fetch_rows(off, (wq, wk, wv), stages, sems)
    for copy in copies:
        copy.wait()
    cs, sn, gain_q, gain_k = c_s[...], s_s[...], gq_s, gk_s
    raw = a_s[...] + product_of(x_s[...], stages, 0)
    k = raw[:, R : R + D]
    k_raw[...] = k
    k_rot[...] = turn(k * gain_k[...], cs, sn)
    v_out[...] = raw[:, R + D :].astype(BF)
    squares[1:2, :] = lane_sums(k * k)
    total = None
    for h in range(G):
        q = raw[:, h * D : (h + 1) * D]
        total = q * q if total is None else total + q * q
        rotated = turn(q * gain_q[:, h * D : (h + 1) * D], cs, sn)
        for i in range(2):
            q_rot[i, h * SPAN : (h + 1) * SPAN, :] = rotated[i * SPAN : (i + 1) * SPAN]
    q_raw[...] = raw[:, :R]
    squares[0:1, :] = lane_sums(total)


def project_end(off, xa, xb, weights, acc, cosine, sine, gain_q, gain_k):
    rows = acc.shape[0]
    feats = xa.shape[1]
    outs = (
        jax.ShapeDtypeStruct((2, R, D), F32),
        jax.ShapeDtypeStruct((rows, R), F32),
        jax.ShapeDtypeStruct((rows, D), F32),
        jax.ShapeDtypeStruct((rows, D), F32),
        jax.ShapeDtypeStruct((rows, D), BF),
        jax.ShapeDtypeStruct((2, rows), F32),
    )
    return pl.pallas_call(
        project_end_kernel,
        out_shape=outs,
        grid_spec=pltpu.PrefetchScalarGridSpec(
            num_scalar_prefetch=1,
            grid=(),
            in_specs=[HB] * 10,
            out_specs=(VM,) * 6,
            scratch_shapes=stages_of(weights, 1, feats)
            + [
                pltpu.VMEM((rows, feats), BF),
                pltpu.VMEM(acc.shape, F32),
                pltpu.VMEM(cosine.shape, F32),
                pltpu.VMEM(sine.shape, F32),
                pltpu.VMEM(gain_q.shape, F32),
                pltpu.VMEM(gain_k.shape, F32),
                pltpu.SemaphoreType.DMA((7,)),
            ],
        ),
        compiler_params=params(56),
        cost_estimate=cost(6e8, 6),
    )(off, xa, xb, *weights, acc, cosine, sine, gain_q, gain_k)


def join_kernel(*refs):
    at = 0
    for ref in refs[:-1]:
        n = ref.shape[0]
        refs[-1][at : at + n, :] = ref[...]
        at += n


def join(*xs):
    rows = sum(x.shape[0] for x in xs)
    return pl.pallas_call(
        join_kernel,
        out_shape=jax.ShapeDtypeStruct((rows,) + xs[0].shape[1:], xs[0].dtype),
        in_specs=[VM] * len(xs),
        out_specs=VM,
        compiler_params=params(8),
        cost_estimate=cost(0, 1),
    )(*xs)


def spans_at(ref, loc, which, j):
    return jnp.concatenate(
        [
            ref[pl.ds(pl.multiple_of(loc[which, CH * j + t] * SPAN, SPAN), SPAN), :]
            for t in range(CH)
        ],
        axis=0,
    )


def load_pieces(refs, whole, core, sems):
    count = len(refs) // 2
    copies = []
    for n, src in enumerate(refs):
        rows = src.shape[0]
        to = core if n < count else 1 - core
        copy = pltpu.make_async_copy(
            src, whole.at[to, pl.ds((n % count) * rows, rows), :], sems.at[n]
        )
        copy.start()
        copies.append(copy)
    for copy in copies:
        copy.wait()


def fwd_kernel(loc, own, q_in, *refs):
    kv_refs, w_ref, (lse_ref, o_ref, kv_out, out) = (
        refs[:PIECES], refs[PIECES], refs[PIECES + 1 : PIECES + 5],
    )
    kv, w_s, y_s, m_s, acc_s, q_ref, sems, wsems, kvsem, ysems, qsem = refs[PIECES + 5 :]
    q_copies = fetch([(q_in, q_ref)], qsem)
    load_pieces(kv_refs, kv, own[2], sems)
    keep = fetch([(kv, kv_out)], kvsem)
    block = y_s.shape[2]
    w_copies = fetch(
        [(w_ref.at[:, pl.ds(b * block, block)], w_s.at[b]) for b in range(4)], wsems
    )
    for copy in q_copies:
        copy.wait()
    k_ref, v_ref = kv.at[0], kv.at[1]
    ones = (lax.broadcasted_iota(jnp.int32, (KC, D), 1) == 0).astype(BF)
    for i in range(2):
        c = own[i]
        m_s[...] = jnp.full_like(m_s, NEG)
        acc_s[...] = jnp.zeros_like(acc_s)

        def step(j, masked):
            kk = spans_at(k_ref, loc, 0, j)
            vv = jnp.concatenate([spans_at(v_ref, loc, 1, j), ones], axis=1)
            for h in range(G):
                at = slice(h * SPAN, (h + 1) * SPAN)
                s = nt(q_ref[i, at, :], kk)
                if masked:
                    key = j * KC + lax.broadcasted_iota(jnp.int32, (SPAN, KC), 1)
                    row = c * SPAN + lax.broadcasted_iota(jnp.int32, (SPAN, KC), 0)
                    s = jnp.where(key <= row, s, NEG)
                m = m_s[at, :]
                new = jnp.maximum(m, jnp.max(s, axis=1, keepdims=True))
                shrink = jnp.exp2((m - new) * (SCALE * LOG2E))
                p = jnp.exp2((s - new[:, :1]) * (SCALE * LOG2E))
                m_s[at, :] = new
                acc_s[at, :] = acc_s[at, :] * shrink[:, :1] + nn(p.astype(BF), vv)

        last = c // CH

        def body(j, _):
            step(j, False)
            return 0

        lax.fori_loop(0, last, body, 0)
        step(last, True)
        total = acc_s[:, D : D + 1]
        o_ref[i] = (acc_s[:, :D] / total).astype(BF)
        lse = m_s[...] * (SCALE * LOG2E) + jnp.log2(jnp.broadcast_to(total, (R, D)))
        lse_ref[i] = lse.T[0:1, :]
    x = jnp.concatenate(
        [
            jnp.concatenate(
                [o_ref[i, h * SPAN : (h + 1) * SPAN, :] for h in range(G)], axis=1
            )
            for i in range(2)
        ],
        axis=0,
    )
    y_copies = []
    for b in range(4):
        w_copies[b].wait()
        y_s[b] = nn(x, w_s[b]).astype(BF)
        copy = pltpu.make_async_copy(y_s.at[b], out.at[b], ysems.at[b])
        copy.start()
        y_copies.append(copy)
    for copy in keep + y_copies:
        copy.wait()


def attn_fwd(table, own, q, pieces, w_out):
    n = sum(x.shape[0] for x in pieces) // 2
    block = w_out.shape[1] // 4
    return pl.pallas_call(
        fwd_kernel,
        out_shape=(
            jax.ShapeDtypeStruct((2, 1, R), F32),
            jax.ShapeDtypeStruct((2, R, D), BF),
            jax.ShapeDtypeStruct((2, n, D), BF),
            jax.ShapeDtypeStruct((4, 2 * SPAN, block), BF),
        ),
        grid_spec=pltpu.PrefetchScalarGridSpec(
            num_scalar_prefetch=2,
            grid=(),
            in_specs=[HB] * (PIECES + 2),
            out_specs=(VM, VM, FAR, FAR),
            scratch_shapes=[
                pltpu.VMEM((2, n, D), BF),
                pltpu.VMEM((4, R, block), BF),
                pltpu.VMEM((4, 2 * SPAN, block), BF),
                pltpu.VMEM((R, D), F32),
                pltpu.VMEM((R, 2 * D), F32),
                pltpu.VMEM((2, R, D), BF),
                pltpu.SemaphoreType.DMA((PIECES,)),
                pltpu.SemaphoreType.DMA((4,)),
                pltpu.SemaphoreType.DMA((1,)),
                pltpu.SemaphoreType.DMA((4,)),
                pltpu.SemaphoreType.DMA((1,)),
            ],
        ),
        compiler_params=params(56),
        cost_estimate=cost(1.8e10, 12, 6e6),
    )(table, own, q, *pieces, w_out)


def bwd_kernel(
    loc, own, *refs,
):
    ins, g_ref, w_ref, (up_ref, mix_ref, gain_ref, mine_ref, theirs_ref) = (
        refs[:8], refs[8], refs[9], refs[10:15],
    )
    stages, (do_ref, g_s, w_s, dkv, dqa, gsems, sems) = refs[15:23], refs[23:]
    q_ref, kv, o_ref, lse_ref, cosine, sine, gain_q, unit_ref = stages
    core = own[2]
    block = g_s.shape[2]
    g_pairs = []
    for b in range(4):
        cols = pl.ds(b * block, block)
        g_pairs += [(w_ref.at[:, cols], w_s.at[b]), (g_ref.at[:, cols], g_s.at[b])]
    g_copies = fetch(g_pairs, gsems)
    copies = fetch(list(zip(ins, stages)), sems)
    late = copies[4:]
    copies = copies[:4]
    k_ref, v_ref = kv.at[0], kv.at[1]
    dkv[...] = jnp.zeros_like(dkv)
    dqa[...] = jnp.zeros_like(dqa)
    grad = None
    for b in range(4):
        g_copies[2 * b].wait()
        g_copies[2 * b + 1].wait()
        part = nt(g_s[b], w_s[b])
        grad = part if grad is None else grad + part
    for i in range(2):
        for h in range(G):
            do_ref[i, h * SPAN : (h + 1) * SPAN, :] = grad[
                i * SPAN : (i + 1) * SPAN, h * D : (h + 1) * D
            ].astype(BF)
    for copy in copies:
        copy.wait()
    for i in range(2):
        c = own[i]
        q, do, lse = q_ref[i], do_ref[i], lse_ref[i]
        delta = lane_sums(do.astype(F32) * o_ref[i].astype(F32))

        def step(j, masked):
            kk = spans_at(k_ref, loc, 0, j)
            vv = spans_at(v_ref, loc, 1, j)
            p = jnp.exp2(nt(kk, q) * (SCALE * LOG2E) - lse)
            if masked:
                key = j * KC + lax.broadcasted_iota(jnp.int32, (KC, R), 0)
                row = c * SPAN + lax.rem(lax.broadcasted_iota(jnp.int32, (KC, R), 1), SPAN)
                p = jnp.where(key <= row, p, 0.0)
            ds = (p * (nt(vv, do) - delta)).astype(BF)
            dqa[i] += tn(kk, ds)
            dv = nn(p.astype(BF), do)
            dk = nn(ds, q) * SCALE
            for t in range(CH):
                part = slice(t * SPAN, (t + 1) * SPAN)
                at = pl.ds(pl.multiple_of(loc[2, CH * j + t] * SPAN, SPAN), SPAN)
                dkv[0, at, :] += dk[part]
                at = pl.ds(pl.multiple_of(loc[3, CH * j + t] * SPAN, SPAN), SPAN)
                dkv[1, at, :] += dv[part]

        last = c // CH

        def body(j, _):
            step(j, False)
            return 0

        lax.fori_loop(0, last, body, 0)
        step(last, True)
    for copy in late:
        copy.wait()
    mine_ref[...] = dkv[core].astype(BF)
    theirs_ref[...] = dkv[1 - core].astype(BF)
    for i in range(2):
        rows = slice(i * SPAN, (i + 1) * SPAN)
        cs, sn = cosine[rows, :], -sine[rows, :]
        mix = None
        for h in range(G):
            cols = slice(h * D, (h + 1) * D)
            grad = turn((dqa[i, :, cols] * SCALE).T, cs, sn)
            unit = unit_ref[rows, cols]
            up = grad * gain_q[:, cols]
            up_ref[rows, cols] = up
            mix = up * unit if mix is None else mix + up * unit
            gain = jnp.sum(grad * unit, axis=0, keepdims=True)
            if i == 0:
                gain_ref[:, cols] = gain
            else:
                gain_ref[:, cols] += gain
        mix_ref[:, rows] = lane_sums(mix)


def attn_bwd(table, own, q, kv, grad_part, w_out, o, lse, cosine, sine, gain_q, unit):
    block = w_out.shape[1] // 4
    n = kv.shape[1]
    rows = 2 * SPAN
    return pl.pallas_call(
        bwd_kernel,
        out_shape=(
            jax.ShapeDtypeStruct((rows, R), F32),
            jax.ShapeDtypeStruct((1, rows), F32),
            jax.ShapeDtypeStruct((1, R), F32),
            jax.ShapeDtypeStruct((n, D), BF),
            jax.ShapeDtypeStruct((n, D), BF),
        ),
        grid_spec=pltpu.PrefetchScalarGridSpec(
            num_scalar_prefetch=2,
            grid=(),
            in_specs=[HB] * 10,
            out_specs=(VM,) * 5,
            scratch_shapes=[
                pltpu.VMEM(x.shape, x.dtype)
                for x in (q, kv, o, lse, cosine, sine, gain_q, unit)
            ]
            + [
                pltpu.VMEM((2, R, D), BF),
                pltpu.VMEM((4, rows, block), BF),
                pltpu.VMEM((4, R, block), BF),
                pltpu.VMEM((2, n, D), F32),
                pltpu.VMEM((2, D, R), F32),
                pltpu.SemaphoreType.DMA((8,)),
                pltpu.SemaphoreType.DMA((8,)),
            ],
        ),
        compiler_params=params(56),
        cost_estimate=cost(2.2e10, 12, 6e6),
    )(table, own, q, kv, o, lse, cosine, sine, gain_q, unit, grad_part, w_out)


def key_gain_kernel(
    loc, own, kv_in, mine_in, theirs_in, cos_r, sin_r, cos_s, sin_s, out, k_s, g_s, sems
):
    core = own[2]
    key_copy = pltpu.make_async_copy(kv_in.at[0], k_s, sems.at[0])
    key_copy.start()

    @pl.when(core == 0)
    def _():
        pltpu.make_async_copy(mine_in, g_s, sems.at[1]).start()

    @pl.when(core != 0)
    def _():
        pltpu.make_async_copy(theirs_in, g_s, sems.at[1]).start()

    key_copy.wait()
    pltpu.make_async_copy(mine_in, g_s, sems.at[1]).wait()
    cr, sr = cos_r[...], sin_r[...]

    def body(s, sums):
        plain, by_cos, by_sin = sums
        k = k_s[pl.ds(pl.multiple_of(loc[0, s] * SPAN, SPAN), SPAN), :].astype(F32)
        g = g_s[pl.ds(pl.multiple_of(loc[2, s] * SPAN, SPAN), SPAN), :].astype(F32)
        cs, sn = cos_s[pl.ds(s, 1), :], sin_s[pl.ds(s, 1), :]
        same = k * g
        cross = g * pltpu.roll(k, D // 2, 1)
        return (
            plain + same,
            by_cos + same * (cs * cr - sn * sr),
            by_sin + cross * (sn * cr + cs * sr),
        )

    zero = jnp.zeros((SPAN, D), F32)
    plain, by_cos, by_sin = lax.fori_loop(0, loc.shape[1], body, (zero, zero, zero), unroll=4)

    def over_rows(x):
        return jnp.broadcast_to(jnp.sum(x, axis=0, keepdims=True), (8, D))

    plain, by_cos, by_sin = over_rows(plain), over_rows(by_cos), over_rows(by_sin)
    half = D // 2
    sign = jnp.where(lax.broadcasted_iota(jnp.int32, (8, D), 1) < half, 1.0, -1.0)
    total = (
        plain
        + pltpu.roll(plain, half, 1)
        + by_cos
        - pltpu.roll(by_cos, half, 1)
        + sign * (by_sin + pltpu.roll(by_sin, half, 1))
    )
    out[...] = 0.5 * total[0:1]


def key_gain_of(table, own, kv, mine, theirs, tables):
    n = kv.shape[1]
    return pl.pallas_call(
        key_gain_kernel,
        out_shape=jax.ShapeDtypeStruct((1, D), F32),
        grid_spec=pltpu.PrefetchScalarGridSpec(
            num_scalar_prefetch=2,
            grid=(),
            in_specs=[HB] * 3 + [VM] * 4,
            out_specs=VM,
            scratch_shapes=[
                pltpu.VMEM((n, D), BF),
                pltpu.VMEM((n, D), BF),
                pltpu.SemaphoreType.DMA((2,)),
            ],
        ),
        compiler_params=params(56),
        cost_estimate=cost(1e9, 6),
    )(table, own, kv, mine, theirs, *tables)


def query_kernel(*refs):
    ins, w_ref, out, stages = refs[:4], refs[4], refs[5], refs[6:10]
    w_s, y_s, sems, ysems, isems = refs[10:]
    block = w_s.shape[1]
    inputs = fetch(list(zip(ins, stages)), isems)
    up, unit, mix, inv = stages
    copies = fetch([(w_ref.at[pl.ds(b * block, block), :], w_s.at[b]) for b in range(4)], sems)
    rows = up.shape[0]

    for copy in inputs:
        copy.wait()

    def column(ref):
        return jnp.broadcast_to(ref[...], (D, rows)).T[:, :1]

    x = (column(inv) * (up[...] - unit[...] * (column(mix) * (1.0 / Q_CHANNELS)))).astype(BF)
    y_copies = []
    for b in range(4):
        copies[b].wait()
        y_s[b] = nt(x, w_s[b]).astype(BF)
        copy = pltpu.make_async_copy(y_s.at[b], out.at[b], ysems.at[b])
        copy.start()
        y_copies.append(copy)
    for copy in y_copies:
        copy.wait()


def query_partial_of(up, unit, mix, inv, w_query):
    rows = up.shape[0]
    feats = w_query.shape[0]
    block = feats // 4
    return pl.pallas_call(
        query_kernel,
        out_shape=jax.ShapeDtypeStruct((4, rows, block), BF),
        in_specs=[HB] * 5,
        out_specs=FAR,
        scratch_shapes=[pltpu.VMEM(x.shape, x.dtype) for x in (up, unit, mix, inv)]
        + [
            pltpu.VMEM((4, block, R), BF),
            pltpu.VMEM((4, rows, block), BF),
            pltpu.SemaphoreType.DMA((4,)),
            pltpu.SemaphoreType.DMA((4,)),
            pltpu.SemaphoreType.DMA((4,)),
        ],
        compiler_params=params(56),
        cost_estimate=cost(1.7e9, 9),
    )(up, unit, mix, inv, w_query)


def last_kernel(g0, g1, g2, g3, u0, u1, u2, u3, inv, w, query_side, out):
    gs, us = (g0, g1, g2, g3), (u0, u1, u2, u3)
    mix = None
    for g, u in zip(gs, us):
        part = g[:, :D].astype(F32) * u[...].astype(F32)
        mix = part if mix is None else mix + part
    mix = jnp.sum(mix, axis=1, keepdims=True) * (1.0 / K_CHANNELS)
    total = query_side[...].astype(F32)
    for n, (g, u) in enumerate(zip(gs, us)):
        raw = (inv[...] * (g[:, :D].astype(F32) - u[...].astype(F32) * mix)).astype(BF)
        total = total + nt(jnp.concatenate([raw, g[:, D:]], axis=1), w[n])
    out[...] = total.astype(BF)


def last_of(grads, units, inv, w, query_side):
    return pl.pallas_call(
        last_kernel,
        out_shape=jax.ShapeDtypeStruct(query_side.shape, BF),
        in_specs=[VM] * 11,
        out_specs=VM,
        compiler_params=params(56),
        cost_estimate=cost(7e8, 5),
    )(*grads, *units, inv, w, query_side)

QUERY_HEADS = 20
KEY_VALUE_HEADS = 4
Q_CHANNELS = QUERY_HEADS * D
K_CHANNELS = KEY_VALUE_HEADS * D
N_Y, N_Z, N_CORE, N_TP = 4, 4, 2, 4


def ctx_index(y, z, c):
    return (y * N_Z + z) * N_CORE + c


def ctx_pairs(move):
    return [
        (ctx_index(y, z, c), ctx_index(*move(y, z, c)))
        for y in range(N_Y)
        for z in range(N_Z)
        for c in range(N_CORE)
    ]


def shift_first(x, d):
    return lax.ppermute(
        x,
        "ctx",
        ctx_pairs(lambda y, z, c: ((y + c * d) % N_Y, (z + (1 - c) * d) % N_Z, c)),
    )


def shift_second(x, d):
    return lax.ppermute(
        x,
        "ctx",
        ctx_pairs(lambda y, z, c: ((y + (1 - c) * d) % N_Y, (z + c * d) % N_Z, c)),
    )


def swap_core(x):
    return lax.ppermute(x, "ctx", ctx_pairs(lambda y, z, c: (y, z, 1 - c)))


def shift_tp(x, d):
    return lax.ppermute(x, "tp", [(i, (i + d) % N_TP) for i in range(N_TP)])


def shifts(shift, x):
    return [x] + [shift(x, d) for d in DIST[1:]]


def sum_tp(x):
    one, three, two = (shift_tp(x, d) for d in DIST[1:])
    return (x + one) + (three + two)


def sum_core_z(x):
    x = x + swap_core(x)
    x = x + lax.ppermute(x, "ctx", ctx_pairs(lambda y, z, c: (y, z ^ 1, c)))
    return x + lax.ppermute(x, "ctx", ctx_pairs(lambda y, z, c: (y, 3 - z, c)))


def sum_y(x):
    x = x + lax.ppermute(x, "ctx", ctx_pairs(lambda y, z, c: (y ^ 1, z, c)))
    return x + lax.ppermute(x, "ctx", ctx_pairs(lambda y, z, c: (3 - y, z, c)))


def after(x, *others):
    return lax.optimization_barrier((x,) + others)[0]


def outgoing(x):
    rows = x.shape[0] // 4
    return [x[d * rows : (d + 1) * rows].astype(BF) for d in DIST[1:]], x[:rows]


def add_up(total, arrived):
    for x in arrived:
        total = total + x.astype(F32)
    return total


def local(tokens, span_order, w_query, w_key, value_weight, w_out, gain_query, gain_key, out_grad):
    rows, feats = tokens.shape
    me = lax.axis_index("ctx")
    tp = lax.axis_index("tp")
    my_y, my_z, my_c = me // 8, (me // 2) % 4, me % 2

    mid = rows // 2
    with jax.named_scope("gather_tokens"):
        upper, lower = tokens[:mid], tokens[mid:]
        left_a = shift_tp(upper, 1)
        right_b = shift_tp(lower, 3)
        left_b = shift_tp(lower, 1)
        right_a = shift_tp(upper, 3)

    place = jnp.arange(64, dtype=jnp.int32)
    stored = jnp.sum(jnp.where(span_order[None, :] == place[:, None], place[None, :], 0), axis=1)
    src, half = stored // 2, stored % 2
    src_y, src_z, src_c = src // 8, (src // 2) % 4, src % 2
    to_y, to_z = (src_y - my_y) % 4, (src_z - my_z) % 4
    back_y, back_z = (4 - to_y) % 4, (4 - to_z) % 4
    slot_y = jnp.where(back_y >= 2, 5 - back_y, back_y)
    slot_z = jnp.where(back_z >= 2, 5 - back_z, back_z)
    table = jnp.stack(
        [
            ((slot_y * 4 + slot_z) * 2 + src_c) * 2 + half,
            ((slot_z * 4 + slot_y) * 2 + 1 - src_c) * 2 + half,
            ((to_z * 4 + to_y) * 2 + src_c) * 2 + half,
            ((to_y * 4 + to_z) * 2 + src_c) * 2 + half,
        ]
    ).astype(jnp.int32)
    own = lax.dynamic_slice_in_dim(span_order, 2 * me, 2)
    own = jnp.concatenate([own, my_c[None]]).astype(jnp.int32)

    query_pos = (own[:2, None] * SPAN + jnp.arange(SPAN)[None, :]).reshape(-1)
    frequency = jnp.exp(jnp.arange(D // 2).astype(F32) * (-2.0 * math.log(500000.0) / D))
    angles = query_pos.astype(F32)[:, None] * frequency[None, :]
    cosine, sine = jnp.cos(angles), jnp.sin(angles)
    cosine = jnp.concatenate([cosine, cosine], axis=1)
    sine = jnp.concatenate([-sine, sine], axis=1)

    offs = jnp.stack([(tp - d) % 4 for d in DIST]).astype(jnp.int32)
    twice = 2.0 * jnp.concatenate([frequency, frequency])[None, :]
    by_row = jnp.arange(SPAN).astype(F32)[:, None] * twice
    by_span = (SPAN * jnp.arange(64)).astype(F32)[:, None] * twice
    tables = (jnp.cos(by_row), jnp.sin(by_row), jnp.cos(by_span), jnp.sin(by_span))

    with jax.named_scope("gather_tokens"):
        weights = (w_query, w_key, value_weight)
        acc = own_acc = project(offs[:1], ((tokens,),), weights)
        left_a, right_b, left_b, right_a, cosine, sine, offs, table, own, acc, *tables = (
            lax.optimization_barrier(
                (left_a, right_b, left_b, right_a, cosine, sine, offs, table, own, acc, *tables)
            )
        )
        far_a = shift_tp(left_a, 1)
        far_b = shift_tp(right_b, 3)
        acc = project(offs[1:3], ((left_a, left_b), (right_a, right_b)), weights, acc)

    with jax.named_scope("weight_rows"):
        share = feats // 32
        key_rows, value_rows, _ = lax.optimization_barrier((w_key, value_weight, own_acc))
        cut = []
        for d in DIST:
            start = feats * ((tp + d) % 4) + share * me
            piece = jnp.concatenate(
                [lax.dynamic_slice_in_dim(w, start, share, 0) for w in (key_rows, value_rows)],
                axis=1,
            )
            cut.append(shift_tp(piece, d) if d else piece)
        cut = jnp.stack(cut)

    far_a, far_b, acc, cut = lax.optimization_barrier((far_a, far_b, acc, cut))
    gain_q, gain_k = gain_query[None, :], gain_key[None, :]
    q_rot, q_raw, k_rot, k_raw, value, squares = project_end(
        offs[3:], far_a, far_b, weights, acc, cosine, sine, gain_q, gain_k
    )
    with jax.named_scope("norm_sums"):
        squares = sum_tp(squares)
    query_inv = lax.rsqrt(squares[0] / Q_CHANNELS + 1e-06)[:, None]
    key_inv = lax.rsqrt(squares[1] / K_CHANNELS + 1e-06)[:, None]
    key = (k_rot * key_inv).astype(BF)

    with jax.named_scope("gather_keys_values"):
        first_core = my_c == 0
        mine = jnp.where(first_core, key, value)
        pair = join(mine, swap_core(jnp.where(first_core, value, key)))
        plane = join(*shifts(shift_first, pair))
        mine = shifts(shift_second, plane)
    with jax.named_scope("weight_rows"):
        w_rows = lax.all_gather(after(cut, pair), "ctx", axis=0, tiled=False)

    query_unit = q_raw * query_inv
    key_unit = (k_raw * key_inv).astype(BF)
    query = (
        (q_rot.reshape(2, G, SPAN, D) * query_inv.reshape(2, 1, SPAN, 1)).astype(BF).reshape(2, R, D)
    )
    with jax.named_scope("gather_key_units"):
        key_units = shifts(shift_tp, key_unit)

    with jax.named_scope("gather_out_grad"):
        grad_part = lax.all_gather(after(out_grad, far_a, far_b), "tp", axis=1, tiled=True)

    with jax.named_scope("swap_keys_values"):
        last, query, query_unit, *key_units = lax.optimization_barrier(
            (mine[3], query, query_unit, *key_units)
        )
        mine = mine[:3] + [last]
        pieces = (*mine, *(swap_core(x) for x in mine))

    log_total, heads, kv, out_partial = attn_fwd(table, own, query, pieces, w_out)
    attn_out = lax.psum_scatter(out_partial, "tp", scatter_dimension=0, tiled=False)

    up_query, mix_query, gain_part, mine, theirs = attn_bwd(
        table, own, query, kv, grad_part, w_out, heads, log_total,
        cosine, sine, gain_q, query_unit,
    )

    with jax.named_scope("sum_key_value_grads"):
        mix_query = sum_tp(mix_query)
        gain_key_part = key_gain_of(table, own, kv, mine, theirs, tables) / gain_k
        gains = jnp.concatenate([gain_part, gain_key_part], axis=1)
        received, mix_query, w_rows, gains = lax.optimization_barrier(
            (swap_core(theirs), mix_query, w_rows, gains)
        )
        summed = mine.astype(F32) + received.astype(F32)
        sent, total = outgoing(summed)
        *sent, gains = lax.optimization_barrier((*sent, gains))
        arrived = [shift_first(x, d) for x, d in zip(sent, DIST[1:])]
        *arrived, gains, attn_out = lax.optimization_barrier(
            (*arrived, sum_core_z(gains), attn_out)
        )
        sent, total = outgoing(add_up(total, arrived))
        *sent, gains = lax.optimization_barrier((*sent, gains))
        arrived = [shift_second(x, d) for x, d in zip(sent, DIST[1:])]
        *arrived, gains = lax.optimization_barrier((*arrived, sum_y(gains)))
        total = add_up(total, arrived)
        ours, its = total[:rows], total[rows:]
        kept = jnp.where(first_core, ours, its)
        swapped = swap_core(jnp.where(first_core, its, ours))
        key_grad_rot = jnp.where(first_core, kept, swapped)
        value_grad = jnp.where(first_core, swapped, kept).astype(BF)

    with jax.named_scope("query_side"):
        query_partial = query_partial_of(
            up_query, query_unit, mix_query, query_inv.reshape(1, rows), w_query
        )
        query_side = lax.psum_scatter(query_partial, "tp", scatter_dimension=0, tiled=False)

    with jax.named_scope("key_value_side"):
        first, second = key_grad_rot[:, : D // 2], key_grad_rot[:, D // 2 :]
        cs, sn = cosine[:, : D // 2], sine[:, D // 2 :]
        key_grad = jnp.concatenate([first * cs + second * sn, second * cs - first * sn], axis=1)
        w_rows = after(w_rows, query_partial).transpose(1, 0, 2, 3).reshape(4, feats, 2 * D)
        key_grad, w_rows = lax.optimization_barrier((key_grad, w_rows))
        both = jnp.concatenate([(key_grad * gain_k).astype(BF), value_grad], axis=1)
        grads = shifts(shift_tp, both)
        gain_query_grad, gain_key_grad = gains[0, :R], gains[0, R:]
        input_grad = last_of(grads, key_units, key_inv, w_rows, query_side)
    return (attn_out, input_grad, gain_query_grad, gain_key_grad)


def solution(mesh):
    return jax.shard_map(
        local,
        mesh=mesh,
        in_specs=(
            P("ctx", "tp"),
            P(),
            P(None, "tp"),
            P(None, "tp"),
            P(None, "tp"),
            P("tp", None),
            P("tp"),
            P("tp"),
            P("ctx", "tp"),
        ),
        out_specs=(P("ctx", "tp"), P("ctx", "tp"), P("tp"), P("tp")),
        check_vma=False,
    )
```
